32 devices in a mesh: wide: 16 (over z, y, core), narrow: 2 (over x).
Axes of the slice: x: 2, y: 2, z: 4, core: 2. Of those that a mesh axis runs over, the one named last changes fastest.
Arguments:
- hidden: bfloat16 [16384, 768], P('wide'), may hold values from -6 to 6
- encoded: bfloat16 [24576, 768], P('wide'), may hold values from -6 to 6
- retrieved: int32 [128, 8], P('wide'), may hold values from 0 to 191, as said below
- self_query: bfloat16 [768, 768], P(None, 'narrow'), may hold values from -0.21875 to 0.21875
- self_key: bfloat16 [768, 768], P(None, 'narrow'), may hold values from -0.21875 to 0.21875
- self_value: bfloat16 [768, 768], P(None, 'narrow'), may hold values from -0.21875 to 0.21875
- self_out: bfloat16 [768, 768], P('narrow'), may hold values from -1.25 to 1.25
- cross_query: bfloat16 [768, 768], P(None, 'narrow'), may hold values from -0.21875 to 0.21875
- cross_key: bfloat16 [768, 768], P(None, 'narrow'), may hold values from -0.21875 to 0.21875
- cross_value: bfloat16 [768, 768], P(None, 'narrow'), may hold values from -0.21875 to 0.21875
- cross_out: bfloat16 [768, 768], P('narrow'), may hold values from -1.75 to 1.75
- expand_weight: bfloat16 [768, 3072], P(None, 'narrow'), may hold values from -0.21875 to 0.21875
- reduce_weight: bfloat16 [3072, 768], P('narrow'), may hold values from -0.109375 to 0.109375
- first_gain: float32 [768], replicated, may hold values from 0.5 to 1.5
- first_shift: float32 [768], replicated, may hold values from -1.5 to 1.5
- second_gain: float32 [768], replicated, may hold values from 0.5 to 1.5
- second_shift: float32 [768], replicated, may hold values from -1.5 to 1.5
- third_gain: float32 [768], replicated, may hold values from 0.5 to 1.5
- third_shift: float32 [768], replicated, may hold values from -1.5 to 1.5
- cotangent: bfloat16 [16384, 768], P('wide'), may hold values from -6 to 6
Outputs:
- output: bfloat16 [16384, 768], P('wide')
- hidden_grad: float32 [16384, 768], P('wide')
- self_query_grad: float32 [768, 768], P(None, 'narrow')
- self_key_grad: float32 [768, 768], P(None, 'narrow')
- self_value_grad: float32 [768, 768], P(None, 'narrow')
- self_out_grad: float32 [768, 768], P('narrow')
- cross_query_grad: float32 [768, 768], P(None, 'narrow')
- cross_key_grad: float32 [768, 768], P(None, 'narrow')
- cross_value_grad: float32 [768, 768], P(None, 'narrow')
- cross_out_grad: float32 [768, 768], P('narrow')
- expand_grad: float32 [768, 3072], P(None, 'narrow')
- reduce_grad: float32 [3072, 768], P('narrow')
- first_gain_grad: float32 [768], replicated
- first_shift_grad: float32 [768], replicated
- second_gain_grad: float32 [768], replicated
- second_shift_grad: float32 [768], replicated
- third_gain_grad: float32 [768], replicated
- third_shift_grad: float32 [768], replicated
The draws below stay inside these ranges and needn't reach their ends.
Inputs may be any that keep to these rules, and one draw needn't show every extreme that they name: `retrieved`: each row names 8 different encoder blocks. Encoder block e belongs to index e // 12 of wide. The rows of one index of wide name at most 8 blocks of any one index, and in every draw some index of wide has exactly 8 of its blocks named by the rows of every index.
All inputs are finite; a program needn't handle non-finite values.
Results may differ from the reference program's by a relative error of at most 0.025.
Values may be sent and summed in bfloat16 or wider, within the bound.
A program may use at most 320 MiB of HBM per device.

```python
import jax
import jax.numpy as jnp
from jax import lax

D = 768
HEADS = 12
HEAD_DIM = 64
FF = 3072
ENC_DEV = 1536
QUERY_ROWS = 128
BLOCK_ROWS = 128
RET_BLOCKS = 8
LENGTH = 1024
SEQS = 16
TOKENS = 16384
ENC = 24576
EBLOCKS = 192
LIVE = 64
CAPACITY = 8
HOT = 2
N_WIDE = 16


def draw_retrieved(key, part):
    key = jax.random.fold_in(key, 7)
    key_hot, key_base, key_rows = jax.random.split(key, 3)
    blocks_dev = ENC_DEV // BLOCK_ROWS
    ranking = jax.random.permutation(key_hot, N_WIDE)
    hot_flag = jnp.zeros((N_WIDE,), jnp.int32).at[ranking[:HOT]].set(1)
    offsets = jax.random.randint(key_base, (N_WIDE,), 0, blocks_dev)
    slot_count = N_WIDE * CAPACITY

    def one_index(sub_key):
        key_score, key_order = jax.random.split(sub_key)
        scores = jax.random.randint(key_score, (N_WIDE, CAPACITY), 0, 1000) + hot_flag[:, None] * 100000
        distinct = scores.reshape(-1) * slot_count + jnp.arange(slot_count, dtype=jnp.int32)
        unused, chosen = lax.top_k(distinct, LIVE)
        chosen = chosen[jax.random.permutation(key_order, LIVE)]
        owners = chosen // CAPACITY
        within = chosen % CAPACITY
        return owners * blocks_dev + (offsets[owners] + within) % blocks_dev
    requests = jax.vmap(one_index)(jax.random.split(key_rows, N_WIDE))
    return requests.reshape(N_WIDE * LIVE // RET_BLOCKS, RET_BLOCKS).astype(jnp.int32)


def level_of(own_key, extent, cuts, low, high):
    gain, own = 1.0, jax.random.fold_in(own_key, 6)
    for axis_at, blocks in cuts:
        heights = jnp.exp(jax.random.uniform(jax.random.fold_in(own, axis_at), (blocks,), jnp.float32, low / len(cuts), high / len(cuts)))
        gain = gain * jnp.repeat(heights, extent[axis_at] // blocks).reshape([-1 if axis == axis_at else 1 for axis in range(len(extent))])
    return gain


def normal_values(stream_key, shape, spread, limit, cuts=(), held_as=jnp.bfloat16):
    factor_of = level_of(stream_key, shape, cuts, -0.22, 0.18) if cuts else 1.0
    drawn = jax.random.normal(stream_key, shape, jnp.float32) * spread * factor_of
    return jnp.minimum(jnp.maximum(drawn, -limit), limit).astype(held_as)


def setup_inputs(seed: int = 0) -> dict:
    arg_keys = jax.random.split(jax.random.key(seed), 21)
    return {
        "hidden": normal_values(arg_keys[0], (TOKENS, D), 1.0, 6.0, ((0, 16),)),
        "encoded": normal_values(arg_keys[1], (ENC, D), 1.0, 6.0, ((0, 16),)),
        "retrieved": draw_retrieved(jax.random.fold_in(arg_keys[20], 71), 0),
        "self_query": normal_values(arg_keys[3], (D, D), D ** -0.5, 0.21875, ((1, 2),)),
        "self_key": normal_values(arg_keys[4], (D, D), D ** -0.5, 0.21875, ((1, 2),)),
        "self_value": normal_values(arg_keys[5], (D, D), D ** -0.5, 0.21875, ((1, 2),)),
        "self_out": normal_values(arg_keys[6], (D, D), (D // 32) ** -0.5, 1.25, ((0, 2),)),
        "cross_query": normal_values(arg_keys[7], (D, D), D ** -0.5, 0.21875, ((1, 2),)),
        "cross_key": normal_values(arg_keys[8], (D, D), D ** -0.5, 0.21875, ((1, 2),)),
        "cross_value": normal_values(arg_keys[9], (D, D), D ** -0.5, 0.21875, ((1, 2),)),
        "cross_out": normal_values(arg_keys[10], (D, D), (D // 64) ** -0.5, 1.75, ((0, 2),)),
        "expand_weight": normal_values(arg_keys[11], (D, FF), D ** -0.5, 0.21875, ((1, 2),)),
        "reduce_weight": normal_values(arg_keys[12], (FF, D), FF ** -0.5, 0.109375, ((0, 2),)),
        "first_gain": jnp.clip(1.0 + 0.1 * jax.random.normal(arg_keys[13], (D,), jnp.float32), 0.5, 1.5),
        "first_shift": normal_values(arg_keys[14], (D,), 0.3, 1.5, (), jnp.float32),
        "second_gain": jnp.clip(1.0 + 0.1 * jax.random.normal(arg_keys[15], (D,), jnp.float32), 0.5, 1.5),
        "second_shift": normal_values(arg_keys[16], (D,), 0.3, 1.5, (), jnp.float32),
        "third_gain": jnp.clip(1.0 + 0.1 * jax.random.normal(arg_keys[17], (D,), jnp.float32), 0.5, 1.5),
        "third_shift": normal_values(arg_keys[18], (D,), 0.3, 1.5, (), jnp.float32),
        "cotangent": normal_values(arg_keys[19], (TOKENS, D), 1.0, 6.0, ((0, 16),)),
    }


highest = lax.Precision.HIGHEST
epsilon = 1e-05

@jax.custom_vjp
def low(v):
    return lax.optimization_barrier(v.astype(jnp.bfloat16)).astype(jnp.float32)

@jax.custom_vjp
def low_back(v):
    return v

def low_keep(v):
    return (low(v), None)

def low_pass(kept, grad):
    return (grad,)

def back_keep(v):
    return (v, None)

def back_low(kept, grad):
    return (low(grad),)
low.defvjp(low_keep, low_pass)
low_back.defvjp(back_keep, back_low)

def round_both(values_in):
    return low_back(low(values_in))

def product(left, right):
    return jnp.dot(left, right, precision=highest, preferred_element_type=jnp.float32)

def layer_norm(summed, norm_gain, norm_shift):
    average = lax.optimization_barrier(jnp.mean(summed, axis=-1, keepdims=True))
    centred = summed - average
    inverse = lax.rsqrt(lax.optimization_barrier(jnp.mean(centred * centred, axis=-1, keepdims=True)) + epsilon)
    return centred * inverse * norm_gain + norm_shift

def self_sequence(items):
    queries, key_rows, value_rows = items
    length_now = queries.shape[0]
    factor = HEAD_DIM ** (-0.5)
    scores = low_back(jnp.einsum('qhd,khd->hqk', queries, key_rows, precision=highest) * factor)
    causal = jnp.arange(length_now)[:, None] >= jnp.arange(length_now)[None, :]
    scores = jnp.where(causal[None], scores, -1e+30)
    chances = low(jax.nn.softmax(scores, axis=-1))
    return jnp.einsum('hqk,khd->qhd', chances, value_rows, precision=highest)

def forward(encoded_float, retrieved, hidden, self_query, self_key, self_value, self_out, cross_query, cross_key, cross_value, cross_out, expand_weight, reduce_weight, first_gain, first_shift, second_gain, second_shift, third_gain, third_shift):

    def split_heads(flat):
        return flat.reshape(SEQS, LENGTH, HEADS, HEAD_DIM)
    hidden_low = low(hidden)
    query_self = split_heads(round_both(product(hidden_low, self_query)))
    key_self = split_heads(round_both(product(hidden_low, self_key)))
    value_self = split_heads(round_both(product(hidden_low, self_value)))
    attended = lax.map(jax.checkpoint(self_sequence), (query_self, key_self, value_self))
    attended = round_both(attended.reshape(TOKENS, D))
    self_result = low_back(product(attended, self_out))
    first = layer_norm(hidden + self_result, first_gain, first_shift)
    first_low = low(first)
    query_cross = split_heads(round_both(product(first_low, cross_query)))
    enc_keys = low(product(encoded_float, cross_key)).reshape(EBLOCKS, BLOCK_ROWS, HEADS, HEAD_DIM)
    enc_values = low(product(encoded_float, cross_value)).reshape(EBLOCKS, BLOCK_ROWS, HEADS, HEAD_DIM)
    picked_all = retrieved.reshape(SEQS, LENGTH // QUERY_ROWS, RET_BLOCKS)

    def cross_sequence(items):
        queries, picked = items
        blocks_q = queries.reshape(-1, QUERY_ROWS, HEADS, HEAD_DIM)
        count_q = blocks_q.shape[0]
        key_rows = enc_keys[picked].reshape(count_q, RET_BLOCKS * BLOCK_ROWS, HEADS, HEAD_DIM)
        value_rows = enc_values[picked].reshape(count_q, RET_BLOCKS * BLOCK_ROWS, HEADS, HEAD_DIM)
        factor = HEAD_DIM ** (-0.5)
        scores = low_back(jnp.einsum('bqhd,bkhd->bhqk', blocks_q, key_rows, precision=highest) * factor)
        chances = low(jax.nn.softmax(scores, axis=-1))
        blended = jnp.einsum('bhqk,bkhd->bqhd', chances, value_rows, precision=highest)
        return blended.reshape(LENGTH, HEADS, HEAD_DIM)
    crossed = lax.map(jax.checkpoint(cross_sequence), (query_cross, picked_all))
    crossed = round_both(crossed.reshape(TOKENS, D))
    cross_result = low_back(product(crossed, cross_out))
    second = layer_norm(first + cross_result, second_gain, second_shift)
    second_low = low(second)
    pre_act = low_back(product(second_low, expand_weight))
    activated = low(jax.nn.gelu(pre_act, approximate=False))
    ffn_result = low_back(product(activated, reduce_weight))
    return layer_norm(second + ffn_result, third_gain, third_shift)

def reference(hidden, encoded, retrieved, self_query, self_key, self_value, self_out, cross_query, cross_key, cross_value, cross_out, expand_weight, reduce_weight, first_gain, first_shift, second_gain, second_shift, third_gain, third_shift, cotangent):
    params = tuple((argument.astype(jnp.float32) for argument in (hidden, self_query, self_key, self_value, self_out, cross_query, cross_key, cross_value, cross_out, expand_weight, reduce_weight, first_gain, first_shift, second_gain, second_shift, third_gain, third_shift)))
    encoded_float = encoded.astype(jnp.float32)

    def wrapped(*inputs):
        return forward(encoded_float, retrieved, *inputs)
    final, pullback = jax.vjp(wrapped, *params)
    grads = pullback(cotangent.astype(jnp.float32))
    return (final.astype(jnp.bfloat16), grads[0], grads[1], grads[2], grads[3], grads[4], grads[5], grads[6], grads[7], grads[8], grads[9], grads[10], grads[11], grads[12], grads[13], grads[14], grads[15], grads[16])
```

```python
import functools

import jax
import jax.numpy as jnp
from jax import lax
from jax.experimental import pallas as pl
from jax.experimental.pallas import tpu as pltpu
from jax.sharding import PartitionSpec as P

HEAD_DIM = 64
BLOCK_ROWS = 128
RET_BLOCKS = 8
PAIR = 2 * HEAD_DIM
VMEM_LIMIT = 56 << 20

epsilon = 1e-05
bf16 = jnp.bfloat16
f32 = jnp.float32
MESH = pl.DeviceIdType.MESH


def norm_forward(summed, norm_gain, norm_shift):
    average = jnp.mean(summed, axis=-1, keepdims=True)
    centred = summed - average
    inverse = lax.rsqrt(jnp.mean(centred * centred, axis=-1, keepdims=True) + epsilon)
    normal = centred * inverse
    return (normal * norm_gain + norm_shift, normal, inverse)


def norm_backward(grad_out, normal, inverse, norm_gain):
    scaled = grad_out * norm_gain
    grad_in = inverse * (
        scaled
        - jnp.mean(scaled, axis=-1, keepdims=True)
        - normal * jnp.mean(scaled * normal, axis=-1, keepdims=True)
    )
    return (grad_in, jnp.sum(grad_out * normal, axis=0), jnp.sum(grad_out, axis=0))


def gelu_slope(pre_act):
    return (
        0.5 * (1.0 + lax.erf(pre_act * 0.7071067811865476))
        + pre_act * jnp.exp(-0.5 * pre_act * pre_act) * 0.3989422804014327
    )


def project(rows_in, weight):
    return jnp.dot(rows_in, weight, preferred_element_type=f32)


def grad_weight(left, right):
    return jnp.einsum("ti,to->io", left, right, preferred_element_type=f32)


def grad_input(grad_rows, weight):
    return jnp.einsum("to,io->ti", grad_rows, weight, preferred_element_type=f32)


def dot_nt(left, right):
    return lax.dot_general(left, right, (((1,), (1,)), ((), ())), preferred_element_type=f32)


def dot_tn(left, right):
    return lax.dot_general(left, right, (((0,), (0,)), ((), ())), preferred_element_type=f32)


def dot_nn(left, right):
    return lax.dot_general(left, right, (((1,), (0,)), ((), ())), preferred_element_type=f32)


def stack_heads(pair_rows):
    lane = lax.broadcasted_iota(jnp.int32, pair_rows.shape, 1)
    wide_rows = pair_rows.astype(f32)
    zero = jnp.zeros_like(wide_rows)
    return jnp.concatenate(
        [
            jnp.where(lane < HEAD_DIM, wide_rows, zero).astype(bf16),
            jnp.where(lane < HEAD_DIM, zero, wide_rows).astype(bf16),
        ],
        axis=0,
    )


def merge_heads(both):
    rows = both.shape[1] // 2
    sublane = lax.broadcasted_iota(jnp.int32, (PAIR, rows), 0)
    return jnp.transpose(jnp.where(sublane < HEAD_DIM, both[:, :rows], both[:, rows:]))


def causal_edge(rows):
    key = lax.broadcasted_iota(jnp.int32, (rows, 2 * rows), 0)
    query = lax.broadcasted_iota(jnp.int32, (rows, 2 * rows), 1)
    return key <= jnp.where(query >= rows, query - rows, query)


def scaled_heads(pair_rows):
    return stack_heads(pair_rows.astype(f32) * HEAD_DIM**-0.5)


def pair_forward(queries, keys, values, edge):
    stacked = scaled_heads(queries)
    scores = dot_nt(keys, stacked)
    if edge is not None:
        split = keys.shape[0] - edge.shape[0]
        last = jnp.where(edge, scores[split:], -1e30)
        scores = jnp.concatenate([scores[:split], last], axis=0) if split else last
    top = jnp.max(scores, axis=0, keepdims=True)
    raised = jnp.exp(scores - top)
    total = jnp.sum(raised, axis=0, keepdims=True)
    blended = dot_tn(values, raised.astype(bf16)) / total
    return merge_heads(blended).astype(bf16), top + jnp.log(total)


def pair_backward(queries, keys, values, edge, log_total, blended, grad_blend):
    rows = queries.shape[0]
    stacked = scaled_heads(queries)
    grads = stack_heads(grad_blend)
    scores = dot_nt(keys, stacked)
    if edge is not None:
        split = keys.shape[0] - edge.shape[0]
        last = jnp.where(edge, scores[split:], -1e30)
        scores = jnp.concatenate([scores[:split], last], axis=0) if split else last
    chances = jnp.exp(scores - log_total)
    weighed = jnp.transpose(blended.astype(f32) * grad_blend.astype(f32))
    centre = jnp.concatenate(
        [
            jnp.sum(weighed[:HEAD_DIM], axis=0, keepdims=True),
            jnp.sum(weighed[HEAD_DIM:], axis=0, keepdims=True),
        ],
        axis=1,
    )
    grad_scores = (chances * (dot_nt(values, grads) - centre)).astype(bf16)
    grad_values = dot_nn(chances.astype(bf16), grads)
    grad_keys = dot_nn(grad_scores, stacked)
    grad_queries = merge_heads(dot_tn(keys, grad_scores)) * HEAD_DIM**-0.5
    return grad_queries, grad_keys, grad_values


def self_variants(narrow, at):
    for n in range(narrow):
        yield 0, n + 1, at == n
        yield 1, 2 * narrow - n, at == n


def self_forward_kernel(narrow, at_ref, q_ref, k_ref, v_ref, o_ref, log_ref):
    rows = q_ref.shape[0] // 2
    for chunk, seen, taken in self_variants(narrow, at_ref[0]):

        @pl.when(taken)
        def _():
            mine = pl.ds(chunk * rows, rows)
            keys = pl.ds(0, seen * rows)
            blended, log_total = pair_forward(
                q_ref[mine], k_ref[keys], v_ref[keys], causal_edge(rows)
            )
            o_ref[mine] = blended
            log_ref[0, pl.ds(chunk, 1)] = log_total


def self_forward(narrow, at, queries, keys, values):
    rows, width = queries.shape
    total_rows = keys.shape[0]
    pairs = width // PAIR
    pair = lambda count: pl.BlockSpec((count, PAIR), lambda g, at: (0, g))
    return pl.pallas_call(
        functools.partial(self_forward_kernel, narrow),
        grid_spec=pltpu.PrefetchScalarGridSpec(
            num_scalar_prefetch=1,
            grid=(pairs,),
            in_specs=[pair(rows), pair(total_rows), pair(total_rows)],
            out_specs=[pair(rows), pl.BlockSpec((1, 2, rows), lambda g, at: (g, 0, 0))],
        ),
        out_shape=[
            jax.ShapeDtypeStruct((rows, width), bf16),
            jax.ShapeDtypeStruct((pairs, 2, rows), f32),
        ],
        compiler_params=pltpu.CompilerParams(vmem_limit_bytes=VMEM_LIMIT),
        name="self_forward",
    )(at, queries, keys, values)


def self_backward_kernel(
    narrow, at_ref, q_ref, k_ref, v_ref, log_ref, o_ref, g_ref, dq_ref, dk_ref, dv_ref, dk_sum, dv_sum
):
    rows = q_ref.shape[0] // 2
    dk_sum[...] = jnp.zeros_like(dk_sum)
    dv_sum[...] = jnp.zeros_like(dv_sum)
    for chunk, seen, taken in self_variants(narrow, at_ref[0]):

        @pl.when(taken)
        def _():
            mine = pl.ds(chunk * rows, rows)
            keys = pl.ds(0, seen * rows)
            grad_q, grad_k, grad_v = pair_backward(
                q_ref[mine],
                k_ref[keys],
                v_ref[keys],
                causal_edge(rows),
                log_ref[0, pl.ds(chunk, 1)],
                o_ref[mine],
                g_ref[mine],
            )
            dq_ref[mine] = grad_q.astype(bf16)
            dk_sum[keys] += grad_k
            dv_sum[keys] += grad_v

    dk_ref[...] = dk_sum[...].astype(bf16)
    dv_ref[...] = dv_sum[...].astype(bf16)


def self_backward(narrow, at, queries, keys, values, logs, blended, grads):
    rows, width = queries.shape
    total_rows = keys.shape[0]
    pairs = width // PAIR
    pair = lambda count: pl.BlockSpec((count, PAIR), lambda g, at: (0, g))
    return pl.pallas_call(
        functools.partial(self_backward_kernel, narrow),
        grid_spec=pltpu.PrefetchScalarGridSpec(
            num_scalar_prefetch=1,
            grid=(pairs,),
            in_specs=[
                pair(rows),
                pair(total_rows),
                pair(total_rows),
                pl.BlockSpec((1, 2, rows), lambda g, at: (g, 0, 0)),
                pair(rows),
                pair(rows),
            ],
            out_specs=[pair(rows), pair(total_rows), pair(total_rows)],
            scratch_shapes=[pltpu.VMEM((total_rows, PAIR), f32)] * 2,
        ),
        out_shape=[
            jax.ShapeDtypeStruct((rows, width), bf16),
            jax.ShapeDtypeStruct((total_rows, width), bf16),
            jax.ShapeDtypeStruct((total_rows, width), bf16),
        ],
        compiler_params=pltpu.CompilerParams(vmem_limit_bytes=VMEM_LIMIT),
        name="self_backward",
    )(at, queries, keys, values, logs, blended, grads)


def cross_forward_kernel(picked_ref, *refs):
    blocks = refs[:RET_BLOCKS]
    wk_ref, wv_ref, q_ref, o_ref, log_ref, k_ref, v_ref, rows_in = refs[RET_BLOCKS:]
    for j in range(RET_BLOCKS):
        rows_in[pl.ds(j * BLOCK_ROWS, BLOCK_ROWS)] = blocks[j][...]
    k_ref[...] = dot_nn(rows_in[...], wk_ref[...]).astype(bf16)
    v_ref[...] = dot_nn(rows_in[...], wv_ref[...]).astype(bf16)
    for g in range(q_ref.shape[1] // PAIR):
        lanes = pl.ds(g * PAIR, PAIR)
        blended, log_total = pair_forward(q_ref[:, lanes], k_ref[:, lanes], v_ref[:, lanes], None)
        o_ref[:, lanes] = blended
        log_ref[0, pl.ds(g, 1)] = log_total


def block_specs(width):
    def spec(j):
        return pl.BlockSpec((BLOCK_ROWS, width), lambda b, picked: (picked[b * RET_BLOCKS + j], 0))

    return [spec(j) for j in range(RET_BLOCKS)]


def cross_forward(picked, everything, cross_key, cross_value, queries):
    rows, width = queries.shape
    count = rows // BLOCK_ROWS
    pairs = width // PAIR
    keys = RET_BLOCKS * BLOCK_ROWS
    whole = pl.BlockSpec((width, width), lambda b, picked: (0, 0))
    by_block = pl.BlockSpec((BLOCK_ROWS, width), lambda b, picked: (b, 0))
    by_keys = pl.BlockSpec((keys, width), lambda b, picked: (b, 0))
    return pl.pallas_call(
        cross_forward_kernel,
        grid_spec=pltpu.PrefetchScalarGridSpec(
            num_scalar_prefetch=1,
            grid=(count,),
            in_specs=block_specs(width) + [whole, whole, by_block],
            out_specs=[
                by_block,
                pl.BlockSpec((1, pairs, 2 * BLOCK_ROWS), lambda b, picked: (b, 0, 0)),
                by_keys,
                by_keys,
            ],
            scratch_shapes=[pltpu.VMEM((keys, width), bf16)],
        ),
        out_shape=[
            jax.ShapeDtypeStruct((rows, width), bf16),
            jax.ShapeDtypeStruct((count, pairs, 2 * BLOCK_ROWS), f32),
            jax.ShapeDtypeStruct((count * keys, width), bf16),
            jax.ShapeDtypeStruct((count * keys, width), bf16),
        ],
        compiler_params=pltpu.CompilerParams(vmem_limit_bytes=VMEM_LIMIT),
        name="cross_forward",
    )(picked, *([everything] * RET_BLOCKS), cross_key, cross_value, queries)


def cross_backward_kernel(picked_ref, *refs):
    blocks = refs[:RET_BLOCKS]
    (k_ref, v_ref, q_ref, log_ref, o_ref, g_ref, dq_ref, dwk_ref, dwv_ref, rows_in, both, sums) = refs[
        RET_BLOCKS:
    ]
    width = q_ref.shape[1]
    step = pl.program_id(0)

    @pl.when(step == 0)
    def _():
        sums[...] = jnp.zeros_like(sums)

    for j in range(RET_BLOCKS):
        rows_in[pl.ds(j * BLOCK_ROWS, BLOCK_ROWS)] = blocks[j][...]
    for g in range(width // PAIR):
        lanes = pl.ds(g * PAIR, PAIR)
        grad_q, grad_k, grad_v = pair_backward(
            q_ref[:, lanes],
            k_ref[:, lanes],
            v_ref[:, lanes],
            None,
            log_ref[0, pl.ds(g, 1)],
            o_ref[:, lanes],
            g_ref[:, lanes],
        )
        dq_ref[:, lanes] = grad_q.astype(bf16)
        both[:, lanes] = grad_k.astype(bf16)
        both[:, pl.ds(width + g * PAIR, PAIR)] = grad_v.astype(bf16)
    sums[...] += dot_tn(rows_in[...], both[...])

    @pl.when(step == pl.num_programs(0) - 1)
    def _():
        dwk_ref[...] = sums[:, :width].astype(bf16)
        dwv_ref[...] = sums[:, width:].astype(bf16)


def cross_backward(picked, everything, keys_in, values_in, queries, logs, blended, grads):
    rows, width = queries.shape
    count = rows // BLOCK_ROWS
    pairs = width // PAIR
    keys = RET_BLOCKS * BLOCK_ROWS
    whole = pl.BlockSpec((width, width), lambda b, picked: (0, 0))
    by_block = pl.BlockSpec((BLOCK_ROWS, width), lambda b, picked: (b, 0))
    by_keys = pl.BlockSpec((keys, width), lambda b, picked: (b, 0))
    return pl.pallas_call(
        cross_backward_kernel,
        grid_spec=pltpu.PrefetchScalarGridSpec(
            num_scalar_prefetch=1,
            grid=(count,),
            in_specs=block_specs(width)
            + [
                by_keys,
                by_keys,
                by_block,
                pl.BlockSpec((1, pairs, 2 * BLOCK_ROWS), lambda b, picked: (b, 0, 0)),
                by_block,
                by_block,
            ],
            out_specs=[by_block, whole, whole],
            scratch_shapes=[
                pltpu.VMEM((keys, width), bf16),
                pltpu.VMEM((keys, 2 * width), bf16),
                pltpu.VMEM((width, 2 * width), f32),
            ],
        ),
        out_shape=[
            jax.ShapeDtypeStruct((rows, width), bf16),
            jax.ShapeDtypeStruct((width, width), bf16),
            jax.ShapeDtypeStruct((width, width), bf16),
        ],
        compiler_params=pltpu.CompilerParams(vmem_limit_bytes=VMEM_LIMIT),
        name="cross_backward",
    )(
        picked,
        *([everything] * RET_BLOCKS),
        keys_in,
        values_in,
        queries,
        logs,
        blended,
        grads,
    )


COLUMNS = (0, 1, 2, 4, 5, 6, 8)


LINE = 4


class Place:
    def __init__(self):
        wide = lax.axis_index("wide")
        self.x = lax.axis_index("narrow")
        self.core = lax.rem(wide, 2)
        self.y = lax.rem(lax.div(wide, 2), 2)
        self.z = lax.div(wide, 4)
        self.wide = wide

    def at(self, z=None, y=None, core=None, x=None):
        z, y = (self.z if z is None else z), (self.y if y is None else y)
        core = self.core if core is None else core
        return (z * 4 + y * 2 + core, self.x if x is None else x)

    def greet(self):
        barrier = pltpu.get_barrier_semaphore()
        targets = [self.at(core=1 - self.core), self.at(y=1 - self.y), self.at(x=1 - self.x)]
        targets += [self.at(z=lax.rem(self.z + step, LINE)) for step in range(1, LINE)]
        for target in targets:
            pl.semaphore_signal(barrier, inc=1, device_id=target, device_id_type=MESH)
        pl.semaphore_wait(barrier, len(targets))


def gather_kernel(a_rows, b_rows, *refs):
    encoded, weights = refs[0], refs[1:11]
    everything, full = refs[11], refs[12:22]
    (own_sem, half_sem, flow_send, flow_recv, weight_send, weight_recv) = refs[22:]
    me = Place()
    rows = encoded.shape[0]
    x, y, z, core = me.x, me.y, me.z, me.core
    low, high = z > 0, z < LINE - 1
    UP_A, DOWN_A, Y_A, UP_B, DOWN_B, Y_B, X_B, CORE_A, CORE_B = range(9)

    own = pltpu.make_async_copy(
        encoded, everything.at[pl.ds(pl.multiple_of(me.wide * rows, 128), rows)], own_sem
    )
    own.start()

    def region(i, ref, plane, part):
        if i in COLUMNS:
            count, columns = ref.shape[0], ref.shape[1] // 2
            start = pl.multiple_of(plane * columns, 128)
            if part is None:
                return ref.at[:, pl.ds(start, columns)]
            first = pl.multiple_of(part * (count // 2), 16)
            return ref.at[pl.ds(first, count // 2), pl.ds(start, columns)]
        count = ref.shape[0] // 2
        if part is None:
            return ref.at[pl.ds(pl.multiple_of(plane * count, 16), count)]
        first = pl.multiple_of(plane * count + part * (count // 2), 16)
        return ref.at[pl.ds(first, count // 2)]

    halves = []
    for i in range(10):
        halves.append(
            pltpu.make_async_copy(weights[i], region(i, full[i], x, None), half_sem.at[i])
        )
        halves[-1].start()

    me.greet()
    own.wait()

    def flow(kind, owner_z, owner_y, plane, target, from_core=None):
        owner = owner_z * 2 + owner_y
        start = owner * (2 * rows) + (core if from_core is None else from_core) * rows
        if plane is None:
            size, slot = a_rows, owner
        else:
            start = start + a_rows + plane * b_rows
            size, slot = b_rows, owner + (plane * 8 if kind == CORE_B else 0)
        piece = everything.at[pl.ds(pl.multiple_of(start, 16), size)]
        return pltpu.make_async_remote_copy(
            src_ref=piece,
            dst_ref=piece,
            send_sem=flow_send.at[kind, slot],
            recv_sem=flow_recv.at[kind, slot],
            device_id=target,
            device_id_type=MESH,
        )

    sibling = me.at(core=1 - core)
    beside = me.at(y=1 - y)
    across = me.at(x=1 - x)
    above, below = me.at(z=z + 1), me.at(z=z - 1)

    def up_a(oz):
        return flow(UP_A, oz, y, None, above)

    def down_a(oz):
        return flow(DOWN_A, oz, y, None, below)

    def up_b(oz, oy):
        return flow(UP_B, oz, oy, x, above)

    def down_b(oz, oy):
        return flow(DOWN_B, oz, oy, x, below)

    def y_a(oz, oy):
        return flow(Y_A, oz, oy, None, beside)

    def y_b(oy):
        return flow(Y_B, z, oy, x, beside)

    def x_b(oz, oy, plane):
        return flow(X_B, oz, oy, plane, across)

    def core_a(oz, oy, from_core=None):
        return flow(CORE_A, oz, oy, None, sibling, from_core)

    def core_b(oz, oy, plane, from_core=None):
        return flow(CORE_B, oz, oy, plane, sibling, from_core)

    def weight(way, i, plane, part):
        piece = region(i, full[i], plane, part)
        if way == 0:
            piece_in = weights[i]
            count = piece_in.shape[0] // 2
            piece_in = piece_in.at[pl.ds(pl.multiple_of(part * count, 16), count)]
        else:
            piece_in = piece
        return pltpu.make_async_remote_copy(
            src_ref=piece_in,
            dst_ref=piece,
            send_sem=weight_send.at[way, i],
            recv_sem=weight_recv.at[way, i],
            device_id=across if way == 0 else sibling,
            device_id_type=MESH,
        )

    y_b(y).start()
    y_a(z, y).start()
    pl.when(high)(lambda: up_a(z).start())
    pl.when(low)(lambda: down_a(z).start())
    core_a(z, y).start()
    core_b(z, y, 0).start()
    core_b(z, y, 1).start()
    for i in range(10):
        weight(0, i, x, core).start()

    y_b(1 - y).wait_recv()
    core_b(z, 1 - y, x).start()
    x_b(z, 1 - y, x).start()

    def beside_arrives(oz):
        y_a(oz, 1 - y).wait_recv()
        core_a(oz, 1 - y).start()

    def pass_a(oz, arrived, onward, further):
        arrived(oz).wait_recv()
        pl.when(onward)(lambda: further(oz).start())
        y_a(oz, y).start()
        core_a(oz, y).start()

    def pass_b(oz, arrived, onward, further):
        for oy in (y, 1 - y):
            arrived(oz, oy).wait_recv()
            pl.when(onward)(lambda: further(oz, oy).start())
            x_b(oz, oy, x).start()
            core_b(oz, oy, x).start()

    for step in range(LINE):
        for kind, back in ((0, 1), (1, 0)):
            under, over = z - back - step, z + back + step
            if kind == 0 and step < LINE - 1:
                pl.when(under >= 0)(lambda: pass_a(under, up_a, high, up_a))
                pl.when(over < LINE)(lambda: pass_a(over, down_a, low, down_a))
            if kind == 1 and step == 0:
                for oy in (y, 1 - y):
                    pl.when(high)(lambda oy=oy: up_b(z, oy).start())
                    pl.when(low)(lambda oy=oy: down_b(z, oy).start())
            if kind == 1 and step > 0:
                pl.when(under >= 0)(lambda: pass_b(under, up_b, high, up_b))
                pl.when(over < LINE)(lambda: pass_b(over, down_b, low, down_b))
    for i in range(10):
        weight(0, i, 1 - x, core).wait_recv()
        weight(1, i, 1 - x, core).start()
    beside_arrives(z)
    for step in range(1, LINE):
        pl.when(z - step >= 0)(lambda: beside_arrives(z - step))
        pl.when(z + step < LINE)(lambda: beside_arrives(z + step))

    def across_arrives(oz, oy):
        x_b(oz, oy, 1 - x).wait_recv()
        core_b(oz, oy, 1 - x).start()

    across_arrives(z, 1 - y)
    for step in range(LINE - 1):
        under, over = z - 1 - step, z + 1 + step
        for oy in (y, 1 - y):
            pl.when(under >= 0)(lambda: across_arrives(under, oy))
            pl.when(over < LINE)(lambda: across_arrives(over, oy))

    y_b(y).wait_send()
    x_b(z, 1 - y, x).wait_send()
    for oz in range(LINE):
        y_a(oz, y).wait_send()
        for oy in range(2):
            core_a(oz, oy).wait_send()
            core_a(oz, oy, 1 - core).wait_recv()
            for plane in range(2):
                core_b(oz, oy, plane).wait_send()
                core_b(oz, oy, plane, 1 - core).wait_recv()
        away = oz != z

        @pl.when(away)
        def _():
            for oy in range(2):
                x_b(oz, oy, x).wait_send()

        @pl.when(jnp.logical_and(high, oz <= z))
        def _():
            up_a(oz).wait_send()
            for oy in range(2):
                up_b(oz, oy).wait_send()

        @pl.when(jnp.logical_and(low, oz >= z))
        def _():
            down_a(oz).wait_send()
            for oy in range(2):
                down_b(oz, oy).wait_send()

    for i in range(10):
        halves[i].wait()
        weight(0, i, x, core).wait_send()
        weight(1, i, 1 - x, core).wait_send()
        weight(1, i, 1 - x, 1 - core).wait_recv()


def gather_by_kernel(encoded, weights):
    rows, width = encoded.shape
    a_rows = rows * 17 // 24 // 16 * 16
    b_rows = (rows - a_rows) // 2
    shapes = [jax.ShapeDtypeStruct((16 * rows, width), bf16)]
    for i, w in enumerate(weights):
        doubled = (w.shape[0], 2 * w.shape[1]) if i in COLUMNS else (2 * w.shape[0], w.shape[1])
        shapes.append(jax.ShapeDtypeStruct(doubled, bf16))
    dma = pltpu.SemaphoreType.DMA
    out = pl.pallas_call(
        functools.partial(gather_kernel, a_rows, b_rows),
        out_shape=shapes,
        in_specs=[pl.BlockSpec(memory_space=pl.ANY)] * 11,
        out_specs=[pl.BlockSpec(memory_space=pl.ANY)] * 11,
        scratch_shapes=[dma, dma((10,)), dma((9, 16)), dma((9, 16)), dma((2, 10)), dma((2, 10))],
        compiler_params=pltpu.CompilerParams(
            collective_id=0, has_side_effects=True, vmem_limit_bytes=4 << 20
        ),
        name="gather",
    )(encoded, *weights)
    return out[0], tuple(out[1:])


TILE = 384
UNITS = 16


def share_of(refs, unit, core, plane):
    narrow_units = (0, 1, 2, 4, 5, 6)
    if unit < 6:
        ref, row, column = refs[narrow_units[unit]], core * TILE, plane * TILE
    elif unit < 8:
        ref, row, column = refs[(3, 7)[unit - 6]], plane * TILE, core * TILE
    elif unit < 12:
        ref, row, column = refs[8], core * TILE, plane * 4 * TILE + (unit - 8) * TILE
    else:
        ref, row, column = refs[9], plane * 4 * TILE + (unit - 12) * TILE, core * TILE
    return ref.at[
        pl.ds(pl.multiple_of(row, 128), TILE), pl.ds(pl.multiple_of(column, 128), TILE)
    ]


def reduce_kernel(*refs):
    grads = refs[:10]
    theirs, mine, made, norms = refs[10:14]
    sums_out, mine_out, theirs_out, made_out, norms_out = refs[14:19]
    (
        own, from_core, from_x, from_y, from_z, total, rows_in, rows_got, norm_all, norm_in,
        own_sem, core_send, core_recv, x_send, x_recv, y_send, y_recv, z_send, z_recv,
        gz_send, gz_recv, gy_send, gy_recv, gc_send, gc_recv, out_sem,
        extra_send, extra_recv, norm_send, norm_recv,
    ) = refs[19:]
    me = Place()
    x, y, z, core = me.x, me.y, me.z, me.core
    half, part = TILE // 2, TILE // 2 // LINE
    sibling, beside, across = me.at(core=1 - core), me.at(y=1 - y), me.at(x=1 - x)

    def remote(src, dst, send, recv, target):
        return pltpu.make_async_remote_copy(
            src_ref=src, dst_ref=dst, send_sem=send, recv_sem=recv,
            device_id=target, device_id_type=MESH,
        )

    def own_copy(unit, plane):
        return pltpu.make_async_copy(
            share_of(grads, unit, core, plane), own.at[unit, plane], own_sem.at[unit, plane]
        )

    def to_core(unit, plane):
        return remote(
            share_of(grads, unit, 1 - core, plane), from_core.at[unit, plane],
            core_send.at[unit, plane], core_recv.at[unit, plane], sibling,
        )

    def to_x(u):
        return remote(own.at[u, 1 - x], from_x.at[u], x_send.at[u], x_recv.at[u], across)

    def to_y(u):
        rows = pl.ds(pl.multiple_of((1 - y) * half, 16), half)
        return remote(own.at[u, x, rows], from_y.at[u], y_send.at[u], y_recv.at[u], beside)

    def to_z(u, d):
        other = lax.rem(z + d, LINE)
        rows = pl.ds(pl.multiple_of(y * half + other * part, 16), part)
        return remote(
            own.at[u, x, rows], from_z.at[u, d - 1], z_send.at[u, d - 1], z_recv.at[u, d - 1],
            me.at(z=other),
        )

    def gather_z(u, d):
        rows = pl.ds(pl.multiple_of(y * half + z * part, 16), part)
        piece = total.at[u, core, rows]
        return remote(
            piece, piece, gz_send.at[u, d - 1], gz_recv.at[u, d - 1],
            me.at(z=lax.rem(z + d, LINE)),
        )

    def gathered_z(u, d):
        rows = pl.ds(pl.multiple_of(y * half + lax.rem(z + LINE - d, LINE) * part, 16), part)
        piece = total.at[u, core, rows]
        return remote(piece, piece, gz_send.at[u, d - 1], gz_recv.at[u, d - 1], beside)

    def gather_y(u, at_y):
        piece = total.at[u, core, pl.ds(pl.multiple_of(at_y * half, 16), half)]
        return remote(piece, piece, gy_send.at[u], gy_recv.at[u], beside)

    def gather_core(u, at_core):
        piece = total.at[u, at_core]
        return remote(piece, piece, gc_send.at[u], gc_recv.at[u], sibling)

    def put_out(u):
        return pltpu.make_async_copy(total.at[u], sums_out.at[u], out_sem.at[u])

    rows_copy = remote(theirs, rows_in, extra_send.at[0], extra_recv.at[0], across)
    made_copy = remote(made, made_out, extra_send.at[1], extra_recv.at[1], across)
    got_copy = remote(rows_got, theirs_out, extra_send.at[2], extra_recv.at[2], across)

    for unit in range(UNITS):
        for plane in range(2):
            own_copy(unit, plane).start()
    me.greet()
    rows_copy.start()
    for unit in range(UNITS):
        for plane in range(2):
            to_core(unit, plane).start()

    norm_all[...] = norms[...]
    along_z = tuple(me.at(z=lax.rem(z + d, LINE)) for d in range(1, LINE))
    slot = 0
    for targets in ((sibling,), (across,), (beside,), along_z):
        copies = []
        for target in targets:
            copies.append(
                remote(norm_all, norm_in.at[slot], norm_send.at[slot], norm_recv.at[slot], target)
            )
            copies[-1].start()
            slot += 1
        for copy in copies:
            copy.wait()
        for k in range(slot - len(copies), slot):
            norm_all[...] += norm_in[k]
    norms_out[...] = norm_all[...]

    for unit in range(UNITS):
        for plane in range(2):
            own_copy(unit, plane).wait()

    def plus(a, b):
        return (a.astype(f32) + b.astype(f32)).astype(bf16)

    def step(t, carry):
        def at(lag):
            u = t - lag
            return u, jnp.logical_and(u >= 0, u < UNITS)

        u0, on0 = at(0)

        @pl.when(on0)
        def _():
            for plane in range(2):
                to_core_wait(u0, plane)
            own[u0] = plus(own[u0], from_core[u0])
            to_x(u0).start()

        u1, on1 = at(2)

        @pl.when(on1)
        def _():
            to_x(u1).wait()
            own[u1, x] = plus(own[u1, x], from_x[u1])
            to_y(u1).start()

        u2, on2 = at(3)

        @pl.when(on2)
        def _():
            to_y(u2).wait()
            rows = pl.ds(pl.multiple_of(y * half, 16), half)
            own[u2, x, rows] = plus(own[u2, x, rows], from_y[u2])
            for d in range(1, LINE):
                to_z(u2, d).start()

        u3, on3 = at(4)

        @pl.when(on3)
        def _():
            for d in range(1, LINE):
                to_z(u3, d).wait()
            rows = pl.ds(pl.multiple_of(y * half + z * part, 16), part)
            summed = own[u3, x, rows].astype(f32)
            for d in range(1, LINE):
                summed += from_z[u3, d - 1].astype(f32)
            total[u3, core, rows] = summed.astype(bf16)
            for d in range(1, LINE):
                gather_z(u3, d).start()

        u4, on4 = at(5)

        @pl.when(on4)
        def _():
            for d in range(1, LINE):
                gathered_z(u4, d).wait_recv()
                gather_z(u4, d).wait_send()
            gather_y(u4, y).start()

        u5, on5 = at(6)

        @pl.when(on5)
        def _():
            gather_y(u5, 1 - y).wait_recv()
            gather_y(u5, y).wait_send()
            gather_core(u5, core).start()

        u6, on6 = at(7)

        @pl.when(on6)
        def _():
            gather_core(u6, 1 - core).wait_recv()
            gather_core(u6, core).wait_send()
            put_out(u6).start()

        @pl.when(t == UNITS)
        def _():
            rows_copy.wait()
            summed = mine[...] + rows_in[...].astype(f32)
            mine_out[...] = summed
            rows_got[...] = summed.astype(bf16)
            got_copy.start()
            made_copy.start()

        return carry

    def to_core_wait(u, plane):
        piece = remote(
            own.at[u, plane], from_core.at[u, plane], core_send.at[u, plane],
            core_recv.at[u, plane], sibling,
        )
        piece.wait_recv()

    lax.fori_loop(0, UNITS + 7, step, 0)
    got_copy.wait()
    made_copy.wait()
    for unit in range(UNITS):
        put_out(unit).wait()
        for plane in range(2):
            to_core(unit, plane).wait_send()


def reduce_by_kernel(grads, theirs, mine, made, norms):
    rows, width = mine.shape
    anywhere = pl.BlockSpec(memory_space=pl.ANY)
    vmem = pl.BlockSpec(memory_space=pltpu.VMEM)
    dma = pltpu.SemaphoreType.DMA
    U, T = UNITS, TILE
    z_only = LINE - 1
    return pl.pallas_call(
        reduce_kernel,
        out_shape=[
            jax.ShapeDtypeStruct((U, 2, T, T), bf16),
            jax.ShapeDtypeStruct((rows, width), f32),
            jax.ShapeDtypeStruct((rows, width), bf16),
            jax.ShapeDtypeStruct((rows, width), bf16),
            jax.ShapeDtypeStruct(norms.shape, f32),
        ],
        in_specs=[anywhere] * 10 + [anywhere, vmem, anywhere, vmem],
        out_specs=[anywhere, vmem, anywhere, anywhere, vmem],
        scratch_shapes=[
            pltpu.VMEM((U, 2, T, T), bf16),
            pltpu.VMEM((U, 2, T, T), bf16),
            pltpu.VMEM((U, T, T), bf16),
            pltpu.VMEM((U, T // 2, T), bf16),
            pltpu.VMEM((U, z_only, T // 2 // LINE, T), bf16),
            pltpu.VMEM((U, 2, T, T), bf16),
            pltpu.VMEM((rows, width), bf16),
            pltpu.VMEM((rows, width), bf16),
            pltpu.VMEM(norms.shape, f32),
            pltpu.VMEM((6,) + norms.shape, f32),
            dma((U, 2)), dma((U, 2)), dma((U, 2)), dma((U,)), dma((U,)), dma((U,)), dma((U,)),
            dma((U, z_only)), dma((U, z_only)), dma((U, z_only)), dma((U, z_only)),
            dma((U,)), dma((U,)), dma((U,)), dma((U,)), dma((U,)), dma((3,)), dma((3,)),
            dma((6,)), dma((6,)),
        ],
        compiler_params=pltpu.CompilerParams(
            collective_id=1, has_side_effects=True, vmem_limit_bytes=VMEM_LIMIT
        ),
        name="reduce",
    )(*grads, theirs, mine, made, norms)


def weight_outputs(sums):
    narrow_ones = [sums[u].reshape(2 * TILE, TILE) for u in range(6)]
    outs = [jnp.concatenate([sums[u, 0], sums[u, 1]], axis=1) for u in (6, 7)]
    grow = jnp.concatenate([sums[u].reshape(2 * TILE, TILE) for u in range(8, 12)], axis=1)
    shrink = jnp.concatenate(
        [jnp.concatenate([sums[u, 0], sums[u, 1]], axis=1) for u in range(12, 16)], axis=0
    )
    ordered = narrow_ones[:3] + outs[:1] + narrow_ones[3:] + outs[1:] + [grow, shrink]
    return tuple(piece.astype(f32) for piece in ordered)


def by_kernels(narrow):
    return lax.axis_size("wide") == 4 * LINE and narrow == 2


def gather_all(encoded, weights):
    if by_kernels(lax.axis_size("narrow")):
        return gather_by_kernel(encoded, weights)
    everything = lax.all_gather(encoded, "wide", tiled=True)
    full = tuple(
        lax.all_gather(w, "narrow", axis=1 if i in COLUMNS else 0, tiled=True)
        for i, w in enumerate(weights)
    )
    return everything, full


def reduce_all(grads):
    shares = tuple(
        lax.psum_scatter(
            g.astype(bf16), "narrow", scatter_dimension=1 if i in COLUMNS else 0, tiled=True
        )
        for i, g in enumerate(grads)
    )
    return tuple(s.astype(f32) for s in lax.psum(shares, "wide"))


def local(
    hidden,
    encoded,
    retrieved,
    self_query,
    self_key,
    self_value,
    self_out,
    cross_query,
    cross_key,
    cross_value,
    cross_out,
    expand_weight,
    reduce_weight,
    first_gain,
    first_shift,
    second_gain,
    second_shift,
    third_gain,
    third_shift,
    cotangent,
):
    tok_rows, width = hidden.shape
    narrow = lax.axis_size("narrow")
    at = lax.axis_index("narrow").astype(jnp.int32)
    chunk = tok_rows // (2 * narrow)

    def own(rows, size=chunk, at=at):
        low = lax.dynamic_slice_in_dim(rows, at * size, size)
        high = lax.dynamic_slice_in_dim(rows, (2 * narrow - 1 - at) * size, size)
        return jnp.concatenate([low, high], axis=0)

    everything, full = gather_all(
        encoded,
        (
            self_query,
            self_key,
            self_value,
            self_out,
            cross_query,
            cross_key,
            cross_value,
            cross_out,
            expand_weight,
            reduce_weight,
        ),
    )
    (
        self_query,
        self_key,
        self_value,
        self_out,
        cross_query,
        cross_key,
        cross_value,
        cross_out,
        expand_weight,
        reduce_weight,
    ) = full
    where_at = at.reshape(1)
    picked = own(retrieved, chunk // BLOCK_ROWS).reshape(-1)
    mine = own(hidden)
    grad_final = own(cotangent).astype(f32)

    query_self = project(mine, self_query).astype(bf16)
    key_self = project(hidden, self_key).astype(bf16)
    value_self = project(hidden, self_value).astype(bf16)
    blend_self, log_self = self_forward(narrow, where_at, query_self, key_self, value_self)
    first, first_normal, first_inverse = norm_forward(
        mine.astype(f32) + project(blend_self, self_out), first_gain, first_shift
    )
    first_low = first.astype(bf16)
    query_cross = project(first_low, cross_query).astype(bf16)
    blend_cross, log_cross, key_cross, value_cross = cross_forward(
        picked, everything, cross_key, cross_value, query_cross
    )
    second, second_normal, second_inverse = norm_forward(
        first + project(blend_cross, cross_out), second_gain, second_shift
    )
    second_low = second.astype(bf16)
    pre_act = project(second_low, expand_weight)
    activated = jax.nn.gelu(pre_act, approximate=False).astype(bf16)
    final, third_normal, third_inverse = norm_forward(
        second + project(activated, reduce_weight), third_gain, third_shift
    )
    output = final.astype(bf16)

    grad_third, third_gain_grad, third_shift_grad = norm_backward(
        grad_final, third_normal, third_inverse, third_gain
    )
    grad_ffn = grad_third.astype(bf16)
    reduce_grad = grad_weight(activated, grad_ffn)
    grad_pre = (grad_input(grad_ffn, reduce_weight) * gelu_slope(pre_act)).astype(bf16)
    expand_grad = grad_weight(second_low, grad_pre)
    grad_second = grad_third + grad_input(grad_pre, expand_weight)
    grad_second_in, second_gain_grad, second_shift_grad = norm_backward(
        grad_second, second_normal, second_inverse, second_gain
    )
    grad_cross = grad_second_in.astype(bf16)
    cross_out_grad = grad_weight(blend_cross, grad_cross)
    grad_blend_cross = grad_input(grad_cross, cross_out).astype(bf16)
    grad_query_cross, cross_key_grad, cross_value_grad = cross_backward(
        picked,
        everything,
        key_cross,
        value_cross,
        query_cross,
        log_cross,
        blend_cross,
        grad_blend_cross,
    )
    cross_query_grad = grad_weight(first_low, grad_query_cross)
    grad_first = grad_second_in + grad_input(grad_query_cross, cross_query)
    grad_first_in, first_gain_grad, first_shift_grad = norm_backward(
        grad_first, first_normal, first_inverse, first_gain
    )
    grad_self = grad_first_in.astype(bf16)
    self_out_grad = grad_weight(blend_self, grad_self)
    grad_blend_self = grad_input(grad_self, self_out).astype(bf16)
    grad_query_self, grad_key_self, grad_value_self = self_backward(
        narrow, where_at, query_self, key_self, value_self, log_self, blend_self, grad_blend_self
    )
    self_query_grad = grad_weight(mine, grad_query_self)
    self_key_grad = grad_weight(hidden, grad_key_self)
    self_value_grad = grad_weight(hidden, grad_value_self)
    grad_rows = grad_input(grad_key_self, self_key) + grad_input(grad_value_self, self_value)
    grad_own = grad_first_in + grad_input(grad_query_self, self_query)
    weight_grads = (
        self_query_grad,
        self_key_grad,
        self_value_grad,
        self_out_grad,
        cross_query_grad,
        cross_key_grad,
        cross_value_grad,
        cross_out_grad,
        expand_grad,
        reduce_grad,
    )
    norm_grads = (
        first_gain_grad,
        first_shift_grad,
        second_gain_grad,
        second_shift_grad,
        third_gain_grad,
        third_shift_grad,
    )

    if by_kernels(narrow):
        zero = jnp.zeros_like(first_gain_grad)
        theirs = own(grad_rows, at=1 - at).astype(bf16)
        sums, grad_mine, grad_theirs, made_theirs, norm_sums = reduce_by_kernel(
            tuple(g.astype(bf16) for g in weight_grads),
            theirs,
            own(grad_rows) + grad_own,
            output,
            jnp.stack(norm_grads + (zero, zero)),
        )

        def ordered(ours, others):
            a, b = ours[:chunk], ours[chunk:]
            c, d = others[:chunk], others[chunk:]
            first_one = at == 0
            return jnp.concatenate(
                [
                    jnp.where(first_one, a, c),
                    jnp.where(first_one, c, a),
                    jnp.where(first_one, d, b),
                    jnp.where(first_one, b, d),
                ],
                axis=0,
            )

        output = ordered(output, made_theirs)
        grad_hidden = ordered(grad_mine, grad_theirs.astype(f32))
        weight_sums = weight_outputs(sums)
    else:

        def spread(rows):
            empty = jnp.zeros((tok_rows, width), rows.dtype)
            placed = lax.dynamic_update_slice_in_dim(empty, rows[:chunk], at * chunk, 0)
            return lax.dynamic_update_slice_in_dim(
                placed, rows[chunk:], (2 * narrow - 1 - at) * chunk, 0
            )

        grad_hidden = lax.psum((grad_rows + spread(grad_own)).astype(bf16), "narrow").astype(f32)
        output = lax.psum(spread(output), "narrow")
        weight_sums = reduce_all(weight_grads)
        norm_sums = lax.psum(jnp.stack(norm_grads), ("wide", "narrow"))
    return (output, grad_hidden) + weight_sums + tuple(norm_sums[i] for i in range(6))


def solution(mesh):
    rows = P("wide", None)
    columns_split = P(None, "narrow")
    rows_split = P("narrow", None)
    weights = (columns_split,) * 3 + (rows_split,) + (columns_split,) * 3 + (rows_split,)
    weights += (columns_split, rows_split)
    return jax.shard_map(
        local,
        mesh=mesh,
        in_specs=(rows, rows, rows) + weights + (P(),) * 6 + (rows,),
        out_specs=(rows, rows) + weights + (P(),) * 6,
        check_vma=False,
    )
```

```python
import functools

import jax
import jax.numpy as jnp
from jax import lax
from jax.experimental import pallas as pl
from jax.experimental.pallas import tpu as pltpu
from jax.sharding import PartitionSpec as P

HEAD_DIM = 64
BLOCK_ROWS = 128
RET_BLOCKS = 8
PAIR = 2 * HEAD_DIM
VMEM_LIMIT = 60 << 20
BACKWARD_VMEM = 63 << 20

epsilon = 1e-05
bf16 = jnp.bfloat16
f32 = jnp.float32
MESH = pl.DeviceIdType.MESH


def norm_forward(summed, norm_gain, norm_shift):
    average = jnp.mean(summed, axis=-1, keepdims=True)
    centred = summed - average
    inverse = lax.rsqrt(jnp.mean(centred * centred, axis=-1, keepdims=True) + epsilon)
    normal = centred * inverse
    return (normal * norm_gain + norm_shift, normal, inverse)


def norm_backward(grad_out, normal, inverse, norm_gain):
    scaled = grad_out * norm_gain
    grad_in = inverse * (
        scaled
        - jnp.mean(scaled, axis=-1, keepdims=True)
        - normal * jnp.mean(scaled * normal, axis=-1, keepdims=True)
    )
    return (grad_in, jnp.sum(grad_out * normal, axis=0), jnp.sum(grad_out, axis=0))


def gelu_slope(pre_act):
    return (
        0.5 * (1.0 + lax.erf(pre_act * 0.7071067811865476))
        + pre_act * jnp.exp(-0.5 * pre_act * pre_act) * 0.3989422804014327
    )


def project(rows_in, weight):
    return jnp.dot(rows_in, weight, preferred_element_type=f32)


def grad_weight(left, right):
    return jnp.einsum("ti,to->io", left, right, preferred_element_type=f32)


def grad_input(grad_rows, weight):
    return jnp.einsum("to,io->ti", grad_rows, weight, preferred_element_type=f32)


def dot_nt(left, right):
    return lax.dot_general(left, right, (((1,), (1,)), ((), ())), preferred_element_type=f32)


def dot_tn(left, right):
    return lax.dot_general(left, right, (((0,), (0,)), ((), ())), preferred_element_type=f32)


def dot_nn(left, right):
    return lax.dot_general(left, right, (((1,), (0,)), ((), ())), preferred_element_type=f32)


def stack_heads(pair_rows):
    lane = lax.broadcasted_iota(jnp.int32, pair_rows.shape, 1)
    wide_rows = pair_rows.astype(f32)
    zero = jnp.zeros_like(wide_rows)
    return jnp.concatenate(
        [
            jnp.where(lane < HEAD_DIM, wide_rows, zero).astype(bf16),
            jnp.where(lane < HEAD_DIM, zero, wide_rows).astype(bf16),
        ],
        axis=0,
    )


def merge_heads(both):
    rows = both.shape[1] // 2
    sublane = lax.broadcasted_iota(jnp.int32, (PAIR, rows), 0)
    return jnp.transpose(jnp.where(sublane < HEAD_DIM, both[:, :rows], both[:, rows:]))


def causal_edge(rows):
    key = lax.broadcasted_iota(jnp.int32, (rows, 2 * rows), 0)
    query = lax.broadcasted_iota(jnp.int32, (rows, 2 * rows), 1)
    return key <= jnp.where(query >= rows, query - rows, query)


def scaled_heads(pair_rows):
    return stack_heads(pair_rows.astype(f32) * HEAD_DIM**-0.5)


def pair_forward(queries, keys, values, edge):
    stacked = scaled_heads(queries)
    scores = dot_nt(keys, stacked)
    if edge is not None:
        split = keys.shape[0] - edge.shape[0]
        last = jnp.where(edge, scores[split:], -1e30)
        scores = jnp.concatenate([scores[:split], last], axis=0) if split else last
    top = jnp.max(scores, axis=0, keepdims=True)
    raised = jnp.exp(scores - top)
    total = jnp.sum(raised, axis=0, keepdims=True)
    blended = dot_tn(values, raised.astype(bf16)) / total
    return merge_heads(blended).astype(bf16), top + jnp.log(total)


def pair_backward(queries, keys, values, edge, log_total, blended, grad_blend):
    rows = queries.shape[0]
    stacked = scaled_heads(queries)
    grads = stack_heads(grad_blend)
    scores = dot_nt(keys, stacked)
    if edge is not None:
        split = keys.shape[0] - edge.shape[0]
        last = jnp.where(edge, scores[split:], -1e30)
        scores = jnp.concatenate([scores[:split], last], axis=0) if split else last
    chances = jnp.exp(scores - log_total)
    weighed = jnp.transpose(blended.astype(f32) * grad_blend.astype(f32))
    centre = jnp.concatenate(
        [
            jnp.sum(weighed[:HEAD_DIM], axis=0, keepdims=True),
            jnp.sum(weighed[HEAD_DIM:], axis=0, keepdims=True),
        ],
        axis=1,
    )
    grad_scores = (chances * (dot_nt(values, grads) - centre)).astype(bf16)
    grad_values = dot_nn(chances.astype(bf16), grads)
    grad_keys = dot_nn(grad_scores, stacked)
    grad_queries = merge_heads(dot_tn(keys, grad_scores)) * HEAD_DIM**-0.5
    return grad_queries, grad_keys, grad_values


def self_blocks(narrow, total_rows, at):
    chunk = total_rows // (2 * narrow)
    for block in range(total_rows // BLOCK_ROWS):
        which, within = divmod(block * BLOCK_ROWS, chunk)
        if which < narrow:
            owner, local_row = which, within
        else:
            owner, local_row = 2 * narrow - 1 - which, chunk + within
        yield local_row, (block + 1) * BLOCK_ROWS, at == owner


def self_forward_kernel(narrow, at_ref, q_ref, k_ref, v_ref, o_ref, log_ref):
    for local_row, seen, taken in self_blocks(narrow, k_ref.shape[0], at_ref[0]):

        @pl.when(taken)
        def _():
            mine = pl.ds(local_row, BLOCK_ROWS)
            keys = pl.ds(0, seen)
            blended, log_total = pair_forward(
                q_ref[mine], k_ref[keys], v_ref[keys], causal_edge(BLOCK_ROWS)
            )
            o_ref[mine] = blended
            log_ref[0, pl.ds(local_row // BLOCK_ROWS, 1)] = log_total


def self_forward(narrow, at, queries, keys, values):
    rows, width = queries.shape
    total_rows = keys.shape[0]
    pairs = width // PAIR
    pair = lambda count: pl.BlockSpec((count, PAIR), lambda g, at: (0, g))
    return pl.pallas_call(
        functools.partial(self_forward_kernel, narrow),
        grid_spec=pltpu.PrefetchScalarGridSpec(
            num_scalar_prefetch=1,
            grid=(pairs,),
            in_specs=[pair(rows), pair(total_rows), pair(total_rows)],
            out_specs=[pair(rows), pl.BlockSpec((1, rows // BLOCK_ROWS, 2 * BLOCK_ROWS), lambda g, at: (g, 0, 0))],
        ),
        out_shape=[
            jax.ShapeDtypeStruct((rows, width), bf16),
            jax.ShapeDtypeStruct((pairs, rows // BLOCK_ROWS, 2 * BLOCK_ROWS), f32),
        ],
        compiler_params=pltpu.CompilerParams(vmem_limit_bytes=VMEM_LIMIT),
        name="self_forward",
    )(at, queries, keys, values)


def self_backward_kernel(
    narrow, at_ref, q_ref, k_ref, v_ref, log_ref, o_ref, g_ref, dq_ref, dk_ref, dv_ref, dk_sum, dv_sum
):
    rows = q_ref.shape[0] // 2
    dk_sum[...] = jnp.zeros_like(dk_sum)
    dv_sum[...] = jnp.zeros_like(dv_sum)
    for local_row, seen, taken in self_blocks(narrow, k_ref.shape[0], at_ref[0]):

        @pl.when(taken)
        def _():
            mine = pl.ds(local_row, BLOCK_ROWS)
            keys = pl.ds(0, seen)
            grad_q, grad_k, grad_v = pair_backward(
                q_ref[mine],
                k_ref[keys],
                v_ref[keys],
                causal_edge(BLOCK_ROWS),
                log_ref[0, pl.ds(local_row // BLOCK_ROWS, 1)],
                o_ref[mine],
                g_ref[mine],
            )
            dq_ref[mine] = grad_q.astype(bf16)
            dk_sum[keys] += grad_k
            dv_sum[keys] += grad_v

    dk_ref[...] = dk_sum[...].astype(bf16)
    dv_ref[...] = dv_sum[...].astype(bf16)


def self_backward(narrow, at, queries, keys, values, logs, blended, grads):
    rows, width = queries.shape
    total_rows = keys.shape[0]
    pairs = width // PAIR
    pair = lambda count: pl.BlockSpec((count, PAIR), lambda g, at: (0, g))
    return pl.pallas_call(
        functools.partial(self_backward_kernel, narrow),
        grid_spec=pltpu.PrefetchScalarGridSpec(
            num_scalar_prefetch=1,
            grid=(pairs,),
            in_specs=[
                pair(rows),
                pair(total_rows),
                pair(total_rows),
                pl.BlockSpec((1, rows // BLOCK_ROWS, 2 * BLOCK_ROWS), lambda g, at: (g, 0, 0)),
                pair(rows),
                pair(rows),
            ],
            out_specs=[pair(rows), pair(total_rows), pair(total_rows)],
            scratch_shapes=[pltpu.VMEM((total_rows, PAIR), f32)] * 2,
        ),
        out_shape=[
            jax.ShapeDtypeStruct((rows, width), bf16),
            jax.ShapeDtypeStruct((total_rows, width), bf16),
            jax.ShapeDtypeStruct((total_rows, width), bf16),
        ],
        compiler_params=pltpu.CompilerParams(vmem_limit_bytes=VMEM_LIMIT),
        name="self_backward",
    )(at, queries, keys, values, logs, blended, grads)


def cross_forward_kernel(picked_ref, *refs):
    blocks = refs[:RET_BLOCKS]
    wk_ref, wv_ref, q_ref, o_ref, log_ref, k_ref, v_ref, rows_in = refs[RET_BLOCKS:]
    for j in range(RET_BLOCKS):
        rows_in[pl.ds(j * BLOCK_ROWS, BLOCK_ROWS)] = blocks[j][...]
    k_ref[...] = dot_nn(rows_in[...], wk_ref[...]).astype(bf16)
    v_ref[...] = dot_nn(rows_in[...], wv_ref[...]).astype(bf16)
    for g in range(q_ref.shape[1] // PAIR):
        lanes = pl.ds(g * PAIR, PAIR)
        blended, log_total = pair_forward(q_ref[:, lanes], k_ref[:, lanes], v_ref[:, lanes], None)
        o_ref[:, lanes] = blended
        log_ref[0, pl.ds(g, 1)] = log_total


def block_specs(width):
    def spec(j):
        return pl.BlockSpec((BLOCK_ROWS, width), lambda b, picked: (picked[b * RET_BLOCKS + j], 0))

    return [spec(j) for j in range(RET_BLOCKS)]


def cross_forward(picked, everything, cross_key, cross_value, queries):
    rows, width = queries.shape
    count = rows // BLOCK_ROWS
    pairs = width // PAIR
    keys = RET_BLOCKS * BLOCK_ROWS
    whole = pl.BlockSpec((width, width), lambda b, picked: (0, 0))
    by_block = pl.BlockSpec((BLOCK_ROWS, width), lambda b, picked: (b, 0))
    by_keys = pl.BlockSpec((keys, width), lambda b, picked: (b, 0))
    return pl.pallas_call(
        cross_forward_kernel,
        grid_spec=pltpu.PrefetchScalarGridSpec(
            num_scalar_prefetch=1,
            grid=(count,),
            in_specs=block_specs(width) + [whole, whole, by_block],
            out_specs=[
                by_block,
                pl.BlockSpec((1, pairs, 2 * BLOCK_ROWS), lambda b, picked: (b, 0, 0)),
                by_keys,
                by_keys,
                by_keys,
            ],
        ),
        out_shape=[
            jax.ShapeDtypeStruct((rows, width), bf16),
            jax.ShapeDtypeStruct((count, pairs, 2 * BLOCK_ROWS), f32),
            jax.ShapeDtypeStruct((count * keys, width), bf16),
            jax.ShapeDtypeStruct((count * keys, width), bf16),
            jax.ShapeDtypeStruct((count * keys, width), bf16),
        ],
        compiler_params=pltpu.CompilerParams(vmem_limit_bytes=VMEM_LIMIT),
        name="cross_forward",
    )(picked, *([everything] * RET_BLOCKS), cross_key, cross_value, queries)


def cross_backward_kernel(picked_ref, *refs):
    blocks = refs[:RET_BLOCKS]
    (k_ref, v_ref, q_ref, log_ref, o_ref, g_ref, dq_ref, dwk_ref, dwv_ref, rows_in, both, sums) = refs[
        RET_BLOCKS:
    ]
    width = q_ref.shape[1]
    step = pl.program_id(0)

    @pl.when(step == 0)
    def _():
        sums[...] = jnp.zeros_like(sums)

    for j in range(RET_BLOCKS):
        rows_in[pl.ds(j * BLOCK_ROWS, BLOCK_ROWS)] = blocks[j][...]
    for g in range(width // PAIR):
        lanes = pl.ds(g * PAIR, PAIR)
        grad_q, grad_k, grad_v = pair_backward(
            q_ref[:, lanes],
            k_ref[:, lanes],
            v_ref[:, lanes],
            None,
            log_ref[0, pl.ds(g, 1)],
            o_ref[:, lanes],
            g_ref[:, lanes],
        )
        dq_ref[:, lanes] = grad_q.astype(bf16)
        both[:, lanes] = grad_k.astype(bf16)
        both[:, pl.ds(width + g * PAIR, PAIR)] = grad_v.astype(bf16)
    sums[...] += dot_tn(rows_in[...], both[...])

    @pl.when(step == pl.num_programs(0) - 1)
    def _():
        dwk_ref[...] = sums[:, :width].astype(bf16)
        dwv_ref[...] = sums[:, width:].astype(bf16)


def cross_backward(picked, everything, keys_in, values_in, queries, logs, blended, grads):
    rows, width = queries.shape
    count = rows // BLOCK_ROWS
    pairs = width // PAIR
    keys = RET_BLOCKS * BLOCK_ROWS
    whole = pl.BlockSpec((width, width), lambda b, picked: (0, 0))
    by_block = pl.BlockSpec((BLOCK_ROWS, width), lambda b, picked: (b, 0))
    by_keys = pl.BlockSpec((keys, width), lambda b, picked: (b, 0))
    return pl.pallas_call(
        cross_backward_kernel,
        grid_spec=pltpu.PrefetchScalarGridSpec(
            num_scalar_prefetch=1,
            grid=(count,),
            in_specs=block_specs(width)
            + [
                by_keys,
                by_keys,
                by_block,
                pl.BlockSpec((1, pairs, 2 * BLOCK_ROWS), lambda b, picked: (b, 0, 0)),
                by_block,
                by_block,
            ],
            out_specs=[by_block, whole, whole],
            scratch_shapes=[
                pltpu.VMEM((keys, width), bf16),
                pltpu.VMEM((keys, 2 * width), bf16),
                pltpu.VMEM((width, 2 * width), f32),
            ],
        ),
        out_shape=[
            jax.ShapeDtypeStruct((rows, width), bf16),
            jax.ShapeDtypeStruct((width, width), bf16),
            jax.ShapeDtypeStruct((width, width), bf16),
        ],
        compiler_params=pltpu.CompilerParams(vmem_limit_bytes=VMEM_LIMIT),
        name="cross_backward",
    )(
        picked,
        *([everything] * RET_BLOCKS),
        keys_in,
        values_in,
        queries,
        logs,
        blended,
        grads,
    )


COLUMNS = (0, 1, 2, 4, 5, 6, 8)


LINE = 4


class Place:
    def __init__(self):
        wide = lax.axis_index("wide")
        self.x = lax.axis_index("narrow")
        self.core = lax.rem(wide, 2)
        self.y = lax.rem(lax.div(wide, 2), 2)
        self.z = lax.div(wide, 4)
        self.wide = wide

    def at(self, z=None, y=None, core=None, x=None):
        z, y = (self.z if z is None else z), (self.y if y is None else y)
        core = self.core if core is None else core
        return (z * 4 + y * 2 + core, self.x if x is None else x)

    def greet(self):
        barrier = pltpu.get_barrier_semaphore()
        targets = [self.at(core=1 - self.core), self.at(y=1 - self.y), self.at(x=1 - self.x)]
        targets += [self.at(z=lax.rem(self.z + step, LINE)) for step in range(1, LINE)]
        for target in targets:
            pl.semaphore_signal(barrier, inc=1, device_id=target, device_id_type=MESH)
        pl.semaphore_wait(barrier, len(targets))


def gather_kernel(a_rows, b_rows, *refs):
    encoded_in, weights_in = refs[0], refs[1:11]
    everything, full = refs[11], refs[12:22]
    encoded, weights = refs[22], refs[23:33]
    load_sem, own_sem, half_sem, flow_send, flow_recv, weight_send, weight_recv = refs[33:]
    me = Place()
    rows = encoded.shape[0]
    x, y, z, core = me.x, me.y, me.z, me.core
    low, high = z > 0, z < LINE - 1
    UP_A, DOWN_A, Y_A, UP_B, DOWN_B, Y_B, X_B, CORE_A, CORE_B = range(9)

    loads = [pltpu.make_async_copy(encoded_in, encoded, load_sem.at[10])]
    for i in range(10):
        loads.append(pltpu.make_async_copy(weights_in[i], weights[i], load_sem.at[i]))
    for load in loads:
        load.start()
    own = pltpu.make_async_copy(
        encoded, everything.at[pl.ds(pl.multiple_of(me.wide * rows, 128), rows)], own_sem
    )

    def region(i, ref, plane, part):
        if i in COLUMNS:
            count, columns = ref.shape[0], ref.shape[1] // 2
            start = pl.multiple_of(plane * columns, 128)
            if part is None:
                return ref.at[:, pl.ds(start, columns)]
            first = pl.multiple_of(part * (count // 2), 16)
            return ref.at[pl.ds(first, count // 2), pl.ds(start, columns)]
        count = ref.shape[0] // 2
        if part is None:
            return ref.at[pl.ds(pl.multiple_of(plane * count, 16), count)]
        first = pl.multiple_of(plane * count + part * (count // 2), 16)
        return ref.at[pl.ds(first, count // 2)]

    halves = []
    for i in range(10):
        halves.append(
            pltpu.make_async_copy(weights[i], region(i, full[i], x, None), half_sem.at[i])
        )

    me.greet()
    for load in loads:
        load.wait()

    def flow(kind, owner_z, owner_y, plane, target, from_core=None, held=False):
        owner = owner_z * 2 + owner_y
        start = owner * (2 * rows) + (core if from_core is None else from_core) * rows
        if plane is None:
            size, slot = a_rows, owner
        else:
            start = start + a_rows + plane * b_rows
            size, slot = b_rows, owner + (plane * 8 if kind == CORE_B else 0)
        piece = everything.at[pl.ds(pl.multiple_of(start, 16), size)]
        source = piece
        if held:
            first = 0 if plane is None else pl.multiple_of(a_rows + plane * b_rows, 16)
            source = encoded.at[pl.ds(first, size)]
        return pltpu.make_async_remote_copy(
            src_ref=source,
            dst_ref=piece,
            send_sem=flow_send.at[kind, slot],
            recv_sem=flow_recv.at[kind, slot],
            device_id=target,
            device_id_type=MESH,
        )

    sibling = me.at(core=1 - core)
    beside = me.at(y=1 - y)
    across = me.at(x=1 - x)
    above, below = me.at(z=z + 1), me.at(z=z - 1)

    def up_a(oz, held=False):
        return flow(UP_A, oz, y, None, above, held=held)

    def down_a(oz, held=False):
        return flow(DOWN_A, oz, y, None, below, held=held)

    def up_b(oz, oy, held=False):
        return flow(UP_B, oz, oy, x, above, held=held)

    def down_b(oz, oy, held=False):
        return flow(DOWN_B, oz, oy, x, below, held=held)

    def y_a(oz, oy, held=False):
        return flow(Y_A, oz, oy, None, beside, held=held)

    def y_b(oy, held=False):
        return flow(Y_B, z, oy, x, beside, held=held)

    def x_b(oz, oy, plane):
        return flow(X_B, oz, oy, plane, across)

    def core_a(oz, oy, from_core=None, held=False):
        return flow(CORE_A, oz, oy, None, sibling, from_core, held)

    def core_b(oz, oy, plane, from_core=None, held=False):
        return flow(CORE_B, oz, oy, plane, sibling, from_core, held)

    def weight(way, i, plane, part):
        piece = region(i, full[i], plane, part)
        if way == 0:
            piece_in = weights[i]
            count = piece_in.shape[0] // 2
            piece_in = piece_in.at[pl.ds(pl.multiple_of(part * count, 16), count)]
        else:
            piece_in = piece
        return pltpu.make_async_remote_copy(
            src_ref=piece_in,
            dst_ref=piece,
            send_sem=weight_send.at[way, i],
            recv_sem=weight_recv.at[way, i],
            device_id=across if way == 0 else sibling,
            device_id_type=MESH,
        )

    y_b(y, True).start()
    y_a(z, y, True).start()
    pl.when(high)(lambda: up_a(z, True).start())
    pl.when(low)(lambda: down_a(z, True).start())
    for i in range(10):
        weight(0, i, x, core).start()
    core_a(z, y, held=True).start()
    core_b(z, y, 0, held=True).start()
    core_b(z, y, 1, held=True).start()
    own.start()
    for i in range(10):
        halves[i].start()

    y_b(1 - y).wait_recv()
    core_b(z, 1 - y, x).start()
    x_b(z, 1 - y, x).start()

    def beside_arrives(oz):
        y_a(oz, 1 - y).wait_recv()
        core_a(oz, 1 - y).start()

    def pass_a(oz, arrived, onward, further):
        arrived(oz).wait_recv()
        pl.when(onward)(lambda: further(oz).start())
        y_a(oz, y).start()
        core_a(oz, y).start()

    def pass_b(oz, arrived, onward, further):
        for oy in (y, 1 - y):
            arrived(oz, oy).wait_recv()
            pl.when(onward)(lambda: further(oz, oy).start())
            x_b(oz, oy, x).start()
            core_b(oz, oy, x).start()

    for step in range(LINE):
        for kind, back in ((0, 1), (1, 0)):
            under, over = z - back - step, z + back + step
            if kind == 0 and step < LINE - 1:
                pl.when(under >= 0)(lambda: pass_a(under, up_a, high, up_a))
                pl.when(over < LINE)(lambda: pass_a(over, down_a, low, down_a))
            if kind == 1 and step == 0:
                for oy, held in ((y, True), (1 - y, False)):
                    pl.when(high)(lambda oy=oy, held=held: up_b(z, oy, held).start())
                    pl.when(low)(lambda oy=oy, held=held: down_b(z, oy, held).start())
            if kind == 1 and step > 0:
                pl.when(under >= 0)(lambda: pass_b(under, up_b, high, up_b))
                pl.when(over < LINE)(lambda: pass_b(over, down_b, low, down_b))
    for i in range(10):
        weight(0, i, 1 - x, core).wait_recv()
        weight(1, i, 1 - x, core).start()
    beside_arrives(z)
    for step in range(1, LINE):
        pl.when(z - step >= 0)(lambda: beside_arrives(z - step))
        pl.when(z + step < LINE)(lambda: beside_arrives(z + step))

    def across_arrives(oz, oy):
        x_b(oz, oy, 1 - x).wait_recv()
        core_b(oz, oy, 1 - x).start()

    across_arrives(z, 1 - y)
    for step in range(LINE - 1):
        under, over = z - 1 - step, z + 1 + step
        for oy in (y, 1 - y):
            pl.when(under >= 0)(lambda: across_arrives(under, oy))
            pl.when(over < LINE)(lambda: across_arrives(over, oy))

    y_b(y).wait_send()
    x_b(z, 1 - y, x).wait_send()
    for oz in range(LINE):
        y_a(oz, y).wait_send()
        for oy in range(2):
            core_a(oz, oy).wait_send()
            core_a(oz, oy, 1 - core).wait_recv()
            for plane in range(2):
                core_b(oz, oy, plane).wait_send()
                core_b(oz, oy, plane, 1 - core).wait_recv()
        away = oz != z

        @pl.when(away)
        def _():
            for oy in range(2):
                x_b(oz, oy, x).wait_send()

        @pl.when(jnp.logical_and(high, oz <= z))
        def _():
            up_a(oz).wait_send()
            for oy in range(2):
                up_b(oz, oy).wait_send()

        @pl.when(jnp.logical_and(low, oz >= z))
        def _():
            down_a(oz).wait_send()
            for oy in range(2):
                down_b(oz, oy).wait_send()

    own.wait()
    for i in range(10):
        halves[i].wait()
        weight(0, i, x, core).wait_send()
        weight(1, i, 1 - x, core).wait_send()
        weight(1, i, 1 - x, 1 - core).wait_recv()


def gather_by_kernel(encoded, weights):
    rows, width = encoded.shape
    a_rows = rows * 17 // 24 // 16 * 16
    b_rows = (rows - a_rows) // 2
    shapes = [jax.ShapeDtypeStruct((16 * rows, width), bf16)]
    for i, w in enumerate(weights):
        doubled = (w.shape[0], 2 * w.shape[1]) if i in COLUMNS else (2 * w.shape[0], w.shape[1])
        shapes.append(jax.ShapeDtypeStruct(doubled, bf16))
    dma = pltpu.SemaphoreType.DMA
    out = pl.pallas_call(
        functools.partial(gather_kernel, a_rows, b_rows),
        out_shape=shapes,
        in_specs=[pl.BlockSpec(memory_space=pl.ANY)] * 11,
        out_specs=[pl.BlockSpec(memory_space=pl.ANY)] * 11,
        scratch_shapes=[pltpu.VMEM((rows, width), bf16)]
        + [pltpu.VMEM(w.shape, bf16) for w in weights]
        + [dma((11,)), dma, dma((10,)), dma((9, 16)), dma((9, 16)), dma((2, 10)), dma((2, 10))],
        compiler_params=pltpu.CompilerParams(
            collective_id=0, has_side_effects=True, vmem_limit_bytes=VMEM_LIMIT
        ),
        name="gather",
    )(encoded, *weights)
    return out[0], tuple(out[1:])


TILE = 384
HALF = TILE // 2
PART = HALF // LINE
UNITS = 16
SLOTS = 8
UNIT_WEIGHTS = (8, 8, 8, 8, 9, 9, 9, 9, 7, 5, 6, 4, 3, 0, 1, 2)
LAST_TICK = UNITS + 6


def share_corner(unit, core, plane):
    if unit < 4:
        return core * TILE, (plane * 4 + unit) * TILE
    if unit < 8:
        return (plane * 4 + unit - 4) * TILE, core * TILE
    if unit in (8, 12):
        return plane * TILE, core * TILE
    return core * TILE, plane * TILE


def backward_kernel(*refs):
    (
        expand_grad, reduce_grad, cross_out_grad, picked_rows, keys_in, values_in, q_cross, a_cross,
        g_cross, log_cross, first_low, cross_query, g_second, first_normal, first_inverse, first_gain,
        a_self, self_out, q_self, k_self, v_self, log_self, hidden, self_query, self_key, self_value,
        made, norms,
    ) = refs[:28]
    sums_out, mine_out, theirs_out, made_out, norms_out = refs[28:33]
    (
        own, from_core, from_a, from_b, from_z, summed, pool, pool32, both, staged, dq_cross, dk_sum,
        dv_sum, theirs, rows_in, rows_got, norm_all, norm_in,
        own_sem, core_send, core_recv, a_send, a_recv, b_send, b_recv, z_send, z_recv, gz_send, gz_recv,
        gy_send, gy_recv, gc_send, gc_recv, keep_sem, load_sem, kv_sem, e_sem, extra_send, extra_recv,
        norm_send, norm_recv,
    ) = refs[33:]
    me = Place()
    x, y, z, core = me.x, me.y, me.z, me.core
    sibling, beside, across = me.at(core=1 - core), me.at(y=1 - y), me.at(x=1 - x)
    width = 2 * TILE
    keys = RET_BLOCKS * BLOCK_ROWS
    rows = q_cross.shape[0]
    blocks = rows // BLOCK_ROWS
    pairs = width // PAIR
    chunk = rows // 2

    def rem(u, n):
        return u % n if isinstance(u, int) else lax.rem(u, n)

    def remote(src, dst, send, recv, target):
        return pltpu.make_async_remote_copy(
            src_ref=src, dst_ref=dst, send_sem=send, recv_sem=recv,
            device_id=target, device_id_type=MESH,
        )


    def share(ref, unit, of_core, plane, part):
        row, column = share_corner(unit, of_core, plane)
        return ref.at[
            pl.ds(pl.multiple_of(row + part * HALF, 64), HALF),
            pl.ds(pl.multiple_of(column, 128), TILE),
        ]

    def own_copy(ref, unit, plane, part):
        return pltpu.make_async_copy(
            share(ref, unit, core, plane, part),
            own.at[unit % SLOTS, plane, part],
            own_sem.at[unit % SLOTS, plane * 2 + part],
        )

    def core_copy(src, u, plane, part):
        return remote(
            src, from_core.at[u, plane, part], core_send.at[u, plane * 2 + part],
            core_recv.at[u, plane * 2 + part], sibling,
        )

    def to_core(ref, unit, plane, part):
        return core_copy(share(ref, unit, 1 - core, plane, part), unit, plane, part)

    def a_first(u, slot):
        return remote(own.at[slot, 1 - x], from_a.at[u], a_send.at[u], a_recv.at[u], across)

    def a_second(u, slot):
        return remote(own.at[slot, :, 1 - y], from_a.at[u], a_send.at[u], a_recv.at[u], beside)

    def b_first(u, slot):
        return remote(own.at[slot, x, 1 - y], from_b.at[u], b_send.at[u], b_recv.at[u], beside)

    def b_second(u, slot):
        return remote(own.at[slot, 1 - x, y], from_b.at[u], b_send.at[u], b_recv.at[u], across)

    def to_z(u, slot, d):
        other = lax.rem(z + d, LINE)
        piece = own.at[slot, x, y, pl.ds(pl.multiple_of(other * PART, 16), PART)]
        return remote(
            piece, from_z.at[u, d - 1], z_send.at[u, d - 1], z_recv.at[u, d - 1], me.at(z=other)
        )

    def result(u, of_z):
        return sums_out.at[u, core, pl.ds(pl.multiple_of(y * HALF + of_z * PART, 16), PART)]

    def keep(u):
        return pltpu.make_async_copy(summed.at[u], result(u, z), keep_sem.at[u])

    def gather_z(u, d):
        return remote(
            summed.at[u], result(u, z), gz_send.at[u, d - 1], gz_recv.at[u, d - 1],
            me.at(z=lax.rem(z + d, LINE)),
        )

    def gathered_z(u, d):
        return remote(
            summed.at[u], result(u, lax.rem(z + LINE - d, LINE)), gz_send.at[u, d - 1],
            gz_recv.at[u, d - 1], beside,
        )

    def gather_y(u, at_y):
        piece = sums_out.at[u, core, pl.ds(pl.multiple_of(at_y * HALF, 16), HALF)]
        return remote(piece, piece, gy_send.at[u], gy_recv.at[u], beside)

    def gather_core(u, at_core):
        piece = sums_out.at[u, at_core]
        return remote(piece, piece, gc_send.at[u], gc_recv.at[u], sibling)

    def plus(a, b):
        return (a.astype(f32) + b.astype(f32)).astype(bf16)

    def by_order(u, first, second):
        if isinstance(u, int):
            (first if u % 2 == 0 else second)()
        else:
            pl.when(lax.rem(u, 2) == 0)(first)
            pl.when(lax.rem(u, 2) == 1)(second)

    def stage_core(u):
        slot = rem(u, SLOTS)
        for plane in range(2):
            for part in range(2):
                core_copy(own.at[slot, plane, part], u, plane, part).wait_recv()
        own[slot] = plus(own[slot], from_core[u])
        by_order(u, lambda: a_first(u, slot).start(), lambda: a_second(u, slot).start())

    def stage_a(u):
        slot = rem(u, SLOTS)

        def first():
            a_first(u, slot).wait()
            own[slot, x] = plus(own[slot, x], from_a[u])
            b_first(u, slot).start()

        def second():
            a_second(u, slot).wait()
            own[slot, :, y] = plus(own[slot, :, y], from_a[u])
            b_second(u, slot).start()

        by_order(u, first, second)

    def stage_b(u):
        slot = rem(u, SLOTS)
        by_order(u, lambda: b_first(u, slot).wait(), lambda: b_second(u, slot).wait())
        own[slot, x, y] = plus(own[slot, x, y], from_b[u])
        for d in range(1, LINE):
            to_z(u, slot, d).start()

    def stage_z(u):
        slot = rem(u, SLOTS)
        for d in range(1, LINE):
            to_z(u, slot, d).wait()
        total = own[slot, x, y, pl.ds(pl.multiple_of(z * PART, 16), PART)].astype(f32)
        for d in range(1, LINE):
            total += from_z[u, d - 1].astype(f32)
        summed[u] = total.astype(bf16)
        keep(u).start()
        for d in range(1, LINE):
            gather_z(u, d).start()

    def stage_gather_z(u):
        keep(u).wait()
        for d in range(1, LINE):
            gathered_z(u, d).wait_recv()
            gather_z(u, d).wait_send()
        gather_y(u, y).start()

    def stage_gather_y(u):
        gather_y(u, 1 - y).wait_recv()
        gather_y(u, y).wait_send()
        gather_core(u, core).start()

    def stage_gather_core(u):
        gather_core(u, 1 - core).wait_recv()
        gather_core(u, core).wait_send()

    stages = (
        (0, stage_core), (2, stage_a), (3, stage_b), (4, stage_z), (5, stage_gather_z),
        (6, stage_gather_y), (7, stage_gather_core),
    )

    def tick(t):
        for lag, stage in stages:
            if isinstance(t, int):
                if 0 <= t - lag < UNITS:
                    stage(t - lag)
            else:
                u = t - lag
                pl.when(jnp.logical_and(u >= 0, u < UNITS))(lambda stage=stage, u=u: stage(u))

    KV, E, Q, O, G, FIRST, CROSS_Q, A_SELF, SELF_OUT = (
        0, 4096, 5120, 5632, 6144, 6656, 7168, 7936, 8448
    )
    QS, KS, VS, DQ, DK, DV, HIDDEN, DA = 0, 512, 1536, 2560, 3072, 4096, 5120, 6144
    WQ, WK, WV = 0, 768, 1536

    def load(src, row, sem, into=pool):
        return pltpu.make_async_copy(src, into.at[pl.ds(row, src.shape[0])], load_sem.at[sem])

    def kv_copy(b, which):
        src = (keys_in, values_in)[which].at[pl.ds(pl.multiple_of(b * keys, 128), keys)]
        row = pl.multiple_of(lax.rem(b, 2) * (2 * keys) + which * keys, 128)
        return pltpu.make_async_copy(src, pool.at[pl.ds(row, keys)], kv_sem.at[lax.rem(b, 2), which])

    def e_copy(b):
        src = picked_rows.at[pl.ds(pl.multiple_of(b * keys, 128), keys)]
        return pltpu.make_async_copy(src, pool.at[pl.ds(E, keys)], e_sem)

    early = [
        load(q_cross, Q, 0), load(a_cross, O, 1), load(g_cross, G, 2), load(first_low, FIRST, 3),
        load(cross_query, CROSS_Q, 4), load(a_self, A_SELF, 5), load(self_out, SELF_OUT, 6),
    ]
    for which in range(2):
        kv_copy(jnp.int32(0), which).start()
    for copy in early:
        copy.start()
    ready = [(expand_grad, u) for u in range(4)] + [(reduce_grad, u) for u in range(4, 8)]
    corners = [(plane, part) for plane in range(2) for part in range(2)]
    for ref, unit in ready:
        for plane, part in corners:
            own_copy(ref, unit, plane, part).start()
    me.greet()
    for ref, unit in ready + [(cross_out_grad, 8)]:
        for plane, part in corners:
            to_core(ref, unit, plane, part).start()
    made_copy = remote(made, made_out, extra_send.at[1], extra_recv.at[1], across)
    made_copy.start()
    both_sums = pool32
    both_sums[...] = jnp.zeros_like(both_sums)
    for copy in early[:3]:
        copy.wait()
    for ref, unit in ready:
        for plane, part in corners:
            own_copy(ref, unit, plane, part).wait()

    def at_row(row):
        return pl.ds(pl.multiple_of(row, 128), BLOCK_ROWS)

    def cross_step(i, carry):
        b, g = lax.div(i, pairs), lax.rem(i, pairs)

        @pl.when(g == 0)
        def _():
            for which in range(2):
                kv_copy(b, which).wait()
            e_copy(b).start()

            @pl.when(b + 1 < blocks)
            def _():
                for which in range(2):
                    kv_copy(b + 1, which).start()

        lanes = pl.ds(pl.multiple_of(g * PAIR, PAIR), PAIR)
        row = pl.multiple_of(b * BLOCK_ROWS, BLOCK_ROWS)
        key_row = pl.multiple_of(lax.rem(b, 2) * (2 * keys), 128)
        grad_q, grad_k, grad_v = pair_backward(
            pool[at_row(Q + row), lanes],
            pool[pl.ds(key_row, keys), lanes],
            pool[pl.ds(pl.multiple_of(key_row + keys, 128), keys), lanes],
            None,
            log_cross[b, pl.ds(g, 1)],
            pool[at_row(O + row), lanes],
            pool[at_row(G + row), lanes],
        )
        dq_cross[pl.ds(row, BLOCK_ROWS), lanes] = grad_q.astype(bf16)
        both[:, lanes] = grad_k.astype(bf16)
        both[:, pl.ds(pl.multiple_of(width + g * PAIR, PAIR), PAIR)] = grad_v.astype(bf16)

        @pl.when(g == pairs - 1)
        def _():
            e_copy(b).wait()
            both_sums[pl.ds(0, width)] += dot_tn(pool[pl.ds(E, keys)], both[:, :width])
            both_sums[pl.ds(width, width)] += dot_tn(pool[pl.ds(E, keys)], both[:, width:])

        pl.when(lax.rem(i, 4) == 3)(lambda: tick(lax.div(i, 4)))
        return carry

    lax.fori_loop(0, blocks * pairs, cross_step, 0)

    def hand_over(unit):
        ref = staged.at[unit % 2]
        for plane, part in corners:
            to_core(ref, unit, plane, part).start()
            own_copy(ref, unit, plane, part).start()

    def kept(unit):
        for plane, part in corners:
            own_copy(staged.at[unit % 2], unit, plane, part).wait()

    def left(unit):
        for plane, part in corners:
            to_core(staged.at[unit % 2], unit, plane, part).wait_send()

    def handed_over(unit):
        kept(unit)
        left(unit)

    late = [load(q_self, QS, 7), load(k_self, KS, 8), load(v_self, VS, 9), load(hidden, HIDDEN, 10)]
    for copy in late:
        copy.start()
    for plane, part in corners:
        own_copy(cross_out_grad, 8, plane, part).start()
    staged[1] = both_sums[pl.ds(0, width)].astype(bf16)
    hand_over(9)
    tick(6)
    staged[0] = both_sums[pl.ds(width, width)].astype(bf16)
    hand_over(10)
    g_copy = load(g_second, 0, 11, pool32)
    n_copy = load(first_normal, rows, 12, pool32)
    g_copy.start()
    n_copy.start()
    for copy in early[3:]:
        copy.wait()
    tick(7)
    handed_over(9)
    staged[1] = dot_tn(pool[pl.ds(FIRST, rows)], dq_cross[...]).astype(bf16)
    hand_over(11)

    g_copy.wait()
    n_copy.wait()
    normal = pool32[pl.ds(rows, rows)]
    grad_out = pool32[pl.ds(0, rows)] + dot_nt(dq_cross[...], pool[pl.ds(CROSS_Q, width)])
    scaled = grad_out * first_gain[...]
    grad_in = first_inverse[...] * (
        scaled
        - jnp.mean(scaled, axis=-1, keepdims=True)
        - normal * jnp.mean(scaled * normal, axis=-1, keepdims=True)
    )
    norm_all[...] = norms[...]
    norm_all[pl.ds(0, 1)] = jnp.sum(grad_out * normal, axis=0, keepdims=True)
    norm_all[pl.ds(1, 1)] = jnp.sum(grad_out, axis=0, keepdims=True)
    pool32[pl.ds(2 * rows, rows)] = grad_in
    grad_low = grad_in.astype(bf16)
    pool[pl.ds(DA, rows)] = dot_nt(grad_low, pool[pl.ds(SELF_OUT, width)]).astype(bf16)
    for plane, part in corners:
        own_copy(cross_out_grad, 8, plane, part).wait()
    tick(8)
    handed_over(10)
    staged[0] = dot_tn(pool[pl.ds(A_SELF, rows)], grad_low).astype(bf16)
    hand_over(12)

    along_z = tuple(me.at(z=lax.rem(z + d, LINE)) for d in range(1, LINE))
    rounds = ((sibling,), (across,), (beside,), along_z)

    def norm_copies(which):
        first = min(which, 3)
        return [
            remote(
                norm_all, norm_in.at[first + k], norm_send.at[first + k], norm_recv.at[first + k], target
            )
            for k, target in enumerate(rounds[which])
        ]

    def norm_start(which):
        for copy in norm_copies(which):
            copy.start()

    def norm_finish(which):
        for copy in norm_copies(which):
            copy.wait()
        for k in range(len(rounds[which])):
            norm_all[...] += norm_in[which + k]

    norm_start(0)

    for copy in late:
        copy.wait()
    kept(11)
    kept(12)

    def self_step(g, carry):
        lanes = pl.ds(pl.multiple_of(g * PAIR, PAIR), PAIR)
        dk_sum[...] = jnp.zeros_like(dk_sum)
        dv_sum[...] = jnp.zeros_like(dv_sum)
        for local_row, seen, taken in self_blocks(2, hidden.shape[0], x):

            @pl.when(taken)
            def _():
                mine = pl.ds(local_row, BLOCK_ROWS)
                grad_q, grad_k, grad_v = pair_backward(
                    pool[pl.ds(QS + local_row, BLOCK_ROWS), lanes],
                    pool[pl.ds(KS, seen), lanes],
                    pool[pl.ds(VS, seen), lanes],
                    causal_edge(BLOCK_ROWS),
                    log_self[g, pl.ds(local_row // BLOCK_ROWS, 1)],
                    a_self_rows(local_row, lanes),
                    pool[pl.ds(DA + local_row, BLOCK_ROWS), lanes],
                )
                pool[pl.ds(DQ + local_row, BLOCK_ROWS), lanes] = grad_q.astype(bf16)
                dk_sum[pl.ds(0, seen)] += grad_k
                dv_sum[pl.ds(0, seen)] += grad_v

        pool[pl.ds(DK, hidden.shape[0]), lanes] = dk_sum[...].astype(bf16)
        pool[pl.ds(DV, hidden.shape[0]), lanes] = dv_sum[...].astype(bf16)
        pl.when(lax.rem(g, 2) == 1)(lambda: tick(9 + lax.div(g, 2)))
        return carry

    def a_self_rows(local_row, lanes):
        return pool[pl.ds(A_SELF + local_row, BLOCK_ROWS), lanes]

    lax.fori_loop(0, pairs, self_step, 0)
    norm_finish(0)
    norm_start(1)
    last_loads = [load(self_query, WQ, 13), load(self_key, WK, 14), load(self_value, WV, 15)]
    for copy in last_loads:
        copy.start()

    left(11)
    low_rows = pl.ds(pl.multiple_of(HIDDEN + x * chunk, 128), chunk)
    high_rows = pl.ds(pl.multiple_of(HIDDEN + (3 - x) * chunk, 128), chunk)
    all_rows = hidden.shape[0]
    staged[1] = (
        dot_tn(pool[low_rows], pool[pl.ds(DQ, chunk)])
        + dot_tn(pool[high_rows], pool[pl.ds(DQ + chunk, chunk)])
    ).astype(bf16)
    hand_over(13)
    norm_finish(1)
    norm_start(2)
    left(12)
    staged[0] = dot_tn(pool[pl.ds(HIDDEN, all_rows)], pool[pl.ds(DK, all_rows)]).astype(bf16)
    hand_over(14)
    tick(12)
    handed_over(13)
    staged[1] = dot_tn(pool[pl.ds(HIDDEN, all_rows)], pool[pl.ds(DV, all_rows)]).astype(bf16)
    hand_over(15)
    norm_finish(2)
    norm_start(3)
    tick(13)
    handed_over(14)
    handed_over(15)

    for copy in last_loads:
        copy.wait()

    def row_grads(at_chunk):
        dk = pool[pl.ds(pl.multiple_of(DK + at_chunk * chunk, 128), chunk)]
        dv = pool[pl.ds(pl.multiple_of(DV + at_chunk * chunk, 128), chunk)]
        return dot_nt(dk, pool[pl.ds(WK, width)]) + dot_nt(dv, pool[pl.ds(WV, width)])

    theirs[pl.ds(0, chunk)] = row_grads(1 - x).astype(bf16)
    theirs[pl.ds(chunk, chunk)] = row_grads(2 + x).astype(bf16)
    rows_copy = remote(theirs, rows_in, extra_send.at[0], extra_recv.at[0], across)
    got_copy = remote(rows_got, theirs_out, extra_send.at[2], extra_recv.at[2], across)
    rows_copy.start()
    tick(14)
    for k, at_chunk in enumerate((x, 3 - x)):
        piece = pl.ds(k * chunk, chunk)
        mine_out[piece] = (
            row_grads(at_chunk)
            + dot_nt(pool[pl.ds(DQ + k * chunk, chunk)], pool[pl.ds(WQ, width)])
            + pool32[pl.ds(2 * rows + k * chunk, chunk)]
        )
    norm_finish(3)
    norms_out[...] = norm_all[...]

    def last_step(t, carry):
        tick(t)

        @pl.when(t == 17)
        def _():
            rows_copy.wait()
            whole = mine_out[...] + rows_in[...].astype(f32)
            mine_out[...] = whole
            rows_got[...] = whole.astype(bf16)
            got_copy.start()

        return carry

    lax.fori_loop(15, LAST_TICK + 1, last_step, 0)
    got_copy.wait()
    made_copy.wait()
    for ref, unit in ready + [(cross_out_grad, 8)]:
        for plane, part in corners:
            to_core(ref, unit, plane, part).wait_send()


def backward_by_kernel(*args):
    rows, width = args[6].shape
    all_rows = args[22].shape[0]
    norms = args[27]
    anywhere = pl.BlockSpec(memory_space=pl.ANY)
    vmem = pl.BlockSpec(memory_space=pltpu.VMEM)
    in_specs = [anywhere] * 28
    for i in (9, 14, 15, 21, 27):
        in_specs[i] = vmem
    dma = pltpu.SemaphoreType.DMA
    U, T, H, Z = UNITS, TILE, HALF, LINE - 1
    return pl.pallas_call(
        backward_kernel,
        out_shape=[
            jax.ShapeDtypeStruct((U, 2, T, T), bf16),
            jax.ShapeDtypeStruct((rows, width), f32),
            jax.ShapeDtypeStruct((rows, width), bf16),
            jax.ShapeDtypeStruct((rows, width), bf16),
            jax.ShapeDtypeStruct(norms.shape, f32),
        ],
        in_specs=in_specs,
        out_specs=[anywhere, vmem, anywhere, anywhere, vmem],
        scratch_shapes=[
            pltpu.VMEM((SLOTS, 2, 2, H, T), bf16),
            pltpu.VMEM((U, 2, 2, H, T), bf16),
            pltpu.VMEM((U, 2, H, T), bf16),
            pltpu.VMEM((U, H, T), bf16),
            pltpu.VMEM((U, Z, PART, T), bf16),
            pltpu.VMEM((U, PART, T), bf16),
            pltpu.VMEM((9216, width), bf16),
            pltpu.VMEM((2 * width, width), f32),
            pltpu.VMEM((RET_BLOCKS * BLOCK_ROWS, 2 * width), bf16),
            pltpu.VMEM((2, width, width), bf16),
            pltpu.VMEM((rows, width), bf16),
            pltpu.VMEM((all_rows, PAIR), f32),
            pltpu.VMEM((all_rows, PAIR), f32),
            pltpu.VMEM((rows, width), bf16),
            pltpu.VMEM((rows, width), bf16),
            pltpu.VMEM((rows, width), bf16),
            pltpu.VMEM(norms.shape, f32),
            pltpu.VMEM((6,) + norms.shape, f32),
            dma((SLOTS, 4)), dma((U, 4)), dma((U, 4)), dma((U,)), dma((U,)), dma((U,)), dma((U,)),
            dma((U, Z)), dma((U, Z)), dma((U, Z)), dma((U, Z)), dma((U,)), dma((U,)), dma((U,)),
            dma((U,)), dma((U,)), dma((16,)), dma((2, 2)), dma, dma((3,)), dma((3,)), dma((6,)),
            dma((6,)),
        ],
        compiler_params=pltpu.CompilerParams(
            collective_id=1, has_side_effects=True, vmem_limit_bytes=BACKWARD_VMEM
        ),
        name="backward",
    )(*args)


def output_place(unit, core):
    row, column = share_corner(unit, core, 0)
    return UNIT_WEIGHTS[unit], row, column


def widen_kernel(sums, *refs):
    outs, (taken, given, in_sem, out_sem) = refs[:10], refs[10:]
    depth = taken.shape[0]
    shares = [(unit, core) for unit in range(UNITS) for core in range(2)]

    def fetch(i):
        unit, core = shares[i]
        return pltpu.make_async_copy(sums.at[unit, core], taken.at[i % depth], in_sem.at[i % depth])

    def place(i):
        weight, row, column = output_place(*shares[i])
        return pltpu.make_async_copy(
            given.at[i % depth],
            outs[weight].at[pl.ds(row, TILE), pl.ds(column, TILE)],
            out_sem.at[i % depth],
        )

    for i in range(depth - 1):
        fetch(i).start()
    for i in range(len(shares)):
        if i + depth - 1 < len(shares):
            fetch(i + depth - 1).start()
        fetch(i).wait()
        if i >= depth:
            place(i - depth).wait()
        given[i % depth] = taken[i % depth].astype(f32)
        place(i).start()
    for i in range(len(shares) - depth, len(shares)):
        place(i).wait()


def weight_outputs(sums):
    shapes = [(2 * TILE, TILE)] * 3 + [(TILE, 2 * TILE)] + [(2 * TILE, TILE)] * 3
    shapes += [(TILE, 2 * TILE), (2 * TILE, 4 * TILE), (4 * TILE, 2 * TILE)]
    depth = 6
    return (
        tuple(pl.pallas_call(
            widen_kernel,
            out_shape=[jax.ShapeDtypeStruct(shape, f32) for shape in shapes],
            in_specs=[pl.BlockSpec(memory_space=pl.ANY)],
            out_specs=[pl.BlockSpec(memory_space=pl.ANY)] * 10,
            scratch_shapes=[
                pltpu.VMEM((depth, TILE, TILE), bf16),
                pltpu.VMEM((depth, TILE, TILE), f32),
                pltpu.SemaphoreType.DMA((depth,)),
                pltpu.SemaphoreType.DMA((depth,)),
            ],
            compiler_params=pltpu.CompilerParams(vmem_limit_bytes=VMEM_LIMIT),
            name="widen",
        )(sums)),
    )


def by_kernels(narrow):
    return lax.axis_size("wide") == 4 * LINE and narrow == 2


def gather_all(encoded, weights):
    if by_kernels(lax.axis_size("narrow")):
        return gather_by_kernel(encoded, weights)
    everything = lax.all_gather(encoded, "wide", tiled=True)
    full = tuple(
        lax.all_gather(w, "narrow", axis=1 if i in COLUMNS else 0, tiled=True)
        for i, w in enumerate(weights)
    )
    return everything, full


def reduce_all(grads):
    shares = tuple(
        lax.psum_scatter(
            g.astype(bf16), "narrow", scatter_dimension=1 if i in COLUMNS else 0, tiled=True
        )
        for i, g in enumerate(grads)
    )
    return tuple(s.astype(f32) for s in lax.psum(shares, "wide"))


def local(
    hidden,
    encoded,
    retrieved,
    self_query,
    self_key,
    self_value,
    self_out,
    cross_query,
    cross_key,
    cross_value,
    cross_out,
    expand_weight,
    reduce_weight,
    first_gain,
    first_shift,
    second_gain,
    second_shift,
    third_gain,
    third_shift,
    cotangent,
):
    tok_rows, width = hidden.shape
    narrow = lax.axis_size("narrow")
    at = lax.axis_index("narrow").astype(jnp.int32)
    chunk = tok_rows // (2 * narrow)

    def own(rows, size=chunk):
        low = lax.dynamic_slice_in_dim(rows, at * size, size)
        high = lax.dynamic_slice_in_dim(rows, (2 * narrow - 1 - at) * size, size)
        return jnp.concatenate([low, high], axis=0)

    everything, full = gather_all(
        encoded,
        (
            self_query,
            self_key,
            self_value,
            self_out,
            cross_query,
            cross_key,
            cross_value,
            cross_out,
            expand_weight,
            reduce_weight,
        ),
    )
    (
        self_query,
        self_key,
        self_value,
        self_out,
        cross_query,
        cross_key,
        cross_value,
        cross_out,
        expand_weight,
        reduce_weight,
    ) = full
    where_at = at.reshape(1)
    picked = own(retrieved, chunk // BLOCK_ROWS).reshape(-1)
    mine = own(hidden)
    grad_final = own(cotangent).astype(f32)

    query_self = project(mine, self_query).astype(bf16)
    key_self = project(hidden, self_key).astype(bf16)
    value_self = project(hidden, self_value).astype(bf16)
    blend_self, log_self = self_forward(narrow, where_at, query_self, key_self, value_self)
    first, first_normal, first_inverse = norm_forward(
        mine.astype(f32) + project(blend_self, self_out), first_gain, first_shift
    )
    first_low = first.astype(bf16)
    query_cross = project(first_low, cross_query).astype(bf16)
    blend_cross, log_cross, key_cross, value_cross, picked_rows = cross_forward(
        picked, everything, cross_key, cross_value, query_cross
    )
    second, second_normal, second_inverse = norm_forward(
        first + project(blend_cross, cross_out), second_gain, second_shift
    )
    second_low = second.astype(bf16)
    pre_act = project(second_low, expand_weight)
    activated = jax.nn.gelu(pre_act, approximate=False).astype(bf16)
    final, third_normal, third_inverse = norm_forward(
        second + project(activated, reduce_weight), third_gain, third_shift
    )
    output = final.astype(bf16)

    grad_third, third_gain_grad, third_shift_grad = norm_backward(
        grad_final, third_normal, third_inverse, third_gain
    )
    grad_ffn = grad_third.astype(bf16)
    reduce_grad = grad_weight(activated, grad_ffn)
    grad_pre = (grad_input(grad_ffn, reduce_weight) * gelu_slope(pre_act)).astype(bf16)
    expand_grad = grad_weight(second_low, grad_pre)
    grad_second = grad_third + grad_input(grad_pre, expand_weight)
    grad_second_in, second_gain_grad, second_shift_grad = norm_backward(
        grad_second, second_normal, second_inverse, second_gain
    )
    grad_cross = grad_second_in.astype(bf16)
    cross_out_grad = grad_weight(blend_cross, grad_cross)
    grad_blend_cross = grad_input(grad_cross, cross_out).astype(bf16)
    if by_kernels(narrow):
        zero = jnp.zeros_like(second_gain_grad)
        norm_grads = (zero, zero, second_gain_grad, second_shift_grad, third_gain_grad)
        sums, grad_mine, grad_theirs, made_theirs, norm_sums = backward_by_kernel(
            expand_grad.astype(bf16),
            reduce_grad.astype(bf16),
            cross_out_grad.astype(bf16),
            picked_rows,
            key_cross,
            value_cross,
            query_cross,
            blend_cross,
            grad_blend_cross,
            log_cross,
            first_low,
            cross_query,
            grad_second_in,
            first_normal,
            first_inverse,
            first_gain.reshape(1, width),
            blend_self,
            self_out,
            query_self,
            key_self,
            value_self,
            log_self,
            hidden,
            self_query,
            self_key,
            self_value,
            output,
            jnp.stack(norm_grads + (third_shift_grad, zero, zero)),
        )

        def ordered(ours, others):
            a, b = ours[:chunk], ours[chunk:]
            c, d = others[:chunk], others[chunk:]
            first_one = at == 0
            return jnp.concatenate(
                [
                    jnp.where(first_one, a, c),
                    jnp.where(first_one, c, a),
                    jnp.where(first_one, d, b),
                    jnp.where(first_one, b, d),
                ],
                axis=0,
            )

        return (
            (ordered(output, made_theirs), ordered(grad_mine, grad_theirs.astype(f32)))
            + weight_outputs(sums)[0]
            + tuple(norm_sums[i] for i in range(6))
        )

    grad_query_cross, cross_key_grad, cross_value_grad = cross_backward(
        picked,
        everything,
        key_cross,
        value_cross,
        query_cross,
        log_cross,
        blend_cross,
        grad_blend_cross,
    )
    cross_query_grad = grad_weight(first_low, grad_query_cross)
    grad_first = grad_second_in + grad_input(grad_query_cross, cross_query)
    grad_first_in, first_gain_grad, first_shift_grad = norm_backward(
        grad_first, first_normal, first_inverse, first_gain
    )
    grad_self = grad_first_in.astype(bf16)
    self_out_grad = grad_weight(blend_self, grad_self)
    grad_blend_self = grad_input(grad_self, self_out).astype(bf16)
    grad_query_self, grad_key_self, grad_value_self = self_backward(
        narrow, where_at, query_self, key_self, value_self, log_self, blend_self, grad_blend_self
    )
    self_query_grad = grad_weight(mine, grad_query_self)
    self_key_grad = grad_weight(hidden, grad_key_self)
    self_value_grad = grad_weight(hidden, grad_value_self)
    grad_rows = grad_input(grad_key_self, self_key) + grad_input(grad_value_self, self_value)
    grad_own = grad_first_in + grad_input(grad_query_self, self_query)

    def spread(rows):
        empty = jnp.zeros((tok_rows, width), rows.dtype)
        placed = lax.dynamic_update_slice_in_dim(empty, rows[:chunk], at * chunk, 0)
        return lax.dynamic_update_slice_in_dim(
            placed, rows[chunk:], (2 * narrow - 1 - at) * chunk, 0
        )

    grad_hidden = lax.psum((grad_rows + spread(grad_own)).astype(bf16), "narrow").astype(f32)
    output = lax.psum(spread(output), "narrow")
    weight_grads = reduce_all(
        (
            self_query_grad,
            self_key_grad,
            self_value_grad,
            self_out_grad,
            cross_query_grad,
            cross_key_grad,
            cross_value_grad,
            cross_out_grad,
            expand_grad,
            reduce_grad,
        )
    )
    norm_grads = lax.psum(
        jnp.stack(
            [
                first_gain_grad,
                first_shift_grad,
                second_gain_grad,
                second_shift_grad,
                third_gain_grad,
                third_shift_grad,
            ]
        ),
        ("wide", "narrow"),
    )
    return (output, grad_hidden) + weight_grads + tuple(norm_grads[i] for i in range(6))


def solution(mesh):
    rows = P("wide", None)
    columns_split = P(None, "narrow")
    rows_split = P("narrow", None)
    weights = (columns_split,) * 3 + (rows_split,) + (columns_split,) * 3 + (rows_split,)
    weights += (columns_split, rows_split)
    return jax.shard_map(
        local,
        mesh=mesh,
        in_specs=(rows, rows, rows) + weights + (P(),) * 6 + (rows,),
        out_specs=(rows, rows) + weights + (P(),) * 6,
        check_vma=False,
    )
```

```python
import functools

import jax
import jax.numpy as jnp
from jax import lax
from jax.experimental import pallas as pl
from jax.experimental.pallas import tpu as pltpu
from jax.sharding import PartitionSpec as P

HEAD_DIM = 64
BLOCK_ROWS = 128
RET_BLOCKS = 8
PAIR = 2 * HEAD_DIM
VMEM_LIMIT = 60 << 20
BACKWARD_VMEM = 63 << 20

epsilon = 1e-05
bf16 = jnp.bfloat16
f32 = jnp.float32
MESH = pl.DeviceIdType.MESH


def norm_forward(summed, norm_gain, norm_shift):
    average = jnp.mean(summed, axis=-1, keepdims=True)
    centred = summed - average
    inverse = lax.rsqrt(jnp.mean(centred * centred, axis=-1, keepdims=True) + epsilon)
    normal = centred * inverse
    return (normal * norm_gain + norm_shift, normal, inverse)


def norm_backward(grad_out, normal, inverse, norm_gain):
    scaled = grad_out * norm_gain
    grad_in = inverse * (
        scaled
        - jnp.mean(scaled, axis=-1, keepdims=True)
        - normal * jnp.mean(scaled * normal, axis=-1, keepdims=True)
    )
    return (grad_in, jnp.sum(grad_out * normal, axis=0), jnp.sum(grad_out, axis=0))


def gelu_slope(pre_act):
    return (
        0.5 * (1.0 + lax.erf(pre_act * 0.7071067811865476))
        + pre_act * jnp.exp(-0.5 * pre_act * pre_act) * 0.3989422804014327
    )


def project(rows_in, weight):
    return jnp.dot(rows_in, weight, preferred_element_type=f32)


def grad_weight(left, right):
    return jnp.einsum("ti,to->io", left, right, preferred_element_type=f32)


def grad_input(grad_rows, weight):
    return jnp.einsum("to,io->ti", grad_rows, weight, preferred_element_type=f32)


def dot_nt(left, right):
    return lax.dot_general(left, right, (((1,), (1,)), ((), ())), preferred_element_type=f32)


def dot_tn(left, right):
    return lax.dot_general(left, right, (((0,), (0,)), ((), ())), preferred_element_type=f32)


def dot_nn(left, right):
    return lax.dot_general(left, right, (((1,), (0,)), ((), ())), preferred_element_type=f32)


def stack_heads(pair_rows):
    lane = lax.broadcasted_iota(jnp.int32, pair_rows.shape, 1)
    wide_rows = pair_rows.astype(f32)
    zero = jnp.zeros_like(wide_rows)
    return jnp.concatenate(
        [
            jnp.where(lane < HEAD_DIM, wide_rows, zero).astype(bf16),
            jnp.where(lane < HEAD_DIM, zero, wide_rows).astype(bf16),
        ],
        axis=0,
    )


def merge_heads(both):
    rows = both.shape[1] // 2
    sublane = lax.broadcasted_iota(jnp.int32, (PAIR, rows), 0)
    return jnp.transpose(jnp.where(sublane < HEAD_DIM, both[:, :rows], both[:, rows:]))


def causal_edge(rows):
    key = lax.broadcasted_iota(jnp.int32, (rows, 2 * rows), 0)
    query = lax.broadcasted_iota(jnp.int32, (rows, 2 * rows), 1)
    return key <= jnp.where(query >= rows, query - rows, query)


def scaled_heads(pair_rows):
    return stack_heads(pair_rows.astype(f32) * HEAD_DIM**-0.5)


def pair_forward(queries, keys, values, edge):
    stacked = scaled_heads(queries)
    scores = dot_nt(keys, stacked)
    if edge is not None:
        split = keys.shape[0] - edge.shape[0]
        last = jnp.where(edge, scores[split:], -1e30)
        scores = jnp.concatenate([scores[:split], last], axis=0) if split else last
    top = jnp.max(scores, axis=0, keepdims=True)
    raised = jnp.exp(scores - top)
    total = jnp.sum(raised, axis=0, keepdims=True)
    blended = dot_tn(values, raised.astype(bf16)) / total
    return merge_heads(blended).astype(bf16), top + jnp.log(total)


def pair_backward(queries, keys, values, edge, log_total, blended, grad_blend):
    rows = queries.shape[0]
    stacked = scaled_heads(queries)
    grads = stack_heads(grad_blend)
    scores = dot_nt(keys, stacked)
    if edge is not None:
        split = keys.shape[0] - edge.shape[0]
        last = jnp.where(edge, scores[split:], -1e30)
        scores = jnp.concatenate([scores[:split], last], axis=0) if split else last
    chances = jnp.exp(scores - log_total)
    weighed = jnp.transpose(blended.astype(f32) * grad_blend.astype(f32))
    centre = jnp.concatenate(
        [
            jnp.sum(weighed[:HEAD_DIM], axis=0, keepdims=True),
            jnp.sum(weighed[HEAD_DIM:], axis=0, keepdims=True),
        ],
        axis=1,
    )
    grad_scores = (chances * (dot_nt(values, grads) - centre)).astype(bf16)
    grad_values = dot_nn(chances.astype(bf16), grads)
    grad_keys = dot_nn(grad_scores, stacked)
    grad_queries = merge_heads(dot_tn(keys, grad_scores)) * HEAD_DIM**-0.5
    return grad_queries, grad_keys, grad_values


def self_blocks(narrow, total_rows, at):
    chunk = total_rows // (2 * narrow)
    for block in range(total_rows // BLOCK_ROWS):
        which, within = divmod(block * BLOCK_ROWS, chunk)
        if which < narrow:
            owner, local_row = which, within
        else:
            owner, local_row = 2 * narrow - 1 - which, chunk + within
        yield local_row, (block + 1) * BLOCK_ROWS, at == owner


def self_forward_kernel(narrow, at_ref, q_ref, k_ref, v_ref, o_ref, log_ref):
    for local_row, seen, taken in self_blocks(narrow, k_ref.shape[0], at_ref[0]):

        @pl.when(taken)
        def _():
            mine = pl.ds(local_row, BLOCK_ROWS)
            keys = pl.ds(0, seen)
            blended, log_total = pair_forward(
                q_ref[mine], k_ref[keys], v_ref[keys], causal_edge(BLOCK_ROWS)
            )
            o_ref[mine] = blended
            log_ref[0, pl.ds(local_row // BLOCK_ROWS, 1)] = log_total


def self_forward(narrow, at, queries, keys, values):
    rows, width = queries.shape
    total_rows = keys.shape[0]
    pairs = width // PAIR
    pair = lambda count: pl.BlockSpec((count, PAIR), lambda g, at: (0, g))
    return pl.pallas_call(
        functools.partial(self_forward_kernel, narrow),
        grid_spec=pltpu.PrefetchScalarGridSpec(
            num_scalar_prefetch=1,
            grid=(pairs,),
            in_specs=[pair(rows), pair(total_rows), pair(total_rows)],
            out_specs=[pair(rows), pl.BlockSpec((1, rows // BLOCK_ROWS, 2 * BLOCK_ROWS), lambda g, at: (g, 0, 0))],
        ),
        out_shape=[
            jax.ShapeDtypeStruct((rows, width), bf16),
            jax.ShapeDtypeStruct((pairs, rows // BLOCK_ROWS, 2 * BLOCK_ROWS), f32),
        ],
        compiler_params=pltpu.CompilerParams(vmem_limit_bytes=VMEM_LIMIT),
        name="self_forward",
    )(at, queries, keys, values)


def self_backward_kernel(
    narrow, at_ref, q_ref, k_ref, v_ref, log_ref, o_ref, g_ref, dq_ref, dk_ref, dv_ref, dk_sum, dv_sum
):
    rows = q_ref.shape[0] // 2
    dk_sum[...] = jnp.zeros_like(dk_sum)
    dv_sum[...] = jnp.zeros_like(dv_sum)
    for local_row, seen, taken in self_blocks(narrow, k_ref.shape[0], at_ref[0]):

        @pl.when(taken)
        def _():
            mine = pl.ds(local_row, BLOCK_ROWS)
            keys = pl.ds(0, seen)
            grad_q, grad_k, grad_v = pair_backward(
                q_ref[mine],
                k_ref[keys],
                v_ref[keys],
                causal_edge(BLOCK_ROWS),
                log_ref[0, pl.ds(local_row // BLOCK_ROWS, 1)],
                o_ref[mine],
                g_ref[mine],
            )
            dq_ref[mine] = grad_q.astype(bf16)
            dk_sum[keys] += grad_k
            dv_sum[keys] += grad_v

    dk_ref[...] = dk_sum[...].astype(bf16)
    dv_ref[...] = dv_sum[...].astype(bf16)


def self_backward(narrow, at, queries, keys, values, logs, blended, grads):
    rows, width = queries.shape
    total_rows = keys.shape[0]
    pairs = width // PAIR
    pair = lambda count: pl.BlockSpec((count, PAIR), lambda g, at: (0, g))
    return pl.pallas_call(
        functools.partial(self_backward_kernel, narrow),
        grid_spec=pltpu.PrefetchScalarGridSpec(
            num_scalar_prefetch=1,
            grid=(pairs,),
            in_specs=[
                pair(rows),
                pair(total_rows),
                pair(total_rows),
                pl.BlockSpec((1, rows // BLOCK_ROWS, 2 * BLOCK_ROWS), lambda g, at: (g, 0, 0)),
                pair(rows),
                pair(rows),
            ],
            out_specs=[pair(rows), pair(total_rows), pair(total_rows)],
            scratch_shapes=[pltpu.VMEM((total_rows, PAIR), f32)] * 2,
        ),
        out_shape=[
            jax.ShapeDtypeStruct((rows, width), bf16),
            jax.ShapeDtypeStruct((total_rows, width), bf16),
            jax.ShapeDtypeStruct((total_rows, width), bf16),
        ],
        compiler_params=pltpu.CompilerParams(vmem_limit_bytes=VMEM_LIMIT),
        name="self_backward",
    )(at, queries, keys, values, logs, blended, grads)


def cross_forward_kernel(picked_ref, *refs):
    blocks = refs[:RET_BLOCKS]
    wk_ref, wv_ref, q_ref, o_ref, log_ref, k_ref, v_ref, rows_in = refs[RET_BLOCKS:]
    for j in range(RET_BLOCKS):
        rows_in[pl.ds(j * BLOCK_ROWS, BLOCK_ROWS)] = blocks[j][...]
    k_ref[...] = dot_nn(rows_in[...], wk_ref[...]).astype(bf16)
    v_ref[...] = dot_nn(rows_in[...], wv_ref[...]).astype(bf16)
    for g in range(q_ref.shape[1] // PAIR):
        lanes = pl.ds(g * PAIR, PAIR)
        blended, log_total = pair_forward(q_ref[:, lanes], k_ref[:, lanes], v_ref[:, lanes], None)
        o_ref[:, lanes] = blended
        log_ref[0, pl.ds(g, 1)] = log_total


def block_specs(width):
    def spec(j):
        return pl.BlockSpec((BLOCK_ROWS, width), lambda b, picked: (picked[b * RET_BLOCKS + j], 0))

    return [spec(j) for j in range(RET_BLOCKS)]


def cross_forward(picked, everything, cross_key, cross_value, queries):
    rows, width = queries.shape
    count = rows // BLOCK_ROWS
    pairs = width // PAIR
    keys = RET_BLOCKS * BLOCK_ROWS
    whole = pl.BlockSpec((width, width), lambda b, picked: (0, 0))
    by_block = pl.BlockSpec((BLOCK_ROWS, width), lambda b, picked: (b, 0))
    by_keys = pl.BlockSpec((keys, width), lambda b, picked: (b, 0))
    return pl.pallas_call(
        cross_forward_kernel,
        grid_spec=pltpu.PrefetchScalarGridSpec(
            num_scalar_prefetch=1,
            grid=(count,),
            in_specs=block_specs(width) + [whole, whole, by_block],
            out_specs=[
                by_block,
                pl.BlockSpec((1, pairs, 2 * BLOCK_ROWS), lambda b, picked: (b, 0, 0)),
                by_keys,
                by_keys,
                by_keys,
            ],
        ),
        out_shape=[
            jax.ShapeDtypeStruct((rows, width), bf16),
            jax.ShapeDtypeStruct((count, pairs, 2 * BLOCK_ROWS), f32),
            jax.ShapeDtypeStruct((count * keys, width), bf16),
            jax.ShapeDtypeStruct((count * keys, width), bf16),
            jax.ShapeDtypeStruct((count * keys, width), bf16),
        ],
        compiler_params=pltpu.CompilerParams(vmem_limit_bytes=VMEM_LIMIT),
        name="cross_forward",
    )(picked, *([everything] * RET_BLOCKS), cross_key, cross_value, queries)


def cross_backward_kernel(picked_ref, *refs):
    blocks = refs[:RET_BLOCKS]
    (k_ref, v_ref, q_ref, log_ref, o_ref, g_ref, dq_ref, dwk_ref, dwv_ref, rows_in, both, sums) = refs[
        RET_BLOCKS:
    ]
    width = q_ref.shape[1]
    step = pl.program_id(0)

    @pl.when(step == 0)
    def _():
        sums[...] = jnp.zeros_like(sums)

    for j in range(RET_BLOCKS):
        rows_in[pl.ds(j * BLOCK_ROWS, BLOCK_ROWS)] = blocks[j][...]
    for g in range(width // PAIR):
        lanes = pl.ds(g * PAIR, PAIR)
        grad_q, grad_k, grad_v = pair_backward(
            q_ref[:, lanes],
            k_ref[:, lanes],
            v_ref[:, lanes],
            None,
            log_ref[0, pl.ds(g, 1)],
            o_ref[:, lanes],
            g_ref[:, lanes],
        )
        dq_ref[:, lanes] = grad_q.astype(bf16)
        both[:, lanes] = grad_k.astype(bf16)
        both[:, pl.ds(width + g * PAIR, PAIR)] = grad_v.astype(bf16)
    sums[...] += dot_tn(rows_in[...], both[...])

    @pl.when(step == pl.num_programs(0) - 1)
    def _():
        dwk_ref[...] = sums[:, :width].astype(bf16)
        dwv_ref[...] = sums[:, width:].astype(bf16)


def cross_backward(picked, everything, keys_in, values_in, queries, logs, blended, grads):
    rows, width = queries.shape
    count = rows // BLOCK_ROWS
    pairs = width // PAIR
    keys = RET_BLOCKS * BLOCK_ROWS
    whole = pl.BlockSpec((width, width), lambda b, picked: (0, 0))
    by_block = pl.BlockSpec((BLOCK_ROWS, width), lambda b, picked: (b, 0))
    by_keys = pl.BlockSpec((keys, width), lambda b, picked: (b, 0))
    return pl.pallas_call(
        cross_backward_kernel,
        grid_spec=pltpu.PrefetchScalarGridSpec(
            num_scalar_prefetch=1,
            grid=(count,),
            in_specs=block_specs(width)
            + [
                by_keys,
                by_keys,
                by_block,
                pl.BlockSpec((1, pairs, 2 * BLOCK_ROWS), lambda b, picked: (b, 0, 0)),
                by_block,
                by_block,
            ],
            out_specs=[by_block, whole, whole],
            scratch_shapes=[
                pltpu.VMEM((keys, width), bf16),
                pltpu.VMEM((keys, 2 * width), bf16),
                pltpu.VMEM((width, 2 * width), f32),
            ],
        ),
        out_shape=[
            jax.ShapeDtypeStruct((rows, width), bf16),
            jax.ShapeDtypeStruct((width, width), bf16),
            jax.ShapeDtypeStruct((width, width), bf16),
        ],
        compiler_params=pltpu.CompilerParams(vmem_limit_bytes=VMEM_LIMIT),
        name="cross_backward",
    )(
        picked,
        *([everything] * RET_BLOCKS),
        keys_in,
        values_in,
        queries,
        logs,
        blended,
        grads,
    )


COLUMNS = (0, 1, 2, 4, 5, 6, 8)


LINE = 4
HELD = 5


class Place:
    def __init__(self):
        wide = lax.axis_index("wide")
        self.x = lax.axis_index("narrow")
        self.core = lax.rem(wide, 2)
        self.y = lax.rem(lax.div(wide, 2), 2)
        self.z = lax.div(wide, 4)
        self.wide = wide

    def at(self, z=None, y=None, core=None, x=None):
        z, y = (self.z if z is None else z), (self.y if y is None else y)
        core = self.core if core is None else core
        return (z * 4 + y * 2 + core, self.x if x is None else x)

    def greet(self):
        barrier = pltpu.get_barrier_semaphore()
        targets = [self.at(core=1 - self.core), self.at(y=1 - self.y), self.at(x=1 - self.x)]
        targets += [self.at(z=lax.rem(self.z + step, LINE)) for step in range(1, LINE)]
        for target in targets:
            pl.semaphore_signal(barrier, inc=1, device_id=target, device_id_type=MESH)
        pl.semaphore_wait(barrier, len(targets))


def forward_kernel(a_rows, b_rows, *refs):
    encoded_in, weights_in = refs[0], refs[1:11]
    hidden_in, first_gain, first_shift = refs[11:14]
    everything, full_out = refs[14], refs[15:25]
    kept_out, (log_self, inverse_out) = refs[25:33], refs[33:35]
    encoded, weights, kept = refs[35], refs[36:46], refs[46:54]
    hidden = refs[54]
    load_sem, own_sem, half_sem, kept_sem, flow_send, flow_recv, weight_send, weight_recv = refs[55:]
    q_self, k_self, v_self, a_self, first, first_normal, first_low, q_cross = kept
    full = weights[:HELD] + full_out[HELD:]
    me = Place()
    rows = encoded.shape[0]
    x, y, z, core = me.x, me.y, me.z, me.core
    low, high = z > 0, z < LINE - 1
    UP_A, DOWN_A, Y_A, UP_B, DOWN_B, Y_B, X_B, CORE_A, CORE_B = range(9)

    own = pltpu.make_async_copy(
        encoded, everything.at[pl.ds(pl.multiple_of(me.wide * rows, 128), rows)], own_sem
    )

    def region(i, ref, plane, part):
        if i in COLUMNS:
            count, columns = ref.shape[0], ref.shape[1] // 2
            start = pl.multiple_of(plane * columns, 128)
            if part is None:
                return ref.at[:, pl.ds(start, columns)]
            first = pl.multiple_of(part * (count // 2), 16)
            return ref.at[pl.ds(first, count // 2), pl.ds(start, columns)]
        count = ref.shape[0] // 2
        if part is None:
            return ref.at[pl.ds(pl.multiple_of(plane * count, 16), count)]
        first = pl.multiple_of(plane * count + part * (count // 2), 16)
        return ref.at[pl.ds(first, count // 2)]

    loads, halves = [], []
    for i in range(10):
        into = region(i, weights[i], x, None) if i < HELD else weights[i]
        loads.append(pltpu.make_async_copy(weights_in[i], into, load_sem.at[i]))
        if i < HELD:
            halves.append(pltpu.make_async_copy(weights[i], full_out[i], half_sem.at[i]))
        else:
            halves.append(
                pltpu.make_async_copy(weights[i], region(i, full[i], x, None), half_sem.at[i])
            )
    loads.append(pltpu.make_async_copy(encoded_in, encoded, load_sem.at[10]))
    loads.append(pltpu.make_async_copy(hidden_in, hidden, load_sem.at[11]))
    loads[10].start()
    for i in range(10):
        loads[i].start()
    loads[11].start()
    me.greet()
    loads[10].wait()

    def flow(kind, owner_z, owner_y, plane, target, from_core=None, held=False):
        owner = owner_z * 2 + owner_y
        start = owner * (2 * rows) + (core if from_core is None else from_core) * rows
        if plane is None:
            size, slot = a_rows, owner
        else:
            start = start + a_rows + plane * b_rows
            size, slot = b_rows, owner + (plane * 8 if kind == CORE_B else 0)
        piece = everything.at[pl.ds(pl.multiple_of(start, 16), size)]
        source = piece
        if held:
            first = 0 if plane is None else pl.multiple_of(a_rows + plane * b_rows, 16)
            source = encoded.at[pl.ds(first, size)]
        return pltpu.make_async_remote_copy(
            src_ref=source,
            dst_ref=piece,
            send_sem=flow_send.at[kind, slot],
            recv_sem=flow_recv.at[kind, slot],
            device_id=target,
            device_id_type=MESH,
        )

    sibling = me.at(core=1 - core)
    beside = me.at(y=1 - y)
    across = me.at(x=1 - x)
    above, below = me.at(z=z + 1), me.at(z=z - 1)

    def up_a(oz, held=False):
        return flow(UP_A, oz, y, None, above, held=held)

    def down_a(oz, held=False):
        return flow(DOWN_A, oz, y, None, below, held=held)

    def up_b(oz, oy, held=False):
        return flow(UP_B, oz, oy, x, above, held=held)

    def down_b(oz, oy, held=False):
        return flow(DOWN_B, oz, oy, x, below, held=held)

    def y_a(oz, oy, held=False):
        return flow(Y_A, oz, oy, None, beside, held=held)

    def y_b(oy, held=False):
        return flow(Y_B, z, oy, x, beside, held=held)

    def x_b(oz, oy, plane):
        return flow(X_B, oz, oy, plane, across)

    def core_a(oz, oy, from_core=None, held=False):
        return flow(CORE_A, oz, oy, None, sibling, from_core, held)

    def core_b(oz, oy, plane, from_core=None, held=False):
        return flow(CORE_B, oz, oy, plane, sibling, from_core, held)

    def weight(way, i, plane, part):
        piece = region(i, full[i], plane, part)
        if way == 0 and i >= HELD:
            piece_in = weights[i]
            count = piece_in.shape[0] // 2
            piece_in = piece_in.at[pl.ds(pl.multiple_of(part * count, 16), count)]
        else:
            piece_in = piece
        return pltpu.make_async_remote_copy(
            src_ref=piece_in,
            dst_ref=piece,
            send_sem=weight_send.at[way, i],
            recv_sem=weight_recv.at[way, i],
            device_id=across if way == 0 else sibling,
            device_id_type=MESH,
        )

    y_b(y, True).start()
    y_a(z, y, True).start()
    pl.when(high)(lambda: up_a(z, True).start())
    pl.when(low)(lambda: down_a(z, True).start())

    def weights_go(some):
        for i in some:
            weight(0, i, x, core).start()

    def weights_come(some):
        for i in some:
            weight(0, i, 1 - x, core).wait_recv()
            weight(1, i, 1 - x, core).start()

    for i in range(3):
        loads[i].wait()
    weights_go(range(3))
    core_a(z, y, held=True).start()
    core_b(z, y, 0, held=True).start()
    core_b(z, y, 1, held=True).start()
    own.start()
    for i in range(3, 12):
        if i != 10:
            loads[i].wait()
    for i in range(HELD, 10):
        halves[i].start()

    y_b(1 - y).wait_recv()
    core_b(z, 1 - y, x).start()
    weights_come(range(3))
    weights_go(range(3, 8))
    for i in range(3):
        weight(1, i, 1 - x, 1 - core).wait_recv()

    total_rows = hidden.shape[0]
    chunk = total_rows // 4
    mine = (
        pl.ds(pl.multiple_of(x * chunk, 128), chunk),
        pl.ds(pl.multiple_of((3 - x) * chunk, 128), chunk),
    )
    places = (pl.ds(0, chunk), pl.ds(chunk, chunk))
    for piece, place in zip(mine, places):
        q_self[place] = dot_nn(hidden[piece], weights[0][...]).astype(bf16)
    k_self[...] = dot_nn(hidden[...], weights[1][...]).astype(bf16)
    v_self[...] = dot_nn(hidden[...], weights[2][...]).astype(bf16)
    put = [pltpu.make_async_copy(kept[i], kept_out[i], kept_sem.at[i]) for i in range(8)]
    for i in range(3):
        put[i].start()

    def self_step(g, carry):
        lanes = pl.ds(pl.multiple_of(g * PAIR, PAIR), PAIR)
        for local_row, seen, taken in self_blocks(2, total_rows, x):

            @pl.when(taken)
            def _():
                some = pl.ds(local_row, BLOCK_ROWS)
                blended, log_total = pair_forward(
                    q_self[some, lanes],
                    k_self[pl.ds(0, seen), lanes],
                    v_self[pl.ds(0, seen), lanes],
                    causal_edge(BLOCK_ROWS),
                )
                a_self[some, lanes] = blended
                log_self[g, pl.ds(local_row // BLOCK_ROWS, 1)] = log_total

        return carry

    pairs = q_self.shape[1] // PAIR
    lax.fori_loop(0, pairs // 2, self_step, 0)

    def beside_arrives(oz):
        y_a(oz, 1 - y).wait_recv()
        core_a(oz, 1 - y).start()

    def pass_a(oz, arrived, onward, further):
        arrived(oz).wait_recv()
        pl.when(onward)(lambda: further(oz).start())
        y_a(oz, y).start()
        core_a(oz, y).start()

    def pass_b(oz, arrived, onward, further):
        for oy in (y, 1 - y):
            arrived(oz, oy).wait_recv()
            pl.when(onward)(lambda: further(oz, oy).start())
            x_b(oz, oy, x).start()
            core_b(oz, oy, x).start()

    def step_a(step):
        under, over = z - 1 - step, z + 1 + step
        pl.when(under >= 0)(lambda: pass_a(under, up_a, high, up_a))
        pl.when(over < LINE)(lambda: pass_a(over, down_a, low, down_a))

    def step_b(step):
        under, over = z - 1 - step, z + 1 + step
        pl.when(under >= 0)(lambda: pass_b(under, up_b, high, up_b))
        pl.when(over < LINE)(lambda: pass_b(over, down_b, low, down_b))

    step_a(0)
    for oy, held in ((y, True), (1 - y, False)):
        pl.when(high)(lambda oy=oy, held=held: up_b(z, oy, held).start())
        pl.when(low)(lambda oy=oy, held=held: down_b(z, oy, held).start())
    weights_go(range(8, 10))
    x_b(z, 1 - y, x).start()
    lax.fori_loop(pairs // 2, pairs, self_step, 0)
    put[3].start()
    weights_come(range(3, 5))
    for i in range(3, 5):
        weight(1, i, 1 - x, 1 - core).wait_recv()
    for i in range(HELD):
        halves[i].start()

    for piece, place in zip(mine, places):
        summed = hidden[piece].astype(f32) + dot_nn(a_self[place], weights[3][...])
        centred = summed - jnp.mean(summed, axis=-1, keepdims=True)
        inverse = lax.rsqrt(jnp.mean(centred * centred, axis=-1, keepdims=True) + epsilon)
        normal = centred * inverse
        result = normal * first_gain[...] + first_shift[...]
        first_normal[place] = normal
        inverse_out[place] = inverse
        first[place] = result
        first_low[place] = result.astype(bf16)
        q_cross[place] = dot_nn(result.astype(bf16), weights[4][...]).astype(bf16)
    for i in range(4, 8):
        put[i].start()

    step_a(1)
    step_b(0)
    step_a(2)
    step_b(1)
    step_b(2)
    weights_come(range(5, 10))
    beside_arrives(z)
    for step in range(1, LINE):
        pl.when(z - step >= 0)(lambda: beside_arrives(z - step))
        pl.when(z + step < LINE)(lambda: beside_arrives(z + step))

    def across_arrives(oz, oy):
        x_b(oz, oy, 1 - x).wait_recv()
        core_b(oz, oy, 1 - x).start()

    across_arrives(z, 1 - y)
    for step in range(LINE - 1):
        under, over = z - 1 - step, z + 1 + step
        for oy in (y, 1 - y):
            pl.when(under >= 0)(lambda: across_arrives(under, oy))
            pl.when(over < LINE)(lambda: across_arrives(over, oy))

    y_b(y).wait_send()
    x_b(z, 1 - y, x).wait_send()
    for oz in range(LINE):
        y_a(oz, y).wait_send()
        for oy in range(2):
            core_a(oz, oy).wait_send()
            core_a(oz, oy, 1 - core).wait_recv()
            for plane in range(2):
                core_b(oz, oy, plane).wait_send()
                core_b(oz, oy, plane, 1 - core).wait_recv()
        away = oz != z

        @pl.when(away)
        def _():
            for oy in range(2):
                x_b(oz, oy, x).wait_send()

        @pl.when(jnp.logical_and(high, oz <= z))
        def _():
            up_a(oz).wait_send()
            for oy in range(2):
                up_b(oz, oy).wait_send()

        @pl.when(jnp.logical_and(low, oz >= z))
        def _():
            down_a(oz).wait_send()
            for oy in range(2):
                down_b(oz, oy).wait_send()

    own.wait()
    for i in range(10):
        halves[i].wait()
        weight(0, i, x, core).wait_send()
        weight(1, i, 1 - x, core).wait_send()
        if i >= HELD:
            weight(1, i, 1 - x, 1 - core).wait_recv()
    for copy in put:
        copy.wait()


def forward_by_kernel(encoded, weights, hidden, first_gain, first_shift):
    rows, width = encoded.shape
    a_rows = rows * 17 // 24 // 16 * 16
    b_rows = (rows - a_rows) // 2
    shapes = [jax.ShapeDtypeStruct((16 * rows, width), bf16)]
    for i, w in enumerate(weights):
        doubled = (w.shape[0], 2 * w.shape[1]) if i in COLUMNS else (2 * w.shape[0], w.shape[1])
        shapes.append(jax.ShapeDtypeStruct(doubled, bf16))
    total_rows = hidden.shape[0]
    mine, pairs = total_rows // 2, width // PAIR
    kept = [(mine, bf16), (total_rows, bf16), (total_rows, bf16), (mine, bf16)]
    kept += [(mine, f32), (mine, f32), (mine, bf16), (mine, bf16)]
    held = [s.shape if i < HELD else w.shape for i, (s, w) in enumerate(zip(shapes[1:], weights))]
    small = [
        jax.ShapeDtypeStruct((pairs, mine // BLOCK_ROWS, 2 * BLOCK_ROWS), f32),
        jax.ShapeDtypeStruct((mine, 1), f32),
    ]
    dma = pltpu.SemaphoreType.DMA
    anywhere = pl.BlockSpec(memory_space=pl.ANY)
    vmem = pl.BlockSpec(memory_space=pltpu.VMEM)
    out = pl.pallas_call(
        functools.partial(forward_kernel, a_rows, b_rows),
        out_shape=shapes + [jax.ShapeDtypeStruct((n, width), dtype) for n, dtype in kept] + small,
        in_specs=[anywhere] * 12 + [vmem] * 2,
        out_specs=[anywhere] * 19 + [vmem] * 2,
        scratch_shapes=[pltpu.VMEM((rows, width), bf16)]
        + [pltpu.VMEM(shape, bf16) for shape in held]
        + [pltpu.VMEM((n, width), dtype) for n, dtype in kept]
        + [pltpu.VMEM((total_rows, width), bf16)]
        + [dma((12,)), dma, dma((10,)), dma((8,))]
        + [dma((9, 16)), dma((9, 16)), dma((2, 10)), dma((2, 10))],
        compiler_params=pltpu.CompilerParams(
            collective_id=0, has_side_effects=True, vmem_limit_bytes=VMEM_LIMIT
        ),
        name="forward",
    )(encoded, *weights, hidden, first_gain.reshape(1, width), first_shift.reshape(1, width))
    return out[0], tuple(out[1:11]), tuple(out[11:])


TILE = 384
HALF = TILE // 2
PART = HALF // LINE
UNITS = 16
SLOTS = 8
UNIT_WEIGHTS = (8, 8, 8, 8, 9, 9, 9, 9, 7, 5, 6, 4, 3, 0, 1, 2)
LAST_TICK = UNITS + 6


def share_corner(unit, core, plane):
    if unit < 4:
        return core * TILE, (plane * 4 + unit) * TILE
    if unit < 8:
        return (plane * 4 + unit - 4) * TILE, core * TILE
    if unit in (8, 12):
        return plane * TILE, core * TILE
    return core * TILE, plane * TILE


def backward_kernel(*refs):
    (
        expand_grad, reduce_grad, cross_out_grad, picked_rows, keys_in, values_in, q_cross, a_cross,
        g_cross, log_cross, first_low, cross_query, g_second, first_normal, first_inverse, first_gain,
        a_self, self_out, q_self, k_self, v_self, log_self, hidden, self_query, self_key, self_value,
        made, norms,
    ) = refs[:28]
    sums_out, mine_out, theirs_out, made_out, norms_out = refs[28:33]
    (
        own, from_core, from_a, from_b, from_z, summed, pool, pool32, both, staged, dq_cross, dk_sum,
        dv_sum, theirs, rows_in, rows_got, norm_all, norm_in,
        own_sem, core_send, core_recv, a_send, a_recv, b_send, b_recv, z_send, z_recv, gz_send, gz_recv,
        gy_send, gy_recv, gc_send, gc_recv, keep_sem, load_sem, kv_sem, e_sem, extra_send, extra_recv,
        norm_send, norm_recv,
    ) = refs[33:]
    me = Place()
    x, y, z, core = me.x, me.y, me.z, me.core
    sibling, beside, across = me.at(core=1 - core), me.at(y=1 - y), me.at(x=1 - x)
    width = 2 * TILE
    keys = RET_BLOCKS * BLOCK_ROWS
    rows = q_cross.shape[0]
    blocks = rows // BLOCK_ROWS
    pairs = width // PAIR
    chunk = rows // 2

    def rem(u, n):
        return u % n if isinstance(u, int) else lax.rem(u, n)

    def remote(src, dst, send, recv, target):
        return pltpu.make_async_remote_copy(
            src_ref=src, dst_ref=dst, send_sem=send, recv_sem=recv,
            device_id=target, device_id_type=MESH,
        )


    def share(ref, unit, of_core, plane, part):
        row, column = share_corner(unit, of_core, plane)
        return ref.at[
            pl.ds(pl.multiple_of(row + part * HALF, 64), HALF),
            pl.ds(pl.multiple_of(column, 128), TILE),
        ]

    def own_copy(ref, unit, plane, part):
        return pltpu.make_async_copy(
            share(ref, unit, core, plane, part),
            own.at[unit % SLOTS, plane, part],
            own_sem.at[unit % SLOTS, plane * 2 + part],
        )

    def core_copy(src, u, plane, part):
        return remote(
            src, from_core.at[u, plane, part], core_send.at[u, plane * 2 + part],
            core_recv.at[u, plane * 2 + part], sibling,
        )

    def to_core(ref, unit, plane, part):
        return core_copy(share(ref, unit, 1 - core, plane, part), unit, plane, part)

    def a_first(u, slot):
        return remote(own.at[slot, 1 - x], from_a.at[u], a_send.at[u], a_recv.at[u], across)

    def a_second(u, slot):
        return remote(own.at[slot, :, 1 - y], from_a.at[u], a_send.at[u], a_recv.at[u], beside)

    def b_first(u, slot):
        return remote(own.at[slot, x, 1 - y], from_b.at[u], b_send.at[u], b_recv.at[u], beside)

    def b_second(u, slot):
        return remote(own.at[slot, 1 - x, y], from_b.at[u], b_send.at[u], b_recv.at[u], across)

    def to_z(u, slot, d):
        other = lax.rem(z + d, LINE)
        piece = own.at[slot, x, y, pl.ds(pl.multiple_of(other * PART, 16), PART)]
        return remote(
            piece, from_z.at[u, d - 1], z_send.at[u, d - 1], z_recv.at[u, d - 1], me.at(z=other)
        )

    def result(u, of_z):
        return sums_out.at[u, core, pl.ds(pl.multiple_of(y * HALF + of_z * PART, 16), PART)]

    def keep(u):
        return pltpu.make_async_copy(summed.at[u], result(u, z), keep_sem.at[u])

    def gather_z(u, d):
        return remote(
            summed.at[u], result(u, z), gz_send.at[u, d - 1], gz_recv.at[u, d - 1],
            me.at(z=lax.rem(z + d, LINE)),
        )

    def gathered_z(u, d):
        return remote(
            summed.at[u], result(u, lax.rem(z + LINE - d, LINE)), gz_send.at[u, d - 1],
            gz_recv.at[u, d - 1], beside,
        )

    def gather_y(u, at_y):
        piece = sums_out.at[u, core, pl.ds(pl.multiple_of(at_y * HALF, 16), HALF)]
        return remote(piece, piece, gy_send.at[u], gy_recv.at[u], beside)

    def gather_core(u, at_core):
        piece = sums_out.at[u, at_core]
        return remote(piece, piece, gc_send.at[u], gc_recv.at[u], sibling)

    def plus(a, b):
        return (a.astype(f32) + b.astype(f32)).astype(bf16)

    def by_order(u, first, second):
        if isinstance(u, int):
            (first if u % 2 == 0 else second)()
        else:
            pl.when(lax.rem(u, 2) == 0)(first)
            pl.when(lax.rem(u, 2) == 1)(second)

    def stage_core(u):
        slot = rem(u, SLOTS)
        for plane in range(2):
            for part in range(2):
                core_copy(own.at[slot, plane, part], u, plane, part).wait_recv()
        own[slot] = plus(own[slot], from_core[u])
        by_order(u, lambda: a_first(u, slot).start(), lambda: a_second(u, slot).start())

    def stage_a(u):
        slot = rem(u, SLOTS)

        def first():
            a_first(u, slot).wait()
            own[slot, x] = plus(own[slot, x], from_a[u])
            b_first(u, slot).start()

        def second():
            a_second(u, slot).wait()
            own[slot, :, y] = plus(own[slot, :, y], from_a[u])
            b_second(u, slot).start()

        by_order(u, first, second)

    def stage_b(u):
        slot = rem(u, SLOTS)
        by_order(u, lambda: b_first(u, slot).wait(), lambda: b_second(u, slot).wait())
        own[slot, x, y] = plus(own[slot, x, y], from_b[u])
        for d in range(1, LINE):
            to_z(u, slot, d).start()

    def stage_z(u):
        slot = rem(u, SLOTS)
        for d in range(1, LINE):
            to_z(u, slot, d).wait()
        total = own[slot, x, y, pl.ds(pl.multiple_of(z * PART, 16), PART)].astype(f32)
        for d in range(1, LINE):
            total += from_z[u, d - 1].astype(f32)
        summed[u] = total.astype(bf16)
        keep(u).start()
        for d in range(1, LINE):
            gather_z(u, d).start()

    def stage_gather_z(u):
        keep(u).wait()
        for d in range(1, LINE):
            gathered_z(u, d).wait_recv()
            gather_z(u, d).wait_send()
        gather_y(u, y).start()

    def stage_gather_y(u):
        gather_y(u, 1 - y).wait_recv()
        gather_y(u, y).wait_send()
        gather_core(u, core).start()

    def stage_gather_core(u):
        gather_core(u, 1 - core).wait_recv()
        gather_core(u, core).wait_send()

    stages = (
        (0, stage_core), (2, stage_a), (3, stage_b), (4, stage_z), (5, stage_gather_z),
        (6, stage_gather_y), (7, stage_gather_core),
    )

    def tick(t):
        for lag, stage in stages:
            if isinstance(t, int):
                if 0 <= t - lag < UNITS:
                    stage(t - lag)
            else:
                u = t - lag
                pl.when(jnp.logical_and(u >= 0, u < UNITS))(lambda stage=stage, u=u: stage(u))

    KV, E, Q, O, G, FIRST, CROSS_Q, A_SELF, SELF_OUT = (
        0, 4096, 5120, 5632, 6144, 6656, 7168, 7936, 8448
    )
    QS, KS, VS, DQ, DK, DV, HIDDEN, DA = 0, 512, 1536, 2560, 3072, 4096, 5120, 6144
    WQ, WK, WV = 0, 768, 1536

    def load(src, row, sem, into=pool):
        return pltpu.make_async_copy(src, into.at[pl.ds(row, src.shape[0])], load_sem.at[sem])

    def kv_copy(b, which):
        src = (keys_in, values_in)[which].at[pl.ds(pl.multiple_of(b * keys, 128), keys)]
        row = pl.multiple_of(lax.rem(b, 2) * (2 * keys) + which * keys, 128)
        return pltpu.make_async_copy(src, pool.at[pl.ds(row, keys)], kv_sem.at[lax.rem(b, 2), which])

    def e_copy(b):
        src = picked_rows.at[pl.ds(pl.multiple_of(b * keys, 128), keys)]
        return pltpu.make_async_copy(src, pool.at[pl.ds(E, keys)], e_sem)

    early = [
        load(q_cross, Q, 0), load(a_cross, O, 1), load(g_cross, G, 2), load(first_low, FIRST, 3),
        load(cross_query, CROSS_Q, 4), load(a_self, A_SELF, 5), load(self_out, SELF_OUT, 6),
    ]
    for which in range(2):
        kv_copy(jnp.int32(0), which).start()
    for copy in early:
        copy.start()
    ready = [(expand_grad, u) for u in range(4)] + [(reduce_grad, u) for u in range(4, 8)]
    corners = [(plane, part) for plane in range(2) for part in range(2)]
    for ref, unit in ready:
        for plane, part in corners:
            own_copy(ref, unit, plane, part).start()
    me.greet()
    for ref, unit in ready + [(cross_out_grad, 8)]:
        for plane, part in corners:
            to_core(ref, unit, plane, part).start()
    made_copy = remote(made, made_out, extra_send.at[1], extra_recv.at[1], across)
    made_copy.start()
    both_sums = pool32
    both_sums[...] = jnp.zeros_like(both_sums)
    for copy in early[:3]:
        copy.wait()
    for ref, unit in ready:
        for plane, part in corners:
            own_copy(ref, unit, plane, part).wait()

    def at_row(row):
        return pl.ds(pl.multiple_of(row, 128), BLOCK_ROWS)

    def cross_step(i, carry):
        b, g = lax.div(i, pairs), lax.rem(i, pairs)

        @pl.when(g == 0)
        def _():
            for which in range(2):
                kv_copy(b, which).wait()
            e_copy(b).start()

            @pl.when(b + 1 < blocks)
            def _():
                for which in range(2):
                    kv_copy(b + 1, which).start()

        lanes = pl.ds(pl.multiple_of(g * PAIR, PAIR), PAIR)
        row = pl.multiple_of(b * BLOCK_ROWS, BLOCK_ROWS)
        key_row = pl.multiple_of(lax.rem(b, 2) * (2 * keys), 128)
        grad_q, grad_k, grad_v = pair_backward(
            pool[at_row(Q + row), lanes],
            pool[pl.ds(key_row, keys), lanes],
            pool[pl.ds(pl.multiple_of(key_row + keys, 128), keys), lanes],
            None,
            log_cross[b, pl.ds(g, 1)],
            pool[at_row(O + row), lanes],
            pool[at_row(G + row), lanes],
        )
        dq_cross[pl.ds(row, BLOCK_ROWS), lanes] = grad_q.astype(bf16)
        both[:, lanes] = grad_k.astype(bf16)
        both[:, pl.ds(pl.multiple_of(width + g * PAIR, PAIR), PAIR)] = grad_v.astype(bf16)

        @pl.when(g == pairs - 1)
        def _():
            e_copy(b).wait()
            both_sums[pl.ds(0, width)] += dot_tn(pool[pl.ds(E, keys)], both[:, :width])
            both_sums[pl.ds(width, width)] += dot_tn(pool[pl.ds(E, keys)], both[:, width:])

        pl.when(lax.rem(i, 4) == 3)(lambda: tick(lax.div(i, 4)))
        return carry

    lax.fori_loop(0, blocks * pairs, cross_step, 0)

    def hand_over(unit):
        ref = staged.at[unit % 2]
        for plane, part in corners:
            to_core(ref, unit, plane, part).start()
            own_copy(ref, unit, plane, part).start()

    def kept(unit):
        for plane, part in corners:
            own_copy(staged.at[unit % 2], unit, plane, part).wait()

    def left(unit):
        for plane, part in corners:
            to_core(staged.at[unit % 2], unit, plane, part).wait_send()

    def handed_over(unit):
        kept(unit)
        left(unit)

    late = [load(q_self, QS, 7), load(k_self, KS, 8), load(v_self, VS, 9), load(hidden, HIDDEN, 10)]
    for copy in late:
        copy.start()
    for plane, part in corners:
        own_copy(cross_out_grad, 8, plane, part).start()
    staged[1] = both_sums[pl.ds(0, width)].astype(bf16)
    hand_over(9)
    tick(6)
    staged[0] = both_sums[pl.ds(width, width)].astype(bf16)
    hand_over(10)
    g_copy = load(g_second, 0, 11, pool32)
    n_copy = load(first_normal, rows, 12, pool32)
    g_copy.start()
    n_copy.start()
    for copy in early[3:]:
        copy.wait()
    tick(7)
    handed_over(9)
    staged[1] = dot_tn(pool[pl.ds(FIRST, rows)], dq_cross[...]).astype(bf16)
    hand_over(11)

    g_copy.wait()
    n_copy.wait()
    normal = pool32[pl.ds(rows, rows)]
    grad_out = pool32[pl.ds(0, rows)] + dot_nt(dq_cross[...], pool[pl.ds(CROSS_Q, width)])
    scaled = grad_out * first_gain[...]
    grad_in = first_inverse[...] * (
        scaled
        - jnp.mean(scaled, axis=-1, keepdims=True)
        - normal * jnp.mean(scaled * normal, axis=-1, keepdims=True)
    )
    norm_all[...] = norms[...]
    norm_all[pl.ds(0, 1)] = jnp.sum(grad_out * normal, axis=0, keepdims=True)
    norm_all[pl.ds(1, 1)] = jnp.sum(grad_out, axis=0, keepdims=True)
    pool32[pl.ds(2 * rows, rows)] = grad_in
    grad_low = grad_in.astype(bf16)
    pool[pl.ds(DA, rows)] = dot_nt(grad_low, pool[pl.ds(SELF_OUT, width)]).astype(bf16)
    for plane, part in corners:
        own_copy(cross_out_grad, 8, plane, part).wait()
    tick(8)
    handed_over(10)
    staged[0] = dot_tn(pool[pl.ds(A_SELF, rows)], grad_low).astype(bf16)
    hand_over(12)

    along_z = tuple(me.at(z=lax.rem(z + d, LINE)) for d in range(1, LINE))
    rounds = ((sibling,), (across,), (beside,), along_z)

    def norm_copies(which):
        first = min(which, 3)
        return [
            remote(
                norm_all, norm_in.at[first + k], norm_send.at[first + k], norm_recv.at[first + k], target
            )
            for k, target in enumerate(rounds[which])
        ]

    def norm_start(which):
        for copy in norm_copies(which):
            copy.start()

    def norm_finish(which):
        for copy in norm_copies(which):
            copy.wait()
        for k in range(len(rounds[which])):
            norm_all[...] += norm_in[which + k]

    norm_start(0)

    for copy in late:
        copy.wait()
    kept(11)
    kept(12)

    def self_step(g, carry):
        lanes = pl.ds(pl.multiple_of(g * PAIR, PAIR), PAIR)
        dk_sum[...] = jnp.zeros_like(dk_sum)
        dv_sum[...] = jnp.zeros_like(dv_sum)
        for local_row, seen, taken in self_blocks(2, hidden.shape[0], x):

            @pl.when(taken)
            def _():
                mine = pl.ds(local_row, BLOCK_ROWS)
                grad_q, grad_k, grad_v = pair_backward(
                    pool[pl.ds(QS + local_row, BLOCK_ROWS), lanes],
                    pool[pl.ds(KS, seen), lanes],
                    pool[pl.ds(VS, seen), lanes],
                    causal_edge(BLOCK_ROWS),
                    log_self[g, pl.ds(local_row // BLOCK_ROWS, 1)],
                    a_self_rows(local_row, lanes),
                    pool[pl.ds(DA + local_row, BLOCK_ROWS), lanes],
                )
                pool[pl.ds(DQ + local_row, BLOCK_ROWS), lanes] = grad_q.astype(bf16)
                dk_sum[pl.ds(0, seen)] += grad_k
                dv_sum[pl.ds(0, seen)] += grad_v

        pool[pl.ds(DK, hidden.shape[0]), lanes] = dk_sum[...].astype(bf16)
        pool[pl.ds(DV, hidden.shape[0]), lanes] = dv_sum[...].astype(bf16)
        pl.when(lax.rem(g, 2) == 1)(lambda: tick(9 + lax.div(g, 2)))
        return carry

    def a_self_rows(local_row, lanes):
        return pool[pl.ds(A_SELF + local_row, BLOCK_ROWS), lanes]

    lax.fori_loop(0, pairs, self_step, 0)
    norm_finish(0)
    norm_start(1)
    last_loads = [load(self_query, WQ, 13), load(self_key, WK, 14), load(self_value, WV, 15)]
    for copy in last_loads:
        copy.start()

    left(11)
    low_rows = pl.ds(pl.multiple_of(HIDDEN + x * chunk, 128), chunk)
    high_rows = pl.ds(pl.multiple_of(HIDDEN + (3 - x) * chunk, 128), chunk)
    all_rows = hidden.shape[0]
    staged[1] = (
        dot_tn(pool[low_rows], pool[pl.ds(DQ, chunk)])
        + dot_tn(pool[high_rows], pool[pl.ds(DQ + chunk, chunk)])
    ).astype(bf16)
    hand_over(13)
    norm_finish(1)
    norm_start(2)
    left(12)
    staged[0] = dot_tn(pool[pl.ds(HIDDEN, all_rows)], pool[pl.ds(DK, all_rows)]).astype(bf16)
    hand_over(14)
    tick(12)
    handed_over(13)
    staged[1] = dot_tn(pool[pl.ds(HIDDEN, all_rows)], pool[pl.ds(DV, all_rows)]).astype(bf16)
    hand_over(15)
    norm_finish(2)
    norm_start(3)
    tick(13)
    handed_over(14)
    handed_over(15)

    for copy in last_loads:
        copy.wait()

    def row_grads(at_chunk):
        dk = pool[pl.ds(pl.multiple_of(DK + at_chunk * chunk, 128), chunk)]
        dv = pool[pl.ds(pl.multiple_of(DV + at_chunk * chunk, 128), chunk)]
        return dot_nt(dk, pool[pl.ds(WK, width)]) + dot_nt(dv, pool[pl.ds(WV, width)])

    theirs[pl.ds(0, chunk)] = row_grads(1 - x).astype(bf16)
    theirs[pl.ds(chunk, chunk)] = row_grads(2 + x).astype(bf16)
    rows_copy = remote(theirs, rows_in, extra_send.at[0], extra_recv.at[0], across)
    got_copy = remote(rows_got, theirs_out, extra_send.at[2], extra_recv.at[2], across)
    rows_copy.start()
    tick(14)
    for k, at_chunk in enumerate((x, 3 - x)):
        piece = pl.ds(k * chunk, chunk)
        mine_out[piece] = (
            row_grads(at_chunk)
            + dot_nt(pool[pl.ds(DQ + k * chunk, chunk)], pool[pl.ds(WQ, width)])
            + pool32[pl.ds(2 * rows + k * chunk, chunk)]
        )
    norm_finish(3)
    norms_out[...] = norm_all[...]

    def last_step(t, carry):
        tick(t)

        @pl.when(t == 17)
        def _():
            rows_copy.wait()
            whole = mine_out[...] + rows_in[...].astype(f32)
            mine_out[...] = whole
            rows_got[...] = whole.astype(bf16)
            got_copy.start()

        return carry

    lax.fori_loop(15, LAST_TICK + 1, last_step, 0)
    got_copy.wait()
    made_copy.wait()
    for ref, unit in ready + [(cross_out_grad, 8)]:
        for plane, part in corners:
            to_core(ref, unit, plane, part).wait_send()


def backward_by_kernel(*args):
    rows, width = args[6].shape
    all_rows = args[22].shape[0]
    norms = args[27]
    anywhere = pl.BlockSpec(memory_space=pl.ANY)
    vmem = pl.BlockSpec(memory_space=pltpu.VMEM)
    in_specs = [anywhere] * 28
    for i in (9, 14, 15, 21, 27):
        in_specs[i] = vmem
    dma = pltpu.SemaphoreType.DMA
    U, T, H, Z = UNITS, TILE, HALF, LINE - 1
    return pl.pallas_call(
        backward_kernel,
        out_shape=[
            jax.ShapeDtypeStruct((U, 2, T, T), bf16),
            jax.ShapeDtypeStruct((rows, width), f32),
            jax.ShapeDtypeStruct((rows, width), bf16),
            jax.ShapeDtypeStruct((rows, width), bf16),
            jax.ShapeDtypeStruct(norms.shape, f32),
        ],
        in_specs=in_specs,
        out_specs=[anywhere, vmem, anywhere, anywhere, vmem],
        scratch_shapes=[
            pltpu.VMEM((SLOTS, 2, 2, H, T), bf16),
            pltpu.VMEM((U, 2, 2, H, T), bf16),
            pltpu.VMEM((U, 2, H, T), bf16),
            pltpu.VMEM((U, H, T), bf16),
            pltpu.VMEM((U, Z, PART, T), bf16),
            pltpu.VMEM((U, PART, T), bf16),
            pltpu.VMEM((9216, width), bf16),
            pltpu.VMEM((2 * width, width), f32),
            pltpu.VMEM((RET_BLOCKS * BLOCK_ROWS, 2 * width), bf16),
            pltpu.VMEM((2, width, width), bf16),
            pltpu.VMEM((rows, width), bf16),
            pltpu.VMEM((all_rows, PAIR), f32),
            pltpu.VMEM((all_rows, PAIR), f32),
            pltpu.VMEM((rows, width), bf16),
            pltpu.VMEM((rows, width), bf16),
            pltpu.VMEM((rows, width), bf16),
            pltpu.VMEM(norms.shape, f32),
            pltpu.VMEM((6,) + norms.shape, f32),
            dma((SLOTS, 4)), dma((U, 4)), dma((U, 4)), dma((U,)), dma((U,)), dma((U,)), dma((U,)),
            dma((U, Z)), dma((U, Z)), dma((U, Z)), dma((U, Z)), dma((U,)), dma((U,)), dma((U,)),
            dma((U,)), dma((U,)), dma((16,)), dma((2, 2)), dma, dma((3,)), dma((3,)), dma((6,)),
            dma((6,)),
        ],
        compiler_params=pltpu.CompilerParams(
            collective_id=1, has_side_effects=True, vmem_limit_bytes=BACKWARD_VMEM
        ),
        name="backward",
    )(*args)


def output_place(unit, core):
    row, column = share_corner(unit, core, 0)
    return UNIT_WEIGHTS[unit], row, column


def widen_kernel(sums, *refs):
    outs, (taken, given, in_sem, out_sem) = refs[:10], refs[10:]
    depth = taken.shape[0]
    shares = [(unit, core) for unit in range(UNITS) for core in range(2)]

    def fetch(i):
        unit, core = shares[i]
        return pltpu.make_async_copy(sums.at[unit, core], taken.at[i % depth], in_sem.at[i % depth])

    def place(i):
        weight, row, column = output_place(*shares[i])
        return pltpu.make_async_copy(
            given.at[i % depth],
            outs[weight].at[pl.ds(row, TILE), pl.ds(column, TILE)],
            out_sem.at[i % depth],
        )

    for i in range(depth - 1):
        fetch(i).start()
    for i in range(len(shares)):
        if i + depth - 1 < len(shares):
            fetch(i + depth - 1).start()
        fetch(i).wait()
        if i >= depth:
            place(i - depth).wait()
        given[i % depth] = taken[i % depth].astype(f32)
        place(i).start()
    for i in range(len(shares) - depth, len(shares)):
        place(i).wait()


def weight_outputs(sums):
    shapes = [(2 * TILE, TILE)] * 3 + [(TILE, 2 * TILE)] + [(2 * TILE, TILE)] * 3
    shapes += [(TILE, 2 * TILE), (2 * TILE, 4 * TILE), (4 * TILE, 2 * TILE)]
    depth = 6
    return (
        tuple(pl.pallas_call(
            widen_kernel,
            out_shape=[jax.ShapeDtypeStruct(shape, f32) for shape in shapes],
            in_specs=[pl.BlockSpec(memory_space=pl.ANY)],
            out_specs=[pl.BlockSpec(memory_space=pl.ANY)] * 10,
            scratch_shapes=[
                pltpu.VMEM((depth, TILE, TILE), bf16),
                pltpu.VMEM((depth, TILE, TILE), f32),
                pltpu.SemaphoreType.DMA((depth,)),
                pltpu.SemaphoreType.DMA((depth,)),
            ],
            compiler_params=pltpu.CompilerParams(vmem_limit_bytes=VMEM_LIMIT),
            name="widen",
        )(sums)),
    )


FF_COLUMNS = 512


def layer_norm(summed, norm_gain, norm_shift):
    centred = summed - jnp.mean(summed, axis=-1, keepdims=True)
    inverse = lax.rsqrt(jnp.mean(centred * centred, axis=-1, keepdims=True) + epsilon)
    normal = centred * inverse
    return normal * norm_gain + norm_shift, normal, inverse


def dense_kernel(
    a_cross, first, cotangent, cross_out, gain_two, shift_two, gain_three, shift_three, expand_in, reduce_in,
    out_ref, g_second, g_across, cross_out_grad, norms, expand_grad, reduce_grad,
    expand, reduce, activated, slope, expand_staged, reduce_staged,
    expand_sem, reduce_sem, expand_out_sem, reduce_out_sem,
):
    count = expand.shape[1] // FF_COLUMNS

    def piece(c):
        return pl.ds(c * FF_COLUMNS, FF_COLUMNS)

    def fetch_expand(c):
        return pltpu.make_async_copy(
            expand_in.at[:, piece(c)], expand.at[:, piece(c)], expand_sem.at[c]
        )

    def fetch_reduce(c):
        return pltpu.make_async_copy(reduce_in.at[piece(c)], reduce.at[piece(c)], reduce_sem.at[c])

    def put_expand(c):
        return pltpu.make_async_copy(
            expand_staged.at[c % 2], expand_grad.at[:, piece(c)], expand_out_sem.at[c % 2]
        )

    def put_reduce(c):
        return pltpu.make_async_copy(
            reduce_staged.at[c % 2], reduce_grad.at[piece(c)], reduce_out_sem.at[c % 2]
        )

    for c in range(count):
        fetch_expand(c).start()
        fetch_reduce(c).start()
    second, normal_two, inverse_two = layer_norm(
        first[...] + dot_nn(a_cross[...], cross_out[...]), gain_two[...], shift_two[...]
    )
    second_low = second.astype(bf16)
    total = second
    for c in range(count):
        fetch_expand(c).wait()
        pre = dot_nn(second_low, expand[:, piece(c)])
        phi = 0.5 * (1.0 + lax.erf(pre * 0.7071067811865476))
        slope[:, piece(c)] = phi + pre * jnp.exp(-0.5 * pre * pre) * 0.3989422804014327
        activated[:, piece(c)] = (pre * phi).astype(bf16)
        fetch_reduce(c).wait()
        total = total + dot_nn(activated[:, piece(c)], reduce[piece(c)])
    final, normal, inverse = layer_norm(total, gain_three[...], shift_three[...])
    out_ref[...] = final.astype(bf16)
    grad = cotangent[...].astype(f32)
    norms[...] = jnp.zeros_like(norms)

    def back(grad, normal, inverse, gain, row):
        norms[pl.ds(row, 1)] = jnp.sum(grad * normal, axis=0, keepdims=True)
        norms[pl.ds(row + 1, 1)] = jnp.sum(grad, axis=0, keepdims=True)
        scaled = grad * gain
        return inverse * (
            scaled
            - jnp.mean(scaled, axis=-1, keepdims=True)
            - normal * jnp.mean(scaled * normal, axis=-1, keepdims=True)
        )

    grad = back(grad, normal, inverse, gain_three[...], 4)
    grad_low = grad.astype(bf16)
    for c in range(count):
        if c >= 2:
            put_reduce(c - 2).wait()
            put_expand(c - 2).wait()
        reduce_staged[c % 2] = dot_tn(activated[:, piece(c)], grad_low).astype(bf16)
        put_reduce(c).start()
        grad_pre = (dot_nt(grad_low, reduce[piece(c)]) * slope[:, piece(c)]).astype(bf16)
        expand_staged[c % 2] = dot_tn(second_low, grad_pre).astype(bf16)
        put_expand(c).start()
        grad = grad + dot_nt(grad_pre, expand[:, piece(c)])
    grad = back(grad, normal_two, inverse_two, gain_two[...], 2)
    g_second[...] = grad
    grad_low = grad.astype(bf16)
    cross_out_grad[...] = dot_tn(a_cross[...], grad_low).astype(bf16)
    g_across[...] = dot_nt(grad_low, cross_out[...]).astype(bf16)
    for c in range(count - 2, count):
        put_reduce(c).wait()
        put_expand(c).wait()


def dense_by_kernel(a_cross, first, cotangent, cross_out, norm_params, expand, reduce):
    rows, width = first.shape
    hidden_units = expand.shape[1]
    count = hidden_units // FF_COLUMNS
    anywhere = pl.BlockSpec(memory_space=pl.ANY)
    vmem = pl.BlockSpec(memory_space=pltpu.VMEM)
    dma = pltpu.SemaphoreType.DMA
    return pl.pallas_call(
        dense_kernel,
        out_shape=[
            jax.ShapeDtypeStruct((rows, width), bf16),
            jax.ShapeDtypeStruct((rows, width), f32),
            jax.ShapeDtypeStruct((rows, width), bf16),
            jax.ShapeDtypeStruct((width, width), bf16),
            jax.ShapeDtypeStruct((8, width), f32),
            jax.ShapeDtypeStruct(expand.shape, bf16),
            jax.ShapeDtypeStruct(reduce.shape, bf16),
        ],
        in_specs=[vmem] * 8 + [anywhere] * 2,
        out_specs=[vmem] * 5 + [anywhere] * 2,
        scratch_shapes=[
            pltpu.VMEM(expand.shape, bf16),
            pltpu.VMEM(reduce.shape, bf16),
            pltpu.VMEM((rows, hidden_units), bf16),
            pltpu.VMEM((rows, hidden_units), f32),
            pltpu.VMEM((2, width, FF_COLUMNS), bf16),
            pltpu.VMEM((2, FF_COLUMNS, width), bf16),
            dma((count,)),
            dma((count,)),
            dma((2,)),
            dma((2,)),
        ],
        compiler_params=pltpu.CompilerParams(vmem_limit_bytes=VMEM_LIMIT),
        name="dense",
    )(a_cross, first, cotangent, cross_out, *[p.reshape(1, width) for p in norm_params], expand, reduce)


def by_kernels(narrow):
    return lax.axis_size("wide") == 4 * LINE and narrow == 2


def gather_all(encoded, weights):
    everything = lax.all_gather(encoded, "wide", tiled=True)
    full = tuple(
        lax.all_gather(w, "narrow", axis=1 if i in COLUMNS else 0, tiled=True)
        for i, w in enumerate(weights)
    )
    return everything, full


def reduce_all(grads):
    shares = tuple(
        lax.psum_scatter(
            g.astype(bf16), "narrow", scatter_dimension=1 if i in COLUMNS else 0, tiled=True
        )
        for i, g in enumerate(grads)
    )
    return tuple(s.astype(f32) for s in lax.psum(shares, "wide"))


def local(
    hidden,
    encoded,
    retrieved,
    self_query,
    self_key,
    self_value,
    self_out,
    cross_query,
    cross_key,
    cross_value,
    cross_out,
    expand_weight,
    reduce_weight,
    first_gain,
    first_shift,
    second_gain,
    second_shift,
    third_gain,
    third_shift,
    cotangent,
):
    tok_rows, width = hidden.shape
    narrow = lax.axis_size("narrow")
    at = lax.axis_index("narrow").astype(jnp.int32)
    chunk = tok_rows // (2 * narrow)

    def own(rows, size=chunk):
        low = lax.dynamic_slice_in_dim(rows, at * size, size)
        high = lax.dynamic_slice_in_dim(rows, (2 * narrow - 1 - at) * size, size)
        return jnp.concatenate([low, high], axis=0)

    where_at = at.reshape(1)
    picked = own(retrieved, chunk // BLOCK_ROWS).reshape(-1)
    if by_kernels(narrow):
        everything, full, kept = forward_by_kernel(
            encoded,
            (
                self_query,
                self_key,
                self_value,
                self_out,
                cross_query,
                cross_key,
                cross_value,
                cross_out,
                expand_weight,
                reduce_weight,
            ),
            hidden,
            first_gain,
            first_shift,
        )
        query_self, key_self, value_self, blend_self, first, first_normal, first_low = kept[:7]
        query_cross, log_self, first_inverse = kept[7:]
        (self_query, self_key, self_value, self_out, cross_query, cross_key, cross_value) = full[:7]
        (cross_out, expand_weight, reduce_weight) = full[7:]
        blend_cross, log_cross, key_cross, value_cross, picked_rows = cross_forward(
            picked, everything, cross_key, cross_value, query_cross
        )
        output, grad_second_in, grad_blend_cross, cross_out_grad, norms, expand_grad, reduce_grad = (
            dense_by_kernel(
                blend_cross,
                first,
                own(cotangent),
                cross_out,
                (second_gain, second_shift, third_gain, third_shift),
                expand_weight,
                reduce_weight,
            )
        )
        sums, grad_mine, grad_theirs, made_theirs, norm_sums = backward_by_kernel(
            expand_grad,
            reduce_grad,
            cross_out_grad,
            picked_rows,
            key_cross,
            value_cross,
            query_cross,
            blend_cross,
            grad_blend_cross,
            log_cross,
            first_low,
            cross_query,
            grad_second_in,
            first_normal,
            first_inverse,
            first_gain.reshape(1, width),
            blend_self,
            self_out,
            query_self,
            key_self,
            value_self,
            log_self,
            hidden,
            self_query,
            self_key,
            self_value,
            output,
            norms,
        )

        def ordered(ours, others):
            a, b = ours[:chunk], ours[chunk:]
            c, d = others[:chunk], others[chunk:]
            first_one = at == 0
            return jnp.concatenate(
                [
                    jnp.where(first_one, a, c),
                    jnp.where(first_one, c, a),
                    jnp.where(first_one, d, b),
                    jnp.where(first_one, b, d),
                ],
                axis=0,
            )

        return (
            (ordered(output, made_theirs), ordered(grad_mine, grad_theirs.astype(f32)))
            + weight_outputs(sums)[0]
            + tuple(norm_sums[i] for i in range(6))
        )

    everything, full = gather_all(
        encoded,
        (
            self_query,
            self_key,
            self_value,
            self_out,
            cross_query,
            cross_key,
            cross_value,
            cross_out,
            expand_weight,
            reduce_weight,
        ),
    )
    (
        self_query,
        self_key,
        self_value,
        self_out,
        cross_query,
        cross_key,
        cross_value,
        cross_out,
        expand_weight,
        reduce_weight,
    ) = full
    mine = own(hidden)
    grad_final = own(cotangent).astype(f32)

    query_self = project(mine, self_query).astype(bf16)
    key_self = project(hidden, self_key).astype(bf16)
    value_self = project(hidden, self_value).astype(bf16)
    blend_self, log_self = self_forward(narrow, where_at, query_self, key_self, value_self)
    first, first_normal, first_inverse = norm_forward(
        mine.astype(f32) + project(blend_self, self_out), first_gain, first_shift
    )
    first_low = first.astype(bf16)
    query_cross = project(first_low, cross_query).astype(bf16)
    blend_cross, log_cross, key_cross, value_cross, picked_rows = cross_forward(
        picked, everything, cross_key, cross_value, query_cross
    )
    second, second_normal, second_inverse = norm_forward(
        first + project(blend_cross, cross_out), second_gain, second_shift
    )
    second_low = second.astype(bf16)
    pre_act = project(second_low, expand_weight)
    activated = jax.nn.gelu(pre_act, approximate=False).astype(bf16)
    final, third_normal, third_inverse = norm_forward(
        second + project(activated, reduce_weight), third_gain, third_shift
    )
    output = final.astype(bf16)

    grad_third, third_gain_grad, third_shift_grad = norm_backward(
        grad_final, third_normal, third_inverse, third_gain
    )
    grad_ffn = grad_third.astype(bf16)
    reduce_grad = grad_weight(activated, grad_ffn)
    grad_pre = (grad_input(grad_ffn, reduce_weight) * gelu_slope(pre_act)).astype(bf16)
    expand_grad = grad_weight(second_low, grad_pre)
    grad_second = grad_third + grad_input(grad_pre, expand_weight)
    grad_second_in, second_gain_grad, second_shift_grad = norm_backward(
        grad_second, second_normal, second_inverse, second_gain
    )
    grad_cross = grad_second_in.astype(bf16)
    cross_out_grad = grad_weight(blend_cross, grad_cross)
    grad_blend_cross = grad_input(grad_cross, cross_out).astype(bf16)
    grad_query_cross, cross_key_grad, cross_value_grad = cross_backward(
        picked,
        everything,
        key_cross,
        value_cross,
        query_cross,
        log_cross,
        blend_cross,
        grad_blend_cross,
    )
    cross_query_grad = grad_weight(first_low, grad_query_cross)
    grad_first = grad_second_in + grad_input(grad_query_cross, cross_query)
    grad_first_in, first_gain_grad, first_shift_grad = norm_backward(
        grad_first, first_normal, first_inverse, first_gain
    )
    grad_self = grad_first_in.astype(bf16)
    self_out_grad = grad_weight(blend_self, grad_self)
    grad_blend_self = grad_input(grad_self, self_out).astype(bf16)
    grad_query_self, grad_key_self, grad_value_self = self_backward(
        narrow, where_at, query_self, key_self, value_self, log_self, blend_self, grad_blend_self
    )
    self_query_grad = grad_weight(mine, grad_query_self)
    self_key_grad = grad_weight(hidden, grad_key_self)
    self_value_grad = grad_weight(hidden, grad_value_self)
    grad_rows = grad_input(grad_key_self, self_key) + grad_input(grad_value_self, self_value)
    grad_own = grad_first_in + grad_input(grad_query_self, self_query)

    def spread(rows):
        empty = jnp.zeros((tok_rows, width), rows.dtype)
        placed = lax.dynamic_update_slice_in_dim(empty, rows[:chunk], at * chunk, 0)
        return lax.dynamic_update_slice_in_dim(
            placed, rows[chunk:], (2 * narrow - 1 - at) * chunk, 0
        )

    grad_hidden = lax.psum((grad_rows + spread(grad_own)).astype(bf16), "narrow").astype(f32)
    output = lax.psum(spread(output), "narrow")
    weight_grads = reduce_all(
        (
            self_query_grad,
            self_key_grad,
            self_value_grad,
            self_out_grad,
            cross_query_grad,
            cross_key_grad,
            cross_value_grad,
            cross_out_grad,
            expand_grad,
            reduce_grad,
        )
    )
    norm_grads = lax.psum(
        jnp.stack(
            [
                first_gain_grad,
                first_shift_grad,
                second_gain_grad,
                second_shift_grad,
                third_gain_grad,
                third_shift_grad,
            ]
        ),
        ("wide", "narrow"),
    )
    return (output, grad_hidden) + weight_grads + tuple(norm_grads[i] for i in range(6))


def solution(mesh):
    rows = P("wide", None)
    columns_split = P(None, "narrow")
    rows_split = P("narrow", None)
    weights = (columns_split,) * 3 + (rows_split,) + (columns_split,) * 3 + (rows_split,)
    weights += (columns_split, rows_split)
    return jax.shard_map(
        local,
        mesh=mesh,
        in_specs=(rows, rows, rows) + weights + (P(),) * 6 + (rows,),
        out_specs=(rows, rows) + weights + (P(),) * 6,
        check_vma=False,
    )
```

```python
import functools

import jax
import jax.numpy as jnp
from jax import lax
from jax.experimental import pallas as pl
from jax.experimental.pallas import tpu as pltpu
from jax.sharding import PartitionSpec as P

HEAD_DIM = 64
BLOCK_ROWS = 128
RET_BLOCKS = 8
PAIR = 2 * HEAD_DIM
VMEM_LIMIT = 60 << 20
BACKWARD_VMEM = 63 << 20

epsilon = 1e-05
bf16 = jnp.bfloat16
f32 = jnp.float32
MESH = pl.DeviceIdType.MESH


def norm_forward(summed, norm_gain, norm_shift):
    average = jnp.mean(summed, axis=-1, keepdims=True)
    centred = summed - average
    inverse = lax.rsqrt(jnp.mean(centred * centred, axis=-1, keepdims=True) + epsilon)
    normal = centred * inverse
    return (normal * norm_gain + norm_shift, normal, inverse)


def norm_backward(grad_out, normal, inverse, norm_gain):
    scaled = grad_out * norm_gain
    grad_in = inverse * (
        scaled
        - jnp.mean(scaled, axis=-1, keepdims=True)
        - normal * jnp.mean(scaled * normal, axis=-1, keepdims=True)
    )
    return (grad_in, jnp.sum(grad_out * normal, axis=0), jnp.sum(grad_out, axis=0))


def gelu_slope(pre_act):
    return (
        0.5 * (1.0 + lax.erf(pre_act * 0.7071067811865476))
        + pre_act * jnp.exp(-0.5 * pre_act * pre_act) * 0.3989422804014327
    )


def project(rows_in, weight):
    return jnp.dot(rows_in, weight, preferred_element_type=f32)


def grad_weight(left, right):
    return jnp.einsum("ti,to->io", left, right, preferred_element_type=f32)


def grad_input(grad_rows, weight):
    return jnp.einsum("to,io->ti", grad_rows, weight, preferred_element_type=f32)


def dot_nt(left, right):
    return lax.dot_general(left, right, (((1,), (1,)), ((), ())), preferred_element_type=f32)


def dot_tn(left, right):
    return lax.dot_general(left, right, (((0,), (0,)), ((), ())), preferred_element_type=f32)


def dot_nn(left, right):
    return lax.dot_general(left, right, (((1,), (0,)), ((), ())), preferred_element_type=f32)


def stack_heads(pair_rows):
    lane = lax.broadcasted_iota(jnp.int32, pair_rows.shape, 1)
    wide_rows = pair_rows.astype(f32)
    zero = jnp.zeros_like(wide_rows)
    return jnp.concatenate(
        [
            jnp.where(lane < HEAD_DIM, wide_rows, zero).astype(bf16),
            jnp.where(lane < HEAD_DIM, zero, wide_rows).astype(bf16),
        ],
        axis=0,
    )


def merge_heads(both):
    rows = both.shape[1] // 2
    sublane = lax.broadcasted_iota(jnp.int32, (PAIR, rows), 0)
    return jnp.transpose(jnp.where(sublane < HEAD_DIM, both[:, :rows], both[:, rows:]))


def causal_edge(rows):
    key = lax.broadcasted_iota(jnp.int32, (rows, 2 * rows), 0)
    query = lax.broadcasted_iota(jnp.int32, (rows, 2 * rows), 1)
    return key <= jnp.where(query >= rows, query - rows, query)


def scaled_heads(pair_rows):
    return stack_heads(pair_rows.astype(f32) * HEAD_DIM**-0.5)


def pair_forward(queries, keys, values, edge):
    stacked = scaled_heads(queries)
    scores = dot_nt(keys, stacked)
    if edge is not None:
        split = keys.shape[0] - edge.shape[0]
        last = jnp.where(edge, scores[split:], -1e30)
        scores = jnp.concatenate([scores[:split], last], axis=0) if split else last
    top = jnp.max(scores, axis=0, keepdims=True)
    raised = jnp.exp(scores - top)
    total = jnp.sum(raised, axis=0, keepdims=True)
    blended = dot_tn(values, raised.astype(bf16)) / total
    return merge_heads(blended).astype(bf16), top + jnp.log(total)


def pair_backward(queries, keys, values, edge, log_total, blended, grad_blend):
    rows = queries.shape[0]
    stacked = scaled_heads(queries)
    grads = stack_heads(grad_blend)
    scores = dot_nt(keys, stacked)
    if edge is not None:
        split = keys.shape[0] - edge.shape[0]
        last = jnp.where(edge, scores[split:], -1e30)
        scores = jnp.concatenate([scores[:split], last], axis=0) if split else last
    chances = jnp.exp(scores - log_total)
    weighed = jnp.transpose(blended.astype(f32) * grad_blend.astype(f32))
    centre = jnp.concatenate(
        [
            jnp.sum(weighed[:HEAD_DIM], axis=0, keepdims=True),
            jnp.sum(weighed[HEAD_DIM:], axis=0, keepdims=True),
        ],
        axis=1,
    )
    grad_scores = (chances * (dot_nt(values, grads) - centre)).astype(bf16)
    grad_values = dot_nn(chances.astype(bf16), grads)
    grad_keys = dot_nn(grad_scores, stacked)
    grad_queries = merge_heads(dot_tn(keys, grad_scores)) * HEAD_DIM**-0.5
    return grad_queries, grad_keys, grad_values


def self_blocks(narrow, total_rows, at):
    chunk = total_rows // (2 * narrow)
    for block in range(total_rows // BLOCK_ROWS):
        which, within = divmod(block * BLOCK_ROWS, chunk)
        if which < narrow:
            owner, local_row = which, within
        else:
            owner, local_row = 2 * narrow - 1 - which, chunk + within
        yield local_row, (block + 1) * BLOCK_ROWS, at == owner


def self_forward_kernel(narrow, at_ref, q_ref, k_ref, v_ref, o_ref, log_ref):
    for local_row, seen, taken in self_blocks(narrow, k_ref.shape[0], at_ref[0]):

        @pl.when(taken)
        def _():
            mine = pl.ds(local_row, BLOCK_ROWS)
            keys = pl.ds(0, seen)
            blended, log_total = pair_forward(
                q_ref[mine], k_ref[keys], v_ref[keys], causal_edge(BLOCK_ROWS)
            )
            o_ref[mine] = blended
            log_ref[0, pl.ds(local_row // BLOCK_ROWS, 1)] = log_total


def self_forward(narrow, at, queries, keys, values):
    rows, width = queries.shape
    total_rows = keys.shape[0]
    pairs = width // PAIR
    pair = lambda count: pl.BlockSpec((count, PAIR), lambda g, at: (0, g))
    return pl.pallas_call(
        functools.partial(self_forward_kernel, narrow),
        grid_spec=pltpu.PrefetchScalarGridSpec(
            num_scalar_prefetch=1,
            grid=(pairs,),
            in_specs=[pair(rows), pair(total_rows), pair(total_rows)],
            out_specs=[pair(rows), pl.BlockSpec((1, rows // BLOCK_ROWS, 2 * BLOCK_ROWS), lambda g, at: (g, 0, 0))],
        ),
        out_shape=[
            jax.ShapeDtypeStruct((rows, width), bf16),
            jax.ShapeDtypeStruct((pairs, rows // BLOCK_ROWS, 2 * BLOCK_ROWS), f32),
        ],
        compiler_params=pltpu.CompilerParams(vmem_limit_bytes=VMEM_LIMIT),
        name="self_forward",
    )(at, queries, keys, values)


def self_backward_kernel(
    narrow, at_ref, q_ref, k_ref, v_ref, log_ref, o_ref, g_ref, dq_ref, dk_ref, dv_ref, dk_sum, dv_sum
):
    rows = q_ref.shape[0] // 2
    dk_sum[...] = jnp.zeros_like(dk_sum)
    dv_sum[...] = jnp.zeros_like(dv_sum)
    for local_row, seen, taken in self_blocks(narrow, k_ref.shape[0], at_ref[0]):

        @pl.when(taken)
        def _():
            mine = pl.ds(local_row, BLOCK_ROWS)
            keys = pl.ds(0, seen)
            grad_q, grad_k, grad_v = pair_backward(
                q_ref[mine],
                k_ref[keys],
                v_ref[keys],
                causal_edge(BLOCK_ROWS),
                log_ref[0, pl.ds(local_row // BLOCK_ROWS, 1)],
                o_ref[mine],
                g_ref[mine],
            )
            dq_ref[mine] = grad_q.astype(bf16)
            dk_sum[keys] += grad_k
            dv_sum[keys] += grad_v

    dk_ref[...] = dk_sum[...].astype(bf16)
    dv_ref[...] = dv_sum[...].astype(bf16)


def self_backward(narrow, at, queries, keys, values, logs, blended, grads):
    rows, width = queries.shape
    total_rows = keys.shape[0]
    pairs = width // PAIR
    pair = lambda count: pl.BlockSpec((count, PAIR), lambda g, at: (0, g))
    return pl.pallas_call(
        functools.partial(self_backward_kernel, narrow),
        grid_spec=pltpu.PrefetchScalarGridSpec(
            num_scalar_prefetch=1,
            grid=(pairs,),
            in_specs=[
                pair(rows),
                pair(total_rows),
                pair(total_rows),
                pl.BlockSpec((1, rows // BLOCK_ROWS, 2 * BLOCK_ROWS), lambda g, at: (g, 0, 0)),
                pair(rows),
                pair(rows),
            ],
            out_specs=[pair(rows), pair(total_rows), pair(total_rows)],
            scratch_shapes=[pltpu.VMEM((total_rows, PAIR), f32)] * 2,
        ),
        out_shape=[
            jax.ShapeDtypeStruct((rows, width), bf16),
            jax.ShapeDtypeStruct((total_rows, width), bf16),
            jax.ShapeDtypeStruct((total_rows, width), bf16),
        ],
        compiler_params=pltpu.CompilerParams(vmem_limit_bytes=VMEM_LIMIT),
        name="self_backward",
    )(at, queries, keys, values, logs, blended, grads)


def cross_forward_kernel(picked_ref, *refs):
    blocks = refs[:RET_BLOCKS]
    wk_ref, wv_ref, q_ref, o_ref, log_ref, k_ref, v_ref, rows_in = refs[RET_BLOCKS:]
    for j in range(RET_BLOCKS):
        rows_in[pl.ds(j * BLOCK_ROWS, BLOCK_ROWS)] = blocks[j][...]
    k_ref[...] = dot_nn(rows_in[...], wk_ref[...]).astype(bf16)
    v_ref[...] = dot_nn(rows_in[...], wv_ref[...]).astype(bf16)
    for g in range(q_ref.shape[1] // PAIR):
        lanes = pl.ds(g * PAIR, PAIR)
        blended, log_total = pair_forward(q_ref[:, lanes], k_ref[:, lanes], v_ref[:, lanes], None)
        o_ref[:, lanes] = blended
        log_ref[0, pl.ds(g, 1)] = log_total


def block_specs(width):
    def spec(j):
        return pl.BlockSpec((BLOCK_ROWS, width), lambda b, picked: (picked[b * RET_BLOCKS + j], 0))

    return [spec(j) for j in range(RET_BLOCKS)]


def cross_forward(picked, everything, cross_key, cross_value, queries):
    rows, width = queries.shape
    count = rows // BLOCK_ROWS
    pairs = width // PAIR
    keys = RET_BLOCKS * BLOCK_ROWS
    whole = pl.BlockSpec((width, width), lambda b, picked: (0, 0))
    by_block = pl.BlockSpec((BLOCK_ROWS, width), lambda b, picked: (b, 0))
    by_keys = pl.BlockSpec((keys, width), lambda b, picked: (b, 0))
    return pl.pallas_call(
        cross_forward_kernel,
        grid_spec=pltpu.PrefetchScalarGridSpec(
            num_scalar_prefetch=1,
            grid=(count,),
            in_specs=block_specs(width) + [whole, whole, by_block],
            out_specs=[
                by_block,
                pl.BlockSpec((1, pairs, 2 * BLOCK_ROWS), lambda b, picked: (b, 0, 0)),
                by_keys,
                by_keys,
                by_keys,
            ],
        ),
        out_shape=[
            jax.ShapeDtypeStruct((rows, width), bf16),
            jax.ShapeDtypeStruct((count, pairs, 2 * BLOCK_ROWS), f32),
            jax.ShapeDtypeStruct((count * keys, width), bf16),
            jax.ShapeDtypeStruct((count * keys, width), bf16),
            jax.ShapeDtypeStruct((count * keys, width), bf16),
        ],
        compiler_params=pltpu.CompilerParams(vmem_limit_bytes=VMEM_LIMIT),
        name="cross_forward",
    )(picked, *([everything] * RET_BLOCKS), cross_key, cross_value, queries)


def cross_backward_kernel(picked_ref, *refs):
    blocks = refs[:RET_BLOCKS]
    (k_ref, v_ref, q_ref, log_ref, o_ref, g_ref, dq_ref, dwk_ref, dwv_ref, rows_in, both, sums) = refs[
        RET_BLOCKS:
    ]
    width = q_ref.shape[1]
    step = pl.program_id(0)

    @pl.when(step == 0)
    def _():
        sums[...] = jnp.zeros_like(sums)

    for j in range(RET_BLOCKS):
        rows_in[pl.ds(j * BLOCK_ROWS, BLOCK_ROWS)] = blocks[j][...]
    for g in range(width // PAIR):
        lanes = pl.ds(g * PAIR, PAIR)
        grad_q, grad_k, grad_v = pair_backward(
            q_ref[:, lanes],
            k_ref[:, lanes],
            v_ref[:, lanes],
            None,
            log_ref[0, pl.ds(g, 1)],
            o_ref[:, lanes],
            g_ref[:, lanes],
        )
        dq_ref[:, lanes] = grad_q.astype(bf16)
        both[:, lanes] = grad_k.astype(bf16)
        both[:, pl.ds(width + g * PAIR, PAIR)] = grad_v.astype(bf16)
    sums[...] += dot_tn(rows_in[...], both[...])

    @pl.when(step == pl.num_programs(0) - 1)
    def _():
        dwk_ref[...] = sums[:, :width].astype(bf16)
        dwv_ref[...] = sums[:, width:].astype(bf16)


def cross_backward(picked, everything, keys_in, values_in, queries, logs, blended, grads):
    rows, width = queries.shape
    count = rows // BLOCK_ROWS
    pairs = width // PAIR
    keys = RET_BLOCKS * BLOCK_ROWS
    whole = pl.BlockSpec((width, width), lambda b, picked: (0, 0))
    by_block = pl.BlockSpec((BLOCK_ROWS, width), lambda b, picked: (b, 0))
    by_keys = pl.BlockSpec((keys, width), lambda b, picked: (b, 0))
    return pl.pallas_call(
        cross_backward_kernel,
        grid_spec=pltpu.PrefetchScalarGridSpec(
            num_scalar_prefetch=1,
            grid=(count,),
            in_specs=block_specs(width)
            + [
                by_keys,
                by_keys,
                by_block,
                pl.BlockSpec((1, pairs, 2 * BLOCK_ROWS), lambda b, picked: (b, 0, 0)),
                by_block,
                by_block,
            ],
            out_specs=[by_block, whole, whole],
            scratch_shapes=[
                pltpu.VMEM((keys, width), bf16),
                pltpu.VMEM((keys, 2 * width), bf16),
                pltpu.VMEM((width, 2 * width), f32),
            ],
        ),
        out_shape=[
            jax.ShapeDtypeStruct((rows, width), bf16),
            jax.ShapeDtypeStruct((width, width), bf16),
            jax.ShapeDtypeStruct((width, width), bf16),
        ],
        compiler_params=pltpu.CompilerParams(vmem_limit_bytes=VMEM_LIMIT),
        name="cross_backward",
    )(
        picked,
        *([everything] * RET_BLOCKS),
        keys_in,
        values_in,
        queries,
        logs,
        blended,
        grads,
    )


COLUMNS = (0, 1, 2, 4, 5, 6, 8)


LINE = 4
HELD = 5


def as_row(ref):
    return ref[...].reshape(1, ref.shape[0])


class Place:
    def __init__(self):
        wide = lax.axis_index("wide")
        self.x = lax.axis_index("narrow")
        self.core = lax.rem(wide, 2)
        self.y = lax.rem(lax.div(wide, 2), 2)
        self.z = lax.div(wide, 4)
        self.wide = wide

    def at(self, z=None, y=None, core=None, x=None):
        z, y = (self.z if z is None else z), (self.y if y is None else y)
        core = self.core if core is None else core
        return (z * 4 + y * 2 + core, self.x if x is None else x)

    def greet(self):
        barrier = pltpu.get_barrier_semaphore()
        targets = [self.at(core=1 - self.core), self.at(y=1 - self.y), self.at(x=1 - self.x)]
        targets += [self.at(z=lax.rem(self.z + step, LINE)) for step in range(1, LINE)]
        for target in targets:
            pl.semaphore_signal(barrier, inc=1, device_id=target, device_id_type=MESH)
        pl.semaphore_wait(barrier, len(targets))


def forward_kernel(a_rows, b_rows, *refs):
    encoded_in, weights_in = refs[0], refs[1:11]
    hidden_in, first_gain, first_shift = refs[11:14]
    everything, full_out = refs[14], refs[15:25]
    kept_out, (log_self, inverse_out) = refs[25:33], refs[33:35]
    encoded, weights, kept = refs[35], refs[36:46], refs[46:54]
    hidden = refs[54]
    load_sem, own_sem, half_sem, kept_sem, flow_send, flow_recv, weight_send, weight_recv = refs[55:]
    q_self, k_self, v_self, a_self, first, first_normal, first_low, q_cross = kept
    full = weights[:HELD] + full_out[HELD:]
    me = Place()
    rows = encoded.shape[0]
    x, y, z, core = me.x, me.y, me.z, me.core
    low, high = z > 0, z < LINE - 1
    UP_A, DOWN_A, Y_A, UP_B, DOWN_B, Y_B, X_B, CORE_A, CORE_B = range(9)

    own = pltpu.make_async_copy(
        encoded, everything.at[pl.ds(pl.multiple_of(me.wide * rows, 128), rows)], own_sem
    )

    def region(i, ref, plane, part):
        if i in COLUMNS:
            count, columns = ref.shape[0], ref.shape[1] // 2
            start = pl.multiple_of(plane * columns, 128)
            if part is None:
                return ref.at[:, pl.ds(start, columns)]
            first = pl.multiple_of(part * (count // 2), 16)
            return ref.at[pl.ds(first, count // 2), pl.ds(start, columns)]
        count = ref.shape[0] // 2
        if part is None:
            return ref.at[pl.ds(pl.multiple_of(plane * count, 16), count)]
        first = pl.multiple_of(plane * count + part * (count // 2), 16)
        return ref.at[pl.ds(first, count // 2)]

    loads, halves = [], []
    for i in range(10):
        into = region(i, weights[i], x, None) if i < HELD else weights[i]
        loads.append(pltpu.make_async_copy(weights_in[i], into, load_sem.at[i]))
        if i < HELD:
            halves.append(pltpu.make_async_copy(weights[i], full_out[i], half_sem.at[i]))
        else:
            halves.append(
                pltpu.make_async_copy(weights[i], region(i, full[i], x, None), half_sem.at[i])
            )
    loads.append(pltpu.make_async_copy(encoded_in, encoded, load_sem.at[10]))
    loads.append(pltpu.make_async_copy(hidden_in, hidden, load_sem.at[11]))
    loads[10].start()
    for i in range(10):
        loads[i].start()
    loads[11].start()
    me.greet()
    loads[10].wait()

    def flow(kind, owner_z, owner_y, plane, target, from_core=None, held=False):
        owner = owner_z * 2 + owner_y
        start = owner * (2 * rows) + (core if from_core is None else from_core) * rows
        if plane is None:
            size, slot = a_rows, owner
        else:
            start = start + a_rows + plane * b_rows
            size, slot = b_rows, owner + (plane * 8 if kind == CORE_B else 0)
        piece = everything.at[pl.ds(pl.multiple_of(start, 16), size)]
        source = piece
        if held:
            first = 0 if plane is None else pl.multiple_of(a_rows + plane * b_rows, 16)
            source = encoded.at[pl.ds(first, size)]
        return pltpu.make_async_remote_copy(
            src_ref=source,
            dst_ref=piece,
            send_sem=flow_send.at[kind, slot],
            recv_sem=flow_recv.at[kind, slot],
            device_id=target,
            device_id_type=MESH,
        )

    sibling = me.at(core=1 - core)
    beside = me.at(y=1 - y)
    across = me.at(x=1 - x)
    above, below = me.at(z=z + 1), me.at(z=z - 1)

    def up_a(oz, held=False):
        return flow(UP_A, oz, y, None, above, held=held)

    def down_a(oz, held=False):
        return flow(DOWN_A, oz, y, None, below, held=held)

    def up_b(oz, oy, held=False):
        return flow(UP_B, oz, oy, x, above, held=held)

    def down_b(oz, oy, held=False):
        return flow(DOWN_B, oz, oy, x, below, held=held)

    def y_a(oz, oy, held=False):
        return flow(Y_A, oz, oy, None, beside, held=held)

    def y_b(oy, held=False):
        return flow(Y_B, z, oy, x, beside, held=held)

    def x_b(oz, oy, plane):
        return flow(X_B, oz, oy, plane, across)

    def core_a(oz, oy, from_core=None, held=False):
        return flow(CORE_A, oz, oy, None, sibling, from_core, held)

    def core_b(oz, oy, plane, from_core=None, held=False):
        return flow(CORE_B, oz, oy, plane, sibling, from_core, held)

    def weight(way, i, plane, part):
        piece = region(i, full[i], plane, part)
        if way == 0 and i >= HELD:
            piece_in = weights[i]
            count = piece_in.shape[0] // 2
            piece_in = piece_in.at[pl.ds(pl.multiple_of(part * count, 16), count)]
        else:
            piece_in = piece
        return pltpu.make_async_remote_copy(
            src_ref=piece_in,
            dst_ref=piece,
            send_sem=weight_send.at[way, i],
            recv_sem=weight_recv.at[way, i],
            device_id=across if way == 0 else sibling,
            device_id_type=MESH,
        )

    y_b(y, True).start()
    y_a(z, y, True).start()
    pl.when(high)(lambda: up_a(z, True).start())
    pl.when(low)(lambda: down_a(z, True).start())

    def weights_go(some):
        for i in some:
            weight(0, i, x, core).start()

    def weights_come(some):
        for i in some:
            weight(0, i, 1 - x, core).wait_recv()
            weight(1, i, 1 - x, core).start()

    for i in range(3):
        loads[i].wait()
    weights_go(range(3))
    core_a(z, y, held=True).start()
    core_b(z, y, 0, held=True).start()
    core_b(z, y, 1, held=True).start()
    own.start()
    for i in range(3, 12):
        if i != 10:
            loads[i].wait()
    for i in range(HELD, 10):
        halves[i].start()

    y_b(1 - y).wait_recv()
    core_b(z, 1 - y, x).start()
    weights_come(range(3))
    weights_go(range(3, 8))
    for i in range(3):
        weight(1, i, 1 - x, 1 - core).wait_recv()

    total_rows = hidden.shape[0]
    chunk = total_rows // 4
    mine = (
        pl.ds(pl.multiple_of(x * chunk, 128), chunk),
        pl.ds(pl.multiple_of((3 - x) * chunk, 128), chunk),
    )
    places = (pl.ds(0, chunk), pl.ds(chunk, chunk))
    for piece, place in zip(mine, places):
        q_self[place] = dot_nn(hidden[piece], weights[0][...]).astype(bf16)
    k_self[...] = dot_nn(hidden[...], weights[1][...]).astype(bf16)
    v_self[...] = dot_nn(hidden[...], weights[2][...]).astype(bf16)
    put = [pltpu.make_async_copy(kept[i], kept_out[i], kept_sem.at[i]) for i in range(8)]
    for i in range(3):
        put[i].start()

    def self_step(g, carry):
        lanes = pl.ds(pl.multiple_of(g * PAIR, PAIR), PAIR)
        for local_row, seen, taken in self_blocks(2, total_rows, x):

            @pl.when(taken)
            def _():
                some = pl.ds(local_row, BLOCK_ROWS)
                blended, log_total = pair_forward(
                    q_self[some, lanes],
                    k_self[pl.ds(0, seen), lanes],
                    v_self[pl.ds(0, seen), lanes],
                    causal_edge(BLOCK_ROWS),
                )
                a_self[some, lanes] = blended
                log_self[g, pl.ds(local_row // BLOCK_ROWS, 1)] = log_total

        return carry

    pairs = q_self.shape[1] // PAIR
    lax.fori_loop(0, pairs // 2, self_step, 0)

    def beside_arrives(oz):
        y_a(oz, 1 - y).wait_recv()
        core_a(oz, 1 - y).start()

    def pass_a(oz, arrived, onward, further):
        arrived(oz).wait_recv()
        pl.when(onward)(lambda: further(oz).start())
        y_a(oz, y).start()
        core_a(oz, y).start()

    def pass_b(oz, arrived, onward, further):
        for oy in (y, 1 - y):
            arrived(oz, oy).wait_recv()
            pl.when(onward)(lambda: further(oz, oy).start())
            x_b(oz, oy, x).start()
            core_b(oz, oy, x).start()

    def step_a(step):
        under, over = z - 1 - step, z + 1 + step
        pl.when(under >= 0)(lambda: pass_a(under, up_a, high, up_a))
        pl.when(over < LINE)(lambda: pass_a(over, down_a, low, down_a))

    def step_b(step):
        under, over = z - 1 - step, z + 1 + step
        pl.when(under >= 0)(lambda: pass_b(under, up_b, high, up_b))
        pl.when(over < LINE)(lambda: pass_b(over, down_b, low, down_b))

    step_a(0)
    for oy, held in ((y, True), (1 - y, False)):
        pl.when(high)(lambda oy=oy, held=held: up_b(z, oy, held).start())
        pl.when(low)(lambda oy=oy, held=held: down_b(z, oy, held).start())
    weights_go(range(8, 10))
    x_b(z, 1 - y, x).start()
    lax.fori_loop(pairs // 2, pairs, self_step, 0)
    put[3].start()
    weights_come(range(3, 5))
    for i in range(3, 5):
        weight(1, i, 1 - x, 1 - core).wait_recv()
    for i in range(HELD):
        halves[i].start()

    for piece, place in zip(mine, places):
        summed = hidden[piece].astype(f32) + dot_nn(a_self[place], weights[3][...])
        centred = summed - jnp.mean(summed, axis=-1, keepdims=True)
        inverse = lax.rsqrt(jnp.mean(centred * centred, axis=-1, keepdims=True) + epsilon)
        normal = centred * inverse
        result = normal * as_row(first_gain) + as_row(first_shift)
        first_normal[place] = normal
        inverse_out[place] = inverse
        first[place] = result
        first_low[place] = result.astype(bf16)
        q_cross[place] = dot_nn(result.astype(bf16), weights[4][...]).astype(bf16)
    for i in range(4, 8):
        put[i].start()

    step_a(1)
    step_b(0)
    step_a(2)
    step_b(1)
    step_b(2)
    weights_come(range(5, 10))
    beside_arrives(z)
    for step in range(1, LINE):
        pl.when(z - step >= 0)(lambda: beside_arrives(z - step))
        pl.when(z + step < LINE)(lambda: beside_arrives(z + step))

    def across_arrives(oz, oy):
        x_b(oz, oy, 1 - x).wait_recv()
        core_b(oz, oy, 1 - x).start()

    across_arrives(z, 1 - y)
    for step in range(LINE - 1):
        under, over = z - 1 - step, z + 1 + step
        for oy in (y, 1 - y):
            pl.when(under >= 0)(lambda: across_arrives(under, oy))
            pl.when(over < LINE)(lambda: across_arrives(over, oy))

    y_b(y).wait_send()
    x_b(z, 1 - y, x).wait_send()
    for oz in range(LINE):
        y_a(oz, y).wait_send()
        for oy in range(2):
            core_a(oz, oy).wait_send()
            core_a(oz, oy, 1 - core).wait_recv()
            for plane in range(2):
                core_b(oz, oy, plane).wait_send()
                core_b(oz, oy, plane, 1 - core).wait_recv()
        away = oz != z

        @pl.when(away)
        def _():
            for oy in range(2):
                x_b(oz, oy, x).wait_send()

        @pl.when(jnp.logical_and(high, oz <= z))
        def _():
            up_a(oz).wait_send()
            for oy in range(2):
                up_b(oz, oy).wait_send()

        @pl.when(jnp.logical_and(low, oz >= z))
        def _():
            down_a(oz).wait_send()
            for oy in range(2):
                down_b(oz, oy).wait_send()

    own.wait()
    for i in range(10):
        halves[i].wait()
        weight(0, i, x, core).wait_send()
        weight(1, i, 1 - x, core).wait_send()
        if i >= HELD:
            weight(1, i, 1 - x, 1 - core).wait_recv()
    for copy in put:
        copy.wait()


def forward_by_kernel(encoded, weights, hidden, first_gain, first_shift):
    rows, width = encoded.shape
    a_rows = rows * 17 // 24 // 16 * 16
    b_rows = (rows - a_rows) // 2
    shapes = [jax.ShapeDtypeStruct((16 * rows, width), bf16)]
    for i, w in enumerate(weights):
        doubled = (w.shape[0], 2 * w.shape[1]) if i in COLUMNS else (2 * w.shape[0], w.shape[1])
        shapes.append(jax.ShapeDtypeStruct(doubled, bf16))
    total_rows = hidden.shape[0]
    mine, pairs = total_rows // 2, width // PAIR
    kept = [(mine, bf16), (total_rows, bf16), (total_rows, bf16), (mine, bf16)]
    kept += [(mine, f32), (mine, f32), (mine, bf16), (mine, bf16)]
    held = [s.shape if i < HELD else w.shape for i, (s, w) in enumerate(zip(shapes[1:], weights))]
    small = [
        jax.ShapeDtypeStruct((pairs, mine // BLOCK_ROWS, 2 * BLOCK_ROWS), f32),
        jax.ShapeDtypeStruct((mine, 1), f32),
    ]
    dma = pltpu.SemaphoreType.DMA
    anywhere = pl.BlockSpec(memory_space=pl.ANY)
    vmem = pl.BlockSpec(memory_space=pltpu.VMEM)
    out = pl.pallas_call(
        functools.partial(forward_kernel, a_rows, b_rows),
        out_shape=shapes + [jax.ShapeDtypeStruct((n, width), dtype) for n, dtype in kept] + small,
        in_specs=[anywhere] * 12 + [vmem] * 2,
        out_specs=[anywhere] * 19 + [vmem] * 2,
        scratch_shapes=[pltpu.VMEM((rows, width), bf16)]
        + [pltpu.VMEM(shape, bf16) for shape in held]
        + [pltpu.VMEM((n, width), dtype) for n, dtype in kept]
        + [pltpu.VMEM((total_rows, width), bf16)]
        + [dma((12,)), dma, dma((10,)), dma((8,))]
        + [dma((9, 16)), dma((9, 16)), dma((2, 10)), dma((2, 10))],
        compiler_params=pltpu.CompilerParams(
            collective_id=0, has_side_effects=True, vmem_limit_bytes=VMEM_LIMIT
        ),
        name="forward",
    )(encoded, *weights, hidden, first_gain, first_shift)
    return out[0], tuple(out[1:11]), tuple(out[11:])


TILE = 384
HALF = TILE // 2
PART = HALF // LINE
UNITS = 16
SLOTS = 12
UNIT_WEIGHTS = (8, 8, 8, 8, 9, 9, 9, 9, 7, 5, 6, 4, 3, 0, 1, 2)
LAST_TICK = UNITS + 11


def share_corner(unit, core, plane):
    if unit < 4:
        return core * TILE, (plane * 4 + unit) * TILE
    if unit < 8:
        return (plane * 4 + unit - 4) * TILE, core * TILE
    if unit in (8, 12):
        return plane * TILE, core * TILE
    return core * TILE, plane * TILE


def backward_kernel(*refs):
    (
        expand_grad, reduce_grad, cross_out_grad, picked_rows, keys_in, values_in, q_cross, a_cross,
        g_cross, log_cross, first_low, cross_query, g_second, first_normal, first_inverse, first_gain,
        a_self, self_out, q_self, k_self, v_self, log_self, hidden, self_query, self_key, self_value,
        norms,
    ) = refs[:27]
    sums_out, mine_out, theirs_out, norms_out = refs[27:31]
    (
        own, from_core, from_a, from_b, from_z, summed, pool, pool32, both, staged, dq_cross, dk_sum,
        dv_sum, theirs, rows_in, rows_got, norm_all, norm_in,
        own_sem, core_send, core_recv, a_send, a_recv, b_send, b_recv, z_send, z_recv, gz_send, gz_recv,
        gy_send, gy_recv, gc_send, gc_recv, keep_sem, load_sem, kv_sem, e_sem, extra_send, extra_recv,
        norm_send, norm_recv,
    ) = refs[31:]
    me = Place()
    x, y, z, core = me.x, me.y, me.z, me.core
    sibling, beside, across = me.at(core=1 - core), me.at(y=1 - y), me.at(x=1 - x)
    width = 2 * TILE
    keys = RET_BLOCKS * BLOCK_ROWS
    rows = q_cross.shape[0]
    blocks = rows // BLOCK_ROWS
    pairs = width // PAIR
    chunk = rows // 2

    def rem(u, n):
        return u % n if isinstance(u, int) else lax.rem(u, n)

    def remote(src, dst, send, recv, target):
        return pltpu.make_async_remote_copy(
            src_ref=src, dst_ref=dst, send_sem=send, recv_sem=recv,
            device_id=target, device_id_type=MESH,
        )


    def share(ref, unit, of_core, plane, part):
        row, column = share_corner(unit, of_core, plane)
        return ref.at[
            pl.ds(pl.multiple_of(row + part * HALF, 64), HALF),
            pl.ds(pl.multiple_of(column, 128), TILE),
        ]

    def own_copy(ref, unit, plane, part):
        return pltpu.make_async_copy(
            share(ref, unit, core, plane, part),
            own.at[unit % SLOTS, plane, part],
            own_sem.at[unit % SLOTS, plane * 2 + part],
        )

    def core_copy(src, u, plane, part):
        return remote(
            src, from_core.at[u, plane, part], core_send.at[u, plane * 2 + part],
            core_recv.at[u, plane * 2 + part], sibling,
        )

    def to_core(ref, unit, plane, part):
        return core_copy(share(ref, unit, 1 - core, plane, part), unit, plane, part)

    def a_first(u, slot):
        return remote(own.at[slot, 1 - x], from_a.at[u], a_send.at[u], a_recv.at[u], across)

    def a_second(u, slot):
        return remote(own.at[slot, :, 1 - y], from_a.at[u], a_send.at[u], a_recv.at[u], beside)

    def b_first(u, slot):
        return remote(own.at[slot, x, 1 - y], from_b.at[u], b_send.at[u], b_recv.at[u], beside)

    def b_second(u, slot):
        return remote(own.at[slot, 1 - x, y], from_b.at[u], b_send.at[u], b_recv.at[u], across)

    def to_z(u, slot, d):
        other = lax.rem(z + d, LINE)
        piece = own.at[slot, x, y, pl.ds(pl.multiple_of(other * PART, 16), PART)]
        return remote(
            piece, from_z.at[u, d - 1], z_send.at[u, d - 1], z_recv.at[u, d - 1], me.at(z=other)
        )

    def result(u, of_z):
        return sums_out.at[u, core, pl.ds(pl.multiple_of(y * HALF + of_z * PART, 16), PART)]

    def keep(u):
        return pltpu.make_async_copy(summed.at[u], result(u, z), keep_sem.at[u])

    def gather_z(u, d):
        return remote(
            summed.at[u], result(u, z), gz_send.at[u, d - 1], gz_recv.at[u, d - 1],
            me.at(z=lax.rem(z + d, LINE)),
        )

    def gathered_z(u, d):
        return remote(
            summed.at[u], result(u, lax.rem(z + LINE - d, LINE)), gz_send.at[u, d - 1],
            gz_recv.at[u, d - 1], beside,
        )

    def gather_y(u, at_y):
        piece = sums_out.at[u, core, pl.ds(pl.multiple_of(at_y * HALF, 16), HALF)]
        return remote(piece, piece, gy_send.at[u], gy_recv.at[u], beside)

    def gather_core(u, at_core):
        piece = sums_out.at[u, at_core]
        return remote(piece, piece, gc_send.at[u], gc_recv.at[u], sibling)

    def plus(a, b):
        return (a.astype(f32) + b.astype(f32)).astype(bf16)

    def by_order(u, first, second):
        if isinstance(u, int):
            (first if u % 2 == 0 else second)()
        else:
            pl.when(lax.rem(u, 2) == 0)(first)
            pl.when(lax.rem(u, 2) == 1)(second)

    def stage_core(u):
        slot = rem(u, SLOTS)
        for plane in range(2):
            for part in range(2):
                core_copy(own.at[slot, plane, part], u, plane, part).wait_recv()
        own[slot] = plus(own[slot], from_core[u])
        by_order(u, lambda: a_first(u, slot).start(), lambda: a_second(u, slot).start())

    def stage_a(u):
        slot = rem(u, SLOTS)

        def first():
            a_first(u, slot).wait()
            own[slot, x] = plus(own[slot, x], from_a[u])
            b_first(u, slot).start()

        def second():
            a_second(u, slot).wait()
            own[slot, :, y] = plus(own[slot, :, y], from_a[u])
            b_second(u, slot).start()

        by_order(u, first, second)

    def stage_b(u):
        slot = rem(u, SLOTS)
        by_order(u, lambda: b_first(u, slot).wait(), lambda: b_second(u, slot).wait())
        own[slot, x, y] = plus(own[slot, x, y], from_b[u])
        for d in range(1, LINE):
            to_z(u, slot, d).start()

    def stage_z(u):
        slot = rem(u, SLOTS)
        for d in range(1, LINE):
            to_z(u, slot, d).wait()
        total = own[slot, x, y, pl.ds(pl.multiple_of(z * PART, 16), PART)].astype(f32)
        for d in range(1, LINE):
            total += from_z[u, d - 1].astype(f32)
        summed[u] = total.astype(bf16)
        keep(u).start()
        for d in range(1, LINE):
            gather_z(u, d).start()

    def stage_gather_z(u):
        keep(u).wait()
        for d in range(1, LINE):
            gathered_z(u, d).wait_recv()
            gather_z(u, d).wait_send()
        gather_y(u, y).start()

    def stage_gather_y(u):
        gather_y(u, 1 - y).wait_recv()
        gather_y(u, y).wait_send()
        gather_core(u, core).start()

    def stage_gather_core(u):
        gather_core(u, 1 - core).wait_recv()
        gather_core(u, core).wait_send()

    stages = (
        (0, stage_core), (2, stage_a), (4, stage_b), (6, stage_z), (8, stage_gather_z),
        (10, stage_gather_y), (12, stage_gather_core),
    )

    def tick(t):
        for lag, stage in stages:
            if isinstance(t, int):
                if 0 <= t - lag < UNITS:
                    stage(t - lag)
            else:
                u = t - lag
                pl.when(jnp.logical_and(u >= 0, u < UNITS))(lambda stage=stage, u=u: stage(u))

    KV, E, Q, O, G, FIRST, CROSS_Q, A_SELF, SELF_OUT = (
        0, 4096, 5120, 5632, 6144, 6656, 7168, 7936, 8448
    )
    QS, KS, VS, DQ, DK, DV, HIDDEN, DA = 0, 512, 1536, 2560, 3072, 4096, 5120, 6144
    WQ, WK, WV = 0, 768, 1536

    def load(src, row, sem, into=pool):
        return pltpu.make_async_copy(src, into.at[pl.ds(row, src.shape[0])], load_sem.at[sem])

    def kv_copy(b, which):
        src = (keys_in, values_in)[which].at[pl.ds(pl.multiple_of(b * keys, 128), keys)]
        row = pl.multiple_of(lax.rem(b, 2) * (2 * keys) + which * keys, 128)
        return pltpu.make_async_copy(src, pool.at[pl.ds(row, keys)], kv_sem.at[lax.rem(b, 2), which])

    def e_copy(b):
        src = picked_rows.at[pl.ds(pl.multiple_of(b * keys, 128), keys)]
        return pltpu.make_async_copy(src, pool.at[pl.ds(E, keys)], e_sem)

    early = [
        load(q_cross, Q, 0), load(a_cross, O, 1), load(g_cross, G, 2), load(first_low, FIRST, 3),
        load(cross_query, CROSS_Q, 4), load(a_self, A_SELF, 5), load(self_out, SELF_OUT, 6),
    ]
    for which in range(2):
        kv_copy(jnp.int32(0), which).start()
    for copy in early:
        copy.start()
    ready = [(expand_grad, u) for u in range(4)] + [(reduce_grad, u) for u in range(4, 8)]
    corners = [(plane, part) for plane in range(2) for part in range(2)]
    for ref, unit in ready:
        for plane, part in corners:
            own_copy(ref, unit, plane, part).start()
    me.greet()
    for ref, unit in ready + [(cross_out_grad, 8)]:
        for plane, part in corners:
            to_core(ref, unit, plane, part).start()
    both_sums = pool32
    both_sums[...] = jnp.zeros_like(both_sums)
    for copy in early[:3]:
        copy.wait()
    for ref, unit in ready:
        for plane, part in corners:
            own_copy(ref, unit, plane, part).wait()

    def at_row(row):
        return pl.ds(pl.multiple_of(row, 128), BLOCK_ROWS)

    def cross_step(i, carry):
        b, g = lax.div(i, pairs), lax.rem(i, pairs)

        @pl.when(g == 0)
        def _():
            for which in range(2):
                kv_copy(b, which).wait()
            e_copy(b).start()

            @pl.when(b + 1 < blocks)
            def _():
                for which in range(2):
                    kv_copy(b + 1, which).start()

        lanes = pl.ds(pl.multiple_of(g * PAIR, PAIR), PAIR)
        row = pl.multiple_of(b * BLOCK_ROWS, BLOCK_ROWS)
        key_row = pl.multiple_of(lax.rem(b, 2) * (2 * keys), 128)
        grad_q, grad_k, grad_v = pair_backward(
            pool[at_row(Q + row), lanes],
            pool[pl.ds(key_row, keys), lanes],
            pool[pl.ds(pl.multiple_of(key_row + keys, 128), keys), lanes],
            None,
            log_cross[b, pl.ds(g, 1)],
            pool[at_row(O + row), lanes],
            pool[at_row(G + row), lanes],
        )
        dq_cross[pl.ds(row, BLOCK_ROWS), lanes] = grad_q.astype(bf16)
        both[:, lanes] = grad_k.astype(bf16)
        both[:, pl.ds(pl.multiple_of(width + g * PAIR, PAIR), PAIR)] = grad_v.astype(bf16)

        @pl.when(g == pairs - 1)
        def _():
            e_copy(b).wait()
            both_sums[pl.ds(0, width)] += dot_tn(pool[pl.ds(E, keys)], both[:, :width])
            both_sums[pl.ds(width, width)] += dot_tn(pool[pl.ds(E, keys)], both[:, width:])

        pl.when(lax.rem(i, 4) == 3)(lambda: tick(lax.div(i, 4)))
        return carry

    lax.fori_loop(0, blocks * pairs, cross_step, 0)

    def hand_over(unit):
        ref = staged.at[unit % 2]
        for plane, part in corners:
            to_core(ref, unit, plane, part).start()
            own_copy(ref, unit, plane, part).start()

    def kept(unit):
        for plane, part in corners:
            own_copy(staged.at[unit % 2], unit, plane, part).wait()

    def left(unit):
        for plane, part in corners:
            to_core(staged.at[unit % 2], unit, plane, part).wait_send()

    def handed_over(unit):
        kept(unit)
        left(unit)

    late = [load(q_self, QS, 7), load(k_self, KS, 8), load(v_self, VS, 9), load(hidden, HIDDEN, 10)]
    for copy in late:
        copy.start()
    for plane, part in corners:
        own_copy(cross_out_grad, 8, plane, part).start()
    staged[1] = both_sums[pl.ds(0, width)].astype(bf16)
    hand_over(9)
    tick(6)
    staged[0] = both_sums[pl.ds(width, width)].astype(bf16)
    hand_over(10)
    g_copy = load(g_second, 0, 11, pool32)
    n_copy = load(first_normal, rows, 12, pool32)
    g_copy.start()
    n_copy.start()
    for copy in early[3:]:
        copy.wait()
    tick(7)
    handed_over(9)
    staged[1] = dot_tn(pool[pl.ds(FIRST, rows)], dq_cross[...]).astype(bf16)
    hand_over(11)

    g_copy.wait()
    n_copy.wait()
    normal = pool32[pl.ds(rows, rows)]
    grad_out = pool32[pl.ds(0, rows)] + dot_nt(dq_cross[...], pool[pl.ds(CROSS_Q, width)])
    scaled = grad_out * as_row(first_gain)
    grad_in = first_inverse[...] * (
        scaled
        - jnp.mean(scaled, axis=-1, keepdims=True)
        - normal * jnp.mean(scaled * normal, axis=-1, keepdims=True)
    )
    norm_all[...] = norms[...]
    norm_all[pl.ds(0, 1)] = jnp.sum(grad_out * normal, axis=0, keepdims=True)
    norm_all[pl.ds(1, 1)] = jnp.sum(grad_out, axis=0, keepdims=True)
    pool32[pl.ds(2 * rows, rows)] = grad_in
    grad_low = grad_in.astype(bf16)
    pool[pl.ds(DA, rows)] = dot_nt(grad_low, pool[pl.ds(SELF_OUT, width)]).astype(bf16)
    for plane, part in corners:
        own_copy(cross_out_grad, 8, plane, part).wait()
    tick(8)
    handed_over(10)
    staged[0] = dot_tn(pool[pl.ds(A_SELF, rows)], grad_low).astype(bf16)
    hand_over(12)

    along_z = tuple(me.at(z=lax.rem(z + d, LINE)) for d in range(1, LINE))
    rounds = ((sibling,), (across,), (beside,), along_z)

    def norm_copies(which):
        first = min(which, 3)
        return [
            remote(
                norm_all, norm_in.at[first + k], norm_send.at[first + k], norm_recv.at[first + k], target
            )
            for k, target in enumerate(rounds[which])
        ]

    def norm_start(which):
        for copy in norm_copies(which):
            copy.start()

    def norm_finish(which):
        for copy in norm_copies(which):
            copy.wait()
        for k in range(len(rounds[which])):
            norm_all[...] += norm_in[which + k]

    norm_start(0)

    for copy in late:
        copy.wait()
    kept(11)
    kept(12)

    def self_step(g, carry):
        lanes = pl.ds(pl.multiple_of(g * PAIR, PAIR), PAIR)
        dk_sum[...] = jnp.zeros_like(dk_sum)
        dv_sum[...] = jnp.zeros_like(dv_sum)
        for local_row, seen, taken in self_blocks(2, hidden.shape[0], x):

            @pl.when(taken)
            def _():
                mine = pl.ds(local_row, BLOCK_ROWS)
                grad_q, grad_k, grad_v = pair_backward(
                    pool[pl.ds(QS + local_row, BLOCK_ROWS), lanes],
                    pool[pl.ds(KS, seen), lanes],
                    pool[pl.ds(VS, seen), lanes],
                    causal_edge(BLOCK_ROWS),
                    log_self[g, pl.ds(local_row // BLOCK_ROWS, 1)],
                    a_self_rows(local_row, lanes),
                    pool[pl.ds(DA + local_row, BLOCK_ROWS), lanes],
                )
                pool[pl.ds(DQ + local_row, BLOCK_ROWS), lanes] = grad_q.astype(bf16)
                dk_sum[pl.ds(0, seen)] += grad_k
                dv_sum[pl.ds(0, seen)] += grad_v

        pool[pl.ds(DK, hidden.shape[0]), lanes] = dk_sum[...].astype(bf16)
        pool[pl.ds(DV, hidden.shape[0]), lanes] = dv_sum[...].astype(bf16)
        pl.when(lax.rem(g, 2) == 1)(lambda: tick(9 + lax.div(g, 2)))
        return carry

    def a_self_rows(local_row, lanes):
        return pool[pl.ds(A_SELF + local_row, BLOCK_ROWS), lanes]

    lax.fori_loop(0, pairs, self_step, 0)
    norm_finish(0)
    norm_start(1)
    last_loads = [load(self_query, WQ, 13), load(self_key, WK, 14), load(self_value, WV, 15)]
    for copy in last_loads:
        copy.start()

    left(11)
    low_rows = pl.ds(pl.multiple_of(HIDDEN + x * chunk, 128), chunk)
    high_rows = pl.ds(pl.multiple_of(HIDDEN + (3 - x) * chunk, 128), chunk)
    all_rows = hidden.shape[0]
    staged[1] = (
        dot_tn(pool[low_rows], pool[pl.ds(DQ, chunk)])
        + dot_tn(pool[high_rows], pool[pl.ds(DQ + chunk, chunk)])
    ).astype(bf16)
    hand_over(13)
    norm_finish(1)
    norm_start(2)
    left(12)
    staged[0] = dot_tn(pool[pl.ds(HIDDEN, all_rows)], pool[pl.ds(DK, all_rows)]).astype(bf16)
    hand_over(14)
    tick(12)
    handed_over(13)
    staged[1] = dot_tn(pool[pl.ds(HIDDEN, all_rows)], pool[pl.ds(DV, all_rows)]).astype(bf16)
    hand_over(15)
    norm_finish(2)
    norm_start(3)
    tick(13)
    handed_over(14)
    handed_over(15)

    for copy in last_loads:
        copy.wait()

    def row_grads(at_chunk):
        dk = pool[pl.ds(pl.multiple_of(DK + at_chunk * chunk, 128), chunk)]
        dv = pool[pl.ds(pl.multiple_of(DV + at_chunk * chunk, 128), chunk)]
        return dot_nt(dk, pool[pl.ds(WK, width)]) + dot_nt(dv, pool[pl.ds(WV, width)])

    theirs[pl.ds(0, chunk)] = row_grads(1 - x).astype(bf16)
    theirs[pl.ds(chunk, chunk)] = row_grads(2 + x).astype(bf16)
    rows_copy = remote(theirs, rows_in, extra_send.at[0], extra_recv.at[0], across)
    got_copy = remote(rows_got, theirs_out, extra_send.at[1], extra_recv.at[1], across)
    rows_copy.start()
    tick(14)
    for k, at_chunk in enumerate((x, 3 - x)):
        piece = pl.ds(k * chunk, chunk)
        mine_out[piece] = (
            row_grads(at_chunk)
            + dot_nt(pool[pl.ds(DQ + k * chunk, chunk)], pool[pl.ds(WQ, width)])
            + pool32[pl.ds(2 * rows + k * chunk, chunk)]
        )
    norm_finish(3)
    norms_out[...] = norm_all[...]

    def last_step(t, carry):
        tick(t)

        @pl.when(t == 17)
        def _():
            rows_copy.wait()
            whole = mine_out[...] + rows_in[...].astype(f32)
            mine_out[...] = whole
            rows_got[...] = whole.astype(bf16)
            got_copy.start()

        return carry

    lax.fori_loop(15, LAST_TICK + 1, last_step, 0)
    got_copy.wait()
    for ref, unit in ready + [(cross_out_grad, 8)]:
        for plane, part in corners:
            to_core(ref, unit, plane, part).wait_send()


def backward_by_kernel(*args):
    rows, width = args[6].shape
    all_rows = args[22].shape[0]
    norms = args[26]
    anywhere = pl.BlockSpec(memory_space=pl.ANY)
    vmem = pl.BlockSpec(memory_space=pltpu.VMEM)
    in_specs = [anywhere] * 27
    for i in (9, 14, 15, 21, 26):
        in_specs[i] = vmem
    dma = pltpu.SemaphoreType.DMA
    U, T, H, Z = UNITS, TILE, HALF, LINE - 1
    return pl.pallas_call(
        backward_kernel,
        out_shape=[
            jax.ShapeDtypeStruct((U, 2, T, T), bf16),
            jax.ShapeDtypeStruct((rows, width), f32),
            jax.ShapeDtypeStruct((rows, width), bf16),
            jax.ShapeDtypeStruct(norms.shape, f32),
        ],
        in_specs=in_specs,
        out_specs=[anywhere, vmem, anywhere, vmem],
        scratch_shapes=[
            pltpu.VMEM((SLOTS, 2, 2, H, T), bf16),
            pltpu.VMEM((U, 2, 2, H, T), bf16),
            pltpu.VMEM((U, 2, H, T), bf16),
            pltpu.VMEM((U, H, T), bf16),
            pltpu.VMEM((U, Z, PART, T), bf16),
            pltpu.VMEM((U, PART, T), bf16),
            pltpu.VMEM((9216, width), bf16),
            pltpu.VMEM((2 * width, width), f32),
            pltpu.VMEM((RET_BLOCKS * BLOCK_ROWS, 2 * width), bf16),
            pltpu.VMEM((2, width, width), bf16),
            pltpu.VMEM((rows, width), bf16),
            pltpu.VMEM((all_rows, PAIR), f32),
            pltpu.VMEM((all_rows, PAIR), f32),
            pltpu.VMEM((rows, width), bf16),
            pltpu.VMEM((rows, width), bf16),
            pltpu.VMEM((rows, width), bf16),
            pltpu.VMEM(norms.shape, f32),
            pltpu.VMEM((6,) + norms.shape, f32),
            dma((SLOTS, 4)), dma((U, 4)), dma((U, 4)), dma((U,)), dma((U,)), dma((U,)), dma((U,)),
            dma((U, Z)), dma((U, Z)), dma((U, Z)), dma((U, Z)), dma((U,)), dma((U,)), dma((U,)),
            dma((U,)), dma((U,)), dma((16,)), dma((2, 2)), dma, dma((2,)), dma((2,)), dma((6,)),
            dma((6,)),
        ],
        compiler_params=pltpu.CompilerParams(
            collective_id=1, has_side_effects=True, vmem_limit_bytes=BACKWARD_VMEM
        ),
        name="backward",
    )(*args)


def output_place(unit, core):
    row, column = share_corner(unit, core, 0)
    return UNIT_WEIGHTS[unit], row, column


def finish_kernel(*refs):
    sums, ours_in, theirs_in, made_in, made_theirs_in, norms = refs[:6]
    output, grad_hidden, outs, norm_outs = refs[6], refs[7], refs[8:18], refs[18:24]
    taken, given, ours, theirs, made, made_theirs, theirs_wide = refs[24:31]
    in_sem, out_sem, row_sem, row_out_sem = refs[31:]
    depth = taken.shape[0]
    shares = [(unit, core) for unit in range(UNITS) for core in range(2)]
    x = lax.axis_index("narrow")
    chunk = ours.shape[0] // 2

    def fetch(i):
        unit, core = shares[i]
        return pltpu.make_async_copy(sums.at[unit, core], taken.at[i % depth], in_sem.at[i % depth])

    def place(i):
        weight, row, column = output_place(*shares[i])
        return pltpu.make_async_copy(
            given.at[i % depth],
            outs[weight].at[pl.ds(row, TILE), pl.ds(column, TILE)],
            out_sem.at[i % depth],
        )

    pairs_in = ((ours_in, ours), (theirs_in, theirs), (made_in, made), (made_theirs_in, made_theirs))
    rows_in = [pltpu.make_async_copy(a, b, row_sem.at[k]) for k, (a, b) in enumerate(pairs_in)]

    def rows_out(src, dst, which, k, at):
        start = (at if k == 0 else 3 - at) * chunk
        return pltpu.make_async_copy(
            src.at[pl.ds(k * chunk, chunk)],
            dst.at[pl.ds(pl.multiple_of(start, 128), chunk)],
            row_out_sem.at[which, k],
        )

    moves = [
        rows_out(src, dst, which, k, at)
        for which, (src, dst, at) in enumerate(
            (
                (ours, grad_hidden, x),
                (theirs_wide, grad_hidden, 1 - x),
                (made, output, x),
                (made_theirs, output, 1 - x),
            )
        )
        for k in range(2)
    ]
    for i in range(depth - 1):
        fetch(i).start()
    for copy in rows_in:
        copy.start()
    for i in range(6):
        norm_outs[i][...] = norms[i]
    for i in range(len(shares)):
        if i + depth - 1 < len(shares):
            fetch(i + depth - 1).start()
        fetch(i).wait()
        if i >= depth:
            place(i - depth).wait()
        given[i % depth] = taken[i % depth].astype(f32)
        place(i).start()
        if i == depth:
            for copy in rows_in:
                copy.wait()
            theirs_wide[...] = theirs[...].astype(f32)
            for copy in moves:
                copy.start()
    for i in range(len(shares) - depth, len(shares)):
        place(i).wait()
    for copy in moves:
        copy.wait()


def finish(sums, ours, theirs, made, made_theirs, norms):
    rows, width = ours.shape
    shapes = [(2 * TILE, TILE)] * 3 + [(TILE, 2 * TILE)] + [(2 * TILE, TILE)] * 3
    shapes += [(TILE, 2 * TILE), (2 * TILE, 4 * TILE), (4 * TILE, 2 * TILE)]
    depth = 6
    anywhere = pl.BlockSpec(memory_space=pl.ANY)
    vmem = pl.BlockSpec(memory_space=pltpu.VMEM)
    return tuple(
        pl.pallas_call(
            finish_kernel,
            out_shape=[
                jax.ShapeDtypeStruct((2 * rows, width), bf16),
                jax.ShapeDtypeStruct((2 * rows, width), f32),
            ]
            + [jax.ShapeDtypeStruct(shape, f32) for shape in shapes]
            + [jax.ShapeDtypeStruct((width,), f32)] * 6,
            in_specs=[anywhere] * 5 + [vmem],
            out_specs=[anywhere] * 12 + [vmem] * 6,
            scratch_shapes=[
                pltpu.VMEM((depth, TILE, TILE), bf16),
                pltpu.VMEM((depth, TILE, TILE), f32),
                pltpu.VMEM((rows, width), f32),
                pltpu.VMEM((rows, width), bf16),
                pltpu.VMEM((rows, width), bf16),
                pltpu.VMEM((rows, width), bf16),
                pltpu.VMEM((rows, width), f32),
                pltpu.SemaphoreType.DMA((depth,)),
                pltpu.SemaphoreType.DMA((depth,)),
                pltpu.SemaphoreType.DMA((4,)),
                pltpu.SemaphoreType.DMA((4, 2)),
            ],
            compiler_params=pltpu.CompilerParams(vmem_limit_bytes=VMEM_LIMIT),
            name="finish",
        )(sums, ours, theirs, made, made_theirs, norms)
    )


FF_COLUMNS = 512


def layer_norm(summed, norm_gain, norm_shift):
    centred = summed - jnp.mean(summed, axis=-1, keepdims=True)
    inverse = lax.rsqrt(jnp.mean(centred * centred, axis=-1, keepdims=True) + epsilon)
    normal = centred * inverse
    return normal * norm_gain + norm_shift, normal, inverse


def dense_kernel(
    a_cross, first, cotangent, cross_out, gain_two, shift_two, gain_three, shift_three, expand_in, reduce_in,
    out_ref, g_second, g_across, cross_out_grad, norms, expand_grad, reduce_grad, made_out,
    expand, reduce, activated, slope, expand_staged, reduce_staged,
    expand_sem, reduce_sem, expand_out_sem, reduce_out_sem, made_send, made_recv,
):
    me = Place()
    across = me.at(x=1 - me.x)
    gain_two, shift_two = as_row(gain_two), as_row(shift_two)
    gain_three, shift_three = as_row(gain_three), as_row(shift_three)
    chunk = cotangent.shape[0] // 4
    count = expand.shape[1] // FF_COLUMNS

    def piece(c):
        return pl.ds(c * FF_COLUMNS, FF_COLUMNS)

    def fetch_expand(c):
        return pltpu.make_async_copy(
            expand_in.at[:, piece(c)], expand.at[:, piece(c)], expand_sem.at[c]
        )

    def fetch_reduce(c):
        return pltpu.make_async_copy(reduce_in.at[piece(c)], reduce.at[piece(c)], reduce_sem.at[c])

    def put_expand(c):
        return pltpu.make_async_copy(
            expand_staged.at[c % 2], expand_grad.at[:, piece(c)], expand_out_sem.at[c % 2]
        )

    def put_reduce(c):
        return pltpu.make_async_copy(
            reduce_staged.at[c % 2], reduce_grad.at[piece(c)], reduce_out_sem.at[c % 2]
        )

    for c in range(count):
        fetch_expand(c).start()
        fetch_reduce(c).start()
    barrier = pltpu.get_barrier_semaphore()
    pl.semaphore_signal(barrier, inc=1, device_id=across, device_id_type=MESH)
    second, normal_two, inverse_two = layer_norm(
        first[...] + dot_nn(a_cross[...], cross_out[...]), gain_two, shift_two
    )
    second_low = second.astype(bf16)
    total = second
    for c in range(count):
        fetch_expand(c).wait()
        pre = dot_nn(second_low, expand[:, piece(c)])
        phi = 0.5 * (1.0 + lax.erf(pre * 0.7071067811865476))
        slope[:, piece(c)] = phi + pre * jnp.exp(-0.5 * pre * pre) * 0.3989422804014327
        activated[:, piece(c)] = (pre * phi).astype(bf16)
        fetch_reduce(c).wait()
        total = total + dot_nn(activated[:, piece(c)], reduce[piece(c)])
    final, normal, inverse = layer_norm(total, gain_three, shift_three)
    out_ref[...] = final.astype(bf16)
    pl.semaphore_wait(barrier, 1)
    made_copy = pltpu.make_async_remote_copy(
        src_ref=out_ref, dst_ref=made_out, send_sem=made_send, recv_sem=made_recv,
        device_id=across, device_id_type=MESH,
    )
    made_copy.start()
    grad = jnp.concatenate(
        [
            cotangent[pl.ds(pl.multiple_of(me.x * chunk, 128), chunk)],
            cotangent[pl.ds(pl.multiple_of((3 - me.x) * chunk, 128), chunk)],
        ],
        axis=0,
    ).astype(f32)
    norms[...] = jnp.zeros_like(norms)

    def back(grad, normal, inverse, gain, row):
        norms[pl.ds(row, 1)] = jnp.sum(grad * normal, axis=0, keepdims=True)
        norms[pl.ds(row + 1, 1)] = jnp.sum(grad, axis=0, keepdims=True)
        scaled = grad * gain
        return inverse * (
            scaled
            - jnp.mean(scaled, axis=-1, keepdims=True)
            - normal * jnp.mean(scaled * normal, axis=-1, keepdims=True)
        )

    grad = back(grad, normal, inverse, gain_three, 4)
    grad_low = grad.astype(bf16)
    for c in range(count):
        if c >= 2:
            put_reduce(c - 2).wait()
            put_expand(c - 2).wait()
        reduce_staged[c % 2] = dot_tn(activated[:, piece(c)], grad_low).astype(bf16)
        put_reduce(c).start()
        grad_pre = (dot_nt(grad_low, reduce[piece(c)]) * slope[:, piece(c)]).astype(bf16)
        expand_staged[c % 2] = dot_tn(second_low, grad_pre).astype(bf16)
        put_expand(c).start()
        grad = grad + dot_nt(grad_pre, expand[:, piece(c)])
    grad = back(grad, normal_two, inverse_two, gain_two, 2)
    g_second[...] = grad
    grad_low = grad.astype(bf16)
    cross_out_grad[...] = dot_tn(a_cross[...], grad_low).astype(bf16)
    g_across[...] = dot_nt(grad_low, cross_out[...]).astype(bf16)
    for c in range(count - 2, count):
        put_reduce(c).wait()
        put_expand(c).wait()
    made_copy.wait()


def dense_by_kernel(a_cross, first, cotangent, cross_out, norm_params, expand, reduce):
    rows, width = first.shape
    hidden_units = expand.shape[1]
    count = hidden_units // FF_COLUMNS
    anywhere = pl.BlockSpec(memory_space=pl.ANY)
    vmem = pl.BlockSpec(memory_space=pltpu.VMEM)
    dma = pltpu.SemaphoreType.DMA
    return pl.pallas_call(
        dense_kernel,
        out_shape=[
            jax.ShapeDtypeStruct((rows, width), bf16),
            jax.ShapeDtypeStruct((rows, width), f32),
            jax.ShapeDtypeStruct((rows, width), bf16),
            jax.ShapeDtypeStruct((width, width), bf16),
            jax.ShapeDtypeStruct((8, width), f32),
            jax.ShapeDtypeStruct(expand.shape, bf16),
            jax.ShapeDtypeStruct(reduce.shape, bf16),
            jax.ShapeDtypeStruct((rows, width), bf16),
        ],
        in_specs=[vmem] * 8 + [anywhere] * 2,
        out_specs=[vmem] * 5 + [anywhere] * 3,
        scratch_shapes=[
            pltpu.VMEM(expand.shape, bf16),
            pltpu.VMEM(reduce.shape, bf16),
            pltpu.VMEM((rows, hidden_units), bf16),
            pltpu.VMEM((rows, hidden_units), f32),
            pltpu.VMEM((2, width, FF_COLUMNS), bf16),
            pltpu.VMEM((2, FF_COLUMNS, width), bf16),
            dma((count,)),
            dma((count,)),
            dma((2,)),
            dma((2,)),
            dma,
            dma,
        ],
        compiler_params=pltpu.CompilerParams(
            collective_id=2, has_side_effects=True, vmem_limit_bytes=VMEM_LIMIT
        ),
        name="dense",
    )(a_cross, first, cotangent, cross_out, *norm_params, expand, reduce)


def by_kernels(narrow):
    return lax.axis_size("wide") == 4 * LINE and narrow == 2


def gather_all(encoded, weights):
    everything = lax.all_gather(encoded, "wide", tiled=True)
    full = tuple(
        lax.all_gather(w, "narrow", axis=1 if i in COLUMNS else 0, tiled=True)
        for i, w in enumerate(weights)
    )
    return everything, full


def reduce_all(grads):
    shares = tuple(
        lax.psum_scatter(
            g.astype(bf16), "narrow", scatter_dimension=1 if i in COLUMNS else 0, tiled=True
        )
        for i, g in enumerate(grads)
    )
    return tuple(s.astype(f32) for s in lax.psum(shares, "wide"))


def local(
    hidden,
    encoded,
    retrieved,
    self_query,
    self_key,
    self_value,
    self_out,
    cross_query,
    cross_key,
    cross_value,
    cross_out,
    expand_weight,
    reduce_weight,
    first_gain,
    first_shift,
    second_gain,
    second_shift,
    third_gain,
    third_shift,
    cotangent,
):
    tok_rows, width = hidden.shape
    narrow = lax.axis_size("narrow")
    at = lax.axis_index("narrow").astype(jnp.int32)
    chunk = tok_rows // (2 * narrow)

    def own(rows, size=chunk):
        low = lax.dynamic_slice_in_dim(rows, at * size, size)
        high = lax.dynamic_slice_in_dim(rows, (2 * narrow - 1 - at) * size, size)
        return jnp.concatenate([low, high], axis=0)

    where_at = at.reshape(1)
    picked = own(retrieved, chunk // BLOCK_ROWS).reshape(-1)
    if by_kernels(narrow):
        everything, full, kept = forward_by_kernel(
            encoded,
            (
                self_query,
                self_key,
                self_value,
                self_out,
                cross_query,
                cross_key,
                cross_value,
                cross_out,
                expand_weight,
                reduce_weight,
            ),
            hidden,
            first_gain,
            first_shift,
        )
        query_self, key_self, value_self, blend_self, first, first_normal, first_low = kept[:7]
        query_cross, log_self, first_inverse = kept[7:]
        (self_query, self_key, self_value, self_out, cross_query, cross_key, cross_value) = full[:7]
        (cross_out, expand_weight, reduce_weight) = full[7:]
        blend_cross, log_cross, key_cross, value_cross, picked_rows = cross_forward(
            picked, everything, cross_key, cross_value, query_cross
        )
        made = dense_by_kernel(
            blend_cross,
            first,
            cotangent,
            cross_out,
            (second_gain, second_shift, third_gain, third_shift),
            expand_weight,
            reduce_weight,
        )
        output, grad_second_in, grad_blend_cross, cross_out_grad, norms = made[:5]
        expand_grad, reduce_grad, made_theirs = made[5:]
        sums, grad_mine, grad_theirs, norm_sums = backward_by_kernel(
            expand_grad,
            reduce_grad,
            cross_out_grad,
            picked_rows,
            key_cross,
            value_cross,
            query_cross,
            blend_cross,
            grad_blend_cross,
            log_cross,
            first_low,
            cross_query,
            grad_second_in,
            first_normal,
            first_inverse,
            first_gain,
            blend_self,
            self_out,
            query_self,
            key_self,
            value_self,
            log_self,
            hidden,
            self_query,
            self_key,
            self_value,
            norms,
        )

        return finish(sums, grad_mine, grad_theirs, output, made_theirs, norm_sums)

    everything, full = gather_all(
        encoded,
        (
            self_query,
            self_key,
            self_value,
            self_out,
            cross_query,
            cross_key,
            cross_value,
            cross_out,
            expand_weight,
            reduce_weight,
        ),
    )
    (
        self_query,
        self_key,
        self_value,
        self_out,
        cross_query,
        cross_key,
        cross_value,
        cross_out,
        expand_weight,
        reduce_weight,
    ) = full
    mine = own(hidden)
    grad_final = own(cotangent).astype(f32)

    query_self = project(mine, self_query).astype(bf16)
    key_self = project(hidden, self_key).astype(bf16)
    value_self = project(hidden, self_value).astype(bf16)
    blend_self, log_self = self_forward(narrow, where_at, query_self, key_self, value_self)
    first, first_normal, first_inverse = norm_forward(
        mine.astype(f32) + project(blend_self, self_out), first_gain, first_shift
    )
    first_low = first.astype(bf16)
    query_cross = project(first_low, cross_query).astype(bf16)
    blend_cross, log_cross, key_cross, value_cross, picked_rows = cross_forward(
        picked, everything, cross_key, cross_value, query_cross
    )
    second, second_normal, second_inverse = norm_forward(
        first + project(blend_cross, cross_out), second_gain, second_shift
    )
    second_low = second.astype(bf16)
    pre_act = project(second_low, expand_weight)
    activated = jax.nn.gelu(pre_act, approximate=False).astype(bf16)
    final, third_normal, third_inverse = norm_forward(
        second + project(activated, reduce_weight), third_gain, third_shift
    )
    output = final.astype(bf16)

    grad_third, third_gain_grad, third_shift_grad = norm_backward(
        grad_final, third_normal, third_inverse, third_gain
    )
    grad_ffn = grad_third.astype(bf16)
    reduce_grad = grad_weight(activated, grad_ffn)
    grad_pre = (grad_input(grad_ffn, reduce_weight) * gelu_slope(pre_act)).astype(bf16)
    expand_grad = grad_weight(second_low, grad_pre)
    grad_second = grad_third + grad_input(grad_pre, expand_weight)
    grad_second_in, second_gain_grad, second_shift_grad = norm_backward(
        grad_second, second_normal, second_inverse, second_gain
    )
    grad_cross = grad_second_in.astype(bf16)
    cross_out_grad = grad_weight(blend_cross, grad_cross)
    grad_blend_cross = grad_input(grad_cross, cross_out).astype(bf16)
    grad_query_cross, cross_key_grad, cross_value_grad = cross_backward(
        picked,
        everything,
        key_cross,
        value_cross,
        query_cross,
        log_cross,
        blend_cross,
        grad_blend_cross,
    )
    cross_query_grad = grad_weight(first_low, grad_query_cross)
    grad_first = grad_second_in + grad_input(grad_query_cross, cross_query)
    grad_first_in, first_gain_grad, first_shift_grad = norm_backward(
        grad_first, first_normal, first_inverse, first_gain
    )
    grad_self = grad_first_in.astype(bf16)
    self_out_grad = grad_weight(blend_self, grad_self)
    grad_blend_self = grad_input(grad_self, self_out).astype(bf16)
    grad_query_self, grad_key_self, grad_value_self = self_backward(
        narrow, where_at, query_self, key_self, value_self, log_self, blend_self, grad_blend_self
    )
    self_query_grad = grad_weight(mine, grad_query_self)
    self_key_grad = grad_weight(hidden, grad_key_self)
    self_value_grad = grad_weight(hidden, grad_value_self)
    grad_rows = grad_input(grad_key_self, self_key) + grad_input(grad_value_self, self_value)
    grad_own = grad_first_in + grad_input(grad_query_self, self_query)

    def spread(rows):
        empty = jnp.zeros((tok_rows, width), rows.dtype)
        placed = lax.dynamic_update_slice_in_dim(empty, rows[:chunk], at * chunk, 0)
        return lax.dynamic_update_slice_in_dim(
            placed, rows[chunk:], (2 * narrow - 1 - at) * chunk, 0
        )

    grad_hidden = lax.psum((grad_rows + spread(grad_own)).astype(bf16), "narrow").astype(f32)
    output = lax.psum(spread(output), "narrow")
    weight_grads = reduce_all(
        (
            self_query_grad,
            self_key_grad,
            self_value_grad,
            self_out_grad,
            cross_query_grad,
            cross_key_grad,
            cross_value_grad,
            cross_out_grad,
            expand_grad,
            reduce_grad,
        )
    )
    norm_grads = lax.psum(
        jnp.stack(
            [
                first_gain_grad,
                first_shift_grad,
                second_gain_grad,
                second_shift_grad,
                third_gain_grad,
                third_shift_grad,
            ]
        ),
        ("wide", "narrow"),
    )
    return (output, grad_hidden) + weight_grads + tuple(norm_grads[i] for i in range(6))


def solution(mesh):
    rows = P("wide", None)
    columns_split = P(None, "narrow")
    rows_split = P("narrow", None)
    weights = (columns_split,) * 3 + (rows_split,) + (columns_split,) * 3 + (rows_split,)
    weights += (columns_split, rows_split)
    return jax.shard_map(
        local,
        mesh=mesh,
        in_specs=(rows, rows, rows) + weights + (P(),) * 6 + (rows,),
        out_specs=(rows, rows) + weights + (P(),) * 6,
        check_vma=False,
    )
```

```python
import functools

import jax
import jax.numpy as jnp
from jax import lax
from jax.experimental import pallas as pl
from jax.experimental.pallas import tpu as pltpu
from jax.sharding import PartitionSpec as P

HEAD_DIM = 64
BLOCK_ROWS = 128
RET_BLOCKS = 8
PAIR = 2 * HEAD_DIM
VMEM_LIMIT = 60 << 20
BACKWARD_VMEM = 63 << 20

epsilon = 1e-05
bf16 = jnp.bfloat16
f32 = jnp.float32
MESH = pl.DeviceIdType.MESH


def norm_forward(summed, norm_gain, norm_shift):
    average = jnp.mean(summed, axis=-1, keepdims=True)
    centred = summed - average
    inverse = lax.rsqrt(jnp.mean(centred * centred, axis=-1, keepdims=True) + epsilon)
    normal = centred * inverse
    return (normal * norm_gain + norm_shift, normal, inverse)


def norm_backward(grad_out, normal, inverse, norm_gain):
    scaled = grad_out * norm_gain
    grad_in = inverse * (
        scaled
        - jnp.mean(scaled, axis=-1, keepdims=True)
        - normal * jnp.mean(scaled * normal, axis=-1, keepdims=True)
    )
    return (grad_in, jnp.sum(grad_out * normal, axis=0), jnp.sum(grad_out, axis=0))


def gelu_slope(pre_act):
    return (
        0.5 * (1.0 + lax.erf(pre_act * 0.7071067811865476))
        + pre_act * jnp.exp(-0.5 * pre_act * pre_act) * 0.3989422804014327
    )


def project(rows_in, weight):
    return jnp.dot(rows_in, weight, preferred_element_type=f32)


def grad_weight(left, right):
    return jnp.einsum("ti,to->io", left, right, preferred_element_type=f32)


def grad_input(grad_rows, weight):
    return jnp.einsum("to,io->ti", grad_rows, weight, preferred_element_type=f32)


def dot_nt(left, right):
    return lax.dot_general(left, right, (((1,), (1,)), ((), ())), preferred_element_type=f32)


def dot_tn(left, right):
    return lax.dot_general(left, right, (((0,), (0,)), ((), ())), preferred_element_type=f32)


def dot_nn(left, right):
    return lax.dot_general(left, right, (((1,), (0,)), ((), ())), preferred_element_type=f32)


def stack_heads(pair_rows):
    lane = lax.broadcasted_iota(jnp.int32, pair_rows.shape, 1)
    wide_rows = pair_rows.astype(f32)
    zero = jnp.zeros_like(wide_rows)
    return jnp.concatenate(
        [
            jnp.where(lane < HEAD_DIM, wide_rows, zero).astype(bf16),
            jnp.where(lane < HEAD_DIM, zero, wide_rows).astype(bf16),
        ],
        axis=0,
    )


def merge_heads(both):
    rows = both.shape[1] // 2
    sublane = lax.broadcasted_iota(jnp.int32, (PAIR, rows), 0)
    return jnp.transpose(jnp.where(sublane < HEAD_DIM, both[:, :rows], both[:, rows:]))


def causal_edge(rows):
    key = lax.broadcasted_iota(jnp.int32, (rows, 2 * rows), 0)
    query = lax.broadcasted_iota(jnp.int32, (rows, 2 * rows), 1)
    return key <= jnp.where(query >= rows, query - rows, query)


def scaled_heads(pair_rows):
    return stack_heads(pair_rows.astype(f32) * HEAD_DIM**-0.5)


KEY_ROWS = 128


def scores_of(keys, stacked, start, edge):
    part = dot_nt(keys[start : start + KEY_ROWS], stacked)
    if edge is not None and start + KEY_ROWS == keys.shape[0]:
        part = jnp.where(edge, part, -1e30)
    return part


def by_rows(part, reduce):
    return reduce(part.reshape(KEY_ROWS // 8, 8, part.shape[1]), axis=0)


def pair_forward(queries, keys, values, edge):
    stacked = scaled_heads(queries)
    starts = range(0, keys.shape[0], KEY_ROWS)
    scores = [scores_of(keys, stacked, start, edge) for start in starts]
    top = by_rows(scores[0], jnp.max)
    for part in scores[1:]:
        top = jnp.maximum(top, by_rows(part, jnp.max))
    top = jnp.max(top, axis=0, keepdims=True)
    total, blended = 0.0, 0.0
    for start, part in zip(starts, scores):
        raised = jnp.exp(part - top)
        total = total + by_rows(raised, jnp.sum)
        blended = blended + dot_tn(values[start : start + KEY_ROWS], raised.astype(bf16))
    total = jnp.sum(total, axis=0, keepdims=True)
    return merge_heads(blended / total).astype(bf16), top + jnp.log(total)


def pair_backward(queries, keys, values, edge, log_total, blended, grad_blend):
    rows = queries.shape[0]
    stacked = scaled_heads(queries)
    grads = stack_heads(grad_blend)
    scores = dot_nt(keys, stacked)
    if edge is not None:
        split = keys.shape[0] - edge.shape[0]
        last = jnp.where(edge, scores[split:], -1e30)
        scores = jnp.concatenate([scores[:split], last], axis=0) if split else last
    chances = jnp.exp(scores - log_total)
    weighed = jnp.transpose(blended.astype(f32) * grad_blend.astype(f32))
    centre = jnp.concatenate(
        [
            jnp.sum(weighed[:HEAD_DIM], axis=0, keepdims=True),
            jnp.sum(weighed[HEAD_DIM:], axis=0, keepdims=True),
        ],
        axis=1,
    )
    grad_scores = (chances * (dot_nt(values, grads) - centre)).astype(bf16)
    grad_values = dot_nn(chances.astype(bf16), grads)
    grad_keys = dot_nn(grad_scores, stacked)
    grad_queries = merge_heads(dot_tn(keys, grad_scores)) * HEAD_DIM**-0.5
    return grad_queries, grad_keys, grad_values


def self_blocks(narrow, total_rows, at):
    chunk = total_rows // (2 * narrow)
    for block in range(total_rows // BLOCK_ROWS):
        which, within = divmod(block * BLOCK_ROWS, chunk)
        if which < narrow:
            owner, local_row = which, within
        else:
            owner, local_row = 2 * narrow - 1 - which, chunk + within
        yield local_row, (block + 1) * BLOCK_ROWS, at == owner


def self_forward_kernel(narrow, at_ref, q_ref, k_ref, v_ref, o_ref, log_ref):
    for local_row, seen, taken in self_blocks(narrow, k_ref.shape[0], at_ref[0]):

        @pl.when(taken)
        def _():
            mine = pl.ds(local_row, BLOCK_ROWS)
            keys = pl.ds(0, seen)
            blended, log_total = pair_forward(
                q_ref[mine], k_ref[keys], v_ref[keys], causal_edge(BLOCK_ROWS)
            )
            o_ref[mine] = blended
            log_ref[0, pl.ds(local_row // BLOCK_ROWS, 1)] = log_total


def self_forward(narrow, at, queries, keys, values):
    rows, width = queries.shape
    total_rows = keys.shape[0]
    pairs = width // PAIR
    pair = lambda count: pl.BlockSpec((count, PAIR), lambda g, at: (0, g))
    return pl.pallas_call(
        functools.partial(self_forward_kernel, narrow),
        grid_spec=pltpu.PrefetchScalarGridSpec(
            num_scalar_prefetch=1,
            grid=(pairs,),
            in_specs=[pair(rows), pair(total_rows), pair(total_rows)],
            out_specs=[pair(rows), pl.BlockSpec((1, rows // BLOCK_ROWS, 2 * BLOCK_ROWS), lambda g, at: (g, 0, 0))],
        ),
        out_shape=[
            jax.ShapeDtypeStruct((rows, width), bf16),
            jax.ShapeDtypeStruct((pairs, rows // BLOCK_ROWS, 2 * BLOCK_ROWS), f32),
        ],
        compiler_params=pltpu.CompilerParams(vmem_limit_bytes=VMEM_LIMIT),
        name="self_forward",
    )(at, queries, keys, values)


def self_backward_kernel(
    narrow, at_ref, q_ref, k_ref, v_ref, log_ref, o_ref, g_ref, dq_ref, dk_ref, dv_ref, dk_sum, dv_sum
):
    rows = q_ref.shape[0] // 2
    dk_sum[...] = jnp.zeros_like(dk_sum)
    dv_sum[...] = jnp.zeros_like(dv_sum)
    for local_row, seen, taken in self_blocks(narrow, k_ref.shape[0], at_ref[0]):

        @pl.when(taken)
        def _():
            mine = pl.ds(local_row, BLOCK_ROWS)
            keys = pl.ds(0, seen)
            grad_q, grad_k, grad_v = pair_backward(
                q_ref[mine],
                k_ref[keys],
                v_ref[keys],
                causal_edge(BLOCK_ROWS),
                log_ref[0, pl.ds(local_row // BLOCK_ROWS, 1)],
                o_ref[mine],
                g_ref[mine],
            )
            dq_ref[mine] = grad_q.astype(bf16)
            dk_sum[keys] += grad_k
            dv_sum[keys] += grad_v

    dk_ref[...] = dk_sum[...].astype(bf16)
    dv_ref[...] = dv_sum[...].astype(bf16)


def self_backward(narrow, at, queries, keys, values, logs, blended, grads):
    rows, width = queries.shape
    total_rows = keys.shape[0]
    pairs = width // PAIR
    pair = lambda count: pl.BlockSpec((count, PAIR), lambda g, at: (0, g))
    return pl.pallas_call(
        functools.partial(self_backward_kernel, narrow),
        grid_spec=pltpu.PrefetchScalarGridSpec(
            num_scalar_prefetch=1,
            grid=(pairs,),
            in_specs=[
                pair(rows),
                pair(total_rows),
                pair(total_rows),
                pl.BlockSpec((1, rows // BLOCK_ROWS, 2 * BLOCK_ROWS), lambda g, at: (g, 0, 0)),
                pair(rows),
                pair(rows),
            ],
            out_specs=[pair(rows), pair(total_rows), pair(total_rows)],
            scratch_shapes=[pltpu.VMEM((total_rows, PAIR), f32)] * 2,
        ),
        out_shape=[
            jax.ShapeDtypeStruct((rows, width), bf16),
            jax.ShapeDtypeStruct((total_rows, width), bf16),
            jax.ShapeDtypeStruct((total_rows, width), bf16),
        ],
        compiler_params=pltpu.CompilerParams(vmem_limit_bytes=VMEM_LIMIT),
        name="self_backward",
    )(at, queries, keys, values, logs, blended, grads)


def cross_forward_kernel(picked_ref, *refs):
    blocks = refs[:RET_BLOCKS]
    wk_ref, wv_ref, q_ref, o_ref, log_ref, k_ref, v_ref, rows_in = refs[RET_BLOCKS:]
    for j in range(RET_BLOCKS):
        rows_in[pl.ds(j * BLOCK_ROWS, BLOCK_ROWS)] = blocks[j][...]
    k_ref[...] = dot_nn(rows_in[...], wk_ref[...]).astype(bf16)
    v_ref[...] = dot_nn(rows_in[...], wv_ref[...]).astype(bf16)
    for g in range(q_ref.shape[1] // PAIR):
        lanes = pl.ds(g * PAIR, PAIR)
        blended, log_total = pair_forward(q_ref[:, lanes], k_ref[:, lanes], v_ref[:, lanes], None)
        o_ref[:, lanes] = blended
        log_ref[0, pl.ds(g, 1)] = log_total


def block_specs(width):
    def spec(j):
        return pl.BlockSpec((BLOCK_ROWS, width), lambda b, picked: (picked[b * RET_BLOCKS + j], 0))

    return [spec(j) for j in range(RET_BLOCKS)]


def cross_forward(picked, everything, cross_key, cross_value, queries):
    rows, width = queries.shape
    count = rows // BLOCK_ROWS
    pairs = width // PAIR
    keys = RET_BLOCKS * BLOCK_ROWS
    whole = pl.BlockSpec((width, width), lambda b, picked: (0, 0))
    by_block = pl.BlockSpec((BLOCK_ROWS, width), lambda b, picked: (b, 0))
    by_keys = pl.BlockSpec((keys, width), lambda b, picked: (b, 0))
    return pl.pallas_call(
        cross_forward_kernel,
        grid_spec=pltpu.PrefetchScalarGridSpec(
            num_scalar_prefetch=1,
            grid=(count,),
            in_specs=block_specs(width) + [whole, whole, by_block],
            out_specs=[
                by_block,
                pl.BlockSpec((1, pairs, 2 * BLOCK_ROWS), lambda b, picked: (b, 0, 0)),
                by_keys,
                by_keys,
                by_keys,
            ],
        ),
        out_shape=[
            jax.ShapeDtypeStruct((rows, width), bf16),
            jax.ShapeDtypeStruct((count, pairs, 2 * BLOCK_ROWS), f32),
            jax.ShapeDtypeStruct((count * keys, width), bf16),
            jax.ShapeDtypeStruct((count * keys, width), bf16),
            jax.ShapeDtypeStruct((count * keys, width), bf16),
        ],
        compiler_params=pltpu.CompilerParams(vmem_limit_bytes=VMEM_LIMIT),
        name="cross_forward",
    )(picked, *([everything] * RET_BLOCKS), cross_key, cross_value, queries)


def cross_backward_kernel(picked_ref, *refs):
    blocks = refs[:RET_BLOCKS]
    (k_ref, v_ref, q_ref, log_ref, o_ref, g_ref, dq_ref, dwk_ref, dwv_ref, rows_in, both, sums) = refs[
        RET_BLOCKS:
    ]
    width = q_ref.shape[1]
    step = pl.program_id(0)

    @pl.when(step == 0)
    def _():
        sums[...] = jnp.zeros_like(sums)

    for j in range(RET_BLOCKS):
        rows_in[pl.ds(j * BLOCK_ROWS, BLOCK_ROWS)] = blocks[j][...]
    for g in range(width // PAIR):
        lanes = pl.ds(g * PAIR, PAIR)
        grad_q, grad_k, grad_v = pair_backward(
            q_ref[:, lanes],
            k_ref[:, lanes],
            v_ref[:, lanes],
            None,
            log_ref[0, pl.ds(g, 1)],
            o_ref[:, lanes],
            g_ref[:, lanes],
        )
        dq_ref[:, lanes] = grad_q.astype(bf16)
        both[:, lanes] = grad_k.astype(bf16)
        both[:, pl.ds(width + g * PAIR, PAIR)] = grad_v.astype(bf16)
    sums[...] += dot_tn(rows_in[...], both[...])

    @pl.when(step == pl.num_programs(0) - 1)
    def _():
        dwk_ref[...] = sums[:, :width].astype(bf16)
        dwv_ref[...] = sums[:, width:].astype(bf16)


def cross_backward(picked, everything, keys_in, values_in, queries, logs, blended, grads):
    rows, width = queries.shape
    count = rows // BLOCK_ROWS
    pairs = width // PAIR
    keys = RET_BLOCKS * BLOCK_ROWS
    whole = pl.BlockSpec((width, width), lambda b, picked: (0, 0))
    by_block = pl.BlockSpec((BLOCK_ROWS, width), lambda b, picked: (b, 0))
    by_keys = pl.BlockSpec((keys, width), lambda b, picked: (b, 0))
    return pl.pallas_call(
        cross_backward_kernel,
        grid_spec=pltpu.PrefetchScalarGridSpec(
            num_scalar_prefetch=1,
            grid=(count,),
            in_specs=block_specs(width)
            + [
                by_keys,
                by_keys,
                by_block,
                pl.BlockSpec((1, pairs, 2 * BLOCK_ROWS), lambda b, picked: (b, 0, 0)),
                by_block,
                by_block,
            ],
            out_specs=[by_block, whole, whole],
            scratch_shapes=[
                pltpu.VMEM((keys, width), bf16),
                pltpu.VMEM((keys, 2 * width), bf16),
                pltpu.VMEM((width, 2 * width), f32),
            ],
        ),
        out_shape=[
            jax.ShapeDtypeStruct((rows, width), bf16),
            jax.ShapeDtypeStruct((width, width), bf16),
            jax.ShapeDtypeStruct((width, width), bf16),
        ],
        compiler_params=pltpu.CompilerParams(vmem_limit_bytes=VMEM_LIMIT),
        name="cross_backward",
    )(
        picked,
        *([everything] * RET_BLOCKS),
        keys_in,
        values_in,
        queries,
        logs,
        blended,
        grads,
    )


COLUMNS = (0, 1, 2, 4, 5, 6, 8)


LINE = 4
HELD = 5


def as_row(ref):
    return ref[...].reshape(1, ref.shape[0])


class Place:
    def __init__(self):
        wide = lax.axis_index("wide")
        self.x = lax.axis_index("narrow")
        self.core = lax.rem(wide, 2)
        self.y = lax.rem(lax.div(wide, 2), 2)
        self.z = lax.div(wide, 4)
        self.wide = wide

    def at(self, z=None, y=None, core=None, x=None):
        z, y = (self.z if z is None else z), (self.y if y is None else y)
        core = self.core if core is None else core
        return (z * 4 + y * 2 + core, self.x if x is None else x)

    def greet(self):
        barrier = pltpu.get_barrier_semaphore()
        targets = [self.at(core=1 - self.core), self.at(y=1 - self.y), self.at(x=1 - self.x)]
        targets += [self.at(z=lax.rem(self.z + step, LINE)) for step in range(1, LINE)]
        for target in targets:
            pl.semaphore_signal(barrier, inc=1, device_id=target, device_id_type=MESH)
        pl.semaphore_wait(barrier, len(targets))


def forward_kernel(a_rows, b_rows, *refs):
    encoded_in, weights_in = refs[0], refs[1:11]
    hidden_in, first_gain, first_shift = refs[11:14]
    everything, full_out = refs[14], refs[15:25]
    kept_out, (log_self, inverse_out) = refs[25:33], refs[33:35]
    encoded, weights, kept = refs[35], refs[36:46], refs[46:54]
    hidden = refs[54]
    load_sem, own_sem, half_sem, kept_sem, flow_send, flow_recv, weight_send, weight_recv = refs[55:]
    q_self, k_self, v_self, a_self, first, first_normal, first_low, q_cross = kept
    full = weights[:HELD] + full_out[HELD:]
    me = Place()
    rows = encoded.shape[0]
    x, y, z, core = me.x, me.y, me.z, me.core
    low, high = z > 0, z < LINE - 1
    UP_A, DOWN_A, Y_A, UP_B, DOWN_B, Y_B, X_B, CORE_A, CORE_B = range(9)

    own = pltpu.make_async_copy(
        encoded, everything.at[pl.ds(pl.multiple_of(me.wide * rows, 128), rows)], own_sem
    )

    def region(i, ref, plane, part):
        if i in COLUMNS:
            count, columns = ref.shape[0], ref.shape[1] // 2
            start = pl.multiple_of(plane * columns, 128)
            if part is None:
                return ref.at[:, pl.ds(start, columns)]
            first = pl.multiple_of(part * (count // 2), 16)
            return ref.at[pl.ds(first, count // 2), pl.ds(start, columns)]
        count = ref.shape[0] // 2
        if part is None:
            return ref.at[pl.ds(pl.multiple_of(plane * count, 16), count)]
        first = pl.multiple_of(plane * count + part * (count // 2), 16)
        return ref.at[pl.ds(first, count // 2)]

    loads, halves = [], []
    for i in range(10):
        into = region(i, weights[i], x, None) if i < HELD else weights[i]
        loads.append(pltpu.make_async_copy(weights_in[i], into, load_sem.at[i]))
        if i < HELD:
            halves.append(pltpu.make_async_copy(weights[i], full_out[i], half_sem.at[i]))
        else:
            halves.append(
                pltpu.make_async_copy(weights[i], region(i, full[i], x, None), half_sem.at[i])
            )
    loads.append(pltpu.make_async_copy(encoded_in, encoded, load_sem.at[10]))
    loads.append(pltpu.make_async_copy(hidden_in, hidden, load_sem.at[11]))
    loads[10].start()
    for i in range(10):
        loads[i].start()
    loads[11].start()
    me.greet()
    loads[10].wait()

    def flow(kind, owner_z, owner_y, plane, target, from_core=None, held=False):
        owner = owner_z * 2 + owner_y
        start = owner * (2 * rows) + (core if from_core is None else from_core) * rows
        if plane is None:
            size, slot = a_rows, owner
        else:
            start = start + a_rows + plane * b_rows
            size, slot = b_rows, owner + (plane * 8 if kind == CORE_B else 0)
        piece = everything.at[pl.ds(pl.multiple_of(start, 16), size)]
        source = piece
        if held:
            first = 0 if plane is None else pl.multiple_of(a_rows + plane * b_rows, 16)
            source = encoded.at[pl.ds(first, size)]
        return pltpu.make_async_remote_copy(
            src_ref=source,
            dst_ref=piece,
            send_sem=flow_send.at[kind, slot],
            recv_sem=flow_recv.at[kind, slot],
            device_id=target,
            device_id_type=MESH,
        )

    sibling = me.at(core=1 - core)
    beside = me.at(y=1 - y)
    across = me.at(x=1 - x)
    above, below = me.at(z=z + 1), me.at(z=z - 1)

    def up_a(oz, held=False):
        return flow(UP_A, oz, y, None, above, held=held)

    def down_a(oz, held=False):
        return flow(DOWN_A, oz, y, None, below, held=held)

    def up_b(oz, oy, held=False):
        return flow(UP_B, oz, oy, x, above, held=held)

    def down_b(oz, oy, held=False):
        return flow(DOWN_B, oz, oy, x, below, held=held)

    def y_a(oz, oy, held=False):
        return flow(Y_A, oz, oy, None, beside, held=held)

    def y_b(oy, held=False):
        return flow(Y_B, z, oy, x, beside, held=held)

    def x_b(oz, oy, plane):
        return flow(X_B, oz, oy, plane, across)

    def core_a(oz, oy, from_core=None, held=False):
        return flow(CORE_A, oz, oy, None, sibling, from_core, held)

    def core_b(oz, oy, plane, from_core=None, held=False):
        return flow(CORE_B, oz, oy, plane, sibling, from_core, held)

    def weight(way, i, plane, part):
        piece = region(i, full[i], plane, part)
        if way == 0 and i >= HELD:
            piece_in = weights[i]
            count = piece_in.shape[0] // 2
            piece_in = piece_in.at[pl.ds(pl.multiple_of(part * count, 16), count)]
        else:
            piece_in = piece
        return pltpu.make_async_remote_copy(
            src_ref=piece_in,
            dst_ref=piece,
            send_sem=weight_send.at[way, i],
            recv_sem=weight_recv.at[way, i],
            device_id=across if way == 0 else sibling,
            device_id_type=MESH,
        )

    y_b(y, True).start()
    y_a(z, y, True).start()
    pl.when(high)(lambda: up_a(z, True).start())
    pl.when(low)(lambda: down_a(z, True).start())

    def weights_go(some):
        for i in some:
            weight(0, i, x, core).start()

    def weights_come(some):
        for i in some:
            weight(0, i, 1 - x, core).wait_recv()
            weight(1, i, 1 - x, core).start()

    for i in range(3):
        loads[i].wait()
    weights_go(range(3))
    core_a(z, y, held=True).start()
    core_b(z, y, 0, held=True).start()
    core_b(z, y, 1, held=True).start()
    own.start()
    for i in range(3, 12):
        if i != 10:
            loads[i].wait()
    for i in range(HELD, 10):
        halves[i].start()

    y_b(1 - y).wait_recv()
    core_b(z, 1 - y, x).start()
    weights_come(range(3))
    weights_go(range(3, 8))
    for i in range(3):
        weight(1, i, 1 - x, 1 - core).wait_recv()

    total_rows = hidden.shape[0]
    chunk = total_rows // 4
    mine = (
        pl.ds(pl.multiple_of(x * chunk, 128), chunk),
        pl.ds(pl.multiple_of((3 - x) * chunk, 128), chunk),
    )
    places = (pl.ds(0, chunk), pl.ds(chunk, chunk))
    for piece, place in zip(mine, places):
        q_self[place] = dot_nn(hidden[piece], weights[0][...]).astype(bf16)
    k_self[...] = dot_nn(hidden[...], weights[1][...]).astype(bf16)
    v_self[...] = dot_nn(hidden[...], weights[2][...]).astype(bf16)
    put = [pltpu.make_async_copy(kept[i], kept_out[i], kept_sem.at[i]) for i in range(8)]
    for i in range(3):
        put[i].start()

    def self_step(g, carry):
        lanes = pl.ds(pl.multiple_of(g * PAIR, PAIR), PAIR)
        for local_row, seen, taken in self_blocks(2, total_rows, x):

            @pl.when(taken)
            def _():
                some = pl.ds(local_row, BLOCK_ROWS)
                blended, log_total = pair_forward(
                    q_self[some, lanes],
                    k_self[pl.ds(0, seen), lanes],
                    v_self[pl.ds(0, seen), lanes],
                    causal_edge(BLOCK_ROWS),
                )
                a_self[some, lanes] = blended
                log_self[g, pl.ds(local_row // BLOCK_ROWS, 1)] = log_total

        return carry

    pairs = q_self.shape[1] // PAIR
    lax.fori_loop(0, pairs // 2, self_step, 0)

    def beside_arrives(oz):
        y_a(oz, 1 - y).wait_recv()
        core_a(oz, 1 - y).start()

    def pass_a(oz, arrived, onward, further):
        arrived(oz).wait_recv()
        pl.when(onward)(lambda: further(oz).start())
        y_a(oz, y).start()
        core_a(oz, y).start()

    def pass_b(oz, arrived, onward, further):
        for oy in (y, 1 - y):
            arrived(oz, oy).wait_recv()
            pl.when(onward)(lambda: further(oz, oy).start())
            x_b(oz, oy, x).start()
            core_b(oz, oy, x).start()

    def step_a(step):
        under, over = z - 1 - step, z + 1 + step
        pl.when(under >= 0)(lambda: pass_a(under, up_a, high, up_a))
        pl.when(over < LINE)(lambda: pass_a(over, down_a, low, down_a))

    def step_b(step):
        under, over = z - 1 - step, z + 1 + step
        pl.when(under >= 0)(lambda: pass_b(under, up_b, high, up_b))
        pl.when(over < LINE)(lambda: pass_b(over, down_b, low, down_b))

    step_a(0)
    for oy, held in ((y, True), (1 - y, False)):
        pl.when(high)(lambda oy=oy, held=held: up_b(z, oy, held).start())
        pl.when(low)(lambda oy=oy, held=held: down_b(z, oy, held).start())
    weights_go(range(8, 10))
    x_b(z, 1 - y, x).start()
    lax.fori_loop(pairs // 2, pairs, self_step, 0)
    put[3].start()
    weights_come(range(3, 5))
    for i in range(3, 5):
        weight(1, i, 1 - x, 1 - core).wait_recv()
    for i in range(HELD):
        halves[i].start()

    for piece, place in zip(mine, places):
        summed = hidden[piece].astype(f32) + dot_nn(a_self[place], weights[3][...])
        centred = summed - jnp.mean(summed, axis=-1, keepdims=True)
        inverse = lax.rsqrt(jnp.mean(centred * centred, axis=-1, keepdims=True) + epsilon)
        normal = centred * inverse
        result = normal * as_row(first_gain) + as_row(first_shift)
        first_normal[place] = normal
        inverse_out[place] = inverse
        first[place] = result
        first_low[place] = result.astype(bf16)
        q_cross[place] = dot_nn(result.astype(bf16), weights[4][...]).astype(bf16)
    for i in range(4, 8):
        put[i].start()

    step_a(1)
    step_b(0)
    step_a(2)
    step_b(1)
    step_b(2)
    weights_come(range(5, 10))
    beside_arrives(z)
    for step in range(1, LINE):
        pl.when(z - step >= 0)(lambda: beside_arrives(z - step))
        pl.when(z + step < LINE)(lambda: beside_arrives(z + step))

    def across_arrives(oz, oy):
        x_b(oz, oy, 1 - x).wait_recv()
        core_b(oz, oy, 1 - x).start()

    across_arrives(z, 1 - y)
    for step in range(LINE - 1):
        under, over = z - 1 - step, z + 1 + step
        for oy in (y, 1 - y):
            pl.when(under >= 0)(lambda: across_arrives(under, oy))
            pl.when(over < LINE)(lambda: across_arrives(over, oy))

    y_b(y).wait_send()
    x_b(z, 1 - y, x).wait_send()
    for oz in range(LINE):
        y_a(oz, y).wait_send()
        for oy in range(2):
            core_a(oz, oy).wait_send()
            core_a(oz, oy, 1 - core).wait_recv()
            for plane in range(2):
                core_b(oz, oy, plane).wait_send()
                core_b(oz, oy, plane, 1 - core).wait_recv()
        away = oz != z

        @pl.when(away)
        def _():
            for oy in range(2):
                x_b(oz, oy, x).wait_send()

        @pl.when(jnp.logical_and(high, oz <= z))
        def _():
            up_a(oz).wait_send()
            for oy in range(2):
                up_b(oz, oy).wait_send()

        @pl.when(jnp.logical_and(low, oz >= z))
        def _():
            down_a(oz).wait_send()
            for oy in range(2):
                down_b(oz, oy).wait_send()

    own.wait()
    for i in range(10):
        halves[i].wait()
        weight(0, i, x, core).wait_send()
        weight(1, i, 1 - x, core).wait_send()
        if i >= HELD:
            weight(1, i, 1 - x, 1 - core).wait_recv()
    for copy in put:
        copy.wait()


def forward_by_kernel(encoded, weights, hidden, first_gain, first_shift):
    rows, width = encoded.shape
    a_rows = rows * 17 // 24 // 16 * 16
    b_rows = (rows - a_rows) // 2
    shapes = [jax.ShapeDtypeStruct((16 * rows, width), bf16)]
    for i, w in enumerate(weights):
        doubled = (w.shape[0], 2 * w.shape[1]) if i in COLUMNS else (2 * w.shape[0], w.shape[1])
        shapes.append(jax.ShapeDtypeStruct(doubled, bf16))
    total_rows = hidden.shape[0]
    mine, pairs = total_rows // 2, width // PAIR
    kept = [(mine, bf16), (total_rows, bf16), (total_rows, bf16), (mine, bf16)]
    kept += [(mine, f32), (mine, f32), (mine, bf16), (mine, bf16)]
    held = [s.shape if i < HELD else w.shape for i, (s, w) in enumerate(zip(shapes[1:], weights))]
    small = [
        jax.ShapeDtypeStruct((pairs, mine // BLOCK_ROWS, 2 * BLOCK_ROWS), f32),
        jax.ShapeDtypeStruct((mine, 1), f32),
    ]
    dma = pltpu.SemaphoreType.DMA
    anywhere = pl.BlockSpec(memory_space=pl.ANY)
    vmem = pl.BlockSpec(memory_space=pltpu.VMEM)
    out = pl.pallas_call(
        functools.partial(forward_kernel, a_rows, b_rows),
        out_shape=shapes + [jax.ShapeDtypeStruct((n, width), dtype) for n, dtype in kept] + small,
        in_specs=[anywhere] * 12 + [vmem] * 2,
        out_specs=[anywhere] * 19 + [vmem] * 2,
        scratch_shapes=[pltpu.VMEM((rows, width), bf16)]
        + [pltpu.VMEM(shape, bf16) for shape in held]
        + [pltpu.VMEM((n, width), dtype) for n, dtype in kept]
        + [pltpu.VMEM((total_rows, width), bf16)]
        + [dma((12,)), dma, dma((10,)), dma((8,))]
        + [dma((9, 16)), dma((9, 16)), dma((2, 10)), dma((2, 10))],
        compiler_params=pltpu.CompilerParams(
            collective_id=0, has_side_effects=True, vmem_limit_bytes=VMEM_LIMIT
        ),
        name="forward",
    )(encoded, *weights, hidden, first_gain, first_shift)
    return out[0], tuple(out[1:11]), tuple(out[11:])


TILE = 384
HALF = TILE // 2
PART = HALF // LINE
UNITS = 16
SLOTS = 12
UNIT_WEIGHTS = (8, 8, 8, 8, 9, 9, 9, 9, 7, 5, 6, 4, 3, 0, 1, 2)
LAST_TICK = UNITS + 11


def share_corner(unit, core, plane):
    if unit < 4:
        return core * TILE, (plane * 4 + unit) * TILE
    if unit < 8:
        return (plane * 4 + unit - 4) * TILE, core * TILE
    if unit in (8, 12):
        return plane * TILE, core * TILE
    return core * TILE, plane * TILE


def backward_kernel(*refs):
    (
        expand_grad, reduce_grad, cross_out_grad, picked_rows, keys_in, values_in, q_cross, a_cross,
        g_cross, log_cross, first_low, cross_query, g_second, first_normal, first_inverse, first_gain,
        a_self, self_out, q_self, k_self, v_self, log_self, hidden, self_query, self_key, self_value,
        norms,
    ) = refs[:27]
    sums_out, mine_out, theirs_out, norms_out = refs[27:31]
    (
        own, from_core, from_a, from_b, from_z, summed, pool, pool32, both, staged, dq_cross, dk_sum,
        dv_sum, theirs, rows_in, rows_got, norm_all, norm_in,
        own_sem, core_send, core_recv, a_send, a_recv, b_send, b_recv, z_send, z_recv, gz_send, gz_recv,
        gy_send, gy_recv, gc_send, gc_recv, keep_sem, load_sem, kv_sem, e_sem, extra_send, extra_recv,
        norm_send, norm_recv,
    ) = refs[31:]
    me = Place()
    x, y, z, core = me.x, me.y, me.z, me.core
    sibling, beside, across = me.at(core=1 - core), me.at(y=1 - y), me.at(x=1 - x)
    width = 2 * TILE
    keys = RET_BLOCKS * BLOCK_ROWS
    rows = q_cross.shape[0]
    blocks = rows // BLOCK_ROWS
    pairs = width // PAIR
    chunk = rows // 2

    def rem(u, n):
        return u % n if isinstance(u, int) else lax.rem(u, n)

    def remote(src, dst, send, recv, target):
        return pltpu.make_async_remote_copy(
            src_ref=src, dst_ref=dst, send_sem=send, recv_sem=recv,
            device_id=target, device_id_type=MESH,
        )


    def share(ref, unit, of_core, plane, part):
        row, column = share_corner(unit, of_core, plane)
        return ref.at[
            pl.ds(pl.multiple_of(row + part * HALF, 64), HALF),
            pl.ds(pl.multiple_of(column, 128), TILE),
        ]

    def own_copy(ref, unit, plane, part):
        return pltpu.make_async_copy(
            share(ref, unit, core, plane, part),
            own.at[unit % SLOTS, plane, part],
            own_sem.at[unit % SLOTS, plane * 2 + part],
        )

    def core_copy(src, u, plane, part):
        return remote(
            src, from_core.at[u, plane, part], core_send.at[u, plane * 2 + part],
            core_recv.at[u, plane * 2 + part], sibling,
        )

    def to_core(ref, unit, plane, part):
        return core_copy(share(ref, unit, 1 - core, plane, part), unit, plane, part)

    def a_first(u, slot):
        return remote(own.at[slot, 1 - x], from_a.at[u], a_send.at[u], a_recv.at[u], across)

    def a_second(u, slot):
        return remote(own.at[slot, :, 1 - y], from_a.at[u], a_send.at[u], a_recv.at[u], beside)

    def b_first(u, slot):
        return remote(own.at[slot, x, 1 - y], from_b.at[u], b_send.at[u], b_recv.at[u], beside)

    def b_second(u, slot):
        return remote(own.at[slot, 1 - x, y], from_b.at[u], b_send.at[u], b_recv.at[u], across)

    def to_z(u, slot, d):
        other = lax.rem(z + d, LINE)
        piece = own.at[slot, x, y, pl.ds(pl.multiple_of(other * PART, 16), PART)]
        return remote(
            piece, from_z.at[u, d - 1], z_send.at[u, d - 1], z_recv.at[u, d - 1], me.at(z=other)
        )

    def result(u, of_z):
        return sums_out.at[u, core, pl.ds(pl.multiple_of(y * HALF + of_z * PART, 16), PART)]

    def keep(u):
        return pltpu.make_async_copy(summed.at[u], result(u, z), keep_sem.at[u])

    def gather_z(u, d):
        return remote(
            summed.at[u], result(u, z), gz_send.at[u, d - 1], gz_recv.at[u, d - 1],
            me.at(z=lax.rem(z + d, LINE)),
        )

    def gathered_z(u, d):
        return remote(
            summed.at[u], result(u, lax.rem(z + LINE - d, LINE)), gz_send.at[u, d - 1],
            gz_recv.at[u, d - 1], beside,
        )

    def gather_y(u, at_y):
        piece = sums_out.at[u, core, pl.ds(pl.multiple_of(at_y * HALF, 16), HALF)]
        return remote(piece, piece, gy_send.at[u], gy_recv.at[u], beside)

    def gather_core(u, at_core):
        piece = sums_out.at[u, at_core]
        return remote(piece, piece, gc_send.at[u], gc_recv.at[u], sibling)

    def plus(a, b):
        return a + b

    def by_order(u, first, second):
        if isinstance(u, int):
            (first if u % 2 == 0 else second)()
        else:
            pl.when(lax.rem(u, 2) == 0)(first)
            pl.when(lax.rem(u, 2) == 1)(second)

    def stage_core(u):
        slot = rem(u, SLOTS)
        early_one = u < len(ready)

        def arrived():
            for plane, part in corners:
                piece = own.at[slot, plane, part]
                pltpu.make_async_copy(piece, piece, own_sem.at[slot, plane * 2 + part]).wait()

        if isinstance(u, int):
            if early_one:
                arrived()
        else:
            pl.when(early_one)(arrived)
        for plane, part in corners:
            core_copy(own.at[slot, plane, part], u, plane, part).wait_recv()
        own[slot] = plus(own[slot], from_core[u])
        by_order(u, lambda: a_first(u, slot).start(), lambda: a_second(u, slot).start())

    def stage_a(u):
        slot = rem(u, SLOTS)

        def first():
            a_first(u, slot).wait()
            own[slot, x] = plus(own[slot, x], from_a[u])
            b_first(u, slot).start()

        def second():
            a_second(u, slot).wait()
            own[slot, :, y] = plus(own[slot, :, y], from_a[u])
            b_second(u, slot).start()

        by_order(u, first, second)

    def stage_b(u):
        slot = rem(u, SLOTS)
        by_order(u, lambda: b_first(u, slot).wait(), lambda: b_second(u, slot).wait())
        own[slot, x, y] = plus(own[slot, x, y], from_b[u])
        for d in range(1, LINE):
            to_z(u, slot, d).start()

    def stage_z(u):
        slot = rem(u, SLOTS)
        for d in range(1, LINE):
            to_z(u, slot, d).wait()
        total = own[slot, x, y, pl.ds(pl.multiple_of(z * PART, 16), PART)].astype(f32)
        for d in range(1, LINE):
            total += from_z[u, d - 1].astype(f32)
        summed[u] = total.astype(bf16)
        keep(u).start()
        for d in range(1, LINE):
            gather_z(u, d).start()

    def stage_gather_z(u):
        keep(u).wait()
        for d in range(1, LINE):
            gathered_z(u, d).wait_recv()
            gather_z(u, d).wait_send()
        gather_y(u, y).start()

    def stage_gather_y(u):
        gather_y(u, 1 - y).wait_recv()
        gather_y(u, y).wait_send()
        gather_core(u, core).start()

    def stage_gather_core(u):
        gather_core(u, 1 - core).wait_recv()
        gather_core(u, core).wait_send()

    stages = (
        (0, stage_core), (2, stage_a), (4, stage_b), (6, stage_z), (8, stage_gather_z),
        (10, stage_gather_y), (12, stage_gather_core),
    )

    def tick(t):
        for lag, stage in stages:
            if isinstance(t, int):
                if 0 <= t - lag < UNITS:
                    stage(t - lag)
            else:
                u = t - lag
                pl.when(jnp.logical_and(u >= 0, u < UNITS))(lambda stage=stage, u=u: stage(u))

    KV, E, Q, O, G, FIRST, CROSS_Q, A_SELF, SELF_OUT = (
        0, 4096, 5120, 5632, 6144, 6656, 7168, 7936, 8448
    )
    QS, KS, VS, DQ, DK, DV, HIDDEN, DA = 0, 512, 1536, 2560, 3072, 4096, 5120, 6144
    WQ, WK, WV = 0, 768, 1536

    def load(src, row, sem, into=pool):
        return pltpu.make_async_copy(src, into.at[pl.ds(row, src.shape[0])], load_sem.at[sem])

    def kv_copy(b, which):
        src = (keys_in, values_in)[which].at[pl.ds(pl.multiple_of(b * keys, 128), keys)]
        row = pl.multiple_of(lax.rem(b, 2) * (2 * keys) + which * keys, 128)
        return pltpu.make_async_copy(src, pool.at[pl.ds(row, keys)], kv_sem.at[lax.rem(b, 2), which])

    def e_copy(b):
        src = picked_rows.at[pl.ds(pl.multiple_of(b * keys, 128), keys)]
        return pltpu.make_async_copy(src, pool.at[pl.ds(E, keys)], e_sem)

    early = [
        load(q_cross, Q, 0), load(a_cross, O, 1), load(g_cross, G, 2), load(first_low, FIRST, 3),
        load(cross_query, CROSS_Q, 4), load(a_self, A_SELF, 5), load(self_out, SELF_OUT, 6),
    ]
    for which in range(2):
        kv_copy(jnp.int32(0), which).start()
    for copy in early:
        copy.start()
    ready = [(expand_grad, u) for u in range(4)] + [(reduce_grad, u) for u in range(4, 8)]
    ready.append((cross_out_grad, 8))
    corners = [(plane, part) for plane in range(2) for part in range(2)]
    for ref, unit in ready:
        for plane, part in corners:
            own_copy(ref, unit, plane, part).start()
    me.greet()
    for ref, unit in ready:
        for plane, part in corners:
            to_core(ref, unit, plane, part).start()
    both_sums = pool32
    both_sums[...] = jnp.zeros_like(both_sums)
    for copy in early[:3]:
        copy.wait()

    def at_row(row):
        return pl.ds(pl.multiple_of(row, 128), BLOCK_ROWS)

    def cross_step(i, carry):
        b, g = lax.div(i, pairs), lax.rem(i, pairs)

        @pl.when(g == 0)
        def _():
            for which in range(2):
                kv_copy(b, which).wait()
            e_copy(b).start()

            @pl.when(b + 1 < blocks)
            def _():
                for which in range(2):
                    kv_copy(b + 1, which).start()

        lanes = pl.ds(pl.multiple_of(g * PAIR, PAIR), PAIR)
        row = pl.multiple_of(b * BLOCK_ROWS, BLOCK_ROWS)
        key_row = pl.multiple_of(lax.rem(b, 2) * (2 * keys), 128)
        grad_q, grad_k, grad_v = pair_backward(
            pool[at_row(Q + row), lanes],
            pool[pl.ds(key_row, keys), lanes],
            pool[pl.ds(pl.multiple_of(key_row + keys, 128), keys), lanes],
            None,
            log_cross[b, pl.ds(g, 1)],
            pool[at_row(O + row), lanes],
            pool[at_row(G + row), lanes],
        )
        dq_cross[pl.ds(row, BLOCK_ROWS), lanes] = grad_q.astype(bf16)
        both[:, lanes] = grad_k.astype(bf16)
        both[:, pl.ds(pl.multiple_of(width + g * PAIR, PAIR), PAIR)] = grad_v.astype(bf16)

        @pl.when(g == pairs - 1)
        def _():
            e_copy(b).wait()
            both_sums[pl.ds(0, width)] += dot_tn(pool[pl.ds(E, keys)], both[:, :width])
            both_sums[pl.ds(width, width)] += dot_tn(pool[pl.ds(E, keys)], both[:, width:])

        pl.when(lax.rem(i, 4) == 3)(lambda: tick(lax.div(i, 4)))
        return carry

    lax.fori_loop(0, blocks * pairs, cross_step, 0)

    def hand_over(unit):
        ref = staged.at[unit % 2]
        for plane, part in corners:
            to_core(ref, unit, plane, part).start()
            own_copy(ref, unit, plane, part).start()

    def kept(unit):
        for plane, part in corners:
            own_copy(staged.at[unit % 2], unit, plane, part).wait()

    def left(unit):
        for plane, part in corners:
            to_core(staged.at[unit % 2], unit, plane, part).wait_send()

    def handed_over(unit):
        kept(unit)
        left(unit)

    late = [load(q_self, QS, 7), load(k_self, KS, 8), load(v_self, VS, 9), load(hidden, HIDDEN, 10)]
    for copy in late:
        copy.start()
    staged[1] = both_sums[pl.ds(0, width)].astype(bf16)
    hand_over(9)
    tick(6)
    staged[0] = both_sums[pl.ds(width, width)].astype(bf16)
    hand_over(10)
    g_copy = load(g_second, 0, 11, pool32)
    n_copy = load(first_normal, rows, 12, pool32)
    g_copy.start()
    n_copy.start()
    for copy in early[3:]:
        copy.wait()
    tick(7)
    handed_over(9)
    staged[1] = dot_tn(pool[pl.ds(FIRST, rows)], dq_cross[...]).astype(bf16)
    hand_over(11)

    g_copy.wait()
    n_copy.wait()
    normal = pool32[pl.ds(rows, rows)]
    grad_out = pool32[pl.ds(0, rows)] + dot_nt(dq_cross[...], pool[pl.ds(CROSS_Q, width)])
    scaled = grad_out * as_row(first_gain)
    grad_in = first_inverse[...] * (
        scaled
        - jnp.mean(scaled, axis=-1, keepdims=True)
        - normal * jnp.mean(scaled * normal, axis=-1, keepdims=True)
    )
    norm_all[...] = norms[...]
    norm_all[pl.ds(0, 1)] = jnp.sum(grad_out * normal, axis=0, keepdims=True)
    norm_all[pl.ds(1, 1)] = jnp.sum(grad_out, axis=0, keepdims=True)
    pool32[pl.ds(2 * rows, rows)] = grad_in
    grad_low = grad_in.astype(bf16)
    pool[pl.ds(DA, rows)] = dot_nt(grad_low, pool[pl.ds(SELF_OUT, width)]).astype(bf16)
    tick(8)
    handed_over(10)
    staged[0] = dot_tn(pool[pl.ds(A_SELF, rows)], grad_low).astype(bf16)
    hand_over(12)

    along_z = tuple(me.at(z=lax.rem(z + d, LINE)) for d in range(1, LINE))
    rounds = ((sibling,), (across,), (beside,), along_z)

    def norm_copies(which):
        first = min(which, 3)
        return [
            remote(
                norm_all, norm_in.at[first + k], norm_send.at[first + k], norm_recv.at[first + k], target
            )
            for k, target in enumerate(rounds[which])
        ]

    def norm_start(which):
        for copy in norm_copies(which):
            copy.start()

    def norm_finish(which):
        for copy in norm_copies(which):
            copy.wait()
        for k in range(len(rounds[which])):
            norm_all[...] += norm_in[which + k]

    norm_start(0)

    for copy in late:
        copy.wait()
    kept(11)
    kept(12)

    def self_step(g, carry):
        lanes = pl.ds(pl.multiple_of(g * PAIR, PAIR), PAIR)
        dk_sum[...] = jnp.zeros_like(dk_sum)
        dv_sum[...] = jnp.zeros_like(dv_sum)
        for local_row, seen, taken in self_blocks(2, hidden.shape[0], x):

            @pl.when(taken)
            def _():
                mine = pl.ds(local_row, BLOCK_ROWS)
                grad_q, grad_k, grad_v = pair_backward(
                    pool[pl.ds(QS + local_row, BLOCK_ROWS), lanes],
                    pool[pl.ds(KS, seen), lanes],
                    pool[pl.ds(VS, seen), lanes],
                    causal_edge(BLOCK_ROWS),
                    log_self[g, pl.ds(local_row // BLOCK_ROWS, 1)],
                    a_self_rows(local_row, lanes),
                    pool[pl.ds(DA + local_row, BLOCK_ROWS), lanes],
                )
                pool[pl.ds(DQ + local_row, BLOCK_ROWS), lanes] = grad_q.astype(bf16)
                dk_sum[pl.ds(0, seen)] += grad_k
                dv_sum[pl.ds(0, seen)] += grad_v

        pool[pl.ds(DK, hidden.shape[0]), lanes] = dk_sum[...].astype(bf16)
        pool[pl.ds(DV, hidden.shape[0]), lanes] = dv_sum[...].astype(bf16)
        pl.when(lax.rem(g, 2) == 1)(lambda: tick(9 + lax.div(g, 2)))
        return carry

    def a_self_rows(local_row, lanes):
        return pool[pl.ds(A_SELF + local_row, BLOCK_ROWS), lanes]

    lax.fori_loop(0, pairs, self_step, 0)
    norm_finish(0)
    norm_start(1)
    last_loads = [load(self_query, WQ, 13), load(self_key, WK, 14), load(self_value, WV, 15)]
    for copy in last_loads:
        copy.start()

    left(11)
    for copy in last_loads:
        copy.wait()

    def row_grads(at_chunk):
        dk = pool[pl.ds(pl.multiple_of(DK + at_chunk * chunk, 128), chunk)]
        dv = pool[pl.ds(pl.multiple_of(DV + at_chunk * chunk, 128), chunk)]
        return dot_nt(dk, pool[pl.ds(WK, width)]) + dot_nt(dv, pool[pl.ds(WV, width)])

    theirs[pl.ds(0, chunk)] = row_grads(1 - x).astype(bf16)
    theirs[pl.ds(chunk, chunk)] = row_grads(2 + x).astype(bf16)
    rows_copy = remote(theirs, rows_in, extra_send.at[0], extra_recv.at[0], across)
    got_copy = remote(rows_got, theirs_out, extra_send.at[1], extra_recv.at[1], across)
    rows_copy.start()
    low_rows = pl.ds(pl.multiple_of(HIDDEN + x * chunk, 128), chunk)
    high_rows = pl.ds(pl.multiple_of(HIDDEN + (3 - x) * chunk, 128), chunk)
    all_rows = hidden.shape[0]
    staged[1] = (
        dot_tn(pool[low_rows], pool[pl.ds(DQ, chunk)])
        + dot_tn(pool[high_rows], pool[pl.ds(DQ + chunk, chunk)])
    ).astype(bf16)
    hand_over(13)
    norm_finish(1)
    norm_start(2)
    left(12)
    staged[0] = dot_tn(pool[pl.ds(HIDDEN, all_rows)], pool[pl.ds(DK, all_rows)]).astype(bf16)
    hand_over(14)
    tick(12)
    handed_over(13)
    staged[1] = dot_tn(pool[pl.ds(HIDDEN, all_rows)], pool[pl.ds(DV, all_rows)]).astype(bf16)
    hand_over(15)
    norm_finish(2)
    norm_start(3)
    tick(13)
    handed_over(14)
    handed_over(15)

    tick(14)
    for k, at_chunk in enumerate((x, 3 - x)):
        piece = pl.ds(k * chunk, chunk)
        mine_out[piece] = (
            row_grads(at_chunk)
            + dot_nt(pool[pl.ds(DQ + k * chunk, chunk)], pool[pl.ds(WQ, width)])
            + pool32[pl.ds(2 * rows + k * chunk, chunk)]
        )
    norm_finish(3)
    norms_out[...] = norm_all[...]

    def last_step(t, carry):
        tick(t)

        @pl.when(t == 17)
        def _():
            rows_copy.wait()
            whole = mine_out[...] + rows_in[...].astype(f32)
            mine_out[...] = whole
            rows_got[...] = whole.astype(bf16)
            got_copy.start()

        return carry

    lax.fori_loop(15, LAST_TICK + 1, last_step, 0)
    got_copy.wait()
    for ref, unit in ready:
        for plane, part in corners:
            to_core(ref, unit, plane, part).wait_send()


def backward_by_kernel(*args):
    rows, width = args[6].shape
    all_rows = args[22].shape[0]
    norms = args[26]
    anywhere = pl.BlockSpec(memory_space=pl.ANY)
    vmem = pl.BlockSpec(memory_space=pltpu.VMEM)
    in_specs = [anywhere] * 27
    for i in (9, 14, 15, 21, 26):
        in_specs[i] = vmem
    dma = pltpu.SemaphoreType.DMA
    U, T, H, Z = UNITS, TILE, HALF, LINE - 1
    return pl.pallas_call(
        backward_kernel,
        out_shape=[
            jax.ShapeDtypeStruct((U, 2, T, T), bf16),
            jax.ShapeDtypeStruct((rows, width), f32),
            jax.ShapeDtypeStruct((rows, width), bf16),
            jax.ShapeDtypeStruct(norms.shape, f32),
        ],
        in_specs=in_specs,
        out_specs=[anywhere, vmem, anywhere, vmem],
        scratch_shapes=[
            pltpu.VMEM((SLOTS, 2, 2, H, T), bf16),
            pltpu.VMEM((U, 2, 2, H, T), bf16),
            pltpu.VMEM((U, 2, H, T), bf16),
            pltpu.VMEM((U, H, T), bf16),
            pltpu.VMEM((U, Z, PART, T), bf16),
            pltpu.VMEM((U, PART, T), bf16),
            pltpu.VMEM((9216, width), bf16),
            pltpu.VMEM((2 * width, width), f32),
            pltpu.VMEM((RET_BLOCKS * BLOCK_ROWS, 2 * width), bf16),
            pltpu.VMEM((2, width, width), bf16),
            pltpu.VMEM((rows, width), bf16),
            pltpu.VMEM((all_rows, PAIR), f32),
            pltpu.VMEM((all_rows, PAIR), f32),
            pltpu.VMEM((rows, width), bf16),
            pltpu.VMEM((rows, width), bf16),
            pltpu.VMEM((rows, width), bf16),
            pltpu.VMEM(norms.shape, f32),
            pltpu.VMEM((6,) + norms.shape, f32),
            dma((SLOTS, 4)), dma((U, 4)), dma((U, 4)), dma((U,)), dma((U,)), dma((U,)), dma((U,)),
            dma((U, Z)), dma((U, Z)), dma((U, Z)), dma((U, Z)), dma((U,)), dma((U,)), dma((U,)),
            dma((U,)), dma((U,)), dma((16,)), dma((2, 2)), dma, dma((2,)), dma((2,)), dma((6,)),
            dma((6,)),
        ],
        compiler_params=pltpu.CompilerParams(
            collective_id=1, has_side_effects=True, vmem_limit_bytes=BACKWARD_VMEM
        ),
        name="backward",
    )(*args)


def output_place(unit, core):
    row, column = share_corner(unit, core, 0)
    return UNIT_WEIGHTS[unit], row, column


def finish_kernel(*refs):
    sums, ours_in, theirs_in, made_in, made_theirs_in, norms = refs[:6]
    output, grad_hidden, outs, norm_outs = refs[6], refs[7], refs[8:18], refs[18:24]
    taken, given, ours, theirs, made, made_theirs, theirs_wide = refs[24:31]
    in_sem, out_sem, row_sem, row_out_sem = refs[31:]
    depth = taken.shape[0]
    shares = [(unit, core) for unit in range(UNITS) for core in range(2)]
    x = lax.axis_index("narrow")
    chunk = ours.shape[0] // 2

    def fetch(i):
        unit, core = shares[i]
        return pltpu.make_async_copy(sums.at[unit, core], taken.at[i % depth], in_sem.at[i % depth])

    def place(i):
        weight, row, column = output_place(*shares[i])
        return pltpu.make_async_copy(
            given.at[i % depth],
            outs[weight].at[pl.ds(row, TILE), pl.ds(column, TILE)],
            out_sem.at[i % depth],
        )

    pairs_in = ((ours_in, ours), (theirs_in, theirs), (made_in, made), (made_theirs_in, made_theirs))
    rows_in = [pltpu.make_async_copy(a, b, row_sem.at[k]) for k, (a, b) in enumerate(pairs_in)]

    def rows_out(src, dst, which, k, at):
        start = (at if k == 0 else 3 - at) * chunk
        return pltpu.make_async_copy(
            src.at[pl.ds(k * chunk, chunk)],
            dst.at[pl.ds(pl.multiple_of(start, 128), chunk)],
            row_out_sem.at[which, k],
        )

    moves = [
        rows_out(src, dst, which, k, at)
        for which, (src, dst, at) in enumerate(
            (
                (ours, grad_hidden, x),
                (theirs_wide, grad_hidden, 1 - x),
                (made, output, x),
                (made_theirs, output, 1 - x),
            )
        )
        for k in range(2)
    ]
    for i in range(depth - 1):
        fetch(i).start()
    for copy in rows_in:
        copy.start()
    for i in range(6):
        norm_outs[i][...] = norms[i]
    for i in range(len(shares)):
        if i + depth - 1 < len(shares):
            fetch(i + depth - 1).start()
        fetch(i).wait()
        if i >= depth:
            place(i - depth).wait()
        given[i % depth] = taken[i % depth].astype(f32)
        place(i).start()
        if i == depth:
            for copy in rows_in:
                copy.wait()
            theirs_wide[...] = theirs[...].astype(f32)
            for copy in moves:
                copy.start()
    for i in range(len(shares) - depth, len(shares)):
        place(i).wait()
    for copy in moves:
        copy.wait()


def finish(sums, ours, theirs, made, made_theirs, norms):
    rows, width = ours.shape
    shapes = [(2 * TILE, TILE)] * 3 + [(TILE, 2 * TILE)] + [(2 * TILE, TILE)] * 3
    shapes += [(TILE, 2 * TILE), (2 * TILE, 4 * TILE), (4 * TILE, 2 * TILE)]
    depth = 6
    anywhere = pl.BlockSpec(memory_space=pl.ANY)
    vmem = pl.BlockSpec(memory_space=pltpu.VMEM)
    return tuple(
        pl.pallas_call(
            finish_kernel,
            out_shape=[
                jax.ShapeDtypeStruct((2 * rows, width), bf16),
                jax.ShapeDtypeStruct((2 * rows, width), f32),
            ]
            + [jax.ShapeDtypeStruct(shape, f32) for shape in shapes]
            + [jax.ShapeDtypeStruct((width,), f32)] * 6,
            in_specs=[anywhere] * 5 + [vmem],
            out_specs=[anywhere] * 12 + [vmem] * 6,
            scratch_shapes=[
                pltpu.VMEM((depth, TILE, TILE), bf16),
                pltpu.VMEM((depth, TILE, TILE), f32),
                pltpu.VMEM((rows, width), f32),
                pltpu.VMEM((rows, width), bf16),
                pltpu.VMEM((rows, width), bf16),
                pltpu.VMEM((rows, width), bf16),
                pltpu.VMEM((rows, width), f32),
                pltpu.SemaphoreType.DMA((depth,)),
                pltpu.SemaphoreType.DMA((depth,)),
                pltpu.SemaphoreType.DMA((4,)),
                pltpu.SemaphoreType.DMA((4, 2)),
            ],
            compiler_params=pltpu.CompilerParams(vmem_limit_bytes=VMEM_LIMIT),
            name="finish",
        )(sums, ours, theirs, made, made_theirs, norms)
    )


FF_COLUMNS = 512


def layer_norm(summed, norm_gain, norm_shift):
    centred = summed - jnp.mean(summed, axis=-1, keepdims=True)
    inverse = lax.rsqrt(jnp.mean(centred * centred, axis=-1, keepdims=True) + epsilon)
    normal = centred * inverse
    return normal * norm_gain + norm_shift, normal, inverse


def dense_kernel(
    a_cross, first, cotangent, cross_out, gain_two, shift_two, gain_three, shift_three, expand_in, reduce_in,
    out_ref, g_second, g_across, cross_out_grad, norms, expand_grad, reduce_grad, made_out,
    expand, reduce, activated, slope, expand_staged, reduce_staged,
    expand_sem, reduce_sem, expand_out_sem, reduce_out_sem, made_send, made_recv,
):
    me = Place()
    across = me.at(x=1 - me.x)
    gain_two, shift_two = as_row(gain_two), as_row(shift_two)
    gain_three, shift_three = as_row(gain_three), as_row(shift_three)
    chunk = cotangent.shape[0] // 4
    count = expand.shape[1] // FF_COLUMNS

    def piece(c):
        return pl.ds(c * FF_COLUMNS, FF_COLUMNS)

    def fetch_expand(c):
        return pltpu.make_async_copy(
            expand_in.at[:, piece(c)], expand.at[:, piece(c)], expand_sem.at[c]
        )

    def fetch_reduce(c):
        return pltpu.make_async_copy(reduce_in.at[piece(c)], reduce.at[piece(c)], reduce_sem.at[c])

    def put_expand(c):
        return pltpu.make_async_copy(
            expand_staged.at[c % 2], expand_grad.at[:, piece(c)], expand_out_sem.at[c % 2]
        )

    def put_reduce(c):
        return pltpu.make_async_copy(
            reduce_staged.at[c % 2], reduce_grad.at[piece(c)], reduce_out_sem.at[c % 2]
        )

    for c in range(count):
        fetch_expand(c).start()
        fetch_reduce(c).start()
    barrier = pltpu.get_barrier_semaphore()
    pl.semaphore_signal(barrier, inc=1, device_id=across, device_id_type=MESH)
    second, normal_two, inverse_two = layer_norm(
        first[...] + dot_nn(a_cross[...], cross_out[...]), gain_two, shift_two
    )
    second_low = second.astype(bf16)
    total = second
    for c in range(count):
        fetch_expand(c).wait()
        pre = dot_nn(second_low, expand[:, piece(c)])
        phi = 0.5 * (1.0 + lax.erf(pre * 0.7071067811865476))
        slope[:, piece(c)] = phi + pre * jnp.exp(-0.5 * pre * pre) * 0.3989422804014327
        activated[:, piece(c)] = (pre * phi).astype(bf16)
        fetch_reduce(c).wait()
        total = total + dot_nn(activated[:, piece(c)], reduce[piece(c)])
    final, normal, inverse = layer_norm(total, gain_three, shift_three)
    out_ref[...] = final.astype(bf16)
    pl.semaphore_wait(barrier, 1)
    made_copy = pltpu.make_async_remote_copy(
        src_ref=out_ref, dst_ref=made_out, send_sem=made_send, recv_sem=made_recv,
        device_id=across, device_id_type=MESH,
    )
    made_copy.start()
    grad = jnp.concatenate(
        [
            cotangent[pl.ds(pl.multiple_of(me.x * chunk, 128), chunk)],
            cotangent[pl.ds(pl.multiple_of((3 - me.x) * chunk, 128), chunk)],
        ],
        axis=0,
    ).astype(f32)
    norms[...] = jnp.zeros_like(norms)

    def back(grad, normal, inverse, gain, row):
        norms[pl.ds(row, 1)] = jnp.sum(grad * normal, axis=0, keepdims=True)
        norms[pl.ds(row + 1, 1)] = jnp.sum(grad, axis=0, keepdims=True)
        scaled = grad * gain
        return inverse * (
            scaled
            - jnp.mean(scaled, axis=-1, keepdims=True)
            - normal * jnp.mean(scaled * normal, axis=-1, keepdims=True)
        )

    grad = back(grad, normal, inverse, gain_three, 4)
    grad_low = grad.astype(bf16)
    for c in range(count):
        if c >= 2:
            put_reduce(c - 2).wait()
            put_expand(c - 2).wait()
        reduce_staged[c % 2] = dot_tn(activated[:, piece(c)], grad_low).astype(bf16)
        put_reduce(c).start()
        grad_pre = (dot_nt(grad_low, reduce[piece(c)]) * slope[:, piece(c)]).astype(bf16)
        expand_staged[c % 2] = dot_tn(second_low, grad_pre).astype(bf16)
        put_expand(c).start()
        grad = grad + dot_nt(grad_pre, expand[:, piece(c)])
    grad = back(grad, normal_two, inverse_two, gain_two, 2)
    g_second[...] = grad
    grad_low = grad.astype(bf16)
    cross_out_grad[...] = dot_tn(a_cross[...], grad_low).astype(bf16)
    g_across[...] = dot_nt(grad_low, cross_out[...]).astype(bf16)
    for c in range(count - 2, count):
        put_reduce(c).wait()
        put_expand(c).wait()
    made_copy.wait()


def dense_by_kernel(a_cross, first, cotangent, cross_out, norm_params, expand, reduce):
    rows, width = first.shape
    hidden_units = expand.shape[1]
    count = hidden_units // FF_COLUMNS
    anywhere = pl.BlockSpec(memory_space=pl.ANY)
    vmem = pl.BlockSpec(memory_space=pltpu.VMEM)
    dma = pltpu.SemaphoreType.DMA
    return pl.pallas_call(
        dense_kernel,
        out_shape=[
            jax.ShapeDtypeStruct((rows, width), bf16),
            jax.ShapeDtypeStruct((rows, width), f32),
            jax.ShapeDtypeStruct((rows, width), bf16),
            jax.ShapeDtypeStruct((width, width), bf16),
            jax.ShapeDtypeStruct((8, width), f32),
            jax.ShapeDtypeStruct(expand.shape, bf16),
            jax.ShapeDtypeStruct(reduce.shape, bf16),
            jax.ShapeDtypeStruct((rows, width), bf16),
        ],
        in_specs=[vmem] * 8 + [anywhere] * 2,
        out_specs=[vmem] * 5 + [anywhere] * 3,
        scratch_shapes=[
            pltpu.VMEM(expand.shape, bf16),
            pltpu.VMEM(reduce.shape, bf16),
            pltpu.VMEM((rows, hidden_units), bf16),
            pltpu.VMEM((rows, hidden_units), f32),
            pltpu.VMEM((2, width, FF_COLUMNS), bf16),
            pltpu.VMEM((2, FF_COLUMNS, width), bf16),
            dma((count,)),
            dma((count,)),
            dma((2,)),
            dma((2,)),
            dma,
            dma,
        ],
        compiler_params=pltpu.CompilerParams(
            collective_id=2, has_side_effects=True, vmem_limit_bytes=VMEM_LIMIT
        ),
        name="dense",
    )(a_cross, first, cotangent, cross_out, *norm_params, expand, reduce)


def by_kernels(narrow):
    return lax.axis_size("wide") == 4 * LINE and narrow == 2


def gather_all(encoded, weights):
    everything = lax.all_gather(encoded, "wide", tiled=True)
    full = tuple(
        lax.all_gather(w, "narrow", axis=1 if i in COLUMNS else 0, tiled=True)
        for i, w in enumerate(weights)
    )
    return everything, full


def reduce_all(grads):
    shares = tuple(
        lax.psum_scatter(
            g.astype(bf16), "narrow", scatter_dimension=1 if i in COLUMNS else 0, tiled=True
        )
        for i, g in enumerate(grads)
    )
    return tuple(s.astype(f32) for s in lax.psum(shares, "wide"))


def local(
    hidden,
    encoded,
    retrieved,
    self_query,
    self_key,
    self_value,
    self_out,
    cross_query,
    cross_key,
    cross_value,
    cross_out,
    expand_weight,
    reduce_weight,
    first_gain,
    first_shift,
    second_gain,
    second_shift,
    third_gain,
    third_shift,
    cotangent,
):
    tok_rows, width = hidden.shape
    narrow = lax.axis_size("narrow")
    at = lax.axis_index("narrow").astype(jnp.int32)
    chunk = tok_rows // (2 * narrow)

    def own(rows, size=chunk):
        low = lax.dynamic_slice_in_dim(rows, at * size, size)
        high = lax.dynamic_slice_in_dim(rows, (2 * narrow - 1 - at) * size, size)
        return jnp.concatenate([low, high], axis=0)

    where_at = at.reshape(1)
    picked = own(retrieved, chunk // BLOCK_ROWS).reshape(-1)
    if by_kernels(narrow):
        everything, full, kept = forward_by_kernel(
            encoded,
            (
                self_query,
                self_key,
                self_value,
                self_out,
                cross_query,
                cross_key,
                cross_value,
                cross_out,
                expand_weight,
                reduce_weight,
            ),
            hidden,
            first_gain,
            first_shift,
        )
        query_self, key_self, value_self, blend_self, first, first_normal, first_low = kept[:7]
        query_cross, log_self, first_inverse = kept[7:]
        (self_query, self_key, self_value, self_out, cross_query, cross_key, cross_value) = full[:7]
        (cross_out, expand_weight, reduce_weight) = full[7:]
        blend_cross, log_cross, key_cross, value_cross, picked_rows = cross_forward(
            picked, everything, cross_key, cross_value, query_cross
        )
        made = dense_by_kernel(
            blend_cross,
            first,
            cotangent,
            cross_out,
            (second_gain, second_shift, third_gain, third_shift),
            expand_weight,
            reduce_weight,
        )
        output, grad_second_in, grad_blend_cross, cross_out_grad, norms = made[:5]
        expand_grad, reduce_grad, made_theirs = made[5:]
        sums, grad_mine, grad_theirs, norm_sums = backward_by_kernel(
            expand_grad,
            reduce_grad,
            cross_out_grad,
            picked_rows,
            key_cross,
            value_cross,
            query_cross,
            blend_cross,
            grad_blend_cross,
            log_cross,
            first_low,
            cross_query,
            grad_second_in,
            first_normal,
            first_inverse,
            first_gain,
            blend_self,
            self_out,
            query_self,
            key_self,
            value_self,
            log_self,
            hidden,
            self_query,
            self_key,
            self_value,
            norms,
        )

        return finish(sums, grad_mine, grad_theirs, output, made_theirs, norm_sums)

    everything, full = gather_all(
        encoded,
        (
            self_query,
            self_key,
            self_value,
            self_out,
            cross_query,
            cross_key,
            cross_value,
            cross_out,
            expand_weight,
            reduce_weight,
        ),
    )
    (
        self_query,
        self_key,
        self_value,
        self_out,
        cross_query,
        cross_key,
        cross_value,
        cross_out,
        expand_weight,
        reduce_weight,
    ) = full
    mine = own(hidden)
    grad_final = own(cotangent).astype(f32)

    query_self = project(mine, self_query).astype(bf16)
    key_self = project(hidden, self_key).astype(bf16)
    value_self = project(hidden, self_value).astype(bf16)
    blend_self, log_self = self_forward(narrow, where_at, query_self, key_self, value_self)
    first, first_normal, first_inverse = norm_forward(
        mine.astype(f32) + project(blend_self, self_out), first_gain, first_shift
    )
    first_low = first.astype(bf16)
    query_cross = project(first_low, cross_query).astype(bf16)
    blend_cross, log_cross, key_cross, value_cross, picked_rows = cross_forward(
        picked, everything, cross_key, cross_value, query_cross
    )
    second, second_normal, second_inverse = norm_forward(
        first + project(blend_cross, cross_out), second_gain, second_shift
    )
    second_low = second.astype(bf16)
    pre_act = project(second_low, expand_weight)
    activated = jax.nn.gelu(pre_act, approximate=False).astype(bf16)
    final, third_normal, third_inverse = norm_forward(
        second + project(activated, reduce_weight), third_gain, third_shift
    )
    output = final.astype(bf16)

    grad_third, third_gain_grad, third_shift_grad = norm_backward(
        grad_final, third_normal, third_inverse, third_gain
    )
    grad_ffn = grad_third.astype(bf16)
    reduce_grad = grad_weight(activated, grad_ffn)
    grad_pre = (grad_input(grad_ffn, reduce_weight) * gelu_slope(pre_act)).astype(bf16)
    expand_grad = grad_weight(second_low, grad_pre)
    grad_second = grad_third + grad_input(grad_pre, expand_weight)
    grad_second_in, second_gain_grad, second_shift_grad = norm_backward(
        grad_second, second_normal, second_inverse, second_gain
    )
    grad_cross = grad_second_in.astype(bf16)
    cross_out_grad = grad_weight(blend_cross, grad_cross)
    grad_blend_cross = grad_input(grad_cross, cross_out).astype(bf16)
    grad_query_cross, cross_key_grad, cross_value_grad = cross_backward(
        picked,
        everything,
        key_cross,
        value_cross,
        query_cross,
        log_cross,
        blend_cross,
        grad_blend_cross,
    )
    cross_query_grad = grad_weight(first_low, grad_query_cross)
    grad_first = grad_second_in + grad_input(grad_query_cross, cross_query)
    grad_first_in, first_gain_grad, first_shift_grad = norm_backward(
        grad_first, first_normal, first_inverse, first_gain
    )
    grad_self = grad_first_in.astype(bf16)
    self_out_grad = grad_weight(blend_self, grad_self)
    grad_blend_self = grad_input(grad_self, self_out).astype(bf16)
    grad_query_self, grad_key_self, grad_value_self = self_backward(
        narrow, where_at, query_self, key_self, value_self, log_self, blend_self, grad_blend_self
    )
    self_query_grad = grad_weight(mine, grad_query_self)
    self_key_grad = grad_weight(hidden, grad_key_self)
    self_value_grad = grad_weight(hidden, grad_value_self)
    grad_rows = grad_input(grad_key_self, self_key) + grad_input(grad_value_self, self_value)
    grad_own = grad_first_in + grad_input(grad_query_self, self_query)

    def spread(rows):
        empty = jnp.zeros((tok_rows, width), rows.dtype)
        placed = lax.dynamic_update_slice_in_dim(empty, rows[:chunk], at * chunk, 0)
        return lax.dynamic_update_slice_in_dim(
            placed, rows[chunk:], (2 * narrow - 1 - at) * chunk, 0
        )

    grad_hidden = lax.psum((grad_rows + spread(grad_own)).astype(bf16), "narrow").astype(f32)
    output = lax.psum(spread(output), "narrow")
    weight_grads = reduce_all(
        (
            self_query_grad,
            self_key_grad,
            self_value_grad,
            self_out_grad,
            cross_query_grad,
            cross_key_grad,
            cross_value_grad,
            cross_out_grad,
            expand_grad,
            reduce_grad,
        )
    )
    norm_grads = lax.psum(
        jnp.stack(
            [
                first_gain_grad,
                first_shift_grad,
                second_gain_grad,
                second_shift_grad,
                third_gain_grad,
                third_shift_grad,
            ]
        ),
        ("wide", "narrow"),
    )
    return (output, grad_hidden) + weight_grads + tuple(norm_grads[i] for i in range(6))


def solution(mesh):
    rows = P("wide", None)
    columns_split = P(None, "narrow")
    rows_split = P("narrow", None)
    weights = (columns_split,) * 3 + (rows_split,) + (columns_split,) * 3 + (rows_split,)
    weights += (columns_split, rows_split)
    return jax.shard_map(
        local,
        mesh=mesh,
        in_specs=(rows, rows, rows) + weights + (P(),) * 6 + (rows,),
        out_specs=(rows, rows) + weights + (P(),) * 6,
        check_vma=False,
    )
```

```python
import functools

import jax
import jax.numpy as jnp
from jax import lax
from jax.experimental import pallas as pl
from jax.experimental.pallas import tpu as pltpu
from jax.sharding import PartitionSpec as P

HEAD_DIM = 64
BLOCK_ROWS = 128
RET_BLOCKS = 8
PAIR = 2 * HEAD_DIM
VMEM_LIMIT = 60 << 20
BACKWARD_VMEM = 63 << 20

epsilon = 1e-05
bf16 = jnp.bfloat16
f32 = jnp.float32
MESH = pl.DeviceIdType.MESH


def norm_forward(summed, norm_gain, norm_shift):
    average = jnp.mean(summed, axis=-1, keepdims=True)
    centred = summed - average
    inverse = lax.rsqrt(jnp.mean(centred * centred, axis=-1, keepdims=True) + epsilon)
    normal = centred * inverse
    return (normal * norm_gain + norm_shift, normal, inverse)


def norm_backward(grad_out, normal, inverse, norm_gain):
    scaled = grad_out * norm_gain
    grad_in = inverse * (
        scaled
        - jnp.mean(scaled, axis=-1, keepdims=True)
        - normal * jnp.mean(scaled * normal, axis=-1, keepdims=True)
    )
    return (grad_in, jnp.sum(grad_out * normal, axis=0), jnp.sum(grad_out, axis=0))


def gelu_slope(pre_act):
    return (
        0.5 * (1.0 + lax.erf(pre_act * 0.7071067811865476))
        + pre_act * jnp.exp(-0.5 * pre_act * pre_act) * 0.3989422804014327
    )


def project(rows_in, weight):
    return jnp.dot(rows_in, weight, preferred_element_type=f32)


def grad_weight(left, right):
    return jnp.einsum("ti,to->io", left, right, preferred_element_type=f32)


def grad_input(grad_rows, weight):
    return jnp.einsum("to,io->ti", grad_rows, weight, preferred_element_type=f32)


def dot_nt(left, right):
    return lax.dot_general(left, right, (((1,), (1,)), ((), ())), preferred_element_type=f32)


def dot_tn(left, right):
    return lax.dot_general(left, right, (((0,), (0,)), ((), ())), preferred_element_type=f32)


def dot_nn(left, right):
    return lax.dot_general(left, right, (((1,), (0,)), ((), ())), preferred_element_type=f32)


def stack_heads(pair_rows):
    lane = lax.broadcasted_iota(jnp.int32, pair_rows.shape, 1)
    wide_rows = pair_rows.astype(f32)
    zero = jnp.zeros_like(wide_rows)
    return jnp.concatenate(
        [
            jnp.where(lane < HEAD_DIM, wide_rows, zero).astype(bf16),
            jnp.where(lane < HEAD_DIM, zero, wide_rows).astype(bf16),
        ],
        axis=0,
    )


def merge_heads(both):
    rows = both.shape[1] // 2
    sublane = lax.broadcasted_iota(jnp.int32, (PAIR, rows), 0)
    return jnp.transpose(jnp.where(sublane < HEAD_DIM, both[:, :rows], both[:, rows:]))


def causal_edge(rows):
    key = lax.broadcasted_iota(jnp.int32, (rows, 2 * rows), 0)
    query = lax.broadcasted_iota(jnp.int32, (rows, 2 * rows), 1)
    return key <= jnp.where(query >= rows, query - rows, query)


def scaled_heads(pair_rows):
    return stack_heads(pair_rows.astype(f32) * HEAD_DIM**-0.5)


KEY_ROWS = 128


def scores_of(keys, stacked, start, edge):
    part = dot_nt(keys[start : start + KEY_ROWS], stacked)
    if edge is not None and start + KEY_ROWS == keys.shape[0]:
        part = jnp.where(edge, part, -1e30)
    return part


def by_rows(part, reduce):
    return reduce(part.reshape(KEY_ROWS // 8, 8, part.shape[1]), axis=0)


def pair_forward(queries, keys, values, edge):
    stacked = scaled_heads(queries)
    starts = range(0, keys.shape[0], KEY_ROWS)
    scores = [scores_of(keys, stacked, start, edge) for start in starts]
    top = by_rows(scores[0], jnp.max)
    for part in scores[1:]:
        top = jnp.maximum(top, by_rows(part, jnp.max))
    top = jnp.max(top, axis=0, keepdims=True)
    total, blended = 0.0, 0.0
    for start, part in zip(starts, scores):
        raised = jnp.exp(part - top)
        total = total + by_rows(raised, jnp.sum)
        blended = blended + dot_tn(values[start : start + KEY_ROWS], raised.astype(bf16))
    total = jnp.sum(total, axis=0, keepdims=True)
    return merge_heads(blended / total).astype(bf16), top + jnp.log(total)


def pair_backward(queries, keys, values, edge, log_total, blended, grad_blend):
    rows = queries.shape[0]
    stacked = scaled_heads(queries)
    grads = stack_heads(grad_blend)
    scores = dot_nt(keys, stacked)
    if edge is not None:
        split = keys.shape[0] - edge.shape[0]
        last = jnp.where(edge, scores[split:], -1e30)
        scores = jnp.concatenate([scores[:split], last], axis=0) if split else last
    chances = jnp.exp(scores - log_total)
    weighed = jnp.transpose(blended.astype(f32) * grad_blend.astype(f32))
    centre = jnp.concatenate(
        [
            jnp.sum(weighed[:HEAD_DIM], axis=0, keepdims=True),
            jnp.sum(weighed[HEAD_DIM:], axis=0, keepdims=True),
        ],
        axis=1,
    )
    grad_scores = (chances * (dot_nt(values, grads) - centre)).astype(bf16)
    grad_values = dot_nn(chances.astype(bf16), grads)
    grad_keys = dot_nn(grad_scores, stacked)
    grad_queries = merge_heads(dot_tn(keys, grad_scores)) * HEAD_DIM**-0.5
    return grad_queries, grad_keys, grad_values


def self_blocks(narrow, total_rows, at):
    chunk = total_rows // (2 * narrow)
    for block in range(total_rows // BLOCK_ROWS):
        which, within = divmod(block * BLOCK_ROWS, chunk)
        if which < narrow:
            owner, local_row = which, within
        else:
            owner, local_row = 2 * narrow - 1 - which, chunk + within
        yield local_row, (block + 1) * BLOCK_ROWS, at == owner


def self_forward_kernel(narrow, at_ref, q_ref, k_ref, v_ref, o_ref, log_ref):
    for local_row, seen, taken in self_blocks(narrow, k_ref.shape[0], at_ref[0]):

        @pl.when(taken)
        def _():
            mine = pl.ds(local_row, BLOCK_ROWS)
            keys = pl.ds(0, seen)
            blended, log_total = pair_forward(
                q_ref[mine], k_ref[keys], v_ref[keys], causal_edge(BLOCK_ROWS)
            )
            o_ref[mine] = blended
            log_ref[0, pl.ds(local_row // BLOCK_ROWS, 1)] = log_total


def self_forward(narrow, at, queries, keys, values):
    rows, width = queries.shape
    total_rows = keys.shape[0]
    pairs = width // PAIR
    pair = lambda count: pl.BlockSpec((count, PAIR), lambda g, at: (0, g))
    return pl.pallas_call(
        functools.partial(self_forward_kernel, narrow),
        grid_spec=pltpu.PrefetchScalarGridSpec(
            num_scalar_prefetch=1,
            grid=(pairs,),
            in_specs=[pair(rows), pair(total_rows), pair(total_rows)],
            out_specs=[pair(rows), pl.BlockSpec((1, rows // BLOCK_ROWS, 2 * BLOCK_ROWS), lambda g, at: (g, 0, 0))],
        ),
        out_shape=[
            jax.ShapeDtypeStruct((rows, width), bf16),
            jax.ShapeDtypeStruct((pairs, rows // BLOCK_ROWS, 2 * BLOCK_ROWS), f32),
        ],
        compiler_params=pltpu.CompilerParams(vmem_limit_bytes=VMEM_LIMIT),
        name="self_forward",
    )(at, queries, keys, values)


def self_backward_kernel(
    narrow, at_ref, q_ref, k_ref, v_ref, log_ref, o_ref, g_ref, dq_ref, dk_ref, dv_ref, dk_sum, dv_sum
):
    rows = q_ref.shape[0] // 2
    dk_sum[...] = jnp.zeros_like(dk_sum)
    dv_sum[...] = jnp.zeros_like(dv_sum)
    for local_row, seen, taken in self_blocks(narrow, k_ref.shape[0], at_ref[0]):

        @pl.when(taken)
        def _():
            mine = pl.ds(local_row, BLOCK_ROWS)
            keys = pl.ds(0, seen)
            grad_q, grad_k, grad_v = pair_backward(
                q_ref[mine],
                k_ref[keys],
                v_ref[keys],
                causal_edge(BLOCK_ROWS),
                log_ref[0, pl.ds(local_row // BLOCK_ROWS, 1)],
                o_ref[mine],
                g_ref[mine],
            )
            dq_ref[mine] = grad_q.astype(bf16)
            dk_sum[keys] += grad_k
            dv_sum[keys] += grad_v

    dk_ref[...] = dk_sum[...].astype(bf16)
    dv_ref[...] = dv_sum[...].astype(bf16)


def self_backward(narrow, at, queries, keys, values, logs, blended, grads):
    rows, width = queries.shape
    total_rows = keys.shape[0]
    pairs = width // PAIR
    pair = lambda count: pl.BlockSpec((count, PAIR), lambda g, at: (0, g))
    return pl.pallas_call(
        functools.partial(self_backward_kernel, narrow),
        grid_spec=pltpu.PrefetchScalarGridSpec(
            num_scalar_prefetch=1,
            grid=(pairs,),
            in_specs=[
                pair(rows),
                pair(total_rows),
                pair(total_rows),
                pl.BlockSpec((1, rows // BLOCK_ROWS, 2 * BLOCK_ROWS), lambda g, at: (g, 0, 0)),
                pair(rows),
                pair(rows),
            ],
            out_specs=[pair(rows), pair(total_rows), pair(total_rows)],
            scratch_shapes=[pltpu.VMEM((total_rows, PAIR), f32)] * 2,
        ),
        out_shape=[
            jax.ShapeDtypeStruct((rows, width), bf16),
            jax.ShapeDtypeStruct((total_rows, width), bf16),
            jax.ShapeDtypeStruct((total_rows, width), bf16),
        ],
        compiler_params=pltpu.CompilerParams(vmem_limit_bytes=VMEM_LIMIT),
        name="self_backward",
    )(at, queries, keys, values, logs, blended, grads)


def cross_forward_kernel(picked_ref, *refs):
    blocks = refs[:RET_BLOCKS]
    wk_ref, wv_ref, q_ref, o_ref, log_ref, k_ref, v_ref, rows_in = refs[RET_BLOCKS:]
    for j in range(RET_BLOCKS):
        rows_in[pl.ds(j * BLOCK_ROWS, BLOCK_ROWS)] = blocks[j][...]
    k_ref[...] = dot_nn(rows_in[...], wk_ref[...]).astype(bf16)
    v_ref[...] = dot_nn(rows_in[...], wv_ref[...]).astype(bf16)
    for g in range(q_ref.shape[1] // PAIR):
        lanes = pl.ds(g * PAIR, PAIR)
        blended, log_total = pair_forward(q_ref[:, lanes], k_ref[:, lanes], v_ref[:, lanes], None)
        o_ref[:, lanes] = blended
        log_ref[0, pl.ds(g, 1)] = log_total


def block_specs(width):
    def spec(j):
        return pl.BlockSpec((BLOCK_ROWS, width), lambda b, picked: (picked[b * RET_BLOCKS + j], 0))

    return [spec(j) for j in range(RET_BLOCKS)]


def cross_forward(picked, everything, cross_key, cross_value, queries):
    rows, width = queries.shape
    count = rows // BLOCK_ROWS
    pairs = width // PAIR
    keys = RET_BLOCKS * BLOCK_ROWS
    whole = pl.BlockSpec((width, width), lambda b, picked: (0, 0))
    by_block = pl.BlockSpec((BLOCK_ROWS, width), lambda b, picked: (b, 0))
    by_keys = pl.BlockSpec((keys, width), lambda b, picked: (b, 0))
    return pl.pallas_call(
        cross_forward_kernel,
        grid_spec=pltpu.PrefetchScalarGridSpec(
            num_scalar_prefetch=1,
            grid=(count,),
            in_specs=block_specs(width) + [whole, whole, by_block],
            out_specs=[
                by_block,
                pl.BlockSpec((1, pairs, 2 * BLOCK_ROWS), lambda b, picked: (b, 0, 0)),
                by_keys,
                by_keys,
                by_keys,
            ],
        ),
        out_shape=[
            jax.ShapeDtypeStruct((rows, width), bf16),
            jax.ShapeDtypeStruct((count, pairs, 2 * BLOCK_ROWS), f32),
            jax.ShapeDtypeStruct((count * keys, width), bf16),
            jax.ShapeDtypeStruct((count * keys, width), bf16),
            jax.ShapeDtypeStruct((count * keys, width), bf16),
        ],
        compiler_params=pltpu.CompilerParams(vmem_limit_bytes=VMEM_LIMIT),
        name="cross_forward",
    )(picked, *([everything] * RET_BLOCKS), cross_key, cross_value, queries)


def cross_backward_kernel(picked_ref, *refs):
    blocks = refs[:RET_BLOCKS]
    (k_ref, v_ref, q_ref, log_ref, o_ref, g_ref, dq_ref, dwk_ref, dwv_ref, rows_in, both, sums) = refs[
        RET_BLOCKS:
    ]
    width = q_ref.shape[1]
    step = pl.program_id(0)

    @pl.when(step == 0)
    def _():
        sums[...] = jnp.zeros_like(sums)

    for j in range(RET_BLOCKS):
        rows_in[pl.ds(j * BLOCK_ROWS, BLOCK_ROWS)] = blocks[j][...]
    for g in range(width // PAIR):
        lanes = pl.ds(g * PAIR, PAIR)
        grad_q, grad_k, grad_v = pair_backward(
            q_ref[:, lanes],
            k_ref[:, lanes],
            v_ref[:, lanes],
            None,
            log_ref[0, pl.ds(g, 1)],
            o_ref[:, lanes],
            g_ref[:, lanes],
        )
        dq_ref[:, lanes] = grad_q.astype(bf16)
        both[:, lanes] = grad_k.astype(bf16)
        both[:, pl.ds(width + g * PAIR, PAIR)] = grad_v.astype(bf16)
    sums[...] += dot_tn(rows_in[...], both[...])

    @pl.when(step == pl.num_programs(0) - 1)
    def _():
        dwk_ref[...] = sums[:, :width].astype(bf16)
        dwv_ref[...] = sums[:, width:].astype(bf16)


def cross_backward(picked, everything, keys_in, values_in, queries, logs, blended, grads):
    rows, width = queries.shape
    count = rows // BLOCK_ROWS
    pairs = width // PAIR
    keys = RET_BLOCKS * BLOCK_ROWS
    whole = pl.BlockSpec((width, width), lambda b, picked: (0, 0))
    by_block = pl.BlockSpec((BLOCK_ROWS, width), lambda b, picked: (b, 0))
    by_keys = pl.BlockSpec((keys, width), lambda b, picked: (b, 0))
    return pl.pallas_call(
        cross_backward_kernel,
        grid_spec=pltpu.PrefetchScalarGridSpec(
            num_scalar_prefetch=1,
            grid=(count,),
            in_specs=block_specs(width)
            + [
                by_keys,
                by_keys,
                by_block,
                pl.BlockSpec((1, pairs, 2 * BLOCK_ROWS), lambda b, picked: (b, 0, 0)),
                by_block,
                by_block,
            ],
            out_specs=[by_block, whole, whole],
            scratch_shapes=[
                pltpu.VMEM((keys, width), bf16),
                pltpu.VMEM((keys, 2 * width), bf16),
                pltpu.VMEM((width, 2 * width), f32),
            ],
        ),
        out_shape=[
            jax.ShapeDtypeStruct((rows, width), bf16),
            jax.ShapeDtypeStruct((width, width), bf16),
            jax.ShapeDtypeStruct((width, width), bf16),
        ],
        compiler_params=pltpu.CompilerParams(vmem_limit_bytes=VMEM_LIMIT),
        name="cross_backward",
    )(
        picked,
        *([everything] * RET_BLOCKS),
        keys_in,
        values_in,
        queries,
        logs,
        blended,
        grads,
    )


COLUMNS = (0, 1, 2, 4, 5, 6, 8)


LINE = 4
HELD = 5


def as_row(ref):
    return ref[...].reshape(1, ref.shape[0])


class Place:
    def __init__(self):
        wide = lax.axis_index("wide")
        self.x = lax.axis_index("narrow")
        self.core = lax.rem(wide, 2)
        self.y = lax.rem(lax.div(wide, 2), 2)
        self.z = lax.div(wide, 4)
        self.wide = wide

    def at(self, z=None, y=None, core=None, x=None):
        z, y = (self.z if z is None else z), (self.y if y is None else y)
        core = self.core if core is None else core
        return (z * 4 + y * 2 + core, self.x if x is None else x)

    def greet(self):
        barrier = pltpu.get_barrier_semaphore()
        targets = [self.at(core=1 - self.core), self.at(y=1 - self.y), self.at(x=1 - self.x)]
        targets += [self.at(z=lax.rem(self.z + step, LINE)) for step in range(1, LINE)]
        for target in targets:
            pl.semaphore_signal(barrier, inc=1, device_id=target, device_id_type=MESH)
        pl.semaphore_wait(barrier, len(targets))


def forward_kernel(a_rows, b_rows, *refs):
    encoded_in, weights_in = refs[0], refs[1:11]
    hidden_in, first_gain, first_shift = refs[11:14]
    everything, full_out = refs[14], refs[15:25]
    kept_out, (log_self, inverse_out) = refs[25:33], refs[33:35]
    encoded, weights, kept = refs[35], refs[36:46], refs[46:54]
    hidden = refs[54]
    load_sem, own_sem, half_sem, kept_sem, flow_send, flow_recv, weight_send, weight_recv = refs[55:]
    q_self, k_self, v_self, a_self, first, first_normal, first_low, q_cross = kept
    full = weights[:HELD] + full_out[HELD:]
    me = Place()
    rows = encoded.shape[0]
    x, y, z, core = me.x, me.y, me.z, me.core
    low, high = z > 0, z < LINE - 1
    UP_A, DOWN_A, Y_A, UP_B, DOWN_B, Y_B, X_B, CORE_A, CORE_B = range(9)

    own = pltpu.make_async_copy(
        encoded, everything.at[pl.ds(pl.multiple_of(me.wide * rows, 128), rows)], own_sem
    )

    def region(i, ref, plane, part):
        if i in COLUMNS:
            count, columns = ref.shape[0], ref.shape[1] // 2
            start = pl.multiple_of(plane * columns, 128)
            if part is None:
                return ref.at[:, pl.ds(start, columns)]
            first = pl.multiple_of(part * (count // 2), 16)
            return ref.at[pl.ds(first, count // 2), pl.ds(start, columns)]
        count = ref.shape[0] // 2
        if part is None:
            return ref.at[pl.ds(pl.multiple_of(plane * count, 16), count)]
        first = pl.multiple_of(plane * count + part * (count // 2), 16)
        return ref.at[pl.ds(first, count // 2)]

    loads, halves = [], []
    for i in range(10):
        into = region(i, weights[i], x, None) if i < HELD else weights[i]
        loads.append(pltpu.make_async_copy(weights_in[i], into, load_sem.at[i]))
        if i < HELD:
            halves.append(pltpu.make_async_copy(weights[i], full_out[i], half_sem.at[i]))
        else:
            halves.append(
                pltpu.make_async_copy(weights[i], region(i, full[i], x, None), half_sem.at[i])
            )
    loads.append(pltpu.make_async_copy(encoded_in, encoded, load_sem.at[10]))
    loads.append(pltpu.make_async_copy(hidden_in, hidden, load_sem.at[11]))
    loads[10].start()
    for i in range(10):
        loads[i].start()
    loads[11].start()
    me.greet()
    loads[10].wait()

    def flow(kind, owner_z, owner_y, plane, target, from_core=None, held=False):
        owner = owner_z * 2 + owner_y
        start = owner * (2 * rows) + (core if from_core is None else from_core) * rows
        if plane is None:
            size, slot = a_rows, owner
        else:
            start = start + a_rows + plane * b_rows
            size, slot = b_rows, owner + (plane * 8 if kind == CORE_B else 0)
        piece = everything.at[pl.ds(pl.multiple_of(start, 16), size)]
        source = piece
        if held:
            first = 0 if plane is None else pl.multiple_of(a_rows + plane * b_rows, 16)
            source = encoded.at[pl.ds(first, size)]
        return pltpu.make_async_remote_copy(
            src_ref=source,
            dst_ref=piece,
            send_sem=flow_send.at[kind, slot],
            recv_sem=flow_recv.at[kind, slot],
            device_id=target,
            device_id_type=MESH,
        )

    sibling = me.at(core=1 - core)
    beside = me.at(y=1 - y)
    across = me.at(x=1 - x)
    above, below = me.at(z=z + 1), me.at(z=z - 1)

    def up_a(oz, held=False):
        return flow(UP_A, oz, y, None, above, held=held)

    def down_a(oz, held=False):
        return flow(DOWN_A, oz, y, None, below, held=held)

    def up_b(oz, oy, held=False):
        return flow(UP_B, oz, oy, x, above, held=held)

    def down_b(oz, oy, held=False):
        return flow(DOWN_B, oz, oy, x, below, held=held)

    def y_a(oz, oy, held=False):
        return flow(Y_A, oz, oy, None, beside, held=held)

    def y_b(oy, held=False):
        return flow(Y_B, z, oy, x, beside, held=held)

    def x_b(oz, oy, plane):
        return flow(X_B, oz, oy, plane, across)

    def core_a(oz, oy, from_core=None, held=False):
        return flow(CORE_A, oz, oy, None, sibling, from_core, held)

    def core_b(oz, oy, plane, from_core=None, held=False):
        return flow(CORE_B, oz, oy, plane, sibling, from_core, held)

    def weight(way, i, plane, part):
        piece = region(i, full[i], plane, part)
        if way == 0 and i >= HELD:
            piece_in = weights[i]
            count = piece_in.shape[0] // 2
            piece_in = piece_in.at[pl.ds(pl.multiple_of(part * count, 16), count)]
        else:
            piece_in = piece
        return pltpu.make_async_remote_copy(
            src_ref=piece_in,
            dst_ref=piece,
            send_sem=weight_send.at[way, i],
            recv_sem=weight_recv.at[way, i],
            device_id=across if way == 0 else sibling,
            device_id_type=MESH,
        )

    y_b(y, True).start()
    y_a(z, y, True).start()
    pl.when(high)(lambda: up_a(z, True).start())
    pl.when(low)(lambda: down_a(z, True).start())

    def weights_go(some):
        for i in some:
            weight(0, i, x, core).start()

    def weights_come(some):
        for i in some:
            weight(0, i, 1 - x, core).wait_recv()
            weight(1, i, 1 - x, core).start()

    for i in range(3):
        loads[i].wait()
    weights_go(range(3))
    core_a(z, y, held=True).start()
    core_b(z, y, 0, held=True).start()
    core_b(z, y, 1, held=True).start()
    own.start()
    for i in range(3, 12):
        if i != 10:
            loads[i].wait()
    for i in range(HELD, 10):
        halves[i].start()

    y_b(1 - y).wait_recv()
    core_b(z, 1 - y, x).start()
    weights_come(range(3))
    weights_go(range(3, 8))
    for i in range(3):
        weight(1, i, 1 - x, 1 - core).wait_recv()

    total_rows = hidden.shape[0]
    chunk = total_rows // 4
    mine = (
        pl.ds(pl.multiple_of(x * chunk, 128), chunk),
        pl.ds(pl.multiple_of((3 - x) * chunk, 128), chunk),
    )
    places = (pl.ds(0, chunk), pl.ds(chunk, chunk))
    for piece, place in zip(mine, places):
        q_self[place] = dot_nn(hidden[piece], weights[0][...]).astype(bf16)
    k_self[...] = dot_nn(hidden[...], weights[1][...]).astype(bf16)
    v_self[...] = dot_nn(hidden[...], weights[2][...]).astype(bf16)
    put = [pltpu.make_async_copy(kept[i], kept_out[i], kept_sem.at[i]) for i in range(8)]
    for i in range(3):
        put[i].start()

    def self_step(g, carry):
        lanes = pl.ds(pl.multiple_of(g * PAIR, PAIR), PAIR)
        for local_row, seen, taken in self_blocks(2, total_rows, x):

            @pl.when(taken)
            def _():
                some = pl.ds(local_row, BLOCK_ROWS)
                blended, log_total = pair_forward(
                    q_self[some, lanes],
                    k_self[pl.ds(0, seen), lanes],
                    v_self[pl.ds(0, seen), lanes],
                    causal_edge(BLOCK_ROWS),
                )
                a_self[some, lanes] = blended
                log_self[g, pl.ds(local_row // BLOCK_ROWS, 1)] = log_total

        return carry

    pairs = q_self.shape[1] // PAIR
    lax.fori_loop(0, pairs // 2, self_step, 0)

    def beside_arrives(oz):
        y_a(oz, 1 - y).wait_recv()
        core_a(oz, 1 - y).start()

    def pass_a(oz, arrived, onward, further):
        arrived(oz).wait_recv()
        pl.when(onward)(lambda: further(oz).start())
        y_a(oz, y).start()
        core_a(oz, y).start()

    def pass_b(oz, arrived, onward, further):
        for oy in (y, 1 - y):
            arrived(oz, oy).wait_recv()
            pl.when(onward)(lambda: further(oz, oy).start())
            x_b(oz, oy, x).start()
            core_b(oz, oy, x).start()

    def step_a(step):
        under, over = z - 1 - step, z + 1 + step
        pl.when(under >= 0)(lambda: pass_a(under, up_a, high, up_a))
        pl.when(over < LINE)(lambda: pass_a(over, down_a, low, down_a))

    def step_b(step):
        under, over = z - 1 - step, z + 1 + step
        pl.when(under >= 0)(lambda: pass_b(under, up_b, high, up_b))
        pl.when(over < LINE)(lambda: pass_b(over, down_b, low, down_b))

    step_a(0)
    for oy, held in ((y, True), (1 - y, False)):
        pl.when(high)(lambda oy=oy, held=held: up_b(z, oy, held).start())
        pl.when(low)(lambda oy=oy, held=held: down_b(z, oy, held).start())
    weights_go(range(8, 10))
    x_b(z, 1 - y, x).start()
    lax.fori_loop(pairs // 2, pairs, self_step, 0)
    put[3].start()
    weights_come(range(3, 5))
    for i in range(3, 5):
        weight(1, i, 1 - x, 1 - core).wait_recv()
    for i in range(HELD):
        halves[i].start()

    for piece, place in zip(mine, places):
        summed = hidden[piece].astype(f32) + dot_nn(a_self[place], weights[3][...])
        centred = summed - jnp.mean(summed, axis=-1, keepdims=True)
        inverse = lax.rsqrt(jnp.mean(centred * centred, axis=-1, keepdims=True) + epsilon)
        normal = centred * inverse
        result = normal * as_row(first_gain) + as_row(first_shift)
        first_normal[place] = normal
        inverse_out[place] = inverse
        first[place] = result
        first_low[place] = result.astype(bf16)
        q_cross[place] = dot_nn(result.astype(bf16), weights[4][...]).astype(bf16)
    for i in range(4, 8):
        put[i].start()

    step_a(1)
    step_b(0)
    step_a(2)
    step_b(1)
    step_b(2)
    weights_come(range(5, 10))
    beside_arrives(z)
    for step in range(1, LINE):
        pl.when(z - step >= 0)(lambda: beside_arrives(z - step))
        pl.when(z + step < LINE)(lambda: beside_arrives(z + step))

    def across_arrives(oz, oy):
        x_b(oz, oy, 1 - x).wait_recv()
        core_b(oz, oy, 1 - x).start()

    across_arrives(z, 1 - y)
    for step in range(LINE - 1):
        under, over = z - 1 - step, z + 1 + step
        for oy in (y, 1 - y):
            pl.when(under >= 0)(lambda: across_arrives(under, oy))
            pl.when(over < LINE)(lambda: across_arrives(over, oy))

    y_b(y).wait_send()
    x_b(z, 1 - y, x).wait_send()
    for oz in range(LINE):
        y_a(oz, y).wait_send()
        for oy in range(2):
            core_a(oz, oy).wait_send()
            core_a(oz, oy, 1 - core).wait_recv()
            for plane in range(2):
                core_b(oz, oy, plane).wait_send()
                core_b(oz, oy, plane, 1 - core).wait_recv()
        away = oz != z

        @pl.when(away)
        def _():
            for oy in range(2):
                x_b(oz, oy, x).wait_send()

        @pl.when(jnp.logical_and(high, oz <= z))
        def _():
            up_a(oz).wait_send()
            for oy in range(2):
                up_b(oz, oy).wait_send()

        @pl.when(jnp.logical_and(low, oz >= z))
        def _():
            down_a(oz).wait_send()
            for oy in range(2):
                down_b(oz, oy).wait_send()

    own.wait()
    for i in range(10):
        halves[i].wait()
        weight(0, i, x, core).wait_send()
        weight(1, i, 1 - x, core).wait_send()
        if i >= HELD:
            weight(1, i, 1 - x, 1 - core).wait_recv()
    for copy in put:
        copy.wait()


def forward_by_kernel(encoded, weights, hidden, first_gain, first_shift):
    rows, width = encoded.shape
    a_rows = rows * 17 // 24 // 16 * 16
    b_rows = (rows - a_rows) // 2
    shapes = [jax.ShapeDtypeStruct((16 * rows, width), bf16)]
    for i, w in enumerate(weights):
        doubled = (w.shape[0], 2 * w.shape[1]) if i in COLUMNS else (2 * w.shape[0], w.shape[1])
        shapes.append(jax.ShapeDtypeStruct(doubled, bf16))
    total_rows = hidden.shape[0]
    mine, pairs = total_rows // 2, width // PAIR
    kept = [(mine, bf16), (total_rows, bf16), (total_rows, bf16), (mine, bf16)]
    kept += [(mine, f32), (mine, f32), (mine, bf16), (mine, bf16)]
    held = [s.shape if i < HELD else w.shape for i, (s, w) in enumerate(zip(shapes[1:], weights))]
    small = [
        jax.ShapeDtypeStruct((pairs, mine // BLOCK_ROWS, 2 * BLOCK_ROWS), f32),
        jax.ShapeDtypeStruct((mine, 1), f32),
    ]
    dma = pltpu.SemaphoreType.DMA
    anywhere = pl.BlockSpec(memory_space=pl.ANY)
    vmem = pl.BlockSpec(memory_space=pltpu.VMEM)
    out = pl.pallas_call(
        functools.partial(forward_kernel, a_rows, b_rows),
        out_shape=shapes + [jax.ShapeDtypeStruct((n, width), dtype) for n, dtype in kept] + small,
        in_specs=[anywhere] * 12 + [vmem] * 2,
        out_specs=[anywhere] * 19 + [vmem] * 2,
        scratch_shapes=[pltpu.VMEM((rows, width), bf16)]
        + [pltpu.VMEM(shape, bf16) for shape in held]
        + [pltpu.VMEM((n, width), dtype) for n, dtype in kept]
        + [pltpu.VMEM((total_rows, width), bf16)]
        + [dma((12,)), dma, dma((10,)), dma((8,))]
        + [dma((9, 16)), dma((9, 16)), dma((2, 10)), dma((2, 10))],
        compiler_params=pltpu.CompilerParams(
            collective_id=0, has_side_effects=True, vmem_limit_bytes=VMEM_LIMIT
        ),
        name="forward",
    )(encoded, *weights, hidden, first_gain, first_shift)
    return out[0], tuple(out[1:11]), tuple(out[11:])


TILE = 384
HALF = TILE // 2
PART = HALF // LINE
UNITS = 16
SLOTS = 12
UNIT_WEIGHTS = (8, 8, 8, 8, 9, 9, 9, 9, 7, 5, 6, 4, 3, 0, 1, 2)
LAST_TICK = UNITS + 11


def share_corner(unit, core, plane):
    if unit < 4:
        return core * TILE, (plane * 4 + unit) * TILE
    if unit < 8:
        return (plane * 4 + unit - 4) * TILE, core * TILE
    if unit in (8, 12):
        return plane * TILE, core * TILE
    return core * TILE, plane * TILE


def backward_kernel(*refs):
    (
        expand_grad, reduce_grad, cross_out_grad, picked_rows, keys_in, values_in, q_cross, a_cross,
        g_cross, log_cross, first_low, cross_query, g_second, first_normal, first_inverse, first_gain,
        a_self, self_out, q_self, k_self, v_self, log_self, hidden, self_query, self_key, self_value,
        norms,
    ) = refs[:27]
    sums_out, mine_out, theirs_out, norms_out = refs[27:31]
    (
        own, from_core, from_a, from_b, from_z, summed, pool, pool32, both, staged, dq_cross, dk_sum,
        dv_sum, theirs, rows_in, rows_got, norm_all, norm_in,
        own_sem, core_send, core_recv, a_send, a_recv, b_send, b_recv, z_send, z_recv, gz_send, gz_recv,
        gy_send, gy_recv, gc_send, gc_recv, keep_sem, load_sem, kv_sem, e_sem, extra_send, extra_recv,
        norm_send, norm_recv,
    ) = refs[31:]
    me = Place()
    x, y, z, core = me.x, me.y, me.z, me.core
    sibling, beside, across = me.at(core=1 - core), me.at(y=1 - y), me.at(x=1 - x)
    width = 2 * TILE
    keys = RET_BLOCKS * BLOCK_ROWS
    rows = q_cross.shape[0]
    blocks = rows // BLOCK_ROWS
    pairs = width // PAIR
    chunk = rows // 2

    def rem(u, n):
        return u % n if isinstance(u, int) else lax.rem(u, n)

    def remote(src, dst, send, recv, target):
        return pltpu.make_async_remote_copy(
            src_ref=src, dst_ref=dst, send_sem=send, recv_sem=recv,
            device_id=target, device_id_type=MESH,
        )


    def share(ref, unit, of_core, plane, part):
        row, column = share_corner(unit, of_core, plane)
        return ref.at[
            pl.ds(pl.multiple_of(row + part * HALF, 64), HALF),
            pl.ds(pl.multiple_of(column, 128), TILE),
        ]

    def own_copy(ref, unit, plane, part):
        return pltpu.make_async_copy(
            share(ref, unit, core, plane, part),
            own.at[unit % SLOTS, plane, part],
            own_sem.at[unit % SLOTS, plane * 2 + part],
        )

    def core_copy(src, u, plane, part):
        return remote(
            src, from_core.at[u, plane, part], core_send.at[u, plane * 2 + part],
            core_recv.at[u, plane * 2 + part], sibling,
        )

    def to_core(ref, unit, plane, part):
        return core_copy(share(ref, unit, 1 - core, plane, part), unit, plane, part)

    def a_first(u, slot):
        return remote(own.at[slot, 1 - x], from_a.at[u], a_send.at[u], a_recv.at[u], across)

    def a_second(u, slot):
        return remote(own.at[slot, :, 1 - y], from_a.at[u], a_send.at[u], a_recv.at[u], beside)

    def b_first(u, slot):
        return remote(own.at[slot, x, 1 - y], from_b.at[u], b_send.at[u], b_recv.at[u], beside)

    def b_second(u, slot):
        return remote(own.at[slot, 1 - x, y], from_b.at[u], b_send.at[u], b_recv.at[u], across)

    def to_z(u, slot, d):
        other = lax.rem(z + d, LINE)
        piece = own.at[slot, x, y, pl.ds(pl.multiple_of(other * PART, 16), PART)]
        return remote(
            piece, from_z.at[u, d - 1], z_send.at[u, d - 1], z_recv.at[u, d - 1], me.at(z=other)
        )

    def result(u, of_z):
        return sums_out.at[u, core, pl.ds(pl.multiple_of(y * HALF + of_z * PART, 16), PART)]

    def keep(u):
        return pltpu.make_async_copy(summed.at[u], result(u, z), keep_sem.at[u])

    def gather_z(u, d):
        return remote(
            summed.at[u], result(u, z), gz_send.at[u, d - 1], gz_recv.at[u, d - 1],
            me.at(z=lax.rem(z + d, LINE)),
        )

    def gathered_z(u, d):
        return remote(
            summed.at[u], result(u, lax.rem(z + LINE - d, LINE)), gz_send.at[u, d - 1],
            gz_recv.at[u, d - 1], beside,
        )

    def gather_y(u, at_y):
        piece = sums_out.at[u, core, pl.ds(pl.multiple_of(at_y * HALF, 16), HALF)]
        return remote(piece, piece, gy_send.at[u], gy_recv.at[u], beside)

    def gather_core(u, at_core):
        piece = sums_out.at[u, at_core]
        return remote(piece, piece, gc_send.at[u], gc_recv.at[u], sibling)

    def plus(a, b):
        return a + b

    def by_order(u, first, second):
        if isinstance(u, int):
            (first if u % 2 == 0 else second)()
        else:
            pl.when(lax.rem(u, 2) == 0)(first)
            pl.when(lax.rem(u, 2) == 1)(second)

    def stage_core(u):
        slot = rem(u, SLOTS)
        early_one = u < len(ready)

        def arrived():
            for plane, part in corners:
                piece = own.at[slot, plane, part]
                pltpu.make_async_copy(piece, piece, own_sem.at[slot, plane * 2 + part]).wait()

        if isinstance(u, int):
            if early_one:
                arrived()
        else:
            pl.when(early_one)(arrived)
        for plane, part in corners:
            core_copy(own.at[slot, plane, part], u, plane, part).wait_recv()
        own[slot] = plus(own[slot], from_core[u])
        by_order(u, lambda: a_first(u, slot).start(), lambda: a_second(u, slot).start())

    def stage_a(u):
        slot = rem(u, SLOTS)

        def first():
            a_first(u, slot).wait()
            own[slot, x] = plus(own[slot, x], from_a[u])
            b_first(u, slot).start()

        def second():
            a_second(u, slot).wait()
            own[slot, :, y] = plus(own[slot, :, y], from_a[u])
            b_second(u, slot).start()

        by_order(u, first, second)

    def stage_b(u):
        slot = rem(u, SLOTS)
        by_order(u, lambda: b_first(u, slot).wait(), lambda: b_second(u, slot).wait())
        own[slot, x, y] = plus(own[slot, x, y], from_b[u])
        for d in range(1, LINE):
            to_z(u, slot, d).start()

    def stage_z(u):
        slot = rem(u, SLOTS)
        for d in range(1, LINE):
            to_z(u, slot, d).wait()
        total = own[slot, x, y, pl.ds(pl.multiple_of(z * PART, 16), PART)].astype(f32)
        for d in range(1, LINE):
            total += from_z[u, d - 1].astype(f32)
        summed[u] = total.astype(bf16)
        keep(u).start()
        for d in range(1, LINE):
            gather_z(u, d).start()

    def stage_gather_z(u):
        keep(u).wait()
        for d in range(1, LINE):
            gathered_z(u, d).wait_recv()
            gather_z(u, d).wait_send()
        gather_y(u, y).start()

    def stage_gather_y(u):
        gather_y(u, 1 - y).wait_recv()
        gather_y(u, y).wait_send()
        gather_core(u, core).start()

    def stage_gather_core(u):
        gather_core(u, 1 - core).wait_recv()
        gather_core(u, core).wait_send()

    stages = (
        (0, stage_core), (2, stage_a), (4, stage_b), (6, stage_z), (8, stage_gather_z),
        (10, stage_gather_y), (12, stage_gather_core),
    )

    def tick(t):
        for lag, stage in stages:
            if isinstance(t, int):
                if 0 <= t - lag < UNITS:
                    stage(t - lag)
            else:
                u = t - lag
                pl.when(jnp.logical_and(u >= 0, u < UNITS))(lambda stage=stage, u=u: stage(u))

    KV, E, Q, O, G, FIRST, CROSS_Q, A_SELF, SELF_OUT = (
        0, 4096, 5120, 5632, 6144, 6656, 7168, 7936, 8448
    )
    QS, KS, VS, DQ, DK, DV, HIDDEN, DA = 0, 512, 1536, 2560, 3072, 4096, 5120, 6144
    WQ, WK, WV = 0, 768, 1536

    def load(src, row, sem, into=pool):
        return pltpu.make_async_copy(src, into.at[pl.ds(row, src.shape[0])], load_sem.at[sem])

    def kv_copy(b, which):
        src = (keys_in, values_in)[which].at[pl.ds(pl.multiple_of(b * keys, 128), keys)]
        row = pl.multiple_of(lax.rem(b, 2) * (2 * keys) + which * keys, 128)
        return pltpu.make_async_copy(src, pool.at[pl.ds(row, keys)], kv_sem.at[lax.rem(b, 2), which])

    def e_copy(b):
        src = picked_rows.at[pl.ds(pl.multiple_of(b * keys, 128), keys)]
        return pltpu.make_async_copy(src, pool.at[pl.ds(E, keys)], e_sem)

    early = [
        load(q_cross, Q, 0), load(a_cross, O, 1), load(g_cross, G, 2), load(first_low, FIRST, 3),
        load(cross_query, CROSS_Q, 4), load(a_self, A_SELF, 5), load(self_out, SELF_OUT, 6),
    ]
    for which in range(2):
        kv_copy(jnp.int32(0), which).start()
    for copy in early:
        copy.start()
    ready = [(expand_grad, u) for u in range(4)] + [(reduce_grad, u) for u in range(4, 8)]
    ready.append((cross_out_grad, 8))
    corners = [(plane, part) for plane in range(2) for part in range(2)]
    for ref, unit in ready:
        for plane, part in corners:
            own_copy(ref, unit, plane, part).start()
    me.greet()
    for ref, unit in ready:
        for plane, part in corners:
            to_core(ref, unit, plane, part).start()
    both_sums = pool32
    both_sums[...] = jnp.zeros_like(both_sums)
    for copy in early[:3]:
        copy.wait()

    def at_row(row):
        return pl.ds(pl.multiple_of(row, 128), BLOCK_ROWS)

    def cross_step(i, carry):
        b, g = lax.div(i, pairs), lax.rem(i, pairs)

        @pl.when(g == 0)
        def _():
            for which in range(2):
                kv_copy(b, which).wait()
            e_copy(b).start()

            @pl.when(b + 1 < blocks)
            def _():
                for which in range(2):
                    kv_copy(b + 1, which).start()

        lanes = pl.ds(pl.multiple_of(g * PAIR, PAIR), PAIR)
        row = pl.multiple_of(b * BLOCK_ROWS, BLOCK_ROWS)
        key_row = pl.multiple_of(lax.rem(b, 2) * (2 * keys), 128)
        grad_q, grad_k, grad_v = pair_backward(
            pool[at_row(Q + row), lanes],
            pool[pl.ds(key_row, keys), lanes],
            pool[pl.ds(pl.multiple_of(key_row + keys, 128), keys), lanes],
            None,
            log_cross[b, pl.ds(g, 1)],
            pool[at_row(O + row), lanes],
            pool[at_row(G + row), lanes],
        )
        dq_cross[pl.ds(row, BLOCK_ROWS), lanes] = grad_q.astype(bf16)
        both[:, lanes] = grad_k.astype(bf16)
        both[:, pl.ds(pl.multiple_of(width + g * PAIR, PAIR), PAIR)] = grad_v.astype(bf16)

        @pl.when(g == pairs - 1)
        def _():
            e_copy(b).wait()
            both_sums[pl.ds(0, width)] += dot_tn(pool[pl.ds(E, keys)], both[:, :width])
            both_sums[pl.ds(width, width)] += dot_tn(pool[pl.ds(E, keys)], both[:, width:])

        pl.when(lax.rem(i, 4) == 1)(lambda: tick(lax.div(i, 4)))
        return carry

    lax.fori_loop(0, blocks * pairs, cross_step, 0)

    def hand_over(unit):
        ref = staged.at[unit % 2]
        for plane, part in corners:
            to_core(ref, unit, plane, part).start()
            own_copy(ref, unit, plane, part).start()

    def kept(unit):
        for plane, part in corners:
            own_copy(staged.at[unit % 2], unit, plane, part).wait()

    def left(unit):
        for plane, part in corners:
            to_core(staged.at[unit % 2], unit, plane, part).wait_send()

    def handed_over(unit):
        kept(unit)
        left(unit)

    late = [load(q_self, QS, 7), load(k_self, KS, 8), load(v_self, VS, 9), load(hidden, HIDDEN, 10)]
    for copy in late:
        copy.start()
    staged[1] = both_sums[pl.ds(0, width)].astype(bf16)
    hand_over(9)
    tick(6)
    staged[0] = both_sums[pl.ds(width, width)].astype(bf16)
    hand_over(10)
    g_copy = load(g_second, 0, 11, pool32)
    n_copy = load(first_normal, rows, 12, pool32)
    g_copy.start()
    n_copy.start()
    for copy in early[3:]:
        copy.wait()
    tick(7)
    handed_over(9)
    staged[1] = dot_tn(pool[pl.ds(FIRST, rows)], dq_cross[...]).astype(bf16)
    hand_over(11)

    g_copy.wait()
    n_copy.wait()
    normal = pool32[pl.ds(rows, rows)]
    grad_out = pool32[pl.ds(0, rows)] + dot_nt(dq_cross[...], pool[pl.ds(CROSS_Q, width)])
    scaled = grad_out * as_row(first_gain)
    grad_in = first_inverse[...] * (
        scaled
        - jnp.mean(scaled, axis=-1, keepdims=True)
        - normal * jnp.mean(scaled * normal, axis=-1, keepdims=True)
    )
    norm_all[...] = norms[...]
    norm_all[pl.ds(0, 1)] = jnp.sum(grad_out * normal, axis=0, keepdims=True)
    norm_all[pl.ds(1, 1)] = jnp.sum(grad_out, axis=0, keepdims=True)
    pool32[pl.ds(2 * rows, rows)] = grad_in
    grad_low = grad_in.astype(bf16)
    pool[pl.ds(DA, rows)] = dot_nt(grad_low, pool[pl.ds(SELF_OUT, width)]).astype(bf16)
    tick(8)
    handed_over(10)
    staged[0] = dot_tn(pool[pl.ds(A_SELF, rows)], grad_low).astype(bf16)
    hand_over(12)

    along_z = tuple(me.at(z=lax.rem(z + d, LINE)) for d in range(1, LINE))
    rounds = ((sibling,), (across,), (beside,), along_z)

    def norm_copies(which):
        first = min(which, 3)
        return [
            remote(
                norm_all, norm_in.at[first + k], norm_send.at[first + k], norm_recv.at[first + k], target
            )
            for k, target in enumerate(rounds[which])
        ]

    def norm_start(which):
        for copy in norm_copies(which):
            copy.start()

    def norm_finish(which):
        for copy in norm_copies(which):
            copy.wait()
        for k in range(len(rounds[which])):
            norm_all[...] += norm_in[which + k]

    norm_start(0)

    for copy in late:
        copy.wait()
    kept(11)
    kept(12)

    def self_step(g, carry):
        lanes = pl.ds(pl.multiple_of(g * PAIR, PAIR), PAIR)
        dk_sum[...] = jnp.zeros_like(dk_sum)
        dv_sum[...] = jnp.zeros_like(dv_sum)
        for local_row, seen, taken in self_blocks(2, hidden.shape[0], x):

            @pl.when(taken)
            def _():
                mine = pl.ds(local_row, BLOCK_ROWS)
                grad_q, grad_k, grad_v = pair_backward(
                    pool[pl.ds(QS + local_row, BLOCK_ROWS), lanes],
                    pool[pl.ds(KS, seen), lanes],
                    pool[pl.ds(VS, seen), lanes],
                    causal_edge(BLOCK_ROWS),
                    log_self[g, pl.ds(local_row // BLOCK_ROWS, 1)],
                    a_self_rows(local_row, lanes),
                    pool[pl.ds(DA + local_row, BLOCK_ROWS), lanes],
                )
                pool[pl.ds(DQ + local_row, BLOCK_ROWS), lanes] = grad_q.astype(bf16)
                dk_sum[pl.ds(0, seen)] += grad_k
                dv_sum[pl.ds(0, seen)] += grad_v

        pool[pl.ds(DK, hidden.shape[0]), lanes] = dk_sum[...].astype(bf16)
        pool[pl.ds(DV, hidden.shape[0]), lanes] = dv_sum[...].astype(bf16)
        pl.when(lax.rem(g, 2) == 1)(lambda: tick(9 + lax.div(g, 2)))
        return carry

    def a_self_rows(local_row, lanes):
        return pool[pl.ds(A_SELF + local_row, BLOCK_ROWS), lanes]

    lax.fori_loop(0, pairs, self_step, 0)
    norm_finish(0)
    norm_start(1)
    last_loads = [load(self_query, WQ, 13), load(self_key, WK, 14), load(self_value, WV, 15)]
    for copy in last_loads:
        copy.start()

    left(11)
    for copy in last_loads:
        copy.wait()

    def row_grads(at_chunk):
        dk = pool[pl.ds(pl.multiple_of(DK + at_chunk * chunk, 128), chunk)]
        dv = pool[pl.ds(pl.multiple_of(DV + at_chunk * chunk, 128), chunk)]
        return dot_nt(dk, pool[pl.ds(WK, width)]) + dot_nt(dv, pool[pl.ds(WV, width)])

    theirs[pl.ds(0, chunk)] = row_grads(1 - x).astype(bf16)
    theirs[pl.ds(chunk, chunk)] = row_grads(2 + x).astype(bf16)
    rows_copy = remote(theirs, rows_in, extra_send.at[0], extra_recv.at[0], across)
    got_copy = remote(rows_got, theirs_out, extra_send.at[1], extra_recv.at[1], across)
    rows_copy.start()
    low_rows = pl.ds(pl.multiple_of(HIDDEN + x * chunk, 128), chunk)
    high_rows = pl.ds(pl.multiple_of(HIDDEN + (3 - x) * chunk, 128), chunk)
    all_rows = hidden.shape[0]
    staged[1] = (
        dot_tn(pool[low_rows], pool[pl.ds(DQ, chunk)])
        + dot_tn(pool[high_rows], pool[pl.ds(DQ + chunk, chunk)])
    ).astype(bf16)
    hand_over(13)
    norm_finish(1)
    norm_start(2)
    left(12)
    staged[0] = dot_tn(pool[pl.ds(HIDDEN, all_rows)], pool[pl.ds(DK, all_rows)]).astype(bf16)
    hand_over(14)
    tick(12)
    handed_over(13)
    staged[1] = dot_tn(pool[pl.ds(HIDDEN, all_rows)], pool[pl.ds(DV, all_rows)]).astype(bf16)
    hand_over(15)
    norm_finish(2)
    norm_start(3)
    tick(13)
    handed_over(14)
    handed_over(15)

    tick(14)
    for k, at_chunk in enumerate((x, 3 - x)):
        piece = pl.ds(k * chunk, chunk)
        mine_out[piece] = (
            row_grads(at_chunk)
            + dot_nt(pool[pl.ds(DQ + k * chunk, chunk)], pool[pl.ds(WQ, width)])
            + pool32[pl.ds(2 * rows + k * chunk, chunk)]
        )
    norm_finish(3)
    norms_out[...] = norm_all[...]

    def last_step(t, carry):
        tick(t)

        @pl.when(t == 17)
        def _():
            rows_copy.wait()
            whole = mine_out[...] + rows_in[...].astype(f32)
            mine_out[...] = whole
            rows_got[...] = whole.astype(bf16)
            got_copy.start()

        return carry

    lax.fori_loop(15, LAST_TICK + 1, last_step, 0)
    got_copy.wait()
    for ref, unit in ready:
        for plane, part in corners:
            to_core(ref, unit, plane, part).wait_send()


def backward_by_kernel(*args):
    rows, width = args[6].shape
    all_rows = args[22].shape[0]
    norms = args[26]
    anywhere = pl.BlockSpec(memory_space=pl.ANY)
    vmem = pl.BlockSpec(memory_space=pltpu.VMEM)
    in_specs = [anywhere] * 27
    for i in (9, 14, 15, 21, 26):
        in_specs[i] = vmem
    dma = pltpu.SemaphoreType.DMA
    U, T, H, Z = UNITS, TILE, HALF, LINE - 1
    return pl.pallas_call(
        backward_kernel,
        out_shape=[
            jax.ShapeDtypeStruct((U, 2, T, T), bf16),
            jax.ShapeDtypeStruct((rows, width), f32),
            jax.ShapeDtypeStruct((rows, width), bf16),
            jax.ShapeDtypeStruct(norms.shape, f32),
        ],
        in_specs=in_specs,
        out_specs=[anywhere, vmem, anywhere, vmem],
        scratch_shapes=[
            pltpu.VMEM((SLOTS, 2, 2, H, T), bf16),
            pltpu.VMEM((U, 2, 2, H, T), bf16),
            pltpu.VMEM((U, 2, H, T), bf16),
            pltpu.VMEM((U, H, T), bf16),
            pltpu.VMEM((U, Z, PART, T), bf16),
            pltpu.VMEM((U, PART, T), bf16),
            pltpu.VMEM((9216, width), bf16),
            pltpu.VMEM((2 * width, width), f32),
            pltpu.VMEM((RET_BLOCKS * BLOCK_ROWS, 2 * width), bf16),
            pltpu.VMEM((2, width, width), bf16),
            pltpu.VMEM((rows, width), bf16),
            pltpu.VMEM((all_rows, PAIR), f32),
            pltpu.VMEM((all_rows, PAIR), f32),
            pltpu.VMEM((rows, width), bf16),
            pltpu.VMEM((rows, width), bf16),
            pltpu.VMEM((rows, width), bf16),
            pltpu.VMEM(norms.shape, f32),
            pltpu.VMEM((6,) + norms.shape, f32),
            dma((SLOTS, 4)), dma((U, 4)), dma((U, 4)), dma((U,)), dma((U,)), dma((U,)), dma((U,)),
            dma((U, Z)), dma((U, Z)), dma((U, Z)), dma((U, Z)), dma((U,)), dma((U,)), dma((U,)),
            dma((U,)), dma((U,)), dma((16,)), dma((2, 2)), dma, dma((2,)), dma((2,)), dma((6,)),
            dma((6,)),
        ],
        compiler_params=pltpu.CompilerParams(
            collective_id=1, has_side_effects=True, vmem_limit_bytes=BACKWARD_VMEM
        ),
        name="backward",
    )(*args)


def output_place(unit, core):
    row, column = share_corner(unit, core, 0)
    return UNIT_WEIGHTS[unit], row, column


def finish_kernel(*refs):
    sums, ours_in, theirs_in, made_in, made_theirs_in, norms = refs[:6]
    output, grad_hidden, outs, norm_outs = refs[6], refs[7], refs[8:18], refs[18:24]
    taken, given, ours, theirs, made, made_theirs, theirs_wide = refs[24:31]
    in_sem, out_sem, row_sem, row_out_sem = refs[31:]
    depth = taken.shape[0]
    shares = [(unit, core) for unit in range(UNITS) for core in range(2)]
    x = lax.axis_index("narrow")
    chunk = ours.shape[0] // 2

    def fetch(i):
        unit, core = shares[i]
        return pltpu.make_async_copy(sums.at[unit, core], taken.at[i % depth], in_sem.at[i % depth])

    def place(i):
        weight, row, column = output_place(*shares[i])
        return pltpu.make_async_copy(
            given.at[i % depth],
            outs[weight].at[pl.ds(row, TILE), pl.ds(column, TILE)],
            out_sem.at[i % depth],
        )

    pairs_in = ((ours_in, ours), (theirs_in, theirs), (made_in, made), (made_theirs_in, made_theirs))
    rows_in = [pltpu.make_async_copy(a, b, row_sem.at[k]) for k, (a, b) in enumerate(pairs_in)]

    def rows_out(src, dst, which, k, at):
        start = (at if k == 0 else 3 - at) * chunk
        return pltpu.make_async_copy(
            src.at[pl.ds(k * chunk, chunk)],
            dst.at[pl.ds(pl.multiple_of(start, 128), chunk)],
            row_out_sem.at[which, k],
        )

    moves = [
        rows_out(src, dst, which, k, at)
        for which, (src, dst, at) in enumerate(
            (
                (ours, grad_hidden, x),
                (theirs_wide, grad_hidden, 1 - x),
                (made, output, x),
                (made_theirs, output, 1 - x),
            )
        )
        for k in range(2)
    ]
    for i in range(depth - 1):
        fetch(i).start()
    for copy in rows_in:
        copy.start()
    for i in range(6):
        norm_outs[i][...] = norms[i]
    for i in range(len(shares)):
        if i + depth - 1 < len(shares):
            fetch(i + depth - 1).start()
        fetch(i).wait()
        if i >= depth:
            place(i - depth).wait()
        given[i % depth] = taken[i % depth].astype(f32)
        place(i).start()
        if i == depth:
            for copy in rows_in:
                copy.wait()
            theirs_wide[...] = theirs[...].astype(f32)
            for copy in moves:
                copy.start()
    for i in range(len(shares) - depth, len(shares)):
        place(i).wait()
    for copy in moves:
        copy.wait()


def finish(sums, ours, theirs, made, made_theirs, norms):
    rows, width = ours.shape
    shapes = [(2 * TILE, TILE)] * 3 + [(TILE, 2 * TILE)] + [(2 * TILE, TILE)] * 3
    shapes += [(TILE, 2 * TILE), (2 * TILE, 4 * TILE), (4 * TILE, 2 * TILE)]
    depth = 6
    anywhere = pl.BlockSpec(memory_space=pl.ANY)
    vmem = pl.BlockSpec(memory_space=pltpu.VMEM)
    return tuple(
        pl.pallas_call(
            finish_kernel,
            out_shape=[
                jax.ShapeDtypeStruct((2 * rows, width), bf16),
                jax.ShapeDtypeStruct((2 * rows, width), f32),
            ]
            + [jax.ShapeDtypeStruct(shape, f32) for shape in shapes]
            + [jax.ShapeDtypeStruct((width,), f32)] * 6,
            in_specs=[anywhere] * 5 + [vmem],
            out_specs=[anywhere] * 12 + [vmem] * 6,
            scratch_shapes=[
                pltpu.VMEM((depth, TILE, TILE), bf16),
                pltpu.VMEM((depth, TILE, TILE), f32),
                pltpu.VMEM((rows, width), f32),
                pltpu.VMEM((rows, width), bf16),
                pltpu.VMEM((rows, width), bf16),
                pltpu.VMEM((rows, width), bf16),
                pltpu.VMEM((rows, width), f32),
                pltpu.SemaphoreType.DMA((depth,)),
                pltpu.SemaphoreType.DMA((depth,)),
                pltpu.SemaphoreType.DMA((4,)),
                pltpu.SemaphoreType.DMA((4, 2)),
            ],
            compiler_params=pltpu.CompilerParams(vmem_limit_bytes=VMEM_LIMIT),
            name="finish",
        )(sums, ours, theirs, made, made_theirs, norms)
    )


FF_COLUMNS = 1024


def layer_norm(summed, norm_gain, norm_shift):
    centred = summed - jnp.mean(summed, axis=-1, keepdims=True)
    inverse = lax.rsqrt(jnp.mean(centred * centred, axis=-1, keepdims=True) + epsilon)
    normal = centred * inverse
    return normal * norm_gain + norm_shift, normal, inverse


def dense_kernel(
    a_cross, first, cotangent, cross_out, gain_two, shift_two, gain_three, shift_three, expand_in, reduce_in,
    out_ref, g_second, g_across, cross_out_grad, norms, expand_grad, reduce_grad, made_out,
    expand, reduce, activated, slope, expand_staged, reduce_staged,
    expand_sem, reduce_sem, expand_out_sem, reduce_out_sem, made_send, made_recv,
):
    me = Place()
    across = me.at(x=1 - me.x)
    gain_two, shift_two = as_row(gain_two), as_row(shift_two)
    gain_three, shift_three = as_row(gain_three), as_row(shift_three)
    chunk = cotangent.shape[0] // 4
    count = expand.shape[1] // FF_COLUMNS

    def piece(c):
        return pl.ds(c * FF_COLUMNS, FF_COLUMNS)

    def fetch_expand(c):
        return pltpu.make_async_copy(
            expand_in.at[:, piece(c)], expand.at[:, piece(c)], expand_sem.at[c]
        )

    def fetch_reduce(c):
        return pltpu.make_async_copy(reduce_in.at[piece(c)], reduce.at[piece(c)], reduce_sem.at[c])

    def put_expand(c):
        return pltpu.make_async_copy(
            expand_staged.at[c % 2], expand_grad.at[:, piece(c)], expand_out_sem.at[c % 2]
        )

    def put_reduce(c):
        return pltpu.make_async_copy(
            reduce_staged.at[c % 2], reduce_grad.at[piece(c)], reduce_out_sem.at[c % 2]
        )

    for c in range(count):
        fetch_expand(c).start()
        fetch_reduce(c).start()
    barrier = pltpu.get_barrier_semaphore()
    pl.semaphore_signal(barrier, inc=1, device_id=across, device_id_type=MESH)
    second, normal_two, inverse_two = layer_norm(
        first[...] + dot_nn(a_cross[...], cross_out[...]), gain_two, shift_two
    )
    second_low = second.astype(bf16)
    total = second
    for c in range(count):
        fetch_expand(c).wait()
        pre = dot_nn(second_low, expand[:, piece(c)])
        phi = 0.5 * (1.0 + lax.erf(pre * 0.7071067811865476))
        slope[:, piece(c)] = phi + pre * jnp.exp(-0.5 * pre * pre) * 0.3989422804014327
        activated[:, piece(c)] = (pre * phi).astype(bf16)
        fetch_reduce(c).wait()
        total = total + dot_nn(activated[:, piece(c)], reduce[piece(c)])
    final, normal, inverse = layer_norm(total, gain_three, shift_three)
    out_ref[...] = final.astype(bf16)
    pl.semaphore_wait(barrier, 1)
    made_copy = pltpu.make_async_remote_copy(
        src_ref=out_ref, dst_ref=made_out, send_sem=made_send, recv_sem=made_recv,
        device_id=across, device_id_type=MESH,
    )
    made_copy.start()
    grad = jnp.concatenate(
        [
            cotangent[pl.ds(pl.multiple_of(me.x * chunk, 128), chunk)],
            cotangent[pl.ds(pl.multiple_of((3 - me.x) * chunk, 128), chunk)],
        ],
        axis=0,
    ).astype(f32)
    norms[...] = jnp.zeros_like(norms)

    def back(grad, normal, inverse, gain, row):
        norms[pl.ds(row, 1)] = jnp.sum(grad * normal, axis=0, keepdims=True)
        norms[pl.ds(row + 1, 1)] = jnp.sum(grad, axis=0, keepdims=True)
        scaled = grad * gain
        return inverse * (
            scaled
            - jnp.mean(scaled, axis=-1, keepdims=True)
            - normal * jnp.mean(scaled * normal, axis=-1, keepdims=True)
        )

    grad = back(grad, normal, inverse, gain_three, 4)
    grad_low = grad.astype(bf16)
    for c in range(count):
        if c >= 2:
            put_reduce(c - 2).wait()
            put_expand(c - 2).wait()
        reduce_staged[c % 2] = dot_tn(activated[:, piece(c)], grad_low).astype(bf16)
        put_reduce(c).start()
        grad_pre = (dot_nt(grad_low, reduce[piece(c)]) * slope[:, piece(c)]).astype(bf16)
        expand_staged[c % 2] = dot_tn(second_low, grad_pre).astype(bf16)
        put_expand(c).start()
        grad = grad + dot_nt(grad_pre, expand[:, piece(c)])
    grad = back(grad, normal_two, inverse_two, gain_two, 2)
    g_second[...] = grad
    grad_low = grad.astype(bf16)
    cross_out_grad[...] = dot_tn(a_cross[...], grad_low).astype(bf16)
    g_across[...] = dot_nt(grad_low, cross_out[...]).astype(bf16)
    for c in range(count - 2, count):
        put_reduce(c).wait()
        put_expand(c).wait()
    made_copy.wait()


def dense_by_kernel(a_cross, first, cotangent, cross_out, norm_params, expand, reduce):
    rows, width = first.shape
    hidden_units = expand.shape[1]
    count = hidden_units // FF_COLUMNS
    anywhere = pl.BlockSpec(memory_space=pl.ANY)
    vmem = pl.BlockSpec(memory_space=pltpu.VMEM)
    dma = pltpu.SemaphoreType.DMA
    return pl.pallas_call(
        dense_kernel,
        out_shape=[
            jax.ShapeDtypeStruct((rows, width), bf16),
            jax.ShapeDtypeStruct((rows, width), f32),
            jax.ShapeDtypeStruct((rows, width), bf16),
            jax.ShapeDtypeStruct((width, width), bf16),
            jax.ShapeDtypeStruct((8, width), f32),
            jax.ShapeDtypeStruct(expand.shape, bf16),
            jax.ShapeDtypeStruct(reduce.shape, bf16),
            jax.ShapeDtypeStruct((rows, width), bf16),
        ],
        in_specs=[vmem] * 8 + [anywhere] * 2,
        out_specs=[vmem] * 5 + [anywhere] * 3,
        scratch_shapes=[
            pltpu.VMEM(expand.shape, bf16),
            pltpu.VMEM(reduce.shape, bf16),
            pltpu.VMEM((rows, hidden_units), bf16),
            pltpu.VMEM((rows, hidden_units), f32),
            pltpu.VMEM((2, width, FF_COLUMNS), bf16),
            pltpu.VMEM((2, FF_COLUMNS, width), bf16),
            dma((count,)),
            dma((count,)),
            dma((2,)),
            dma((2,)),
            dma,
            dma,
        ],
        compiler_params=pltpu.CompilerParams(
            collective_id=2, has_side_effects=True, vmem_limit_bytes=VMEM_LIMIT
        ),
        name="dense",
    )(a_cross, first, cotangent, cross_out, *norm_params, expand, reduce)


def by_kernels(narrow):
    return lax.axis_size("wide") == 4 * LINE and narrow == 2


def gather_all(encoded, weights):
    everything = lax.all_gather(encoded, "wide", tiled=True)
    full = tuple(
        lax.all_gather(w, "narrow", axis=1 if i in COLUMNS else 0, tiled=True)
        for i, w in enumerate(weights)
    )
    return everything, full


def reduce_all(grads):
    shares = tuple(
        lax.psum_scatter(
            g.astype(bf16), "narrow", scatter_dimension=1 if i in COLUMNS else 0, tiled=True
        )
        for i, g in enumerate(grads)
    )
    return tuple(s.astype(f32) for s in lax.psum(shares, "wide"))


def local(
    hidden,
    encoded,
    retrieved,
    self_query,
    self_key,
    self_value,
    self_out,
    cross_query,
    cross_key,
    cross_value,
    cross_out,
    expand_weight,
    reduce_weight,
    first_gain,
    first_shift,
    second_gain,
    second_shift,
    third_gain,
    third_shift,
    cotangent,
):
    tok_rows, width = hidden.shape
    narrow = lax.axis_size("narrow")
    at = lax.axis_index("narrow").astype(jnp.int32)
    chunk = tok_rows // (2 * narrow)

    def own(rows, size=chunk):
        low = lax.dynamic_slice_in_dim(rows, at * size, size)
        high = lax.dynamic_slice_in_dim(rows, (2 * narrow - 1 - at) * size, size)
        return jnp.concatenate([low, high], axis=0)

    where_at = at.reshape(1)
    picked = own(retrieved, chunk // BLOCK_ROWS).reshape(-1)
    if by_kernels(narrow):
        everything, full, kept = forward_by_kernel(
            encoded,
            (
                self_query,
                self_key,
                self_value,
                self_out,
                cross_query,
                cross_key,
                cross_value,
                cross_out,
                expand_weight,
                reduce_weight,
            ),
            hidden,
            first_gain,
            first_shift,
        )
        query_self, key_self, value_self, blend_self, first, first_normal, first_low = kept[:7]
        query_cross, log_self, first_inverse = kept[7:]
        (self_query, self_key, self_value, self_out, cross_query, cross_key, cross_value) = full[:7]
        (cross_out, expand_weight, reduce_weight) = full[7:]
        blend_cross, log_cross, key_cross, value_cross, picked_rows = cross_forward(
            picked, everything, cross_key, cross_value, query_cross
        )
        made = dense_by_kernel(
            blend_cross,
            first,
            cotangent,
            cross_out,
            (second_gain, second_shift, third_gain, third_shift),
            expand_weight,
            reduce_weight,
        )
        output, grad_second_in, grad_blend_cross, cross_out_grad, norms = made[:5]
        expand_grad, reduce_grad, made_theirs = made[5:]
        sums, grad_mine, grad_theirs, norm_sums = backward_by_kernel(
            expand_grad,
            reduce_grad,
            cross_out_grad,
            picked_rows,
            key_cross,
            value_cross,
            query_cross,
            blend_cross,
            grad_blend_cross,
            log_cross,
            first_low,
            cross_query,
            grad_second_in,
            first_normal,
            first_inverse,
            first_gain,
            blend_self,
            self_out,
            query_self,
            key_self,
            value_self,
            log_self,
            hidden,
            self_query,
            self_key,
            self_value,
            norms,
        )

        return finish(sums, grad_mine, grad_theirs, output, made_theirs, norm_sums)

    everything, full = gather_all(
        encoded,
        (
            self_query,
            self_key,
            self_value,
            self_out,
            cross_query,
            cross_key,
            cross_value,
            cross_out,
            expand_weight,
            reduce_weight,
        ),
    )
    (
        self_query,
        self_key,
        self_value,
        self_out,
        cross_query,
        cross_key,
        cross_value,
        cross_out,
        expand_weight,
        reduce_weight,
    ) = full
    mine = own(hidden)
    grad_final = own(cotangent).astype(f32)

    query_self = project(mine, self_query).astype(bf16)
    key_self = project(hidden, self_key).astype(bf16)
    value_self = project(hidden, self_value).astype(bf16)
    blend_self, log_self = self_forward(narrow, where_at, query_self, key_self, value_self)
    first, first_normal, first_inverse = norm_forward(
        mine.astype(f32) + project(blend_self, self_out), first_gain, first_shift
    )
    first_low = first.astype(bf16)
    query_cross = project(first_low, cross_query).astype(bf16)
    blend_cross, log_cross, key_cross, value_cross, picked_rows = cross_forward(
        picked, everything, cross_key, cross_value, query_cross
    )
    second, second_normal, second_inverse = norm_forward(
        first + project(blend_cross, cross_out), second_gain, second_shift
    )
    second_low = second.astype(bf16)
    pre_act = project(second_low, expand_weight)
    activated = jax.nn.gelu(pre_act, approximate=False).astype(bf16)
    final, third_normal, third_inverse = norm_forward(
        second + project(activated, reduce_weight), third_gain, third_shift
    )
    output = final.astype(bf16)

    grad_third, third_gain_grad, third_shift_grad = norm_backward(
        grad_final, third_normal, third_inverse, third_gain
    )
    grad_ffn = grad_third.astype(bf16)
    reduce_grad = grad_weight(activated, grad_ffn)
    grad_pre = (grad_input(grad_ffn, reduce_weight) * gelu_slope(pre_act)).astype(bf16)
    expand_grad = grad_weight(second_low, grad_pre)
    grad_second = grad_third + grad_input(grad_pre, expand_weight)
    grad_second_in, second_gain_grad, second_shift_grad = norm_backward(
        grad_second, second_normal, second_inverse, second_gain
    )
    grad_cross = grad_second_in.astype(bf16)
    cross_out_grad = grad_weight(blend_cross, grad_cross)
    grad_blend_cross = grad_input(grad_cross, cross_out).astype(bf16)
    grad_query_cross, cross_key_grad, cross_value_grad = cross_backward(
        picked,
        everything,
        key_cross,
        value_cross,
        query_cross,
        log_cross,
        blend_cross,
        grad_blend_cross,
    )
    cross_query_grad = grad_weight(first_low, grad_query_cross)
    grad_first = grad_second_in + grad_input(grad_query_cross, cross_query)
    grad_first_in, first_gain_grad, first_shift_grad = norm_backward(
        grad_first, first_normal, first_inverse, first_gain
    )
    grad_self = grad_first_in.astype(bf16)
    self_out_grad = grad_weight(blend_self, grad_self)
    grad_blend_self = grad_input(grad_self, self_out).astype(bf16)
    grad_query_self, grad_key_self, grad_value_self = self_backward(
        narrow, where_at, query_self, key_self, value_self, log_self, blend_self, grad_blend_self
    )
    self_query_grad = grad_weight(mine, grad_query_self)
    self_key_grad = grad_weight(hidden, grad_key_self)
    self_value_grad = grad_weight(hidden, grad_value_self)
    grad_rows = grad_input(grad_key_self, self_key) + grad_input(grad_value_self, self_value)
    grad_own = grad_first_in + grad_input(grad_query_self, self_query)

    def spread(rows):
        empty = jnp.zeros((tok_rows, width), rows.dtype)
        placed = lax.dynamic_update_slice_in_dim(empty, rows[:chunk], at * chunk, 0)
        return lax.dynamic_update_slice_in_dim(
            placed, rows[chunk:], (2 * narrow - 1 - at) * chunk, 0
        )

    grad_hidden = lax.psum((grad_rows + spread(grad_own)).astype(bf16), "narrow").astype(f32)
    output = lax.psum(spread(output), "narrow")
    weight_grads = reduce_all(
        (
            self_query_grad,
            self_key_grad,
            self_value_grad,
            self_out_grad,
            cross_query_grad,
            cross_key_grad,
            cross_value_grad,
            cross_out_grad,
            expand_grad,
            reduce_grad,
        )
    )
    norm_grads = lax.psum(
        jnp.stack(
            [
                first_gain_grad,
                first_shift_grad,
                second_gain_grad,
                second_shift_grad,
                third_gain_grad,
                third_shift_grad,
            ]
        ),
        ("wide", "narrow"),
    )
    return (output, grad_hidden) + weight_grads + tuple(norm_grads[i] for i in range(6))


def solution(mesh):
    rows = P("wide", None)
    columns_split = P(None, "narrow")
    rows_split = P("narrow", None)
    weights = (columns_split,) * 3 + (rows_split,) + (columns_split,) * 3 + (rows_split,)
    weights += (columns_split, rows_split)
    return jax.shard_map(
        local,
        mesh=mesh,
        in_specs=(rows, rows, rows) + weights + (P(),) * 6 + (rows,),
        out_specs=(rows, rows) + weights + (P(),) * 6,
        check_vma=False,
    )
```

```python
import functools

import jax
import jax.numpy as jnp
from jax import lax
from jax.experimental import pallas as pl
from jax.experimental.pallas import tpu as pltpu
from jax.sharding import PartitionSpec as P

HEAD_DIM = 64
BLOCK_ROWS = 128
RET_BLOCKS = 8
PAIR = 2 * HEAD_DIM
VMEM_LIMIT = 60 << 20
BACKWARD_VMEM = 63 << 20

epsilon = 1e-05
bf16 = jnp.bfloat16
f32 = jnp.float32
MESH = pl.DeviceIdType.MESH


def norm_forward(summed, norm_gain, norm_shift):
    average = jnp.mean(summed, axis=-1, keepdims=True)
    centred = summed - average
    inverse = lax.rsqrt(jnp.mean(centred * centred, axis=-1, keepdims=True) + epsilon)
    normal = centred * inverse
    return (normal * norm_gain + norm_shift, normal, inverse)


def norm_backward(grad_out, normal, inverse, norm_gain):
    scaled = grad_out * norm_gain
    grad_in = inverse * (
        scaled
        - jnp.mean(scaled, axis=-1, keepdims=True)
        - normal * jnp.mean(scaled * normal, axis=-1, keepdims=True)
    )
    return (grad_in, jnp.sum(grad_out * normal, axis=0), jnp.sum(grad_out, axis=0))


def gelu_slope(pre_act):
    return (
        0.5 * (1.0 + lax.erf(pre_act * 0.7071067811865476))
        + pre_act * jnp.exp(-0.5 * pre_act * pre_act) * 0.3989422804014327
    )


def project(rows_in, weight):
    return jnp.dot(rows_in, weight, preferred_element_type=f32)


def grad_weight(left, right):
    return jnp.einsum("ti,to->io", left, right, preferred_element_type=f32)


def grad_input(grad_rows, weight):
    return jnp.einsum("to,io->ti", grad_rows, weight, preferred_element_type=f32)


def dot_nt(left, right):
    return lax.dot_general(left, right, (((1,), (1,)), ((), ())), preferred_element_type=f32)


def dot_tn(left, right):
    return lax.dot_general(left, right, (((0,), (0,)), ((), ())), preferred_element_type=f32)


def dot_nn(left, right):
    return lax.dot_general(left, right, (((1,), (0,)), ((), ())), preferred_element_type=f32)


def stack_heads(pair_rows):
    lane = lax.broadcasted_iota(jnp.int32, pair_rows.shape, 1)
    wide_rows = pair_rows.astype(f32)
    zero = jnp.zeros_like(wide_rows)
    return jnp.concatenate(
        [
            jnp.where(lane < HEAD_DIM, wide_rows, zero).astype(bf16),
            jnp.where(lane < HEAD_DIM, zero, wide_rows).astype(bf16),
        ],
        axis=0,
    )


def merge_heads(both):
    rows = both.shape[1] // 2
    sublane = lax.broadcasted_iota(jnp.int32, (PAIR, rows), 0)
    return jnp.transpose(jnp.where(sublane < HEAD_DIM, both[:, :rows], both[:, rows:]))


def causal_edge(rows):
    key = lax.broadcasted_iota(jnp.int32, (rows, 2 * rows), 0)
    query = lax.broadcasted_iota(jnp.int32, (rows, 2 * rows), 1)
    return key <= jnp.where(query >= rows, query - rows, query)


def scaled_heads(pair_rows):
    return stack_heads(pair_rows.astype(f32) * HEAD_DIM**-0.5)


KEY_ROWS = 128


def scores_of(keys, stacked, start, edge):
    part = dot_nt(keys[start : start + KEY_ROWS], stacked)
    if edge is not None and start + KEY_ROWS == keys.shape[0]:
        part = jnp.where(edge, part, -1e30)
    return part


def by_rows(part, reduce):
    return reduce(part.reshape(KEY_ROWS // 8, 8, part.shape[1]), axis=0)


def pair_forward(queries, keys, values, edge):
    stacked = scaled_heads(queries)
    starts = range(0, keys.shape[0], KEY_ROWS)
    scores = [scores_of(keys, stacked, start, edge) for start in starts]
    top = by_rows(scores[0], jnp.max)
    for part in scores[1:]:
        top = jnp.maximum(top, by_rows(part, jnp.max))
    top = jnp.max(top, axis=0, keepdims=True)
    total, blended = 0.0, 0.0
    for start, part in zip(starts, scores):
        raised = jnp.exp(part - top)
        total = total + by_rows(raised, jnp.sum)
        blended = blended + dot_tn(values[start : start + KEY_ROWS], raised.astype(bf16))
    total = jnp.sum(total, axis=0, keepdims=True)
    return merge_heads(blended / total).astype(bf16), top + jnp.log(total)


def pair_backward(queries, keys, values, edge, log_total, blended, grad_blend):
    rows = queries.shape[0]
    stacked = scaled_heads(queries)
    grads = stack_heads(grad_blend)
    scores = dot_nt(keys, stacked)
    if edge is not None:
        split = keys.shape[0] - edge.shape[0]
        last = jnp.where(edge, scores[split:], -1e30)
        scores = jnp.concatenate([scores[:split], last], axis=0) if split else last
    chances = jnp.exp(scores - log_total)
    weighed = jnp.transpose(blended.astype(f32) * grad_blend.astype(f32))
    centre = jnp.concatenate(
        [
            jnp.sum(weighed[:HEAD_DIM], axis=0, keepdims=True),
            jnp.sum(weighed[HEAD_DIM:], axis=0, keepdims=True),
        ],
        axis=1,
    )
    grad_scores = (chances * (dot_nt(values, grads) - centre)).astype(bf16)
    grad_values = dot_nn(chances.astype(bf16), grads)
    grad_keys = dot_nn(grad_scores, stacked)
    grad_queries = merge_heads(dot_tn(keys, grad_scores)) * HEAD_DIM**-0.5
    return grad_queries, grad_keys, grad_values


def self_blocks(narrow, total_rows, at):
    chunk = total_rows // (2 * narrow)
    for block in range(total_rows // BLOCK_ROWS):
        which, within = divmod(block * BLOCK_ROWS, chunk)
        if which < narrow:
            owner, local_row = which, within
        else:
            owner, local_row = 2 * narrow - 1 - which, chunk + within
        yield local_row, (block + 1) * BLOCK_ROWS, at == owner


def self_forward_kernel(narrow, at_ref, q_ref, k_ref, v_ref, o_ref, log_ref):
    for local_row, seen, taken in self_blocks(narrow, k_ref.shape[0], at_ref[0]):

        @pl.when(taken)
        def _():
            mine = pl.ds(local_row, BLOCK_ROWS)
            keys = pl.ds(0, seen)
            blended, log_total = pair_forward(
                q_ref[mine], k_ref[keys], v_ref[keys], causal_edge(BLOCK_ROWS)
            )
            o_ref[mine] = blended
            log_ref[0, pl.ds(local_row // BLOCK_ROWS, 1)] = log_total


def self_forward(narrow, at, queries, keys, values):
    rows, width = queries.shape
    total_rows = keys.shape[0]
    pairs = width // PAIR
    pair = lambda count: pl.BlockSpec((count, PAIR), lambda g, at: (0, g))
    return pl.pallas_call(
        functools.partial(self_forward_kernel, narrow),
        grid_spec=pltpu.PrefetchScalarGridSpec(
            num_scalar_prefetch=1,
            grid=(pairs,),
            in_specs=[pair(rows), pair(total_rows), pair(total_rows)],
            out_specs=[pair(rows), pl.BlockSpec((1, rows // BLOCK_ROWS, 2 * BLOCK_ROWS), lambda g, at: (g, 0, 0))],
        ),
        out_shape=[
            jax.ShapeDtypeStruct((rows, width), bf16),
            jax.ShapeDtypeStruct((pairs, rows // BLOCK_ROWS, 2 * BLOCK_ROWS), f32),
        ],
        compiler_params=pltpu.CompilerParams(vmem_limit_bytes=VMEM_LIMIT),
        name="self_forward",
    )(at, queries, keys, values)


def self_backward_kernel(
    narrow, at_ref, q_ref, k_ref, v_ref, log_ref, o_ref, g_ref, dq_ref, dk_ref, dv_ref, dk_sum, dv_sum
):
    rows = q_ref.shape[0] // 2
    dk_sum[...] = jnp.zeros_like(dk_sum)
    dv_sum[...] = jnp.zeros_like(dv_sum)
    for local_row, seen, taken in self_blocks(narrow, k_ref.shape[0], at_ref[0]):

        @pl.when(taken)
        def _():
            mine = pl.ds(local_row, BLOCK_ROWS)
            keys = pl.ds(0, seen)
            grad_q, grad_k, grad_v = pair_backward(
                q_ref[mine],
                k_ref[keys],
                v_ref[keys],
                causal_edge(BLOCK_ROWS),
                log_ref[0, pl.ds(local_row // BLOCK_ROWS, 1)],
                o_ref[mine],
                g_ref[mine],
            )
            dq_ref[mine] = grad_q.astype(bf16)
            dk_sum[keys] += grad_k
            dv_sum[keys] += grad_v

    dk_ref[...] = dk_sum[...].astype(bf16)
    dv_ref[...] = dv_sum[...].astype(bf16)


def self_backward(narrow, at, queries, keys, values, logs, blended, grads):
    rows, width = queries.shape
    total_rows = keys.shape[0]
    pairs = width // PAIR
    pair = lambda count: pl.BlockSpec((count, PAIR), lambda g, at: (0, g))
    return pl.pallas_call(
        functools.partial(self_backward_kernel, narrow),
        grid_spec=pltpu.PrefetchScalarGridSpec(
            num_scalar_prefetch=1,
            grid=(pairs,),
            in_specs=[
                pair(rows),
                pair(total_rows),
                pair(total_rows),
                pl.BlockSpec((1, rows // BLOCK_ROWS, 2 * BLOCK_ROWS), lambda g, at: (g, 0, 0)),
                pair(rows),
                pair(rows),
            ],
            out_specs=[pair(rows), pair(total_rows), pair(total_rows)],
            scratch_shapes=[pltpu.VMEM((total_rows, PAIR), f32)] * 2,
        ),
        out_shape=[
            jax.ShapeDtypeStruct((rows, width), bf16),
            jax.ShapeDtypeStruct((total_rows, width), bf16),
            jax.ShapeDtypeStruct((total_rows, width), bf16),
        ],
        compiler_params=pltpu.CompilerParams(vmem_limit_bytes=VMEM_LIMIT),
        name="self_backward",
    )(at, queries, keys, values, logs, blended, grads)


def cross_forward_kernel(picked_ref, *refs):
    blocks = refs[:RET_BLOCKS]
    wk_ref, wv_ref, q_ref, o_ref, log_ref, k_ref, v_ref, rows_in = refs[RET_BLOCKS:]
    for j in range(RET_BLOCKS):
        rows_in[pl.ds(j * BLOCK_ROWS, BLOCK_ROWS)] = blocks[j][...]
    k_ref[...] = dot_nn(rows_in[...], wk_ref[...]).astype(bf16)
    v_ref[...] = dot_nn(rows_in[...], wv_ref[...]).astype(bf16)
    for g in range(q_ref.shape[1] // PAIR):
        lanes = pl.ds(g * PAIR, PAIR)
        blended, log_total = pair_forward(q_ref[:, lanes], k_ref[:, lanes], v_ref[:, lanes], None)
        o_ref[:, lanes] = blended
        log_ref[0, pl.ds(g, 1)] = log_total


def block_specs(width):
    def spec(j):
        return pl.BlockSpec((BLOCK_ROWS, width), lambda b, picked: (picked[b * RET_BLOCKS + j], 0))

    return [spec(j) for j in range(RET_BLOCKS)]


def cross_forward(picked, everything, cross_key, cross_value, queries):
    rows, width = queries.shape
    count = rows // BLOCK_ROWS
    pairs = width // PAIR
    keys = RET_BLOCKS * BLOCK_ROWS
    whole = pl.BlockSpec((width, width), lambda b, picked: (0, 0))
    by_block = pl.BlockSpec((BLOCK_ROWS, width), lambda b, picked: (b, 0))
    by_keys = pl.BlockSpec((keys, width), lambda b, picked: (b, 0))
    return pl.pallas_call(
        cross_forward_kernel,
        grid_spec=pltpu.PrefetchScalarGridSpec(
            num_scalar_prefetch=1,
            grid=(count,),
            in_specs=block_specs(width) + [whole, whole, by_block],
            out_specs=[
                by_block,
                pl.BlockSpec((1, pairs, 2 * BLOCK_ROWS), lambda b, picked: (b, 0, 0)),
                by_keys,
                by_keys,
                by_keys,
            ],
        ),
        out_shape=[
            jax.ShapeDtypeStruct((rows, width), bf16),
            jax.ShapeDtypeStruct((count, pairs, 2 * BLOCK_ROWS), f32),
            jax.ShapeDtypeStruct((count * keys, width), bf16),
            jax.ShapeDtypeStruct((count * keys, width), bf16),
            jax.ShapeDtypeStruct((count * keys, width), bf16),
        ],
        compiler_params=pltpu.CompilerParams(vmem_limit_bytes=VMEM_LIMIT),
        name="cross_forward",
    )(picked, *([everything] * RET_BLOCKS), cross_key, cross_value, queries)


def cross_backward_kernel(picked_ref, *refs):
    blocks = refs[:RET_BLOCKS]
    (k_ref, v_ref, q_ref, log_ref, o_ref, g_ref, dq_ref, dwk_ref, dwv_ref, rows_in, both, sums) = refs[
        RET_BLOCKS:
    ]
    width = q_ref.shape[1]
    step = pl.program_id(0)

    @pl.when(step == 0)
    def _():
        sums[...] = jnp.zeros_like(sums)

    for j in range(RET_BLOCKS):
        rows_in[pl.ds(j * BLOCK_ROWS, BLOCK_ROWS)] = blocks[j][...]
    for g in range(width // PAIR):
        lanes = pl.ds(g * PAIR, PAIR)
        grad_q, grad_k, grad_v = pair_backward(
            q_ref[:, lanes],
            k_ref[:, lanes],
            v_ref[:, lanes],
            None,
            log_ref[0, pl.ds(g, 1)],
            o_ref[:, lanes],
            g_ref[:, lanes],
        )
        dq_ref[:, lanes] = grad_q.astype(bf16)
        both[:, lanes] = grad_k.astype(bf16)
        both[:, pl.ds(width + g * PAIR, PAIR)] = grad_v.astype(bf16)
    sums[...] += dot_tn(rows_in[...], both[...])

    @pl.when(step == pl.num_programs(0) - 1)
    def _():
        dwk_ref[...] = sums[:, :width].astype(bf16)
        dwv_ref[...] = sums[:, width:].astype(bf16)


def cross_backward(picked, everything, keys_in, values_in, queries, logs, blended, grads):
    rows, width = queries.shape
    count = rows // BLOCK_ROWS
    pairs = width // PAIR
    keys = RET_BLOCKS * BLOCK_ROWS
    whole = pl.BlockSpec((width, width), lambda b, picked: (0, 0))
    by_block = pl.BlockSpec((BLOCK_ROWS, width), lambda b, picked: (b, 0))
    by_keys = pl.BlockSpec((keys, width), lambda b, picked: (b, 0))
    return pl.pallas_call(
        cross_backward_kernel,
        grid_spec=pltpu.PrefetchScalarGridSpec(
            num_scalar_prefetch=1,
            grid=(count,),
            in_specs=block_specs(width)
            + [
                by_keys,
                by_keys,
                by_block,
                pl.BlockSpec((1, pairs, 2 * BLOCK_ROWS), lambda b, picked: (b, 0, 0)),
                by_block,
                by_block,
            ],
            out_specs=[by_block, whole, whole],
            scratch_shapes=[
                pltpu.VMEM((keys, width), bf16),
                pltpu.VMEM((keys, 2 * width), bf16),
                pltpu.VMEM((width, 2 * width), f32),
            ],
        ),
        out_shape=[
            jax.ShapeDtypeStruct((rows, width), bf16),
            jax.ShapeDtypeStruct((width, width), bf16),
            jax.ShapeDtypeStruct((width, width), bf16),
        ],
        compiler_params=pltpu.CompilerParams(vmem_limit_bytes=VMEM_LIMIT),
        name="cross_backward",
    )(
        picked,
        *([everything] * RET_BLOCKS),
        keys_in,
        values_in,
        queries,
        logs,
        blended,
        grads,
    )


COLUMNS = (0, 1, 2, 4, 5, 6, 8)


LINE = 4
HELD = 5


def as_row(ref):
    return ref[...].reshape(1, ref.shape[0])


class Place:
    def __init__(self):
        wide = lax.axis_index("wide")
        self.x = lax.axis_index("narrow")
        self.core = lax.rem(wide, 2)
        self.y = lax.rem(lax.div(wide, 2), 2)
        self.z = lax.div(wide, 4)
        self.wide = wide

    def at(self, z=None, y=None, core=None, x=None):
        z, y = (self.z if z is None else z), (self.y if y is None else y)
        core = self.core if core is None else core
        return (z * 4 + y * 2 + core, self.x if x is None else x)

    def greet(self):
        barrier = pltpu.get_barrier_semaphore()
        targets = [self.at(core=1 - self.core), self.at(y=1 - self.y), self.at(x=1 - self.x)]
        targets += [self.at(z=lax.rem(self.z + step, LINE)) for step in range(1, LINE)]
        for target in targets:
            pl.semaphore_signal(barrier, inc=1, device_id=target, device_id_type=MESH)
        pl.semaphore_wait(barrier, len(targets))


def forward_kernel(a_rows, b_rows, *refs):
    encoded_in, weights_in = refs[0], refs[1:11]
    hidden_in, first_gain, first_shift = refs[11:14]
    everything, full_out = refs[14], refs[15:25]
    kept_out, (log_self, inverse_out) = refs[25:33], refs[33:35]
    encoded, weights, kept = refs[35], refs[36:46], refs[46:54]
    hidden = refs[54]
    load_sem, own_sem, half_sem, kept_sem, flow_send, flow_recv, weight_send, weight_recv = refs[55:]
    q_self, k_self, v_self, a_self, first, first_normal, first_low, q_cross = kept
    full = weights[:HELD] + full_out[HELD:]
    me = Place()
    rows = encoded.shape[0]
    x, y, z, core = me.x, me.y, me.z, me.core
    low, high = z > 0, z < LINE - 1
    UP_A, DOWN_A, Y_A, UP_B, DOWN_B, Y_B, X_B, CORE_A, CORE_B = range(9)

    own = pltpu.make_async_copy(
        encoded, everything.at[pl.ds(pl.multiple_of(me.wide * rows, 128), rows)], own_sem
    )

    def region(i, ref, plane, part):
        if i in COLUMNS:
            count, columns = ref.shape[0], ref.shape[1] // 2
            start = pl.multiple_of(plane * columns, 128)
            if part is None:
                return ref.at[:, pl.ds(start, columns)]
            first = pl.multiple_of(part * (count // 2), 16)
            return ref.at[pl.ds(first, count // 2), pl.ds(start, columns)]
        count = ref.shape[0] // 2
        if part is None:
            return ref.at[pl.ds(pl.multiple_of(plane * count, 16), count)]
        first = pl.multiple_of(plane * count + part * (count // 2), 16)
        return ref.at[pl.ds(first, count // 2)]

    loads, halves = [], []
    for i in range(10):
        into = region(i, weights[i], x, None) if i < HELD else weights[i]
        loads.append(pltpu.make_async_copy(weights_in[i], into, load_sem.at[i]))
        if i < HELD:
            halves.append(pltpu.make_async_copy(weights[i], full_out[i], half_sem.at[i]))
        else:
            halves.append(
                pltpu.make_async_copy(weights[i], region(i, full[i], x, None), half_sem.at[i])
            )
    loads.append(pltpu.make_async_copy(encoded_in, encoded, load_sem.at[10]))
    loads.append(pltpu.make_async_copy(hidden_in, hidden, load_sem.at[11]))
    loads[10].start()
    for i in range(10):
        loads[i].start()
    loads[11].start()
    me.greet()
    loads[10].wait()

    def flow(kind, owner_z, owner_y, plane, target, from_core=None, held=False):
        owner = owner_z * 2 + owner_y
        start = owner * (2 * rows) + (core if from_core is None else from_core) * rows
        if plane is None:
            size, slot = a_rows, owner
        else:
            start = start + a_rows + plane * b_rows
            size, slot = b_rows, owner + (plane * 8 if kind == CORE_B else 0)
        piece = everything.at[pl.ds(pl.multiple_of(start, 16), size)]
        source = piece
        if held:
            first = 0 if plane is None else pl.multiple_of(a_rows + plane * b_rows, 16)
            source = encoded.at[pl.ds(first, size)]
        return pltpu.make_async_remote_copy(
            src_ref=source,
            dst_ref=piece,
            send_sem=flow_send.at[kind, slot],
            recv_sem=flow_recv.at[kind, slot],
            device_id=target,
            device_id_type=MESH,
        )

    sibling = me.at(core=1 - core)
    beside = me.at(y=1 - y)
    across = me.at(x=1 - x)
    above, below = me.at(z=z + 1), me.at(z=z - 1)

    def up_a(oz, held=False):
        return flow(UP_A, oz, y, None, above, held=held)

    def down_a(oz, held=False):
        return flow(DOWN_A, oz, y, None, below, held=held)

    def up_b(oz, oy, held=False):
        return flow(UP_B, oz, oy, x, above, held=held)

    def down_b(oz, oy, held=False):
        return flow(DOWN_B, oz, oy, x, below, held=held)

    def y_a(oz, oy, held=False):
        return flow(Y_A, oz, oy, None, beside, held=held)

    def y_b(oy, held=False):
        return flow(Y_B, z, oy, x, beside, held=held)

    def x_b(oz, oy, plane):
        return flow(X_B, oz, oy, plane, across)

    def core_a(oz, oy, from_core=None, held=False):
        return flow(CORE_A, oz, oy, None, sibling, from_core, held)

    def core_b(oz, oy, plane, from_core=None, held=False):
        return flow(CORE_B, oz, oy, plane, sibling, from_core, held)

    def weight(way, i, plane, part):
        piece = region(i, full[i], plane, part)
        if way == 0 and i >= HELD:
            piece_in = weights[i]
            count = piece_in.shape[0] // 2
            piece_in = piece_in.at[pl.ds(pl.multiple_of(part * count, 16), count)]
        else:
            piece_in = piece
        return pltpu.make_async_remote_copy(
            src_ref=piece_in,
            dst_ref=piece,
            send_sem=weight_send.at[way, i],
            recv_sem=weight_recv.at[way, i],
            device_id=across if way == 0 else sibling,
            device_id_type=MESH,
        )

    y_b(y, True).start()
    y_a(z, y, True).start()
    pl.when(high)(lambda: up_a(z, True).start())
    pl.when(low)(lambda: down_a(z, True).start())

    def weights_go(some):
        for i in some:
            weight(0, i, x, core).start()

    def weights_come(some):
        for i in some:
            weight(0, i, 1 - x, core).wait_recv()
            weight(1, i, 1 - x, core).start()

    for i in range(3):
        loads[i].wait()
    weights_go(range(3))
    core_a(z, y, held=True).start()
    core_b(z, y, 0, held=True).start()
    core_b(z, y, 1, held=True).start()
    own.start()
    for i in range(3, 12):
        if i != 10:
            loads[i].wait()
    for i in range(HELD, 10):
        halves[i].start()

    y_b(1 - y).wait_recv()
    core_b(z, 1 - y, x).start()
    weights_come(range(3))
    weights_go(range(3, 8))
    for i in range(3):
        weight(1, i, 1 - x, 1 - core).wait_recv()

    total_rows = hidden.shape[0]
    chunk = total_rows // 4
    mine = (
        pl.ds(pl.multiple_of(x * chunk, 128), chunk),
        pl.ds(pl.multiple_of((3 - x) * chunk, 128), chunk),
    )
    places = (pl.ds(0, chunk), pl.ds(chunk, chunk))
    for piece, place in zip(mine, places):
        q_self[place] = dot_nn(hidden[piece], weights[0][...]).astype(bf16)
    k_self[...] = dot_nn(hidden[...], weights[1][...]).astype(bf16)
    v_self[...] = dot_nn(hidden[...], weights[2][...]).astype(bf16)
    put = [pltpu.make_async_copy(kept[i], kept_out[i], kept_sem.at[i]) for i in range(8)]
    for i in range(3):
        put[i].start()

    def self_step(g, carry):
        lanes = pl.ds(pl.multiple_of(g * PAIR, PAIR), PAIR)
        for local_row, seen, taken in self_blocks(2, total_rows, x):

            @pl.when(taken)
            def _():
                some = pl.ds(local_row, BLOCK_ROWS)
                blended, log_total = pair_forward(
                    q_self[some, lanes],
                    k_self[pl.ds(0, seen), lanes],
                    v_self[pl.ds(0, seen), lanes],
                    causal_edge(BLOCK_ROWS),
                )
                a_self[some, lanes] = blended
                log_self[g, pl.ds(local_row // BLOCK_ROWS, 1)] = log_total

        return carry

    pairs = q_self.shape[1] // PAIR
    lax.fori_loop(0, pairs // 2, self_step, 0)

    def beside_arrives(oz):
        y_a(oz, 1 - y).wait_recv()
        core_a(oz, 1 - y).start()

    def pass_a(oz, arrived, onward, further):
        arrived(oz).wait_recv()
        pl.when(onward)(lambda: further(oz).start())
        y_a(oz, y).start()
        core_a(oz, y).start()

    def pass_b(oz, arrived, onward, further):
        for oy in (y, 1 - y):
            arrived(oz, oy).wait_recv()
            pl.when(onward)(lambda: further(oz, oy).start())
            x_b(oz, oy, x).start()
            core_b(oz, oy, x).start()

    def step_a(step):
        under, over = z - 1 - step, z + 1 + step
        pl.when(under >= 0)(lambda: pass_a(under, up_a, high, up_a))
        pl.when(over < LINE)(lambda: pass_a(over, down_a, low, down_a))

    def step_b(step):
        under, over = z - 1 - step, z + 1 + step
        pl.when(under >= 0)(lambda: pass_b(under, up_b, high, up_b))
        pl.when(over < LINE)(lambda: pass_b(over, down_b, low, down_b))

    step_a(0)
    for oy, held in ((y, True), (1 - y, False)):
        pl.when(high)(lambda oy=oy, held=held: up_b(z, oy, held).start())
        pl.when(low)(lambda oy=oy, held=held: down_b(z, oy, held).start())
    weights_go(range(8, 10))
    x_b(z, 1 - y, x).start()
    lax.fori_loop(pairs // 2, pairs, self_step, 0)
    put[3].start()
    weights_come(range(3, 5))
    for i in range(3, 5):
        weight(1, i, 1 - x, 1 - core).wait_recv()
    for i in range(HELD):
        halves[i].start()

    for piece, place in zip(mine, places):
        summed = hidden[piece].astype(f32) + dot_nn(a_self[place], weights[3][...])
        centred = summed - jnp.mean(summed, axis=-1, keepdims=True)
        inverse = lax.rsqrt(jnp.mean(centred * centred, axis=-1, keepdims=True) + epsilon)
        normal = centred * inverse
        result = normal * as_row(first_gain) + as_row(first_shift)
        first_normal[place] = normal
        inverse_out[place] = inverse
        first[place] = result
        first_low[place] = result.astype(bf16)
        q_cross[place] = dot_nn(result.astype(bf16), weights[4][...]).astype(bf16)
    for i in range(4, 8):
        put[i].start()

    step_a(1)
    step_b(0)
    step_a(2)
    step_b(1)
    step_b(2)
    weights_come(range(5, 10))
    beside_arrives(z)
    for step in range(1, LINE):
        pl.when(z - step >= 0)(lambda: beside_arrives(z - step))
        pl.when(z + step < LINE)(lambda: beside_arrives(z + step))

    def across_arrives(oz, oy):
        x_b(oz, oy, 1 - x).wait_recv()
        core_b(oz, oy, 1 - x).start()

    across_arrives(z, 1 - y)
    for step in range(LINE - 1):
        under, over = z - 1 - step, z + 1 + step
        for oy in (y, 1 - y):
            pl.when(under >= 0)(lambda: across_arrives(under, oy))
            pl.when(over < LINE)(lambda: across_arrives(over, oy))

    y_b(y).wait_send()
    x_b(z, 1 - y, x).wait_send()
    for oz in range(LINE):
        y_a(oz, y).wait_send()
        for oy in range(2):
            core_a(oz, oy).wait_send()
            core_a(oz, oy, 1 - core).wait_recv()
            for plane in range(2):
                core_b(oz, oy, plane).wait_send()
                core_b(oz, oy, plane, 1 - core).wait_recv()
        away = oz != z

        @pl.when(away)
        def _():
            for oy in range(2):
                x_b(oz, oy, x).wait_send()

        @pl.when(jnp.logical_and(high, oz <= z))
        def _():
            up_a(oz).wait_send()
            for oy in range(2):
                up_b(oz, oy).wait_send()

        @pl.when(jnp.logical_and(low, oz >= z))
        def _():
            down_a(oz).wait_send()
            for oy in range(2):
                down_b(oz, oy).wait_send()

    own.wait()
    for i in range(10):
        halves[i].wait()
        weight(0, i, x, core).wait_send()
        weight(1, i, 1 - x, core).wait_send()
        if i >= HELD:
            weight(1, i, 1 - x, 1 - core).wait_recv()
    for copy in put:
        copy.wait()


def forward_by_kernel(encoded, weights, hidden, first_gain, first_shift):
    rows, width = encoded.shape
    a_rows = rows * 17 // 24 // 16 * 16
    b_rows = (rows - a_rows) // 2
    shapes = [jax.ShapeDtypeStruct((16 * rows, width), bf16)]
    for i, w in enumerate(weights):
        doubled = (w.shape[0], 2 * w.shape[1]) if i in COLUMNS else (2 * w.shape[0], w.shape[1])
        shapes.append(jax.ShapeDtypeStruct(doubled, bf16))
    total_rows = hidden.shape[0]
    mine, pairs = total_rows // 2, width // PAIR
    kept = [(mine, bf16), (total_rows, bf16), (total_rows, bf16), (mine, bf16)]
    kept += [(mine, f32), (mine, f32), (mine, bf16), (mine, bf16)]
    held = [s.shape if i < HELD else w.shape for i, (s, w) in enumerate(zip(shapes[1:], weights))]
    small = [
        jax.ShapeDtypeStruct((pairs, mine // BLOCK_ROWS, 2 * BLOCK_ROWS), f32),
        jax.ShapeDtypeStruct((mine, 1), f32),
    ]
    dma = pltpu.SemaphoreType.DMA
    anywhere = pl.BlockSpec(memory_space=pl.ANY)
    vmem = pl.BlockSpec(memory_space=pltpu.VMEM)
    out = pl.pallas_call(
        functools.partial(forward_kernel, a_rows, b_rows),
        out_shape=shapes + [jax.ShapeDtypeStruct((n, width), dtype) for n, dtype in kept] + small,
        in_specs=[anywhere] * 12 + [vmem] * 2,
        out_specs=[anywhere] * 19 + [vmem] * 2,
        scratch_shapes=[pltpu.VMEM((rows, width), bf16)]
        + [pltpu.VMEM(shape, bf16) for shape in held]
        + [pltpu.VMEM((n, width), dtype) for n, dtype in kept]
        + [pltpu.VMEM((total_rows, width), bf16)]
        + [dma((12,)), dma, dma((10,)), dma((8,))]
        + [dma((9, 16)), dma((9, 16)), dma((2, 10)), dma((2, 10))],
        compiler_params=pltpu.CompilerParams(
            collective_id=0, has_side_effects=True, vmem_limit_bytes=VMEM_LIMIT
        ),
        name="forward",
    )(encoded, *weights, hidden, first_gain, first_shift)
    return out[0], tuple(out[1:11]), tuple(out[11:])


TILE = 384
HALF = TILE // 2
PART = HALF // LINE
UNITS = 16
SLOTS = 12
UNIT_WEIGHTS = (8, 8, 8, 8, 9, 9, 9, 9, 7, 5, 6, 4, 3, 0, 1, 2)
LAST_TICK = UNITS + 11


def share_corner(unit, core, plane):
    if unit < 4:
        return core * TILE, (plane * 4 + unit) * TILE
    if unit < 8:
        return (plane * 4 + unit - 4) * TILE, core * TILE
    if unit in (8, 12):
        return plane * TILE, core * TILE
    return core * TILE, plane * TILE


def backward_kernel(*refs):
    (
        expand_grad, reduce_grad, cross_out_grad, picked_rows, keys_in, values_in, q_cross, a_cross,
        g_cross, log_cross, first_low, cross_query, g_second, first_normal, first_inverse, first_gain,
        a_self, self_out, q_self, k_self, v_self, log_self, hidden, self_query, self_key, self_value,
        norms,
    ) = refs[:27]
    sums_out, mine_out, theirs_out, norms_out = refs[27:31]
    (
        own, from_core, from_a, from_b, from_z, summed, pool, pool32, both, staged, dq_cross, dk_sum,
        dv_sum, theirs, rows_in, rows_got, norm_all, norm_in,
        own_sem, core_send, core_recv, a_send, a_recv, b_send, b_recv, z_send, z_recv, gz_send, gz_recv,
        gy_send, gy_recv, gc_send, gc_recv, keep_sem, load_sem, kv_sem, e_sem, extra_send, extra_recv,
        norm_send, norm_recv,
    ) = refs[31:]
    me = Place()
    x, y, z, core = me.x, me.y, me.z, me.core
    sibling, beside, across = me.at(core=1 - core), me.at(y=1 - y), me.at(x=1 - x)
    width = 2 * TILE
    keys = RET_BLOCKS * BLOCK_ROWS
    rows = q_cross.shape[0]
    blocks = rows // BLOCK_ROWS
    pairs = width // PAIR
    chunk = rows // 2

    def rem(u, n):
        return u % n if isinstance(u, int) else lax.rem(u, n)

    def remote(src, dst, send, recv, target):
        return pltpu.make_async_remote_copy(
            src_ref=src, dst_ref=dst, send_sem=send, recv_sem=recv,
            device_id=target, device_id_type=MESH,
        )


    def share(ref, unit, of_core, plane, part):
        row, column = share_corner(unit, of_core, plane)
        return ref.at[
            pl.ds(pl.multiple_of(row + part * HALF, 64), HALF),
            pl.ds(pl.multiple_of(column, 128), TILE),
        ]

    def own_copy(ref, unit, plane, part):
        return pltpu.make_async_copy(
            share(ref, unit, core, plane, part),
            own.at[unit % SLOTS, plane, part],
            own_sem.at[unit % SLOTS, plane * 2 + part],
        )

    def core_copy(src, u, plane, part):
        return remote(
            src, from_core.at[u, plane, part], core_send.at[u, plane * 2 + part],
            core_recv.at[u, plane * 2 + part], sibling,
        )

    def to_core(ref, unit, plane, part):
        return core_copy(share(ref, unit, 1 - core, plane, part), unit, plane, part)

    def a_first(u, slot):
        return remote(own.at[slot, 1 - x], from_a.at[u], a_send.at[u], a_recv.at[u], across)

    def a_second(u, slot):
        return remote(own.at[slot, :, 1 - y], from_a.at[u], a_send.at[u], a_recv.at[u], beside)

    def b_first(u, slot):
        return remote(own.at[slot, x, 1 - y], from_b.at[u], b_send.at[u], b_recv.at[u], beside)

    def b_second(u, slot):
        return remote(own.at[slot, 1 - x, y], from_b.at[u], b_send.at[u], b_recv.at[u], across)

    def to_z(u, slot, d):
        other = lax.rem(z + d, LINE)
        piece = own.at[slot, x, y, pl.ds(pl.multiple_of(other * PART, 16), PART)]
        return remote(
            piece, from_z.at[u, d - 1], z_send.at[u, d - 1], z_recv.at[u, d - 1], me.at(z=other)
        )

    def result(u, of_z):
        return sums_out.at[u, core, pl.ds(pl.multiple_of(y * HALF + of_z * PART, 16), PART)]

    def keep(u):
        return pltpu.make_async_copy(summed.at[u], result(u, z), keep_sem.at[u])

    def gather_z(u, d):
        return remote(
            summed.at[u], result(u, z), gz_send.at[u, d - 1], gz_recv.at[u, d - 1],
            me.at(z=lax.rem(z + d, LINE)),
        )

    def gathered_z(u, d):
        return remote(
            summed.at[u], result(u, lax.rem(z + LINE - d, LINE)), gz_send.at[u, d - 1],
            gz_recv.at[u, d - 1], beside,
        )

    def gather_y(u, at_y):
        piece = sums_out.at[u, core, pl.ds(pl.multiple_of(at_y * HALF, 16), HALF)]
        return remote(piece, piece, gy_send.at[u], gy_recv.at[u], beside)

    def gather_core(u, at_core):
        piece = sums_out.at[u, at_core]
        return remote(piece, piece, gc_send.at[u], gc_recv.at[u], sibling)

    def plus(a, b):
        return a + b

    def by_order(u, first, second):
        if isinstance(u, int):
            (first if u % 2 == 0 else second)()
        else:
            pl.when(lax.rem(u, 2) == 0)(first)
            pl.when(lax.rem(u, 2) == 1)(second)

    def stage_core(u):
        slot = rem(u, SLOTS)
        early_one = u < len(ready)

        def arrived():
            for plane, part in corners:
                piece = own.at[slot, plane, part]
                pltpu.make_async_copy(piece, piece, own_sem.at[slot, plane * 2 + part]).wait()

        if isinstance(u, int):
            if early_one:
                arrived()
        else:
            pl.when(early_one)(arrived)
        for plane, part in corners:
            core_copy(own.at[slot, plane, part], u, plane, part).wait_recv()
        own[slot] = plus(own[slot], from_core[u])
        by_order(u, lambda: a_first(u, slot).start(), lambda: a_second(u, slot).start())

    def stage_a(u):
        slot = rem(u, SLOTS)

        def first():
            a_first(u, slot).wait()
            own[slot, x] = plus(own[slot, x], from_a[u])
            b_first(u, slot).start()

        def second():
            a_second(u, slot).wait()
            own[slot, :, y] = plus(own[slot, :, y], from_a[u])
            b_second(u, slot).start()

        by_order(u, first, second)

    def stage_b(u):
        slot = rem(u, SLOTS)
        by_order(u, lambda: b_first(u, slot).wait(), lambda: b_second(u, slot).wait())
        own[slot, x, y] = plus(own[slot, x, y], from_b[u])
        for d in range(1, LINE):
            to_z(u, slot, d).start()

    def stage_z(u):
        slot = rem(u, SLOTS)
        for d in range(1, LINE):
            to_z(u, slot, d).wait()
        total = own[slot, x, y, pl.ds(pl.multiple_of(z * PART, 16), PART)].astype(f32)
        for d in range(1, LINE):
            total += from_z[u, d - 1].astype(f32)
        summed[u] = total.astype(bf16)
        keep(u).start()
        for d in range(1, LINE):
            gather_z(u, d).start()

    def stage_gather_z(u):
        keep(u).wait()
        for d in range(1, LINE):
            gathered_z(u, d).wait_recv()
            gather_z(u, d).wait_send()
        gather_y(u, y).start()

    def stage_gather_y(u):
        gather_y(u, 1 - y).wait_recv()
        gather_y(u, y).wait_send()
        gather_core(u, core).start()

    def stage_gather_core(u):
        gather_core(u, 1 - core).wait_recv()
        gather_core(u, core).wait_send()

    stages = (
        (0, stage_core), (2, stage_a), (4, stage_b), (6, stage_z), (8, stage_gather_z),
        (10, stage_gather_y), (12, stage_gather_core),
    )

    def tick(t):
        for lag, stage in stages:
            if isinstance(t, int):
                if 0 <= t - lag < UNITS:
                    stage(t - lag)
            else:
                u = t - lag
                pl.when(jnp.logical_and(u >= 0, u < UNITS))(lambda stage=stage, u=u: stage(u))

    KV, E, Q, O, G, FIRST, CROSS_Q, A_SELF, SELF_OUT = (
        0, 4096, 5120, 5632, 6144, 6656, 7168, 7936, 8448
    )
    QS, KS, VS, DQ, DK, DV, HIDDEN, DA = 0, 512, 1536, 2560, 3072, 4096, 5120, 6144
    WQ, WK, WV = 0, 768, 1536

    def load(src, row, sem, into=pool):
        return pltpu.make_async_copy(src, into.at[pl.ds(row, src.shape[0])], load_sem.at[sem])

    def kv_copy(b, which):
        src = (keys_in, values_in)[which].at[pl.ds(pl.multiple_of(b * keys, 128), keys)]
        row = pl.multiple_of(lax.rem(b, 2) * (2 * keys) + which * keys, 128)
        return pltpu.make_async_copy(src, pool.at[pl.ds(row, keys)], kv_sem.at[lax.rem(b, 2), which])

    def e_copy(b):
        src = picked_rows.at[pl.ds(pl.multiple_of(b * keys, 128), keys)]
        return pltpu.make_async_copy(src, pool.at[pl.ds(E, keys)], e_sem)

    early = [
        load(q_cross, Q, 0), load(a_cross, O, 1), load(g_cross, G, 2), load(first_low, FIRST, 3),
        load(cross_query, CROSS_Q, 4), load(a_self, A_SELF, 5), load(self_out, SELF_OUT, 6),
    ]
    for which in range(2):
        kv_copy(jnp.int32(0), which).start()
    for copy in early:
        copy.start()
    ready = [(expand_grad, u) for u in range(4)] + [(reduce_grad, u) for u in range(4, 8)]
    ready.append((cross_out_grad, 8))
    corners = [(plane, part) for plane in range(2) for part in range(2)]
    for ref, unit in ready:
        for plane, part in corners:
            own_copy(ref, unit, plane, part).start()
    me.greet()
    for ref, unit in ready:
        for plane, part in corners:
            to_core(ref, unit, plane, part).start()
    both_sums = pool32
    both_sums[...] = jnp.zeros_like(both_sums)
    for copy in early[:3]:
        copy.wait()

    def at_row(row):
        return pl.ds(pl.multiple_of(row, 128), BLOCK_ROWS)

    def cross_step(i, carry):
        b, g = lax.div(i, pairs), lax.rem(i, pairs)

        @pl.when(g == 0)
        def _():
            for which in range(2):
                kv_copy(b, which).wait()
            e_copy(b).start()

            @pl.when(b + 1 < blocks)
            def _():
                for which in range(2):
                    kv_copy(b + 1, which).start()

        lanes = pl.ds(pl.multiple_of(g * PAIR, PAIR), PAIR)
        row = pl.multiple_of(b * BLOCK_ROWS, BLOCK_ROWS)
        key_row = pl.multiple_of(lax.rem(b, 2) * (2 * keys), 128)
        grad_q, grad_k, grad_v = pair_backward(
            pool[at_row(Q + row), lanes],
            pool[pl.ds(key_row, keys), lanes],
            pool[pl.ds(pl.multiple_of(key_row + keys, 128), keys), lanes],
            None,
            log_cross[b, pl.ds(g, 1)],
            pool[at_row(O + row), lanes],
            pool[at_row(G + row), lanes],
        )
        dq_cross[pl.ds(row, BLOCK_ROWS), lanes] = grad_q.astype(bf16)
        both[:, lanes] = grad_k.astype(bf16)
        both[:, pl.ds(pl.multiple_of(width + g * PAIR, PAIR), PAIR)] = grad_v.astype(bf16)

        @pl.when(g == pairs - 1)
        def _():
            e_copy(b).wait()
            both_sums[pl.ds(0, width)] += dot_tn(pool[pl.ds(E, keys)], both[:, :width])
            both_sums[pl.ds(width, width)] += dot_tn(pool[pl.ds(E, keys)], both[:, width:])

        pl.when(lax.rem(i, 4) == 0)(lambda: tick(lax.div(i, 4)))
        return carry

    lax.fori_loop(0, blocks * pairs, cross_step, 0)

    def hand_over(unit):
        ref = staged.at[unit % 2]
        for plane, part in corners:
            to_core(ref, unit, plane, part).start()
            own_copy(ref, unit, plane, part).start()

    def kept(unit):
        for plane, part in corners:
            own_copy(staged.at[unit % 2], unit, plane, part).wait()

    def left(unit):
        for plane, part in corners:
            to_core(staged.at[unit % 2], unit, plane, part).wait_send()

    def handed_over(unit):
        kept(unit)
        left(unit)

    late = [load(q_self, QS, 7), load(k_self, KS, 8), load(v_self, VS, 9), load(hidden, HIDDEN, 10)]
    for copy in late:
        copy.start()
    staged[1] = both_sums[pl.ds(0, width)].astype(bf16)
    hand_over(9)
    tick(6)
    staged[0] = both_sums[pl.ds(width, width)].astype(bf16)
    hand_over(10)
    g_copy = load(g_second, 0, 11, pool32)
    n_copy = load(first_normal, rows, 12, pool32)
    g_copy.start()
    n_copy.start()
    for copy in early[3:]:
        copy.wait()
    tick(7)
    handed_over(9)
    staged[1] = dot_tn(pool[pl.ds(FIRST, rows)], dq_cross[...]).astype(bf16)
    hand_over(11)

    g_copy.wait()
    n_copy.wait()
    normal = pool32[pl.ds(rows, rows)]
    grad_out = pool32[pl.ds(0, rows)] + dot_nt(dq_cross[...], pool[pl.ds(CROSS_Q, width)])
    scaled = grad_out * as_row(first_gain)
    grad_in = first_inverse[...] * (
        scaled
        - jnp.mean(scaled, axis=-1, keepdims=True)
        - normal * jnp.mean(scaled * normal, axis=-1, keepdims=True)
    )
    norm_all[...] = norms[...]
    norm_all[pl.ds(0, 1)] = jnp.sum(grad_out * normal, axis=0, keepdims=True)
    norm_all[pl.ds(1, 1)] = jnp.sum(grad_out, axis=0, keepdims=True)
    pool32[pl.ds(2 * rows, rows)] = grad_in
    grad_low = grad_in.astype(bf16)
    pool[pl.ds(DA, rows)] = dot_nt(grad_low, pool[pl.ds(SELF_OUT, width)]).astype(bf16)
    tick(8)
    handed_over(10)
    staged[0] = dot_tn(pool[pl.ds(A_SELF, rows)], grad_low).astype(bf16)
    hand_over(12)

    along_z = tuple(me.at(z=lax.rem(z + d, LINE)) for d in range(1, LINE))
    rounds = ((sibling,), (across,), (beside,), along_z)

    def norm_copies(which):
        first = min(which, 3)
        return [
            remote(
                norm_all, norm_in.at[first + k], norm_send.at[first + k], norm_recv.at[first + k], target
            )
            for k, target in enumerate(rounds[which])
        ]

    def norm_start(which):
        for copy in norm_copies(which):
            copy.start()

    def norm_finish(which):
        for copy in norm_copies(which):
            copy.wait()
        for k in range(len(rounds[which])):
            norm_all[...] += norm_in[which + k]

    norm_start(0)

    for copy in late:
        copy.wait()
    kept(11)
    kept(12)

    def self_step(g, carry):
        lanes = pl.ds(pl.multiple_of(g * PAIR, PAIR), PAIR)
        dk_sum[...] = jnp.zeros_like(dk_sum)
        dv_sum[...] = jnp.zeros_like(dv_sum)
        for local_row, seen, taken in self_blocks(2, hidden.shape[0], x):

            @pl.when(taken)
            def _():
                mine = pl.ds(local_row, BLOCK_ROWS)
                grad_q, grad_k, grad_v = pair_backward(
                    pool[pl.ds(QS + local_row, BLOCK_ROWS), lanes],
                    pool[pl.ds(KS, seen), lanes],
                    pool[pl.ds(VS, seen), lanes],
                    causal_edge(BLOCK_ROWS),
                    log_self[g, pl.ds(local_row // BLOCK_ROWS, 1)],
                    a_self_rows(local_row, lanes),
                    pool[pl.ds(DA + local_row, BLOCK_ROWS), lanes],
                )
                pool[pl.ds(DQ + local_row, BLOCK_ROWS), lanes] = grad_q.astype(bf16)
                dk_sum[pl.ds(0, seen)] += grad_k
                dv_sum[pl.ds(0, seen)] += grad_v

        pool[pl.ds(DK, hidden.shape[0]), lanes] = dk_sum[...].astype(bf16)
        pool[pl.ds(DV, hidden.shape[0]), lanes] = dv_sum[...].astype(bf16)
        pl.when(lax.rem(g, 2) == 1)(lambda: tick(9 + lax.div(g, 2)))
        return carry

    def a_self_rows(local_row, lanes):
        return pool[pl.ds(A_SELF + local_row, BLOCK_ROWS), lanes]

    lax.fori_loop(0, pairs, self_step, 0)
    norm_finish(0)
    norm_start(1)
    last_loads = [load(self_query, WQ, 13), load(self_key, WK, 14), load(self_value, WV, 15)]
    for copy in last_loads:
        copy.start()

    left(11)
    for copy in last_loads:
        copy.wait()

    def row_grads(at_chunk):
        dk = pool[pl.ds(pl.multiple_of(DK + at_chunk * chunk, 128), chunk)]
        dv = pool[pl.ds(pl.multiple_of(DV + at_chunk * chunk, 128), chunk)]
        return dot_nt(dk, pool[pl.ds(WK, width)]) + dot_nt(dv, pool[pl.ds(WV, width)])

    theirs[pl.ds(0, chunk)] = row_grads(1 - x).astype(bf16)
    theirs[pl.ds(chunk, chunk)] = row_grads(2 + x).astype(bf16)
    rows_copy = remote(theirs, rows_in, extra_send.at[0], extra_recv.at[0], across)
    got_copy = remote(rows_got, theirs_out, extra_send.at[1], extra_recv.at[1], across)
    rows_copy.start()
    low_rows = pl.ds(pl.multiple_of(HIDDEN + x * chunk, 128), chunk)
    high_rows = pl.ds(pl.multiple_of(HIDDEN + (3 - x) * chunk, 128), chunk)
    all_rows = hidden.shape[0]
    staged[1] = (
        dot_tn(pool[low_rows], pool[pl.ds(DQ, chunk)])
        + dot_tn(pool[high_rows], pool[pl.ds(DQ + chunk, chunk)])
    ).astype(bf16)
    hand_over(13)
    norm_finish(1)
    norm_start(2)
    left(12)
    staged[0] = dot_tn(pool[pl.ds(HIDDEN, all_rows)], pool[pl.ds(DK, all_rows)]).astype(bf16)
    hand_over(14)
    tick(12)
    handed_over(13)
    staged[1] = dot_tn(pool[pl.ds(HIDDEN, all_rows)], pool[pl.ds(DV, all_rows)]).astype(bf16)
    hand_over(15)
    norm_finish(2)
    norm_start(3)
    tick(13)
    handed_over(14)
    handed_over(15)

    tick(14)
    for k, at_chunk in enumerate((x, 3 - x)):
        piece = pl.ds(k * chunk, chunk)
        mine_out[piece] = (
            row_grads(at_chunk)
            + dot_nt(pool[pl.ds(DQ + k * chunk, chunk)], pool[pl.ds(WQ, width)])
            + pool32[pl.ds(2 * rows + k * chunk, chunk)]
        )
    norm_finish(3)
    norms_out[...] = norm_all[...]

    def last_step(t, carry):
        tick(t)

        @pl.when(t == 17)
        def _():
            rows_copy.wait()
            whole = mine_out[...] + rows_in[...].astype(f32)
            mine_out[...] = whole
            rows_got[...] = whole.astype(bf16)
            got_copy.start()

        return carry

    lax.fori_loop(15, LAST_TICK + 1, last_step, 0)
    got_copy.wait()
    for ref, unit in ready:
        for plane, part in corners:
            to_core(ref, unit, plane, part).wait_send()


def backward_by_kernel(*args):
    rows, width = args[6].shape
    all_rows = args[22].shape[0]
    norms = args[26]
    anywhere = pl.BlockSpec(memory_space=pl.ANY)
    vmem = pl.BlockSpec(memory_space=pltpu.VMEM)
    in_specs = [anywhere] * 27
    for i in (9, 14, 15, 21, 26):
        in_specs[i] = vmem
    dma = pltpu.SemaphoreType.DMA
    U, T, H, Z = UNITS, TILE, HALF, LINE - 1
    return pl.pallas_call(
        backward_kernel,
        out_shape=[
            jax.ShapeDtypeStruct((U, 2, T, T), bf16),
            jax.ShapeDtypeStruct((rows, width), f32),
            jax.ShapeDtypeStruct((rows, width), bf16),
            jax.ShapeDtypeStruct(norms.shape, f32),
        ],
        in_specs=in_specs,
        out_specs=[anywhere, vmem, anywhere, vmem],
        scratch_shapes=[
            pltpu.VMEM((SLOTS, 2, 2, H, T), bf16),
            pltpu.VMEM((U, 2, 2, H, T), bf16),
            pltpu.VMEM((U, 2, H, T), bf16),
            pltpu.VMEM((U, H, T), bf16),
            pltpu.VMEM((U, Z, PART, T), bf16),
            pltpu.VMEM((U, PART, T), bf16),
            pltpu.VMEM((9216, width), bf16),
            pltpu.VMEM((2 * width, width), f32),
            pltpu.VMEM((RET_BLOCKS * BLOCK_ROWS, 2 * width), bf16),
            pltpu.VMEM((2, width, width), bf16),
            pltpu.VMEM((rows, width), bf16),
            pltpu.VMEM((all_rows, PAIR), f32),
            pltpu.VMEM((all_rows, PAIR), f32),
            pltpu.VMEM((rows, width), bf16),
            pltpu.VMEM((rows, width), bf16),
            pltpu.VMEM((rows, width), bf16),
            pltpu.VMEM(norms.shape, f32),
            pltpu.VMEM((6,) + norms.shape, f32),
            dma((SLOTS, 4)), dma((U, 4)), dma((U, 4)), dma((U,)), dma((U,)), dma((U,)), dma((U,)),
            dma((U, Z)), dma((U, Z)), dma((U, Z)), dma((U, Z)), dma((U,)), dma((U,)), dma((U,)),
            dma((U,)), dma((U,)), dma((16,)), dma((2, 2)), dma, dma((2,)), dma((2,)), dma((6,)),
            dma((6,)),
        ],
        compiler_params=pltpu.CompilerParams(
            collective_id=1, has_side_effects=True, vmem_limit_bytes=BACKWARD_VMEM
        ),
        name="backward",
    )(*args)


def output_place(unit, core):
    row, column = share_corner(unit, core, 0)
    return UNIT_WEIGHTS[unit], row, column


def finish_kernel(*refs):
    sums, ours_in, theirs_in, made_in, made_theirs_in, norms = refs[:6]
    output, grad_hidden, outs, norm_outs = refs[6], refs[7], refs[8:18], refs[18:24]
    taken, given, ours, theirs, made, made_theirs, theirs_wide = refs[24:31]
    in_sem, out_sem, row_sem, row_out_sem = refs[31:]
    depth = taken.shape[0]
    shares = [(unit, core) for unit in range(UNITS) for core in range(2)]
    x = lax.axis_index("narrow")
    chunk = ours.shape[0] // 2

    def fetch(i):
        unit, core = shares[i]
        return pltpu.make_async_copy(sums.at[unit, core], taken.at[i % depth], in_sem.at[i % depth])

    def place(i):
        weight, row, column = output_place(*shares[i])
        return pltpu.make_async_copy(
            given.at[i % depth],
            outs[weight].at[pl.ds(row, TILE), pl.ds(column, TILE)],
            out_sem.at[i % depth],
        )

    pairs_in = ((ours_in, ours), (theirs_in, theirs), (made_in, made), (made_theirs_in, made_theirs))
    rows_in = [pltpu.make_async_copy(a, b, row_sem.at[k]) for k, (a, b) in enumerate(pairs_in)]

    def rows_out(src, dst, which, k, at):
        start = (at if k == 0 else 3 - at) * chunk
        return pltpu.make_async_copy(
            src.at[pl.ds(k * chunk, chunk)],
            dst.at[pl.ds(pl.multiple_of(start, 128), chunk)],
            row_out_sem.at[which, k],
        )

    moves = [
        rows_out(src, dst, which, k, at)
        for which, (src, dst, at) in enumerate(
            (
                (ours, grad_hidden, x),
                (theirs_wide, grad_hidden, 1 - x),
                (made, output, x),
                (made_theirs, output, 1 - x),
            )
        )
        for k in range(2)
    ]
    for i in range(depth - 1):
        fetch(i).start()
    for copy in rows_in:
        copy.start()
    for i in range(6):
        norm_outs[i][...] = norms[i]
    for i in range(len(shares)):
        if i + depth - 1 < len(shares):
            fetch(i + depth - 1).start()
        fetch(i).wait()
        if i >= depth:
            place(i - depth).wait()
        given[i % depth] = taken[i % depth].astype(f32)
        place(i).start()
        if i == depth:
            for copy in rows_in:
                copy.wait()
            theirs_wide[...] = theirs[...].astype(f32)
            for copy in moves:
                copy.start()
    for i in range(len(shares) - depth, len(shares)):
        place(i).wait()
    for copy in moves:
        copy.wait()


def finish(sums, ours, theirs, made, made_theirs, norms):
    rows, width = ours.shape
    shapes = [(2 * TILE, TILE)] * 3 + [(TILE, 2 * TILE)] + [(2 * TILE, TILE)] * 3
    shapes += [(TILE, 2 * TILE), (2 * TILE, 4 * TILE), (4 * TILE, 2 * TILE)]
    depth = 8
    anywhere = pl.BlockSpec(memory_space=pl.ANY)
    vmem = pl.BlockSpec(memory_space=pltpu.VMEM)
    return tuple(
        pl.pallas_call(
            finish_kernel,
            out_shape=[
                jax.ShapeDtypeStruct((2 * rows, width), bf16),
                jax.ShapeDtypeStruct((2 * rows, width), f32),
            ]
            + [jax.ShapeDtypeStruct(shape, f32) for shape in shapes]
            + [jax.ShapeDtypeStruct((width,), f32)] * 6,
            in_specs=[anywhere] * 5 + [vmem],
            out_specs=[anywhere] * 12 + [vmem] * 6,
            scratch_shapes=[
                pltpu.VMEM((depth, TILE, TILE), bf16),
                pltpu.VMEM((depth, TILE, TILE), f32),
                pltpu.VMEM((rows, width), f32),
                pltpu.VMEM((rows, width), bf16),
                pltpu.VMEM((rows, width), bf16),
                pltpu.VMEM((rows, width), bf16),
                pltpu.VMEM((rows, width), f32),
                pltpu.SemaphoreType.DMA((depth,)),
                pltpu.SemaphoreType.DMA((depth,)),
                pltpu.SemaphoreType.DMA((4,)),
                pltpu.SemaphoreType.DMA((4, 2)),
            ],
            compiler_params=pltpu.CompilerParams(vmem_limit_bytes=VMEM_LIMIT),
            name="finish",
        )(sums, ours, theirs, made, made_theirs, norms)
    )


FF_COLUMNS = 1024


def layer_norm(summed, norm_gain, norm_shift):
    centred = summed - jnp.mean(summed, axis=-1, keepdims=True)
    inverse = lax.rsqrt(jnp.mean(centred * centred, axis=-1, keepdims=True) + epsilon)
    normal = centred * inverse
    return normal * norm_gain + norm_shift, normal, inverse


def dense_kernel(
    a_cross, first, cotangent, cross_out, gain_two, shift_two, gain_three, shift_three, expand_in, reduce_in,
    out_ref, g_second, g_across, cross_out_grad, norms, expand_grad, reduce_grad, made_out,
    expand, reduce, activated, slope, expand_staged, reduce_staged,
    expand_sem, reduce_sem, expand_out_sem, reduce_out_sem, made_send, made_recv,
):
    me = Place()
    across = me.at(x=1 - me.x)
    gain_two, shift_two = as_row(gain_two), as_row(shift_two)
    gain_three, shift_three = as_row(gain_three), as_row(shift_three)
    chunk = cotangent.shape[0] // 4
    count = expand.shape[1] // FF_COLUMNS

    def piece(c):
        return pl.ds(c * FF_COLUMNS, FF_COLUMNS)

    def fetch_expand(c):
        return pltpu.make_async_copy(
            expand_in.at[:, piece(c)], expand.at[:, piece(c)], expand_sem.at[c]
        )

    def fetch_reduce(c):
        return pltpu.make_async_copy(reduce_in.at[piece(c)], reduce.at[piece(c)], reduce_sem.at[c])

    def put_expand(c):
        return pltpu.make_async_copy(
            expand_staged.at[c % 2], expand_grad.at[:, piece(c)], expand_out_sem.at[c % 2]
        )

    def put_reduce(c):
        return pltpu.make_async_copy(
            reduce_staged.at[c % 2], reduce_grad.at[piece(c)], reduce_out_sem.at[c % 2]
        )

    for c in range(count):
        fetch_expand(c).start()
        fetch_reduce(c).start()
    barrier = pltpu.get_barrier_semaphore()
    pl.semaphore_signal(barrier, inc=1, device_id=across, device_id_type=MESH)
    second, normal_two, inverse_two = layer_norm(
        first[...] + dot_nn(a_cross[...], cross_out[...]), gain_two, shift_two
    )
    second_low = second.astype(bf16)
    total = second
    for c in range(count):
        fetch_expand(c).wait()
        pre = dot_nn(second_low, expand[:, piece(c)])
        phi = 0.5 * (1.0 + lax.erf(pre * 0.7071067811865476))
        slope[:, piece(c)] = phi + pre * jnp.exp(-0.5 * pre * pre) * 0.3989422804014327
        activated[:, piece(c)] = (pre * phi).astype(bf16)
        fetch_reduce(c).wait()
        total = total + dot_nn(activated[:, piece(c)], reduce[piece(c)])
    final, normal, inverse = layer_norm(total, gain_three, shift_three)
    out_ref[...] = final.astype(bf16)
    pl.semaphore_wait(barrier, 1)
    made_copy = pltpu.make_async_remote_copy(
        src_ref=out_ref, dst_ref=made_out, send_sem=made_send, recv_sem=made_recv,
        device_id=across, device_id_type=MESH,
    )
    made_copy.start()
    grad = jnp.concatenate(
        [
            cotangent[pl.ds(pl.multiple_of(me.x * chunk, 128), chunk)],
            cotangent[pl.ds(pl.multiple_of((3 - me.x) * chunk, 128), chunk)],
        ],
        axis=0,
    ).astype(f32)
    norms[...] = jnp.zeros_like(norms)

    def back(grad, normal, inverse, gain, row):
        norms[pl.ds(row, 1)] = jnp.sum(grad * normal, axis=0, keepdims=True)
        norms[pl.ds(row + 1, 1)] = jnp.sum(grad, axis=0, keepdims=True)
        scaled = grad * gain
        return inverse * (
            scaled
            - jnp.mean(scaled, axis=-1, keepdims=True)
            - normal * jnp.mean(scaled * normal, axis=-1, keepdims=True)
        )

    grad = back(grad, normal, inverse, gain_three, 4)
    grad_low = grad.astype(bf16)
    for c in range(count):
        if c >= 2:
            put_reduce(c - 2).wait()
            put_expand(c - 2).wait()
        reduce_staged[c % 2] = dot_tn(activated[:, piece(c)], grad_low).astype(bf16)
        put_reduce(c).start()
        grad_pre = (dot_nt(grad_low, reduce[piece(c)]) * slope[:, piece(c)]).astype(bf16)
        expand_staged[c % 2] = dot_tn(second_low, grad_pre).astype(bf16)
        put_expand(c).start()
        grad = grad + dot_nt(grad_pre, expand[:, piece(c)])
    grad = back(grad, normal_two, inverse_two, gain_two, 2)
    g_second[...] = grad
    grad_low = grad.astype(bf16)
    cross_out_grad[...] = dot_tn(a_cross[...], grad_low).astype(bf16)
    g_across[...] = dot_nt(grad_low, cross_out[...]).astype(bf16)
    for c in range(count - 2, count):
        put_reduce(c).wait()
        put_expand(c).wait()
    made_copy.wait()


def dense_by_kernel(a_cross, first, cotangent, cross_out, norm_params, expand, reduce):
    rows, width = first.shape
    hidden_units = expand.shape[1]
    count = hidden_units // FF_COLUMNS
    anywhere = pl.BlockSpec(memory_space=pl.ANY)
    vmem = pl.BlockSpec(memory_space=pltpu.VMEM)
    dma = pltpu.SemaphoreType.DMA
    return pl.pallas_call(
        dense_kernel,
        out_shape=[
            jax.ShapeDtypeStruct((rows, width), bf16),
            jax.ShapeDtypeStruct((rows, width), f32),
            jax.ShapeDtypeStruct((rows, width), bf16),
            jax.ShapeDtypeStruct((width, width), bf16),
            jax.ShapeDtypeStruct((8, width), f32),
            jax.ShapeDtypeStruct(expand.shape, bf16),
            jax.ShapeDtypeStruct(reduce.shape, bf16),
            jax.ShapeDtypeStruct((rows, width), bf16),
        ],
        in_specs=[vmem] * 8 + [anywhere] * 2,
        out_specs=[vmem] * 5 + [anywhere] * 3,
        scratch_shapes=[
            pltpu.VMEM(expand.shape, bf16),
            pltpu.VMEM(reduce.shape, bf16),
            pltpu.VMEM((rows, hidden_units), bf16),
            pltpu.VMEM((rows, hidden_units), f32),
            pltpu.VMEM((2, width, FF_COLUMNS), bf16),
            pltpu.VMEM((2, FF_COLUMNS, width), bf16),
            dma((count,)),
            dma((count,)),
            dma((2,)),
            dma((2,)),
            dma,
            dma,
        ],
        compiler_params=pltpu.CompilerParams(
            collective_id=2, has_side_effects=True, vmem_limit_bytes=VMEM_LIMIT
        ),
        name="dense",
    )(a_cross, first, cotangent, cross_out, *norm_params, expand, reduce)


def by_kernels(narrow):
    return lax.axis_size("wide") == 4 * LINE and narrow == 2


def gather_all(encoded, weights):
    everything = lax.all_gather(encoded, "wide", tiled=True)
    full = tuple(
        lax.all_gather(w, "narrow", axis=1 if i in COLUMNS else 0, tiled=True)
        for i, w in enumerate(weights)
    )
    return everything, full


def reduce_all(grads):
    shares = tuple(
        lax.psum_scatter(
            g.astype(bf16), "narrow", scatter_dimension=1 if i in COLUMNS else 0, tiled=True
        )
        for i, g in enumerate(grads)
    )
    return tuple(s.astype(f32) for s in lax.psum(shares, "wide"))


def local(
    hidden,
    encoded,
    retrieved,
    self_query,
    self_key,
    self_value,
    self_out,
    cross_query,
    cross_key,
    cross_value,
    cross_out,
    expand_weight,
    reduce_weight,
    first_gain,
    first_shift,
    second_gain,
    second_shift,
    third_gain,
    third_shift,
    cotangent,
):
    tok_rows, width = hidden.shape
    narrow = lax.axis_size("narrow")
    at = lax.axis_index("narrow").astype(jnp.int32)
    chunk = tok_rows // (2 * narrow)

    def own(rows, size=chunk):
        low = lax.dynamic_slice_in_dim(rows, at * size, size)
        high = lax.dynamic_slice_in_dim(rows, (2 * narrow - 1 - at) * size, size)
        return jnp.concatenate([low, high], axis=0)

    where_at = at.reshape(1)
    picked = own(retrieved, chunk // BLOCK_ROWS).reshape(-1)
    if by_kernels(narrow):
        everything, full, kept = forward_by_kernel(
            encoded,
            (
                self_query,
                self_key,
                self_value,
                self_out,
                cross_query,
                cross_key,
                cross_value,
                cross_out,
                expand_weight,
                reduce_weight,
            ),
            hidden,
            first_gain,
            first_shift,
        )
        query_self, key_self, value_self, blend_self, first, first_normal, first_low = kept[:7]
        query_cross, log_self, first_inverse = kept[7:]
        (self_query, self_key, self_value, self_out, cross_query, cross_key, cross_value) = full[:7]
        (cross_out, expand_weight, reduce_weight) = full[7:]
        blend_cross, log_cross, key_cross, value_cross, picked_rows = cross_forward(
            picked, everything, cross_key, cross_value, query_cross
        )
        made = dense_by_kernel(
            blend_cross,
            first,
            cotangent,
            cross_out,
            (second_gain, second_shift, third_gain, third_shift),
            expand_weight,
            reduce_weight,
        )
        output, grad_second_in, grad_blend_cross, cross_out_grad, norms = made[:5]
        expand_grad, reduce_grad, made_theirs = made[5:]
        sums, grad_mine, grad_theirs, norm_sums = backward_by_kernel(
            expand_grad,
            reduce_grad,
            cross_out_grad,
            picked_rows,
            key_cross,
            value_cross,
            query_cross,
            blend_cross,
            grad_blend_cross,
            log_cross,
            first_low,
            cross_query,
            grad_second_in,
            first_normal,
            first_inverse,
            first_gain,
            blend_self,
            self_out,
            query_self,
            key_self,
            value_self,
            log_self,
            hidden,
            self_query,
            self_key,
            self_value,
            norms,
        )

        return finish(sums, grad_mine, grad_theirs, output, made_theirs, norm_sums)

    everything, full = gather_all(
        encoded,
        (
            self_query,
            self_key,
            self_value,
            self_out,
            cross_query,
            cross_key,
            cross_value,
            cross_out,
            expand_weight,
            reduce_weight,
        ),
    )
    (
        self_query,
        self_key,
        self_value,
        self_out,
        cross_query,
        cross_key,
        cross_value,
        cross_out,
        expand_weight,
        reduce_weight,
    ) = full
    mine = own(hidden)
    grad_final = own(cotangent).astype(f32)

    query_self = project(mine, self_query).astype(bf16)
    key_self = project(hidden, self_key).astype(bf16)
    value_self = project(hidden, self_value).astype(bf16)
    blend_self, log_self = self_forward(narrow, where_at, query_self, key_self, value_self)
    first, first_normal, first_inverse = norm_forward(
        mine.astype(f32) + project(blend_self, self_out), first_gain, first_shift
    )
    first_low = first.astype(bf16)
    query_cross = project(first_low, cross_query).astype(bf16)
    blend_cross, log_cross, key_cross, value_cross, picked_rows = cross_forward(
        picked, everything, cross_key, cross_value, query_cross
    )
    second, second_normal, second_inverse = norm_forward(
        first + project(blend_cross, cross_out), second_gain, second_shift
    )
    second_low = second.astype(bf16)
    pre_act = project(second_low, expand_weight)
    activated = jax.nn.gelu(pre_act, approximate=False).astype(bf16)
    final, third_normal, third_inverse = norm_forward(
        second + project(activated, reduce_weight), third_gain, third_shift
    )
    output = final.astype(bf16)

    grad_third, third_gain_grad, third_shift_grad = norm_backward(
        grad_final, third_normal, third_inverse, third_gain
    )
    grad_ffn = grad_third.astype(bf16)
    reduce_grad = grad_weight(activated, grad_ffn)
    grad_pre = (grad_input(grad_ffn, reduce_weight) * gelu_slope(pre_act)).astype(bf16)
    expand_grad = grad_weight(second_low, grad_pre)
    grad_second = grad_third + grad_input(grad_pre, expand_weight)
    grad_second_in, second_gain_grad, second_shift_grad = norm_backward(
        grad_second, second_normal, second_inverse, second_gain
    )
    grad_cross = grad_second_in.astype(bf16)
    cross_out_grad = grad_weight(blend_cross, grad_cross)
    grad_blend_cross = grad_input(grad_cross, cross_out).astype(bf16)
    grad_query_cross, cross_key_grad, cross_value_grad = cross_backward(
        picked,
        everything,
        key_cross,
        value_cross,
        query_cross,
        log_cross,
        blend_cross,
        grad_blend_cross,
    )
    cross_query_grad = grad_weight(first_low, grad_query_cross)
    grad_first = grad_second_in + grad_input(grad_query_cross, cross_query)
    grad_first_in, first_gain_grad, first_shift_grad = norm_backward(
        grad_first, first_normal, first_inverse, first_gain
    )
    grad_self = grad_first_in.astype(bf16)
    self_out_grad = grad_weight(blend_self, grad_self)
    grad_blend_self = grad_input(grad_self, self_out).astype(bf16)
    grad_query_self, grad_key_self, grad_value_self = self_backward(
        narrow, where_at, query_self, key_self, value_self, log_self, blend_self, grad_blend_self
    )
    self_query_grad = grad_weight(mine, grad_query_self)
    self_key_grad = grad_weight(hidden, grad_key_self)
    self_value_grad = grad_weight(hidden, grad_value_self)
    grad_rows = grad_input(grad_key_self, self_key) + grad_input(grad_value_self, self_value)
    grad_own = grad_first_in + grad_input(grad_query_self, self_query)

    def spread(rows):
        empty = jnp.zeros((tok_rows, width), rows.dtype)
        placed = lax.dynamic_update_slice_in_dim(empty, rows[:chunk], at * chunk, 0)
        return lax.dynamic_update_slice_in_dim(
            placed, rows[chunk:], (2 * narrow - 1 - at) * chunk, 0
        )

    grad_hidden = lax.psum((grad_rows + spread(grad_own)).astype(bf16), "narrow").astype(f32)
    output = lax.psum(spread(output), "narrow")
    weight_grads = reduce_all(
        (
            self_query_grad,
            self_key_grad,
            self_value_grad,
            self_out_grad,
            cross_query_grad,
            cross_key_grad,
            cross_value_grad,
            cross_out_grad,
            expand_grad,
            reduce_grad,
        )
    )
    norm_grads = lax.psum(
        jnp.stack(
            [
                first_gain_grad,
                first_shift_grad,
                second_gain_grad,
                second_shift_grad,
                third_gain_grad,
                third_shift_grad,
            ]
        ),
        ("wide", "narrow"),
    )
    return (output, grad_hidden) + weight_grads + tuple(norm_grads[i] for i in range(6))


def solution(mesh):
    rows = P("wide", None)
    columns_split = P(None, "narrow")
    rows_split = P("narrow", None)
    weights = (columns_split,) * 3 + (rows_split,) + (columns_split,) * 3 + (rows_split,)
    weights += (columns_split, rows_split)
    return jax.shard_map(
        local,
        mesh=mesh,
        in_specs=(rows, rows, rows) + weights + (P(),) * 6 + (rows,),
        out_specs=(rows, rows) + weights + (P(),) * 6,
        check_vma=False,
    )
```
